32 devices in a mesh: shard: 4 (over z), ctx: 2 (over core), tp: 4 (over y, x).
Axes of the slice: x: 2, y: 2, z: 4, core: 2. Of those that a mesh axis runs over, the one named last changes fastest.
Arguments:
- hidden: bfloat16 [4, 2048, 1024], P('shard', 'ctx'), may hold values from -6 to 6
- cotangent: bfloat16 [4, 2048, 1024], P('shard', 'ctx'), may hold values from -6 to 6
- lengths: int32 [4], P('shard'), may hold values from 1024 to 2048, as said below
- norm1_gain: bfloat16 [1024], P(('shard', 'ctx')), may hold values from 0.25 to 1.75
- w_z: bfloat16 [1024, 1536], P(('shard', 'ctx'), 'tp'), may hold values from -0.1875 to 0.1875
- w_x: bfloat16 [1024, 1536], P(('shard', 'ctx'), 'tp'), may hold values from -0.1875 to 0.1875
- w_shared: bfloat16 [1024, 512], P(('shard', 'ctx')), may hold values from -0.1875 to 0.1875
- w_dt: bfloat16 [1024, 24], P(('shard', 'ctx')), may hold values from -0.1875 to 0.1875
- dt_bias: bfloat16 [24], replicated, may hold values from -10 to -3
- a_log: bfloat16 [24], replicated, may hold values from -1 to 1
- d_skip: bfloat16 [24], replicated, may hold values from 0.5 to 1.5
- conv_w: bfloat16 [4, 1792], replicated, may hold values from -3 to 3
- conv_b: bfloat16 [1792], replicated, may hold values from -0.5 to 0.5
- gated_gain: bfloat16 [1536], replicated, may hold values from 0.25 to 1.75
- w_out: bfloat16 [1536, 1024], P('tp', ('shard', 'ctx')), may hold values from -0.15625 to 0.15625
- w_q: bfloat16 [1024, 512], P(('shard', 'ctx'), 'tp'), may hold values from -0.1875 to 0.1875
- w_o: bfloat16 [512, 1024], P('tp', ('shard', 'ctx')), may hold values from -2 to 2
- norm2_gain: bfloat16 [1024], P(('shard', 'ctx')), may hold values from 0.25 to 1.75
- w_gate: bfloat16 [1024, 2048], P(('shard', 'ctx'), 'tp'), may hold values from -0.1875 to 0.1875
- w_up: bfloat16 [1024, 2048], P(('shard', 'ctx'), 'tp'), may hold values from -0.1875 to 0.1875
- w_down: bfloat16 [2048, 1024], P('tp', ('shard', 'ctx')), may hold values from -0.125 to 0.125
Outputs:
- output: bfloat16 [4, 2048, 1024], P('shard', 'ctx', 'tp')
- grad_hidden: float32 [4, 2048, 1024], P('shard', 'ctx')
- grad_norm1_gain: float32 [1024], P(('shard', 'ctx', 'tp'))
- grad_w_z: float32 [1024, 1536], P(('shard', 'ctx'), 'tp')
- grad_w_x: float32 [1024, 1536], P(('shard', 'ctx'), 'tp')
- grad_w_shared: float32 [1024, 512], P(('shard', 'ctx', 'tp'))
- grad_w_dt: float32 [1024, 24], P(('shard', 'ctx', 'tp'))
- grad_dt_bias: float32 [24], replicated
- grad_a_log: float32 [24], replicated
- grad_d_skip: float32 [24], replicated
- grad_conv_w: float32 [4, 1792], replicated
- grad_conv_b: float32 [1792], replicated
- grad_gated_gain: float32 [1536], replicated
- grad_w_out: float32 [1536, 1024], P('tp', ('shard', 'ctx'))
- grad_w_q: float32 [1024, 512], P(('shard', 'ctx'), 'tp')
- grad_w_o: float32 [512, 1024], P('tp', ('shard', 'ctx'))
- grad_norm2_gain: float32 [1024], P(('shard', 'ctx', 'tp'))
- grad_w_gate: float32 [1024, 2048], P(('shard', 'ctx'), 'tp')
- grad_w_up: float32 [1024, 2048], P(('shard', 'ctx'), 'tp')
- grad_w_down: float32 [2048, 1024], P('tp', ('shard', 'ctx'))
The draws below stay inside these ranges and needn't reach their ends.
Inputs may be any that keep to these rules, and one draw needn't show every extreme that they name: `lengths`: each slot holds one sequence from position 0; positions from its length on are padding. In every draw some slot has exactly 2048 positions and another exactly 1024.
All inputs are finite; a program needn't handle non-finite values.
Results may differ from the reference program's by a relative error of at most 0.015.
Values may be sent and summed in bfloat16 or wider, within the bound.
A program may use at most 192 MiB of HBM per device.

```python
import jax
import jax.numpy as jnp
from jax import lax

D = 1024
H = 24
P_SIZE = 64
N = 128
NQ = 8
KV = 2
HD = 64
FF = 2048
CONVW = 4
SCAN_BLOCK = 256
QUERY_BLOCK = 512
SLOT = 2048
DI = 1536
CONV = 1792
SHARED = 512
SLOTS = 4


def draw_lengths(key, part):
    first_key, second_key, third_key = jax.random.split(key, 3)
    drawn = jax.random.randint(first_key, (SLOTS,), SLOT // 2, SLOT + 1)
    longest = jax.random.randint(second_key, (), 0, SLOTS)
    stride = jax.random.randint(third_key, (), 1, SLOTS)
    shortest = (longest + stride) % SLOTS
    slot_ids = jnp.arange(SLOTS)
    drawn = jnp.where(slot_ids == longest, SLOT, drawn)
    drawn = jnp.where(slot_ids == shortest, SLOT // 2, drawn)
    return drawn.astype(jnp.int32)


def level_of(own_key, dims, pieces, least, high):
    def one(position, parts):
        draws = jax.random.uniform(jax.random.fold_in(jax.random.fold_in(own_key, 6), position), (parts,), jnp.float32, least / len(pieces), high / len(pieces))
        return jnp.repeat(jnp.exp(draws), dims[position] // parts).reshape((-1,) + (1,) * (len(dims) - position - 1))

    factor_of = one(*pieces[0])
    for cut in pieces[1:]:
        factor_of = factor_of * one(*cut)
    return factor_of


def gaussian(stream_key, dims, scale, limit, cuts=(), kind=jnp.bfloat16):
    array = jax.random.normal(stream_key, dims, jnp.float32) * scale
    if len(cuts) > 0:
        array = level_of(stream_key, dims, cuts, -0.22, 0.18) * array
    return jnp.clip(array, min=-limit, max=limit).astype(kind)


def setup_inputs(seed: int = 0) -> dict:
    streams_of = jax.random.split(jax.random.key(seed), 22)
    hidden = gaussian(streams_of[0], (SLOTS, SLOT, D), 1.0, 6.0, ((0, 4), (1, 2)))
    cotangent = gaussian(streams_of[1], (SLOTS, SLOT, D), 1.0, 6.0, ((0, 4), (1, 2)))
    lengths = draw_lengths(jax.random.fold_in(streams_of[21], 71), 0)
    norm1_gain = jnp.clip(1.0 + 0.15 * jax.random.normal(streams_of[3], (D,), jnp.float32), 0.25, 1.75).astype(jnp.bfloat16)
    w_z = gaussian(streams_of[4], (D, DI), D ** -0.5, 0.1875, ((0, 8), (1, 4)))
    w_x = gaussian(streams_of[5], (D, DI), D ** -0.5, 0.1875, ((0, 8), (1, 4)))
    w_shared = gaussian(streams_of[6], (D, SHARED), D ** -0.5, 0.1875, ((0, 8),))
    w_dt = gaussian(streams_of[7], (D, H), D ** -0.5, 0.1875, ((0, 8),))
    dt_bias = jnp.clip(jax.random.uniform(streams_of[8], (H,), jnp.float32, -10.0, -3.0), -10.0, -3.0).astype(jnp.bfloat16)
    a_log = jnp.clip(jax.random.uniform(streams_of[9], (H,), jnp.float32, -1.0, 1.0), -1.0, 1.0).astype(jnp.bfloat16)
    d_skip = jnp.clip(jax.random.uniform(streams_of[10], (H,), jnp.float32, 0.5, 1.5), 0.5, 1.5).astype(jnp.bfloat16)
    conv_w = gaussian(streams_of[11], (CONVW, CONV), 0.5, 3.0)
    conv_b = jnp.clip(jax.random.uniform(streams_of[12], (CONV,), jnp.float32, -0.5, 0.5), -0.5, 0.5).astype(jnp.bfloat16)
    gated_gain = jnp.clip(1.0 + 0.15 * jax.random.normal(streams_of[13], (DI,), jnp.float32), 0.25, 1.75).astype(jnp.bfloat16)
    w_out = gaussian(streams_of[14], (DI, D), DI ** -0.5, 0.15625, ((0, 4), (1, 8)))
    w_q = gaussian(streams_of[15], (D, NQ * HD), D ** -0.5, 0.1875, ((0, 8), (1, 4)))
    w_o = gaussian(streams_of[16], (NQ * HD, D), (NQ * HD // 64) ** -0.5, 2.0, ((0, 4), (1, 8)))
    norm2_gain = jnp.clip(1.0 + 0.15 * jax.random.normal(streams_of[17], (D,), jnp.float32), 0.25, 1.75).astype(jnp.bfloat16)
    w_gate = gaussian(streams_of[18], (D, FF), D ** -0.5, 0.1875, ((0, 8), (1, 4)))
    w_up = gaussian(streams_of[19], (D, FF), D ** -0.5, 0.1875, ((0, 8), (1, 4)))
    w_down = gaussian(streams_of[20], (FF, D), FF ** -0.5, 0.125, ((0, 4), (1, 8)))
    return dict(hidden=hidden, cotangent=cotangent, lengths=lengths, norm1_gain=norm1_gain, w_z=w_z, w_x=w_x, w_shared=w_shared, w_dt=w_dt, dt_bias=dt_bias, a_log=a_log, d_skip=d_skip, conv_w=conv_w, conv_b=conv_b, gated_gain=gated_gain, w_out=w_out, w_q=w_q, w_o=w_o, norm2_gain=norm2_gain, w_gate=w_gate, w_up=w_up, w_down=w_down)


norm_epsilon = 1e-05
rope_base = 10000.0
mask_fill = -1e+30
highest = lax.Precision.HIGHEST

@jax.custom_vjp
def low(v):
    return lax.optimization_barrier(v.astype(jnp.bfloat16)).astype(jnp.float32)

@jax.custom_vjp
def low_back(v):
    return v

def low_keep(v):
    return (low(v), None)

def low_pass(kept, grad):
    return (grad,)

def back_keep(v):
    return (v, None)

def back_low(kept, grad):
    return (low(grad),)
low.defvjp(low_keep, low_pass)
low_back.defvjp(back_keep, back_low)

def rotary_tables(positions, width):
    freq_index = jnp.arange(width // 2, dtype=jnp.float32)
    inverse = rope_base ** (-2.0 * freq_index / width)
    angles = positions[:, None] * inverse[None, :]
    angles = jnp.concatenate([angles, angles], axis=-1)
    return (jnp.cos(angles), jnp.sin(angles))

def turn_half(values):
    half_width = values.shape[-1] // 2
    return jnp.concatenate([-values[..., half_width:], values[..., :half_width]], axis=-1)

def rotate(values, cosine, sine):
    return values * cosine + turn_half(values) * sine

def causal_conv(inputs, history, kernel, offset):
    padded = jnp.concatenate([history, inputs], axis=1)
    row_count = inputs.shape[1]
    result = offset + jnp.zeros_like(inputs)
    for tap_index in range(kernel.shape[0]):
        result = result + kernel[tap_index] * padded[:, tap_index:tap_index + row_count]
    return result

def state_blocks(values, in_map, out_map, steps, rates, skip, start, block):
    batch_count, row_count, head_count, head_width = values.shape
    block_count = row_count // block
    state_width = in_map.shape[-1]
    value_blocks = values.reshape(batch_count, block_count, block, head_count, head_width)
    in_blocks = in_map.reshape(batch_count, block_count, block, state_width)
    out_blocks = out_map.reshape(batch_count, block_count, block, state_width)
    step_blocks = steps.reshape(batch_count, block_count, block, head_count)
    cumul = jnp.cumsum(rates.reshape(batch_count, block_count, block, head_count), axis=2)
    totals = cumul[:, :, -1, :]
    gram = jnp.einsum('bcin,bcjn->bcij', out_blocks, in_blocks, precision=highest)
    lower_mask = jnp.arange(block)[:, None] >= jnp.arange(block)[None, :]
    differ = cumul[:, :, :, None, :] - cumul[:, :, None, :, :]
    decay = jnp.exp(jnp.where(lower_mask[None, None, :, :, None], differ, mask_fill))
    mixing = gram[..., None] * decay * step_blocks[:, :, None, :, :]
    inner = jnp.einsum('bcijh,bcjhp->bcihp', mixing, value_blocks, precision=highest)
    weight_end = jnp.exp(totals[:, :, None, :] - cumul) * step_blocks
    states = jnp.einsum('bcjh,bcjn,bcjhp->bchnp', weight_end, in_blocks, value_blocks, precision=highest)

    def advance(carry, packed):
        total_now, state_now = packed
        return (jnp.exp(total_now)[..., None, None] * carry + state_now, carry)
    final_state, starts = lax.scan(advance, start, (jnp.moveaxis(totals, 1, 0), jnp.moveaxis(states, 1, 0)))
    starts = jnp.moveaxis(starts, 0, 1)
    carried = jnp.einsum('bcin,bchnp->bcihp', out_blocks, starts, precision=highest) * jnp.exp(cumul)[..., None]
    output = inner + carried + skip[:, None] * value_blocks
    offsets = jnp.cumsum(totals, axis=1) - totals
    cum_device = (cumul + offsets[:, :, None, :]).reshape(batch_count, row_count, head_count)
    decay_all = jnp.exp(lax.optimization_barrier(jnp.sum(totals, axis=1)))
    return (output.reshape(batch_count, row_count, head_count, head_width), final_state, cum_device, decay_all)

def matmul(lhs_matrix, rhs_matrix):
    return jnp.dot(lhs_matrix, rhs_matrix, precision=highest, preferred_element_type=jnp.float32)

def slot_layer(hidden_row, length, weights):
    norm1_gain, w_z, w_x, w_shared, w_dt, dt_bias, a_log, d_skip, conv_w, conv_b, gated_gain, w_out, w_q, w_o, norm2_gain, w_gate, w_up, w_down = weights
    scale_one = lax.rsqrt(lax.optimization_barrier(jnp.mean(hidden_row * hidden_row, -1, keepdims=True)) + norm_epsilon)
    normed = low(hidden_row * scale_one * norm1_gain)
    gate_z = low_back(matmul(normed, w_z))
    inner_x = low_back(matmul(normed, w_x))
    shared = matmul(normed, w_shared)
    step_raw = low_back(matmul(normed, w_dt))
    conv_in = low(jnp.concatenate([inner_x, shared[:, :2 * N]], axis=-1))
    history = jnp.zeros((1, CONVW - 1, DI + 2 * N), jnp.float32)
    conv_act = jax.nn.silu(causal_conv(conv_in[None], history, conv_w, conv_b))[0]
    values = conv_act[:, :DI].reshape(SLOT, H, P_SIZE)
    in_map = conv_act[:, DI:DI + N]
    out_map = conv_act[:, DI + N:]
    steps = jax.nn.softplus(step_raw + dt_bias)
    rates = steps * -jnp.exp(a_log)
    start = jnp.zeros((1, H, N, P_SIZE), jnp.float32)
    ssd_out = state_blocks(values[None], in_map[None], out_map[None], steps[None], rates[None], d_skip, start, SCAN_BLOCK)[0][0]
    gated = ssd_out.reshape(SLOT, DI) * jax.nn.silu(gate_z)
    mamba_scale = lax.rsqrt(lax.optimization_barrier(jnp.sum(gated * gated, -1, keepdims=True)) / DI + norm_epsilon)
    projected = low_back(matmul(low(gated * gated_gain), w_out))
    mamba = mamba_scale * projected
    positions = jnp.arange(SLOT, dtype=jnp.int32).astype(jnp.float32)
    cosine, sine = rotary_tables(positions, HD)
    query_lin = low_back(matmul(normed, w_q)).reshape(SLOT, NQ, HD)
    queries = low(rotate(query_lin, cosine[:, None], sine[:, None]))
    key_lin = shared[:, 2 * N:2 * N + KV * HD].reshape(SLOT, KV, HD)
    keys = low(rotate(key_lin, cosine[:, None], sine[:, None]))
    values_kv = low(shared[:, 2 * N + KV * HD:].reshape(SLOT, KV, HD))
    keys = jnp.repeat(keys, NQ // KV, axis=1)
    values_kv = jnp.repeat(values_kv, NQ // KV, axis=1)
    key_pos = jnp.arange(SLOT, dtype=jnp.int32)
    attn_scale = HD ** (-0.5)

    def attend(block_index):
        query_block = lax.dynamic_slice_in_dim(queries, block_index * QUERY_BLOCK, QUERY_BLOCK, 0)
        scores = low_back(jnp.einsum('qhd,khd->hqk', query_block, keys, precision=highest) * attn_scale)
        query_pos = block_index * QUERY_BLOCK + jnp.arange(QUERY_BLOCK, dtype=jnp.int32)
        allowed = (key_pos[None, :] <= query_pos[:, None]) & (key_pos[None, :] < length)
        masked = jnp.where(allowed[None], scores, mask_fill)
        peak = lax.optimization_barrier(jnp.max(masked, axis=-1, keepdims=True))
        expo = jnp.exp(masked - peak)
        probs = expo / lax.optimization_barrier(jnp.sum(expo, axis=-1, keepdims=True))
        return jnp.einsum('hqk,khd->qhd', low(probs), values_kv, precision=highest)
    attended = lax.map(jax.checkpoint(attend), jnp.arange(SLOT // QUERY_BLOCK, dtype=jnp.int32))
    attended = attended.reshape(SLOT, NQ * HD)
    attn = low_back(matmul(low(low_back(attended)), w_o))
    resid = hidden_row + mamba + attn
    scale_two = lax.rsqrt(lax.optimization_barrier(jnp.mean(resid * resid, -1, keepdims=True)) + norm_epsilon)
    normed_two = low(resid * scale_two * norm2_gain)
    gate_h = low_back(matmul(normed_two, w_gate))
    up_h = low_back(matmul(normed_two, w_up))
    act_low = low(jax.nn.silu(gate_h) * up_h)
    return resid + matmul(act_low, w_down)

def reference(hidden, cotangent, lengths, norm1_gain, w_z, w_x, w_shared, w_dt, dt_bias, a_log, d_skip, conv_w, conv_b, gated_gain, w_out, w_q, w_o, norm2_gain, w_gate, w_up, w_down):
    weights = tuple((weight_item.astype(jnp.float32) for weight_item in (norm1_gain, w_z, w_x, w_shared, w_dt, dt_bias, a_log, d_skip, conv_w, conv_b, gated_gain, w_out, w_q, w_o, norm2_gain, w_gate, w_up, w_down)))
    inputs = hidden.astype(jnp.float32)

    def whole(layer_in, layer_weights):

        def one_slot(packed):
            return slot_layer(packed[0], packed[1], layer_weights)
        return lax.map(jax.checkpoint(one_slot), (layer_in, lengths))
    outputs, pullback = jax.vjp(whole, inputs, weights)
    keep = (jnp.arange(SLOT, dtype=jnp.int32)[None, :] < lengths[:, None]).astype(jnp.float32)
    grad_in, grads = pullback(cotangent.astype(jnp.float32) * keep[:, :, None])
    return (outputs.astype(jnp.bfloat16), grad_in, grads[0], grads[1], grads[2], grads[3], grads[4], grads[5], grads[6], grads[7], grads[8], grads[9], grads[10], grads[11], grads[12], grads[13], grads[14], grads[15], grads[16], grads[17])
```

```python
import functools

import jax
import jax.numpy as jnp
from jax import lax
from jax.experimental import pallas as pl
from jax.experimental.pallas import tpu as pltpu
from jax.sharding import PartitionSpec as P

H = 24
P_SIZE = 64
N = 128
NQ = 8
KV = 2
HD = 64
CONVW = 4
DI = 1536
D = 1024
FFL = 512
TP = 4
HL = H // TP
WI = HL * P_SIZE
CH = WI + 2 * N
L = 256

CZ, CX, CM, CQ, CK, CS, CA = 0, 384, 768, 1024, 1152, 1280, 1408
GAIN_COL = 24
CO, CW, CG, CU, CD, CB = 0, 384, 512, 1024, 1536, 2048

EPS = 1e-05
rope_base = 10000.0
FILL = -1e30
HI = lax.Precision.HIGHEST
MESH = pl.DeviceIdType.MESH
f32 = jnp.float32
bf16 = jnp.bfloat16
VLIMIT = 60 * 1024 * 1024


def nn(a, b, precision=None):
    return lax.dot_general(
        a, b, (((1,), (0,)), ((), ())), precision=precision, preferred_element_type=f32
    )


def nt(a, b, precision=None):
    return lax.dot_general(
        a, b, (((1,), (1,)), ((), ())), precision=precision, preferred_element_type=f32
    )


def tn(a, b, precision=None):
    return lax.dot_general(
        a, b, (((0,), (0,)), ((), ())), precision=precision, preferred_element_type=f32
    )


def rows_of(index, size=L):
    return pl.ds(pl.multiple_of(index * size, size), size)


def remote(src, dst, send, recv, **where):
    return pltpu.make_async_remote_copy(
        src_ref=src,
        dst_ref=dst,
        send_sem=send,
        recv_sem=recv,
        device_id=where,
        device_id_type=MESH,
    )


def iota(shape, dim):
    return lax.broadcasted_iota(jnp.int32, shape, dim)


def loop(n, body):
    lax.fori_loop(0, n, lambda i, c: (body(i), c)[1], 0)


def greet(shards, tp_too, ctx_too=True, shard_too=True):
    barrier = pltpu.get_barrier_semaphore()
    count = 0
    z, c, t = lax.axis_index("shard"), lax.axis_index("ctx"), lax.axis_index("tp")
    if ctx_too:
        pl.semaphore_signal(barrier, inc=1, device_id={"ctx": 1 - c}, device_id_type=MESH)
        count += 1
    if shard_too:

        def one(k):
            pl.semaphore_signal(
                barrier, inc=1, device_id={"shard": lax.rem(z + 1 + k, shards)}, device_id_type=MESH
            )

        loop(shards - 1, one)
        count += shards - 1
    if tp_too:
        for d in range(1, TP):
            pl.semaphore_signal(
                barrier, inc=1, device_id={"tp": lax.rem(t + d, TP)}, device_id_type=MESH
            )
            count += 1
    pl.semaphore_wait(barrier, count)


class Gather:
    def __init__(self, shards, src, dst, zsend, csend, recv, own):
        self.s, self.src, self.dst = shards, src, dst
        self.zsend, self.csend, self.recv, self.own = zsend, csend, recv, own
        self.z, self.c = lax.axis_index("shard"), lax.axis_index("ctx")
        self.r = src.shape[0]

    def block(self, g):
        return self.dst.at[rows_of(g, self.r)]

    def to_shard(self, k):
        g = 2 * self.z + self.c
        return remote(
            self.src,
            self.block(g),
            self.zsend.at[k],
            self.recv.at[g],
            shard=lax.rem(self.z + k, self.s),
        )

    def to_core(self, k):
        zz = lax.rem(self.z + k, self.s)
        g = 2 * zz + self.c
        return remote(self.block(g), self.block(g), self.csend.at[k], self.recv.at[g], ctx=1 - self.c)

    def got(self, k, core):
        zz = lax.rem(self.z + k, self.s)
        g = 2 * zz + core
        return remote(self.block(g), self.block(g), self.csend.at[k], self.recv.at[g], ctx=1 - self.c)

    def start(self):
        keep = pltpu.make_async_copy(self.src, self.block(2 * self.z + self.c), self.own)
        keep.start()
        loop(self.s - 1, lambda k: self.to_shard(k + 1).start())
        keep.wait()
        self.to_core(0).start()

    def forward(self):
        def one(k):
            self.got(k + 1, self.c).wait_recv()
            self.to_core(k + 1).start()

        loop(self.s - 1, one)

    def finish(self):
        loop(self.s, lambda k: self.got(k, 1 - self.c).wait_recv())
        loop(self.s, lambda k: self.to_core(k).wait_send())
        loop(self.s - 1, lambda k: self.to_shard(k + 1).wait_send())

    @staticmethod
    def sems(shards):
        dma = pltpu.SemaphoreType.DMA
        return [dma((shards,)), dma((shards,)), dma((2 * shards,)), dma(())]


class Scatter:
    def __init__(self, shards, src, sib, stage, land, csend, crecv, zsend, zrecv):
        self.s, self.src, self.sib, self.stage, self.land = shards, src, sib, stage, land
        self.csend, self.crecv, self.zsend, self.zrecv = csend, crecv, zsend, zrecv
        self.z, self.c = lax.axis_index("shard"), lax.axis_index("ctx")
        self.r = src.shape[0] // (2 * shards)

    def to_core(self, k):
        zz = lax.rem(self.z + k, self.s)
        return remote(
            self.src.at[rows_of(2 * zz + 1 - self.c, self.r)],
            self.sib.at[zz],
            self.csend.at[zz],
            self.crecv.at[zz],
            ctx=1 - self.c,
        )

    def to_shard(self, k):
        zz = lax.rem(self.z + k, self.s)
        return remote(
            self.stage.at[zz], self.land.at[self.z], self.zsend.at[zz], self.zrecv.at[self.z], shard=zz
        )

    def arrive(self, k):
        zz = lax.rem(self.z + k, self.s)
        return remote(
            self.stage.at[zz], self.land.at[zz], self.zsend.at[zz], self.zrecv.at[zz], shard=zz
        )

    def start(self):
        loop(self.s - 1, lambda k: self.to_core(k + 1).start())
        self.to_core(0).start()

    def middle(self):
        def one(k):
            zz = lax.rem(self.z + 1 + k, self.s)
            self.to_core(k + 1).wait_recv()
            both = self.src[rows_of(2 * zz + self.c, self.r), :].astype(f32)
            self.stage[zz] = (both + self.sib[zz].astype(f32)).astype(bf16)
            self.to_shard(k + 1).start()

        loop(self.s - 1, one)

    def finish(self, out, cols=None):
        self.to_core(0).wait_recv()
        own = self.src[rows_of(2 * self.z + self.c, self.r), :].astype(f32)
        out[...] = own + self.sib[self.z].astype(f32)

        def one(k):
            zz = lax.rem(self.z + 1 + k, self.s)
            self.arrive(k + 1).wait_recv()
            out[...] += self.land[zz].astype(f32)

        loop(self.s - 1, one)
        loop(self.s, lambda k: self.to_core(k).wait_send())
        loop(self.s - 1, lambda k: self.to_shard(k + 1).wait_send())

    @staticmethod
    def scratch(shards, rows, cols):
        dma = pltpu.SemaphoreType.DMA
        block = pltpu.VMEM((shards, rows // (2 * shards), cols), bf16)
        return [block, block, block] + [dma((shards,))] * 4


def sigmoid(v):
    return 1.0 / (1.0 + jnp.exp(-v))


def softplus(v):
    return jnp.maximum(v, 0.0) + jnp.log1p(jnp.exp(-jnp.abs(v)))


def swap_half(v):
    width = v.shape[1]
    low = iota(v.shape, 1) % HD < HD // 2
    return jnp.where(low, pltpu.roll(v, width - HD // 2, 1), pltpu.roll(v, HD // 2, 1))


def low_lanes(shape):
    return iota(shape, 1) < 64


def spread():
    return (iota((N, WI), 1) // P_SIZE == iota((N, WI), 0)).astype(f32)


def first_row():
    return (iota((8, N), 0) == 0).astype(f32)


def wide(column, width):
    return jnp.concatenate([column] * (width // column.shape[1]), axis=1)


def lower_ones():
    return (iota((L, L), 0) >= iota((L, L), 1)).astype(f32)


def project_kernel(shards, hid, wa, wfull, normed, gains, z_out, cin, q_out, kv_out, dt_out, *sems):
    greet(shards, False)
    gather = Gather(shards, wa, wfull, *sems)
    gather.start()
    gather.forward()
    gather.finish()
    turned = wfull[:, CS:CA].astype(f32).T
    gains[...] = turned[GAIN_COL : GAIN_COL + 8]
    gain = gains[0:1, :]

    def block(i):
        rows = rows_of(i)
        x = hid[rows, :].astype(f32)
        scale = lax.rsqrt(jnp.mean(x * x, -1, keepdims=True) + EPS)
        low = (x * scale * gain).astype(bf16)
        normed[rows, :] = low
        z_out[rows, :] = nn(low, wfull[:, CZ:CX])
        cin[rows, :] = nn(low, wfull[:, CX:CQ]).astype(bf16)
        rest = nn(low, wfull[:, CQ:CA])
        q_out[rows, :] = rest[:, : CK - CQ]
        kv_out[rows, :] = rest[:, CK - CQ : CS - CQ]
        dt_out[rows, :] = rest[:, CS - CQ :]

    loop(hid.shape[0] // L, block)


def project(shards, hid, wa):
    t = hid.shape[0]
    out = [
        ((D, CA), bf16),
        ((t, D), bf16),
        ((8, D), f32),
        ((t, WI), f32),
        ((t, CH), bf16),
        ((t, 128), f32),
        ((t, 128), f32),
        ((t, 128), f32),
    ]
    return pl.pallas_call(
        functools.partial(project_kernel, shards),
        out_shape=[jax.ShapeDtypeStruct(*o) for o in out],
        in_specs=[pl.BlockSpec(memory_space=pltpu.VMEM)] * 2,
        out_specs=[pl.BlockSpec(memory_space=pltpu.VMEM)] * len(out),
        scratch_shapes=Gather.sems(shards),
        compiler_params=pltpu.CompilerParams(
            collective_id=0, has_side_effects=True, vmem_limit_bytes=VLIMIT
        ),
        name="project",
    )(hid, wa)


def head_scalars(dt_raw, prm):
    real = iota(dt_raw.shape, 1) < HL
    steps = jnp.where(real, softplus(dt_raw + prm[0:1, :]), 0.0)
    rates = steps * prm[1:2, :]
    return steps, rates


def pair_columns(v, pair):
    return v[:, 128 * pair : 128 * pair + 128]


def own_half(v, half):
    return jnp.where(low_lanes(v.shape) == (half == 0), v, jnp.zeros_like(v))


def forward_kernel(
    shards,
    cin, q_in, kv_in, dt_raw, z_in, cos, sin, wb, taps, prm, chan, length,
    wfull, pre, hist, q_low, kk, vv, att, lse, lse_row, ssd, start, steps_out, cum_out, tot_out,
    gated_low, square,
    pad, act, state, carried, scores_m, scores_l,
    hist_in, zs, cs, gr, own_sem, xs, xr,
):
    c = lax.axis_index("ctx")
    t = cin.shape[0]
    blocks = t // L
    greet(shards, False)
    gather = Gather(shards, wb, wfull, zs, cs, gr, own_sem)
    gather.start()

    def swap(src, dst, i):
        return remote(src, dst, xs.at[i], xr.at[i], ctx=1 - c)

    tail = swap(cin.at[pl.ds(t - 16, 16)], hist_in, 0)
    tail.start()
    low128 = low_lanes((L, 128))

    def rotary(i):
        rows = rows_of(i)
        cosine, sine = cos[rows, :], sin[rows, :]
        v = q_in[rows, :]
        q_low[rows, :] = (v * cosine + swap_half(v) * sine).astype(bf16)
        v = kv_in[rows, :]
        other = pltpu.roll(v, 64, 1)
        twice = jnp.where(low128, v, other)
        kk[0, rows, :] = (twice * cosine + swap_half(twice) * sine).astype(bf16)
        vv[0, rows, :] = jnp.where(low128, other, v).astype(bf16)

    loop(blocks, rotary)
    keys = swap(kk.at[0], kk.at[1], 1)
    keys.start()
    vals = swap(vv.at[0], vv.at[1], 2)
    vals.start()

    tail.wait_recv()
    before = hist_in[8:16, :].astype(f32)
    hist[...] = jnp.where((iota((8, CH), 0) >= 5) & (c > 0), before, 0.0)
    pad[0:8, :] = hist[...]

    def fill(i):
        pad[pl.ds(pl.multiple_of(i * L + 8, 8), L), :] = cin[rows_of(i), :].astype(f32)

    loop(blocks, fill)
    ones = lower_ones()
    expand = spread()
    state[...] = jnp.zeros_like(state)

    for i in range(blocks):
        rows = pl.ds(i * L, L)
        v = taps[4:5, :] + taps[0:1, :] * pad[pl.ds(i * L + 5, L), :]
        for j in range(1, CONVW):
            v = v + taps[j : j + 1, :] * pad[pl.ds(i * L + 5 + j, L), :]
        pre[rows, :] = v
        a = v * sigmoid(v)
        act[rows, :] = a
        steps, rates = head_scalars(dt_raw[rows, :], prm)
        cum = nn(ones, rates, HI)
        tot = cum[L - 1 : L, :]
        steps_out[rows, :] = steps
        cum_out[rows, :] = cum
        tot_out[i] = jnp.broadcast_to(tot, (8, 128))
        weight = nn(jnp.exp(tot - cum) * steps, expand, HI)
        start[i] = state[...]
        add = tn(a[:, WI : WI + N].astype(bf16), (weight * a[:, :WI]).astype(bf16))
        decay = nn(jnp.broadcast_to(jnp.exp(tot), (8, 128)), expand, HI)[0:1, :]
        state[...] = decay * state[...] + add

    states = swap(state, carried, 3)
    states.start()
    gather.forward()

    keys.wait_recv()
    vals.wait_recv()
    scale = HD ** (-0.5)
    limit = length[0] - c * t

    def stacked(v):
        return jnp.concatenate([own_half(v, 0), own_half(v, 1)], axis=0)

    for i in range(blocks):
        rows = pl.ds(i * L, L)
        width = (i + 1) * L
        q2 = stacked(q_low[rows, :].astype(f32)).astype(bf16)
        s = nt(q2, kk[0, 0:width, :]) * scale
        at = iota(s.shape, 0) % L + i * L
        col = iota(s.shape, 1)
        s = jnp.where((col <= at) & (col < limit), s, FILL)
        peak = jnp.max(s, -1, keepdims=True)
        e = jnp.exp(s - peak)
        total = jnp.sum(e, -1, keepdims=True)
        o = nn(e.astype(bf16), vv[0, 0:width, :])
        scores_m[...] = jnp.broadcast_to(peak, (2 * L, 128))
        scores_l[0] = jnp.broadcast_to(total, (2 * L, 128))
        scores_l[1] = o

        @pl.when(c > 0)
        def earlier():
            s2 = nt(q2, kk[1]) * scale
            old = scores_m[:, 0:1]
            new = jnp.maximum(old, jnp.max(s2, -1, keepdims=True))
            e2 = jnp.exp(s2 - new)
            fade = jnp.exp(old - new)
            scores_m[...] = jnp.broadcast_to(new, (2 * L, 128))
            scores_l[0] = fade * scores_l[0] + jnp.sum(e2, -1, keepdims=True)
            scores_l[1] = fade * scores_l[1] + nn(e2.astype(bf16), vv[1])

        total = scores_l[0]
        o = scores_l[1] / total
        att[rows, :] = jnp.where(low128, o[:L], o[L:])
        logs = scores_m[...] + jnp.log(total)
        both = jnp.where(low128, logs[:L], logs[L:])
        lse[rows, :] = both
        turned = both.T
        lse_row[0:1, rows] = turned[0:1]
        lse_row[1:2, rows] = turned[64:65]
        lse_row[2:8, rows] = jnp.zeros((6, L), f32)

    states.wait_recv()
    carried[...] = jnp.where(c > 0, carried[...], 0.0)
    mask = iota((L, L), 0) >= iota((L, L), 1)
    for i in range(blocks):
        rows = pl.ds(i * L, L)
        if i > 0:
            decay = nn(jnp.exp(tot_out[i - 1]), expand, HI)[0:1, :]
            carried[...] = carried[...] * decay
        start[i] = start[i] + carried[...]
        s0 = start[i].astype(bf16)
        steps, cum = steps_out[rows, :], cum_out[rows, :]
        x = act[rows, 0:WI]
        xl = x.astype(bf16)
        in_map = act[rows, WI : WI + N].astype(bf16)
        out_map = act[rows, WI + N : CH].astype(bf16)
        gram = nt(out_map, in_map)
        cum_t, steps_t = cum.T, steps.T
        inner = []
        for pair in range(HL // 2):
            halves = []
            for half in range(2):
                h = 2 * pair + half
                decay = jnp.exp(jnp.where(mask, cum[:, h : h + 1] - cum_t[h : h + 1, :], FILL))
                mixing = gram * decay * steps_t[h : h + 1, :]
                halves.append(nn(mixing.astype(bf16), pair_columns(xl, pair)))
            inner.append(jnp.where(low128, halves[0], halves[1]))
        y = jnp.concatenate(inner, axis=1)
        y = y + nn(jnp.exp(cum), expand, HI) * nn(out_map, s0) + chan[1:2, :] * x
        ssd[rows, :] = y
        zz = z_in[rows, :]
        gated = y * zz * sigmoid(zz)
        gated_low[rows, :] = (gated * chan[0:1, :]).astype(bf16)
        square[:, rows] = nt(jnp.ones((8, WI), f32), gated * gated, HI)

    gather.finish()
    for copy in (tail, keys, vals, states):
        copy.wait_send()


def forward(shards, cin, q, kv, dt, z, cos, sin, wb, taps, prm, chan, length):
    t = cin.shape[0]
    out = [
        ((D, CB), bf16),
        ((t, CH), f32),
        ((8, CH), f32),
        ((t, 128), bf16),
        ((2, t, 128), bf16),
        ((2, t, 128), bf16),
        ((t, 128), f32),
        ((t, 128), f32),
        ((8, t), f32),
        ((t, WI), f32),
        ((t // L, N, WI), f32),
        ((t, 128), f32),
        ((t, 128), f32),
        ((t // L, 8, 128), f32),
        ((t, WI), bf16),
        ((8, t), f32),
    ]
    dma = pltpu.SemaphoreType.DMA
    vmem = pl.BlockSpec(memory_space=pltpu.VMEM)
    return pl.pallas_call(
        functools.partial(forward_kernel, shards),
        out_shape=[jax.ShapeDtypeStruct(*o) for o in out],
        in_specs=[vmem] * 11 + [pl.BlockSpec(memory_space=pltpu.SMEM)],
        out_specs=[vmem] * len(out),
        scratch_shapes=[
            pltpu.VMEM((t + 8, CH), f32),
            pltpu.VMEM((t, CH), f32),
            pltpu.VMEM((N, WI), f32),
            pltpu.VMEM((N, WI), f32),
            pltpu.VMEM((2 * L, 128), f32),
            pltpu.VMEM((2, 2 * L, 128), f32),
            pltpu.VMEM((16, CH), bf16),
        ]
        + Gather.sems(shards)
        + [dma((4,)), dma((4,))],
        compiler_params=pltpu.CompilerParams(
            collective_id=1, has_side_effects=True, vmem_limit_bytes=VLIMIT
        ),
        name="mix_forward",
    )(cin, q, kv, dt, z, cos, sin, wb, taps, prm, chan, length)


def ffn_kernel(
    hid, cot, gl, att, square, wb, gains, length,
    output, grad_own, grads, gain_grad, total_square, ggl, grad_att, dots,
    grad_res, partial, seed, send1, recv1, low_two, grad_act, act, gg, gu, gown,
    unit, scale_keep, osend, orecv, gsend, grecv, sqall,
    sqs, sqr, s1, r1, ns, nr, os, orr, gs, gr, hs, hr,
):
    t = hid.shape[0]
    tp, c = lax.axis_index("tp"), lax.axis_index("ctx")
    chunk = t // TP
    width = D // TP
    greet(1, True, False, False)

    def peer(d):
        return lax.rem(tp + d, TP)

    def crow(i):
        return rows_of(i, chunk)

    def square_to(d):
        return remote(sqall.at[tp], sqall.at[tp], sqs.at[d], sqr.at[tp], tp=peer(d))

    def square_from(d):
        return remote(sqall.at[tp], sqall.at[peer(d)], sqs.at[d], sqr.at[peer(d)], tp=peer(d))

    sqall[tp] = square[...]
    for d in range(1, TP):
        square_to(d).start()
    limit = length[0] - c * t

    def mask_seed(i):
        rows = crow(i)
        live = iota((chunk, D), 0) + i * chunk < limit
        seed[rows, :] = jnp.where(live, cot[rows, :].astype(f32), 0.0).astype(bf16)

    loop(TP, mask_seed)
    for d in range(1, TP):
        square_from(d).wait_recv()
    total_square[...] = sqall[0] + sqall[1] + sqall[2] + sqall[3]

    def first_to(d):
        return remote(send1.at[d], recv1.at[tp], s1.at[d], r1.at[tp], tp=peer(d))

    def first_from(d):
        return remote(send1.at[d], recv1.at[peer(d)], s1.at[d], r1.at[peer(d)], tp=peer(d))

    def mix(k):
        d = lax.rem(k + 1, TP)
        rows = crow(peer(d))
        scale = lax.rsqrt(total_square[:, rows] / DI + EPS)
        column = wide(tn(scale, first_row(), HI), D)
        both = nt(gl[rows, :], wb[:, CO:CW]) * column + nt(att[rows, :], wb[:, CW:CG])
        partial[rows, :] = both

        @pl.when(d > 0)
        def go():
            send1[d] = both.astype(bf16)
            first_to(d).start()

    loop(TP, mix)

    def act_grad(i):
        rows = crow(i)
        grad_act[rows, :] = nn(seed[rows, :], wb[:, CD:CB])

    loop(TP, act_grad)
    for d in range(1, TP):
        first_from(d).wait_recv()
    own = crow(tp)
    acc = hid[own, :].astype(f32) + partial[own, :]
    for d in range(1, TP):
        acc = acc + recv1[peer(d)].astype(f32)
    scale = lax.rsqrt(jnp.mean(acc * acc, -1, keepdims=True) + EPS)
    scale_keep[...] = jnp.broadcast_to(scale, scale_keep.shape)
    unit[...] = acc * scale
    gain = gains[1:2, :]
    low_two[own, :] = (unit[...] * gain).astype(bf16)

    def norm_to(d):
        return remote(low_two.at[own], low_two.at[own], ns.at[d], nr.at[tp], tp=peer(d))

    def norm_from(d):
        there = low_two.at[crow(peer(d))]
        return remote(there, there, ns.at[d], nr.at[peer(d)], tp=peer(d))

    for d in range(1, TP):
        norm_to(d).start()

    def grad_to(d):
        return remote(gsend.at[d], grecv.at[tp], gs.at[d], gr.at[tp], tp=peer(d))

    def grad_from(d):
        return remote(gsend.at[d], grecv.at[peer(d)], gs.at[d], gr.at[peer(d)], tp=peer(d))

    def out_to(e, i):
        rows = crow(i)
        return remote(
            osend.at[e, rows], orecv.at[tp, rows], os.at[e, i], orr.at[tp, i], tp=peer(e)
        )

    def out_from(e, i):
        rows = crow(i)
        return remote(
            osend.at[e, rows], orecv.at[peer(e), rows], os.at[e, i], orr.at[peer(e), i], tp=peer(e)
        )

    def hidden_units(d):
        i = peer(d)
        rows = crow(i)

        @pl.when(d > 0)
        def arrive():
            norm_from(d).wait_recv()

        low = low_two[rows, :]
        gate, up = nn(low, wb[:, CG:CU]), nn(low, wb[:, CU:CD])
        sig = sigmoid(gate)
        silu = gate * sig
        hidden_act = (silu * up).astype(bf16)
        act[rows, :] = hidden_act
        ga = grad_act[rows, :]
        g1 = (ga * up * (sig * (1.0 + gate * (1.0 - sig)))).astype(bf16)
        g2 = (ga * silu).astype(bf16)
        gg[rows, :] = g1
        gu[rows, :] = g2
        back = nt(g1, wb[:, CG:CU]) + nt(g2, wb[:, CU:CD])

        @pl.when(d > 0)
        def go():
            gsend[d] = back.astype(bf16)
            grad_to(d).start()

        @pl.when(d == 0)
        def keep():
            gown[...] = back

        partial[rows, :] = partial[rows, :] + nt(hidden_act, wb[:, CD:CB])
        for e in range(1, TP):
            osend[e, rows, :] = partial[rows, rows_of(peer(e), width)].astype(bf16)
            out_to(e, i).start()

    loop(TP, hidden_units)

    def weight_grads(i):
        feats = rows_of(i)
        low = low_two[:, feats]
        grads[feats, CG:CU] = tn(low, gg[...]).astype(bf16)
        grads[feats, CU:CD] = tn(low, gu[...]).astype(bf16)

    loop(D // L, weight_grads)
    for d in range(1, TP):
        grad_from(d).wait_recv()
    back = gown[...]
    for d in range(1, TP):
        back = back + grecv[peer(d)].astype(f32)
    gain_grad[...] = jnp.broadcast_to(jnp.sum(back * unit[...], 0, keepdims=True), (8, D))
    weighted = back * gain
    mean = jnp.mean(weighted * unit[...], -1, keepdims=True)
    res = seed[own, :].astype(f32) + scale_keep[:, 0:1] * (weighted - unit[...] * mean)
    grad_own[...] = res
    grad_res[own, :] = res.astype(bf16)

    def res_to(d):
        return remote(grad_res.at[own], grad_res.at[own], hs.at[d], hr.at[tp], tp=peer(d))

    def res_from(d):
        there = grad_res.at[crow(peer(d))]
        return remote(there, there, hs.at[d], hr.at[peer(d)], tp=peer(d))

    for d in range(1, TP):
        res_to(d).start()

    def down_grads(i):
        feats = rows_of(i)
        grads[feats, CD:CB] = tn(seed[:, feats], act[...]).astype(bf16)

    loop(D // L, down_grads)
    for d in range(1, TP):
        for i in range(TP):
            out_from(d, i).wait_recv()
    mine = rows_of(tp, width)
    total = hid[:, mine].astype(f32) + partial[:, mine]
    for d in range(1, TP):
        total = total + orecv[peer(d)].astype(f32)
    output[...] = total.astype(bf16)
    for d in range(1, TP):
        norm_to(d).wait_send()

    def out_back(d):
        i = peer(d)
        rows = crow(i)

        @pl.when(d > 0)
        def arrive():
            res_from(d).wait_recv()

        square_scale = lax.rsqrt(total_square[:, rows] / DI + EPS)
        column = wide(tn(square_scale, first_row(), HI), D)
        got = grad_res[rows, :]
        proj = (column * got.astype(f32)).astype(bf16)
        low_two[rows, :] = proj
        product = nn(proj, wb[:, CO:CW])
        ggl[rows, :] = product
        dots[:, rows] = nt(jnp.ones((8, WI), f32), product * gl[rows, :].astype(f32), HI)
        grad_att[rows, :] = nn(got, wb[:, CW:CG]).astype(bf16)

    loop(TP, out_back)

    def out_grads(i):
        feats = rows_of(i)
        grads[feats, CO:CW] = tn(low_two[:, feats], gl[...]).astype(bf16)
        grads[feats, CW:CG] = tn(grad_res[:, feats], att[...]).astype(bf16)

    loop(D // L, out_grads)
    for d in range(1, TP):
        square_to(d).wait_send()
        first_to(d).wait_send()
        grad_to(d).wait_send()
        res_to(d).wait_send()
        for i in range(TP):
            out_to(d, i).wait_send()


def ffn(hid, cot, gl, att, square, wb, gains, length):
    t = hid.shape[0]
    chunk = t // TP
    out = [
        ((t, D // TP), bf16),
        ((chunk, D), f32),
        ((D, CB), bf16),
        ((8, D), f32),
        ((8, t), f32),
        ((t, WI), f32),
        ((t, 128), bf16),
        ((8, t), f32),
    ]
    dma = pltpu.SemaphoreType.DMA
    vmem = pl.BlockSpec(memory_space=pltpu.VMEM)
    return pl.pallas_call(
        ffn_kernel,
        out_shape=[jax.ShapeDtypeStruct(*o) for o in out],
        in_specs=[vmem] * 7 + [pl.BlockSpec(memory_space=pltpu.SMEM)],
        out_specs=[vmem] * len(out),
        scratch_shapes=[
            pltpu.VMEM((t, D), bf16),
            pltpu.VMEM((t, D), f32),
            pltpu.VMEM((t, D), bf16),
            pltpu.VMEM((TP, chunk, D), bf16),
            pltpu.VMEM((TP, chunk, D), bf16),
            pltpu.VMEM((t, D), bf16),
            pltpu.VMEM((t, FFL), f32),
            pltpu.VMEM((t, FFL), bf16),
            pltpu.VMEM((t, FFL), bf16),
            pltpu.VMEM((t, FFL), bf16),
            pltpu.VMEM((chunk, D), f32),
            pltpu.VMEM((chunk, D), f32),
            pltpu.VMEM((chunk, 128), f32),
            pltpu.VMEM((TP, t, D // TP), bf16),
            pltpu.VMEM((TP, t, D // TP), bf16),
            pltpu.VMEM((TP, chunk, D), bf16),
            pltpu.VMEM((TP, chunk, D), bf16),
            pltpu.VMEM((TP, 8, t), f32),
        ]
        + [dma((TP,))] * 6
        + [dma((TP, TP))] * 2
        + [dma((TP,))] * 4,
        compiler_params=pltpu.CompilerParams(
            collective_id=2, has_side_effects=True, vmem_limit_bytes=VLIMIT
        ),
        name="feed_forward",
    )(hid, cot, gl, att, square, wb, gains, length)


def backward_kernel(
    shards,
    ggl, grad_att, dots_in, total_square, grads,
    pre, cin, hist, q_low, kk, vv, att, lse_row, ssd, start, steps_in, cum_in, tot_in, dt_raw, z_in,
    cos, sin, taps, prm, chan, length,
    lin, grad_b, conv_grads, chan_grads, head_grads,
    dots, dk, dv, dy, dpre, ends, dstate, carry, kv_out, kv_in, pad, edge_out, edge_in,
    sib, stage, land, csend, crecv, zsend, zrecv, xs, xr, ts, tr,
):
    c, tp = lax.axis_index("ctx"), lax.axis_index("tp")
    t = cin.shape[0]
    blocks = t // L
    greet(shards, True)
    scatter = Scatter(shards, grads, sib, stage, land, csend, crecv, zsend, zrecv)
    scatter.start()

    def swap(src, dst, i):
        return remote(src, dst, xs.at[i], xr.at[i], ctx=1 - c)

    def peer(d):
        return lax.rem(tp + d, TP)

    def dot_to(d):
        return remote(dots.at[tp], dots.at[tp], ts.at[d], tr.at[tp], tp=peer(d))

    def dot_from(d):
        return remote(dots.at[tp], dots.at[peer(d)], ts.at[d], tr.at[peer(d)], tp=peer(d))

    dots[tp] = dots_in[...]
    for d in range(1, TP):
        dot_to(d).start()
    expand = spread()
    low128 = low_lanes((L, 128))
    chan_grads[...] = jnp.zeros_like(chan_grads)
    head_grads[...] = jnp.zeros_like(head_grads)
    conv_grads[...] = jnp.zeros_like(conv_grads)
    for d in range(1, TP):
        dot_from(d).wait_recv()

    def gated_back(i):
        rows = rows_of(i)
        both = dots[0, :, rows] + dots[1, :, rows] + dots[2, :, rows] + dots[3, :, rows]
        share = both / ((total_square[:, rows] / DI + EPS) * DI)
        column = wide(tn(share, first_row(), HI), WI)
        zz, y = z_in[rows, :], ssd[rows, :]
        sig = sigmoid(zz)
        silu = zz * sig
        gated = y * silu
        product = ggl[rows, :]
        chan_grads[0:1, :] += jnp.sum(product * gated, 0, keepdims=True)
        grad_gated = product * chan[0:1, :] - column * gated
        grad_y = grad_gated * silu
        dy[rows, :] = grad_y
        lin[rows, CZ:CX] = (grad_gated * y * (sig * (1.0 + zz * (1.0 - sig)))).astype(bf16)
        v = pre[rows, WI + N : CH]
        out_map = (v * sigmoid(v)).astype(bf16)
        ends[i] = tn(out_map, (nn(jnp.exp(cum_in[rows, :]), expand, HI) * grad_y).astype(bf16))

    loop(blocks, gated_back)
    dstate[...] = jnp.zeros_like(dstate)

    def chain(k):
        i = blocks - 1 - k
        add = ends[i]
        ends[i] = dstate[...]
        dstate[...] = nn(jnp.exp(tot_in[i]), expand, HI)[0:1, :] * dstate[...] + add

    loop(blocks, chain)
    states = swap(dstate, carry, 0)
    states.start()
    scatter.middle()

    scale = HD ** (-0.5)
    limit = length[0] - c * t
    dk[...] = jnp.zeros_like(dk)
    dv[...] = jnp.zeros_like(dv)
    head_of = ((iota((8, 128), 1) // HD) == iota((8, 128), 0)).astype(f32)

    def stacked(v):
        return jnp.concatenate([own_half(v, 0), own_half(v, 1)], axis=0).astype(bf16)

    def side_by_side(v):
        return jnp.concatenate([v[0:1, :], v[1:2, :]], axis=1)

    for i in range(blocks):
        rows = pl.ds(i * L, L)
        width = (i + 1) * L
        q2 = stacked(q_low[rows, :].astype(f32))
        go = grad_att[rows, :].astype(f32)
        go2 = stacked(go)
        row_dot = side_by_side(nt(head_of, go * att[rows, :], HI))
        logs = side_by_side(lse_row[:, rows])
        turn = cos[rows, :], sin[rows, :]

        def keys_of(part, size, masked):
            k, v = kk[part, 0:size, :], vv[part, 0:size, :]
            s = nt(k, q2) * scale - logs
            if masked:
                at = iota(s.shape, 1) % L + i * L
                row = iota(s.shape, 0)
                s = jnp.where((row <= at) & (row < limit), s, FILL)
            p = jnp.exp(s)
            ds = (p * (nt(v, go2) - row_dot)).astype(bf16)
            dv[part, 0:size, :] += nn(p.astype(bf16), go2)
            dk[part, 0:size, :] += nn(ds, q2)
            out = tn(ds, k) * scale
            out = jnp.where(low128, out[:L], out[L:])
            return out * turn[0] - swap_half(out) * turn[1]

        pad[rows, 0:128] = keys_of(0, width, True)

        @pl.when(c > 0)
        def earlier():
            pad[rows, 0:128] += keys_of(1, t, False)

        lin[rows, CQ:CK] = pad[rows, 0:128].astype(bf16)

    def key_values(part, rows):
        gk, gv = dk[part, rows, :] * scale, dv[part, rows, :]
        return jnp.where(low128, gk + pltpu.roll(gk, 64, 1), gv + pltpu.roll(gv, 64, 1))

    def pack(i):
        rows = rows_of(i)
        kv_out[rows, :] = key_values(1, rows).astype(bf16)

    loop(blocks, pack)
    pairs = swap(kv_out, kv_in, 1)
    pairs.start()

    pad[0:8, :] = hist[...]

    def fill(i):
        pad[pl.ds(pl.multiple_of(i * L + 8, 8), L), :] = cin[rows_of(i), :].astype(f32)

    loop(blocks, fill)
    states.wait_recv()
    carry[...] = jnp.where(c == 0, carry[...], 0.0)

    def add_carry(k):
        i = blocks - 1 - k
        ends[i] = ends[i] + carry[...]
        carry[...] = nn(jnp.exp(tot_in[i]), expand, HI)[0:1, :] * carry[...]

    loop(blocks, add_carry)
    mask = iota((L, L), 0) >= iota((L, L), 1)
    ones = lower_ones()
    lane = iota((L, 128), 1)

    def fold(v):
        return nt(v, expand, HI)

    def scan_back(i):
        rows = rows_of(i)
        v = pre[rows, :]
        sig = sigmoid(v)
        a = v * sig
        x = a[:, :WI]
        xl, bl, cl = x.astype(bf16), a[:, WI : WI + N].astype(bf16), a[:, WI + N :].astype(bf16)
        steps, cum = steps_in[rows, :], cum_in[rows, :]
        tot = cum[L - 1 : L, :]
        ecum, wend = jnp.exp(cum), jnp.exp(tot - cum)
        weight = wend * steps
        ecum_x, weight_x = nn(ecum, expand, HI), nn(weight, expand, HI)
        grad_y = dy[rows, :]
        dyl = grad_y.astype(bf16)
        s0, d1 = start[i], ends[i]
        s0l, d1l = s0.astype(bf16), d1.astype(bf16)
        bd, cs = nn(bl, d1l), nn(cl, s0l)
        dw = fold(x * bd)
        crossing = jnp.broadcast_to(jnp.sum(s0 * d1, 0, keepdims=True), (8, WI))
        dtot = jnp.sum(weight * dw, 0, keepdims=True) + jnp.exp(tot) * fold(crossing)[0:1, :]
        gram = nt(cl, bl)
        cum_t, steps_t = cum.T, steps.T
        dgram = jnp.zeros((L, L), f32)
        row_sums = jnp.zeros((L, 128), f32)
        col_sums, inner = [], []
        for pair in range(HL // 2):
            xp, dp = pair_columns(xl, pair), pair_columns(dyl, pair)
            dpf = pair_columns(grad_y, pair)
            halves = []
            for half in range(2):
                h = 2 * pair + half
                decay = jnp.exp(jnp.where(mask, cum[:, h : h + 1] - cum_t[h : h + 1, :], FILL))
                q = nt(own_half(dpf, half).astype(bf16), xp)
                mixed = gram * decay
                srow = steps_t[h : h + 1, :]
                f = mixed * q
                col_sums.append(jnp.sum(f, 0, keepdims=True))
                row_sums = jnp.where(lane == h, jnp.sum(f * srow, -1, keepdims=True), row_sums)
                dgram = dgram + decay * srow * q
                halves.append(tn((mixed * srow).astype(bf16), dp))
            inner.append(jnp.where(low128, halves[0], halves[1]))
        cols = jnp.concatenate(col_sums + [jnp.zeros((128 - HL, L), f32)], axis=0).T
        dcum = fold(grad_y * cs) * ecum - weight * dw + row_sums - steps * cols
        dcum = dcum + jnp.where(iota((L, 128), 0) == L - 1, dtot, 0.0)
        drate = tn(ones, dcum, HI)
        rate_of = prm[1:2, :]
        raw = dt_raw[rows, :] + prm[0:1, :]
        dstep = (wend * dw + cols + drate * rate_of) * sigmoid(raw)
        dstep = jnp.where(lane < HL, dstep, 0.0)
        lin[rows, CS:CA] = dstep.astype(bf16)
        head_grads[0:1, :] += jnp.sum(dstep, 0, keepdims=True)
        head_grads[1:2, :] += jnp.sum(drate * steps * rate_of, 0, keepdims=True)
        head_grads[2:3, :] += jnp.sum(fold(grad_y * x), 0, keepdims=True)
        slope = sig * (1.0 + v * (1.0 - sig))
        dx = chan[1:2, :] * grad_y + weight_x * bd + jnp.concatenate(inner, axis=1)
        dg = dgram.astype(bf16)
        db = tn(dg, cl) + nt((weight_x * x).astype(bf16), d1l)
        dc = nn(dg, bl) + nt((ecum_x * grad_y).astype(bf16), s0l)
        dpre[rows, 0:WI] = dx * slope[:, :WI]
        dpre[rows, WI : WI + N] = db * slope[:, WI : WI + N]
        dpre[rows, WI + N : CH] = dc * slope[:, WI + N :]

    loop(blocks, scan_back)
    edge_out[...] = dpre[0:8, :]
    edge = swap(edge_out, edge_in, 2)
    edge.start()
    pairs.wait_recv()

    def keys_back(i):
        rows = rows_of(i)
        v = key_values(0, rows) + kv_in[rows, :].astype(f32)
        cosine = jnp.where(low128, cos[rows, :], 1.0)
        sine = jnp.where(low128, sin[rows, :], 0.0)
        lin[rows, CK:CS] = (v * cosine - swap_half(v) * sine).astype(bf16)

    loop(blocks, keys_back)
    edge.wait_recv()
    dpre[pl.ds(t, 8), :] = jnp.where(c == 0, edge_in[...], 0.0)
    for i in range(blocks):
        rows = pl.ds(i * L, L)
        g = dpre[rows, :]
        conv_grads[4:5, :] += jnp.sum(g, 0, keepdims=True)
        back = jnp.zeros_like(g)
        for j in range(CONVW):
            back = back + taps[j : j + 1, :] * dpre[pl.ds(i * L + CONVW - 1 - j, L), :]
            conv_grads[j : j + 1, :] += jnp.sum(g * pad[pl.ds(i * L + 5 + j, L), :], 0, keepdims=True)
        lin[rows, CX:CQ] = back.astype(bf16)
    scatter.finish(grad_b)
    for copy in (states, pairs, edge):
        copy.wait_send()
    for d in range(1, TP):
        dot_to(d).wait_send()


def backward(shards, *args):
    t = args[6].shape[0]
    rows = D // (2 * shards)
    out = [
        ((t, CA), bf16),
        ((rows, CB), f32),
        ((8, CH), f32),
        ((8, WI), f32),
        ((8, 128), f32),
    ]
    dma = pltpu.SemaphoreType.DMA
    vmem = pl.BlockSpec(memory_space=pltpu.VMEM)
    return pl.pallas_call(
        functools.partial(backward_kernel, shards),
        out_shape=[jax.ShapeDtypeStruct(*o) for o in out],
        in_specs=[vmem] * (len(args) - 1) + [pl.BlockSpec(memory_space=pltpu.SMEM)],
        out_specs=[vmem] * len(out),
        scratch_shapes=[
            pltpu.VMEM((TP, 8, t), f32),
            pltpu.VMEM((2, t, 128), f32),
            pltpu.VMEM((2, t, 128), f32),
            pltpu.VMEM((t, WI), f32),
            pltpu.VMEM((t + 8, CH), f32),
            pltpu.VMEM((t // L, N, WI), f32),
            pltpu.VMEM((N, WI), f32),
            pltpu.VMEM((N, WI), f32),
            pltpu.VMEM((t, 128), bf16),
            pltpu.VMEM((t, 128), bf16),
            pltpu.VMEM((t + 8, CH), f32),
            pltpu.VMEM((8, CH), f32),
            pltpu.VMEM((8, CH), f32),
        ]
        + Scatter.scratch(shards, D, CB)
        + [dma((3,)), dma((3,)), dma((TP,)), dma((TP,))],
        compiler_params=pltpu.CompilerParams(
            collective_id=3, has_side_effects=True, vmem_limit_bytes=VLIMIT
        ),
        name="mix_backward",
    )(*args)


def finish_kernel(
    shards,
    lin, normed, wfull, hid, grad_own, gains, gain_two,
    grad_hidden, grad_a, shared,
    gsend, grecv, gown, grads, misc, misc_low, misc_sum, low, shsend,
    sib, stage, land, csend, crecv, zsend, zrecv,
    sib2, stage2, land2, csend2, crecv2, zsend2, zrecv2,
    gs, gr, hs, hr, ss, sr,
):
    tp = lax.axis_index("tp")
    t = lin.shape[0]
    chunk = t // TP
    greet(shards, True)
    scatter = Scatter(shards, grads, sib, stage, land, csend, crecv, zsend, zrecv)
    small = Scatter(shards, misc_low, sib2, stage2, land2, csend2, crecv2, zsend2, zrecv2)

    def peer(d):
        return lax.rem(tp + d, TP)

    def crow(i):
        return rows_of(i, chunk)

    def grad_to(d):
        return remote(gsend.at[d], grecv.at[tp], gs.at[d], gr.at[tp], tp=peer(d))

    def grad_from(d):
        return remote(gsend.at[d], grecv.at[peer(d)], gs.at[d], gr.at[peer(d)], tp=peer(d))

    def product(k):
        d = lax.rem(k + 1, TP)
        back = nt(lin[crow(peer(d)), :], wfull[...])

        @pl.when(d > 0)
        def go():
            gsend[d] = back.astype(bf16)
            grad_to(d).start()

        @pl.when(d == 0)
        def keep():
            gown[...] = back

    loop(TP, product)

    def weight_grads(i):
        feats = rows_of(i)
        both = tn(normed[:, feats], lin[...])
        grads[feats, :] = both[:, :CS].astype(bf16)
        misc[feats, :] = both[:, CS:]

    loop(D // L, weight_grads)
    scatter.start()
    for d in range(1, TP):
        grad_from(d).wait_recv()
    own = crow(tp)
    back = gown[...]
    for d in range(1, TP):
        back = back + grecv[peer(d)].astype(f32)
    x = hid[own, :].astype(f32)
    scale = lax.rsqrt(jnp.mean(x * x, -1, keepdims=True) + EPS)
    unit = x * scale
    gain_one = jnp.broadcast_to(jnp.sum(back * unit, 0, keepdims=True), (8, D))
    weighted = back * gains[0:1, :]
    mean = jnp.mean(weighted * unit, -1, keepdims=True)
    low[own, :] = (grad_own[...] + scale * (weighted - unit * mean)).astype(bf16)

    def low_to(d):
        return remote(low.at[own], low.at[own], hs.at[d], hr.at[tp], tp=peer(d))

    def low_from(d):
        there = low.at[crow(peer(d))]
        return remote(there, there, hs.at[d], hr.at[peer(d)], tp=peer(d))

    for d in range(1, TP):
        low_to(d).start()
    gain_rows = jnp.where(iota((8, D), 0) == 0, gain_one, gain_two[...])
    row, lane = iota((8, 128), 0), iota((8, 128), 1)
    pick = ((row < 2) & (lane == GAIN_COL + row)).astype(f32)
    misc_low[...] = (misc[...] + tn(gain_rows, pick, HI)).astype(bf16)
    small.start()
    scatter.middle()
    small.middle()
    grad_hidden[own, :] = low[own, :].astype(f32)
    for d in range(1, TP):
        low_from(d).wait_recv()
        rows = crow(peer(d))
        grad_hidden[rows, :] = low[rows, :].astype(f32)
    scatter.finish(grad_a)
    small.finish(misc_sum)
    part = grad_a.shape[0] // TP
    for i in range(TP):
        shsend[i, :, 0:256] = grad_a[i * part : (i + 1) * part, CM:CQ]
        shsend[i, :, 256:384] = grad_a[i * part : (i + 1) * part, CK:CS]
        shsend[i, :, 384:512] = misc_sum[i * part : (i + 1) * part, :]

    def share_to(d):
        return remote(shsend.at[peer(d)], shared.at[tp], ss.at[d], sr.at[tp], tp=peer(d))

    def share_from(d):
        return remote(shsend.at[peer(d)], shared.at[peer(d)], ss.at[d], sr.at[peer(d)], tp=peer(d))

    for d in range(1, TP):
        share_to(d).start()
    shared[tp] = shsend[tp]
    for d in range(1, TP):
        share_from(d).wait_recv()
    for d in range(1, TP):
        share_to(d).wait_send()
        grad_to(d).wait_send()
        low_to(d).wait_send()


def finish(shards, *args):
    t = args[0].shape[0]
    rows = D // (2 * shards)
    chunk = t // TP
    out = [((t, D), f32), ((rows, CS), f32), ((TP, rows // TP, 512), f32)]
    dma = pltpu.SemaphoreType.DMA
    vmem = pl.BlockSpec(memory_space=pltpu.VMEM)
    return pl.pallas_call(
        functools.partial(finish_kernel, shards),
        out_shape=[jax.ShapeDtypeStruct(*o) for o in out],
        in_specs=[vmem] * len(args),
        out_specs=[vmem] * len(out),
        scratch_shapes=[
            pltpu.VMEM((TP, chunk, D), bf16),
            pltpu.VMEM((TP, chunk, D), bf16),
            pltpu.VMEM((chunk, D), f32),
            pltpu.VMEM((D, CS), bf16),
            pltpu.VMEM((D, 128), f32),
            pltpu.VMEM((D, 128), bf16),
            pltpu.VMEM((rows, 128), f32),
            pltpu.VMEM((t, D), bf16),
            pltpu.VMEM((TP, rows // TP, 512), f32),
        ]
        + Scatter.scratch(shards, D, CS)
        + Scatter.scratch(shards, D, 128)
        + [dma((TP,))] * 6,
        compiler_params=pltpu.CompilerParams(
            collective_id=4, has_side_effects=True, vmem_limit_bytes=VLIMIT
        ),
        name="project_backward",
    )(*args)


def rotary_tables(positions):
    index = jnp.arange(HD // 2, dtype=f32)
    inverse = rope_base ** (-2.0 * index / HD)
    angles = positions[:, None] * inverse[None, :]
    cosine, sine = jnp.cos(angles), jnp.sin(angles)
    return jnp.tile(cosine, (1, 4)), jnp.concatenate([-sine, sine, -sine, sine], axis=1)


def local(
    hidden, cotangent, lengths, norm1_gain, w_z, w_x, w_shared, w_dt, dt_bias, a_log, d_skip,
    conv_w, conv_b, gated_gain, w_out, w_q, w_o, norm2_gain, w_gate, w_up, w_down,
):
    t = hidden.shape[1]
    shards = lax.axis_size("shard")
    tp, c = lax.axis_index("tp"), lax.axis_index("ctx")
    kv_rank = tp * (NQ // TP) // (NQ // KV)
    hid, cot = hidden[0], cotangent[0]

    def cut(v, start, size, axis):
        return lax.dynamic_slice_in_dim(v, start, size, axis)

    key_start = 2 * N + kv_rank * HD
    dt_cols = cut(w_dt, tp * HL, HL, 1)
    rows = w_z.shape[0]
    misc = [
        dt_cols,
        jnp.zeros((rows, GAIN_COL - HL), bf16),
        norm1_gain[:, None],
        norm2_gain[:, None],
        jnp.zeros((rows, 128 - GAIN_COL - 2), bf16),
    ]
    wa = jnp.concatenate(
        [
            w_z,
            w_x,
            w_shared[:, : 2 * N],
            w_q,
            cut(w_shared, key_start, HD, 1),
            cut(w_shared, key_start + KV * HD, HD, 1),
        ]
        + misc,
        axis=1,
    )
    wb = jnp.concatenate([w_out.T, w_o.T, w_gate, w_up, w_down.T], axis=1)
    taps = jnp.concatenate([conv_w, conv_b[None], jnp.zeros((3, DI + 2 * N), bf16)], axis=0)
    taps = jnp.concatenate([cut(taps, tp * WI, WI, 1), taps[:, DI:]], axis=1).astype(f32)
    bias = cut(dt_bias.astype(f32), tp * HL, HL, 0)
    rate = -jnp.exp(cut(a_log.astype(f32), tp * HL, HL, 0))
    prm = jnp.pad(jnp.stack([bias, rate]), ((0, 6), (0, 128 - HL)))
    skip = jnp.repeat(cut(d_skip.astype(f32), tp * HL, HL, 0), P_SIZE)
    gain_gate = cut(gated_gain.astype(f32), tp * WI, WI, 0)
    chan = jnp.pad(jnp.stack([gain_gate, skip]), ((0, 6), (0, 0)))
    cos, sin = rotary_tables((c * t + jnp.arange(t, dtype=jnp.int32)).astype(f32))

    wfull_a, normed, gains, z, cin, q, kv, dt = project(shards, hid, wa)
    (
        wfull_b, pre, hist, q_low, kk, vv, att, lse, lse_row, ssd, start, steps, cum, tot, gl, square,
    ) = forward(shards, cin, q, kv, dt, z, cos, sin, wb, taps, prm, chan, lengths)
    output, grad_own, grads, gain_two, total_square, ggl, grad_att, dots = ffn(
        hid, cot, gl, att.astype(bf16), square, wfull_b, gains, lengths
    )
    lin, grad_b, conv_grads, chan_grads, head_grads = backward(
        shards, ggl, grad_att, dots, total_square, grads, pre, cin, hist, q_low, kk, vv, att,
        lse_row, ssd, start, steps, cum, tot, dt, z, cos, sin, taps, prm, chan, lengths,
    )
    grad_hidden, grad_a, shared = finish(
        shards, lin, normed, wfull_a, hid, grad_own, gains, gain_two
    )

    def place(v, width, start, axis=0):
        shape = list(v.shape)
        shape[axis] = width
        return lax.dynamic_update_slice_in_dim(jnp.zeros(shape, f32), v, start, axis)

    conv_full = place(conv_grads[:5, :WI], DI, tp * WI, 1)
    conv_full = jnp.concatenate([conv_full, conv_grads[:5, WI:]], axis=1).reshape(-1)
    gate_full = place(chan_grads[0], DI, tp * WI)
    heads = place(head_grads[:3, :HL], H, tp * HL, 1).reshape(-1)
    small = lax.psum(jnp.concatenate([conv_full, gate_full, heads]), ("shard", "ctx", "tp"))
    width = DI + 2 * N
    conv_all = small[: 5 * width].reshape(5, width)
    gate_all = small[5 * width : 5 * width + DI]
    head_all = small[5 * width + DI :].reshape(3, H)

    maps = shared.sum(0)
    first, second = shared[0] + shared[1], shared[2] + shared[3]
    grad_shared = jnp.concatenate(
        [
            maps[:, : 2 * N],
            first[:, 256 : 256 + HD],
            second[:, 256 : 256 + HD],
            first[:, 256 + HD : 384],
            second[:, 256 + HD : 384],
        ],
        axis=1,
    )
    grad_dt = jnp.concatenate([shared[i, :, 384 : 384 + HL] for i in range(TP)], axis=1)
    return (
        output[None],
        grad_hidden[None],
        maps[:, 384 + GAIN_COL],
        grad_a[:, CZ:CX],
        grad_a[:, CX:CM],
        grad_shared,
        grad_dt,
        head_all[0],
        head_all[1],
        head_all[2],
        conv_all[:4],
        conv_all[4],
        gate_all,
        grad_b[:, CO:CW].T,
        grad_a[:, CQ:CK],
        grad_b[:, CW:CG].T,
        maps[:, 384 + GAIN_COL + 1],
        grad_b[:, CG:CU],
        grad_b[:, CU:CD],
        grad_b[:, CD:CB].T,
    )


def solution(mesh):
    placed = (
        P("shard", "ctx", None),
        P("shard", "ctx", None),
        P("shard"),
        P(("shard", "ctx")),
        P(("shard", "ctx"), "tp"),
        P(("shard", "ctx"), "tp"),
        P(("shard", "ctx"), None),
        P(("shard", "ctx"), None),
        P(),
        P(),
        P(),
        P(),
        P(),
        P(),
        P("tp", ("shard", "ctx")),
        P(("shard", "ctx"), "tp"),
        P("tp", ("shard", "ctx")),
        P(("shard", "ctx")),
        P(("shard", "ctx"), "tp"),
        P(("shard", "ctx"), "tp"),
        P("tp", ("shard", "ctx")),
    )
    return jax.shard_map(
        local,
        mesh=mesh,
        in_specs=placed,
        out_specs=(
            P("shard", "ctx", "tp"),
            P("shard", "ctx", None),
            P(("shard", "ctx", "tp")),
            P(("shard", "ctx"), "tp"),
            P(("shard", "ctx"), "tp"),
            P(("shard", "ctx", "tp"), None),
            P(("shard", "ctx", "tp"), None),
            P(),
            P(),
            P(),
            P(),
            P(),
            P(),
            P("tp", ("shard", "ctx")),
            P(("shard", "ctx"), "tp"),
            P("tp", ("shard", "ctx")),
            P(("shard", "ctx", "tp")),
            P(("shard", "ctx"), "tp"),
            P(("shard", "ctx"), "tp"),
            P("tp", ("shard", "ctx")),
        ),
        check_vma=False,
    )
```

```python
import functools

import jax
import jax.numpy as jnp
from jax import lax
from jax.experimental import pallas as pl
from jax.experimental.pallas import tpu as pltpu
from jax.sharding import PartitionSpec as P

H = 24
P_SIZE = 64
N = 128
NQ = 8
KV = 2
HD = 64
CONVW = 4
DI = 1536
D = 1024
FFL = 512
TP = 4
HL = H // TP
WI = HL * P_SIZE
CH = WI + 2 * N
L = 256

CZ, CX, CM, CQ, CK, CS, CA = 0, 384, 768, 1024, 1152, 1280, 1408
GAIN_COL = 24
CO, CW, CG, CU, CD, CB = 0, 384, 512, 1024, 1536, 2048

EPS = 1e-05
rope_base = 10000.0
FILL = -1e30
HI = lax.Precision.HIGHEST
MESH = pl.DeviceIdType.MESH
f32 = jnp.float32
bf16 = jnp.bfloat16
VLIMIT = 60 * 1024 * 1024


def nn(a, b, precision=None):
    return lax.dot_general(
        a, b, (((1,), (0,)), ((), ())), precision=precision, preferred_element_type=f32
    )


def nt(a, b, precision=None):
    return lax.dot_general(
        a, b, (((1,), (1,)), ((), ())), precision=precision, preferred_element_type=f32
    )


def tn(a, b, precision=None):
    return lax.dot_general(
        a, b, (((0,), (0,)), ((), ())), precision=precision, preferred_element_type=f32
    )


def rows_of(index, size=L):
    return pl.ds(pl.multiple_of(index * size, size), size)


def remote(src, dst, send, recv, **where):
    return pltpu.make_async_remote_copy(
        src_ref=src,
        dst_ref=dst,
        send_sem=send,
        recv_sem=recv,
        device_id=where,
        device_id_type=MESH,
    )


def iota(shape, dim):
    return lax.broadcasted_iota(jnp.int32, shape, dim)


def loop(n, body):
    lax.fori_loop(0, n, lambda i, c: (body(i), c)[1], 0)


def greet(shards, tp_too, ctx_too=True, shard_too=True):
    barrier = pltpu.get_barrier_semaphore()
    count = 0
    z, c, t = lax.axis_index("shard"), lax.axis_index("ctx"), lax.axis_index("tp")
    if ctx_too:
        pl.semaphore_signal(barrier, inc=1, device_id={"ctx": 1 - c}, device_id_type=MESH)
        count += 1
    if shard_too:

        def one(k):
            pl.semaphore_signal(
                barrier, inc=1, device_id={"shard": lax.rem(z + 1 + k, shards)}, device_id_type=MESH
            )

        loop(shards - 1, one)
        count += shards - 1
    if tp_too:
        for d in range(1, TP):
            pl.semaphore_signal(
                barrier, inc=1, device_id={"tp": lax.rem(t + d, TP)}, device_id_type=MESH
            )
            count += 1
    pl.semaphore_wait(barrier, count)


class Gather:
    def __init__(self, shards, src, dst, zsend, csend, recv, own):
        self.s, self.src, self.dst = shards, src, dst
        self.zsend, self.csend, self.recv, self.own = zsend, csend, recv, own
        self.z, self.c = lax.axis_index("shard"), lax.axis_index("ctx")
        self.r = src.shape[0]

    def block(self, g):
        return self.dst.at[rows_of(g, self.r)]

    def to_shard(self, k):
        g = 2 * self.z + self.c
        return remote(
            self.src,
            self.block(g),
            self.zsend.at[k],
            self.recv.at[g],
            shard=lax.rem(self.z + k, self.s),
        )

    def to_core(self, k):
        zz = lax.rem(self.z + k, self.s)
        g = 2 * zz + self.c
        return remote(self.block(g), self.block(g), self.csend.at[k], self.recv.at[g], ctx=1 - self.c)

    def got(self, k, core):
        zz = lax.rem(self.z + k, self.s)
        g = 2 * zz + core
        return remote(self.block(g), self.block(g), self.csend.at[k], self.recv.at[g], ctx=1 - self.c)

    def start(self):
        keep = pltpu.make_async_copy(self.src, self.block(2 * self.z + self.c), self.own)
        keep.start()
        loop(self.s - 1, lambda k: self.to_shard(k + 1).start())
        keep.wait()
        self.to_core(0).start()

    def forward(self, first=0, last=None):
        def one(k):
            self.got(k + 1, self.c).wait_recv()
            self.to_core(k + 1).start()

        lax.fori_loop(
            first, self.s - 1 if last is None else last, lambda k, carry: (one(k), carry)[1], 0
        )

    def finish(self):
        loop(self.s, lambda k: self.got(k, 1 - self.c).wait_recv())
        loop(self.s, lambda k: self.to_core(k).wait_send())
        loop(self.s - 1, lambda k: self.to_shard(k + 1).wait_send())

    @staticmethod
    def sems(shards):
        dma = pltpu.SemaphoreType.DMA
        return [dma((shards,)), dma((shards,)), dma((2 * shards,)), dma(())]


class Scatter:
    def __init__(self, shards, src, sib, stage, land, csend, crecv, zsend, zrecv):
        self.s, self.src, self.sib, self.stage, self.land = shards, src, sib, stage, land
        self.csend, self.crecv, self.zsend, self.zrecv = csend, crecv, zsend, zrecv
        self.z, self.c = lax.axis_index("shard"), lax.axis_index("ctx")
        self.r = src.shape[0] // (2 * shards)

    def to_core(self, k):
        zz = lax.rem(self.z + k, self.s)
        return remote(
            self.src.at[rows_of(2 * zz + 1 - self.c, self.r)],
            self.sib.at[zz],
            self.csend.at[zz],
            self.crecv.at[zz],
            ctx=1 - self.c,
        )

    def to_shard(self, k):
        zz = lax.rem(self.z + k, self.s)
        return remote(
            self.stage.at[zz], self.land.at[self.z], self.zsend.at[zz], self.zrecv.at[self.z], shard=zz
        )

    def arrive(self, k):
        zz = lax.rem(self.z + k, self.s)
        return remote(
            self.stage.at[zz], self.land.at[zz], self.zsend.at[zz], self.zrecv.at[zz], shard=zz
        )

    def start(self):
        loop(self.s - 1, lambda k: self.to_core(k + 1).start())
        self.to_core(0).start()

    def middle(self):
        def one(k):
            zz = lax.rem(self.z + 1 + k, self.s)
            self.to_core(k + 1).wait_recv()
            both = self.src[rows_of(2 * zz + self.c, self.r), :].astype(f32)
            self.stage[zz] = (both + self.sib[zz].astype(f32)).astype(bf16)
            self.to_shard(k + 1).start()

        loop(self.s - 1, one)

    def finish(self, out, cols=None):
        self.to_core(0).wait_recv()
        own = self.src[rows_of(2 * self.z + self.c, self.r), :].astype(f32)
        out[...] = own + self.sib[self.z].astype(f32)

        def one(k):
            zz = lax.rem(self.z + 1 + k, self.s)
            self.arrive(k + 1).wait_recv()
            out[...] += self.land[zz].astype(f32)

        loop(self.s - 1, one)
        loop(self.s, lambda k: self.to_core(k).wait_send())
        loop(self.s - 1, lambda k: self.to_shard(k + 1).wait_send())

    @staticmethod
    def scratch(shards, rows, cols):
        dma = pltpu.SemaphoreType.DMA
        block = pltpu.VMEM((shards, rows // (2 * shards), cols), bf16)
        return [block, block, block] + [dma((shards,))] * 4


def sigmoid(v):
    return 1.0 / (1.0 + jnp.exp(-v))


def softplus(v):
    return jnp.maximum(v, 0.0) + jnp.log1p(jnp.exp(-jnp.abs(v)))


def swap_half(v):
    width = v.shape[1]
    low = iota(v.shape, 1) % HD < HD // 2
    return jnp.where(low, pltpu.roll(v, width - HD // 2, 1), pltpu.roll(v, HD // 2, 1))


def low_lanes(shape):
    return iota(shape, 1) < 64


def spread():
    return (iota((N, WI), 1) // P_SIZE == iota((N, WI), 0)).astype(f32)


def first_row():
    return (iota((8, N), 0) == 0).astype(f32)


def wide(column, width):
    return jnp.concatenate([column] * (width // column.shape[1]), axis=1)


def lower_ones():
    return (iota((L, L), 0) >= iota((L, L), 1)).astype(f32)


def project_kernel(shards, hid, wa, wfull, normed, gains, z_out, cin, q_out, kv_out, dt_out, *sems):
    greet(shards, False)
    gather = Gather(shards, wa, wfull, *sems)
    gather.start()
    gather.forward()
    gather.finish()
    turned = wfull[:, CS:CA].astype(f32).T
    gains[...] = turned[GAIN_COL : GAIN_COL + 8]
    gain = gains[0:1, :]

    def block(i):
        rows = rows_of(i)
        x = hid[rows, :].astype(f32)
        scale = lax.rsqrt(jnp.mean(x * x, -1, keepdims=True) + EPS)
        low = (x * scale * gain).astype(bf16)
        normed[rows, :] = low
        z_out[rows, :] = nn(low, wfull[:, CZ:CX])
        cin[rows, :] = nn(low, wfull[:, CX:CQ]).astype(bf16)
        rest = nn(low, wfull[:, CQ:CA])
        q_out[rows, :] = rest[:, : CK - CQ]
        kv_out[rows, :] = rest[:, CK - CQ : CS - CQ]
        dt_out[rows, :] = rest[:, CS - CQ :]

    loop(hid.shape[0] // L, block)


def project(shards, hid, wa):
    t = hid.shape[0]
    out = [
        ((D, CA), bf16),
        ((t, D), bf16),
        ((8, D), f32),
        ((t, WI), f32),
        ((t, CH), bf16),
        ((t, 128), f32),
        ((t, 128), f32),
        ((t, 128), f32),
    ]
    return pl.pallas_call(
        functools.partial(project_kernel, shards),
        out_shape=[jax.ShapeDtypeStruct(*o) for o in out],
        in_specs=[pl.BlockSpec(memory_space=pltpu.VMEM)] * 2,
        out_specs=[pl.BlockSpec(memory_space=pltpu.VMEM)] * len(out),
        scratch_shapes=Gather.sems(shards),
        compiler_params=pltpu.CompilerParams(
            collective_id=0, has_side_effects=True, vmem_limit_bytes=VLIMIT
        ),
        name="project",
    )(hid, wa)


def head_scalars(dt_raw, prm):
    real = iota(dt_raw.shape, 1) < HL
    steps = jnp.where(real, softplus(dt_raw + prm[0:1, :]), 0.0)
    rates = steps * prm[1:2, :]
    return steps, rates


def pair_columns(v, pair):
    return v[:, 128 * pair : 128 * pair + 128]


def own_half(v, half):
    return jnp.where(low_lanes(v.shape) == (half == 0), v, jnp.zeros_like(v))


def forward_kernel(
    shards,
    cin, q_in, kv_in, dt_raw, z_in, cos, sin, wb, taps, prm, chan, length,
    wfull, pre, hist, q_low, kk, vv, att, lse, lse_row, ssd, start, steps_out, cum_out, tot_out,
    gated_low, square,
    pad, act, state, carried, scores_m, scores_l,
    hist_in, zs, cs, gr, own_sem, xs, xr,
):
    c = lax.axis_index("ctx")
    t = cin.shape[0]
    blocks = t // L
    greet(shards, False)
    gather = Gather(shards, wb, wfull, zs, cs, gr, own_sem)
    gather.start()

    def swap(src, dst, i):
        return remote(src, dst, xs.at[i], xr.at[i], ctx=1 - c)

    tail = swap(cin.at[pl.ds(t - 16, 16)], hist_in, 0)
    tail.start()
    low128 = low_lanes((L, 128))

    def rotary(i):
        rows = rows_of(i)
        cosine, sine = cos[rows, :], sin[rows, :]
        v = q_in[rows, :]
        q_low[rows, :] = (v * cosine + swap_half(v) * sine).astype(bf16)
        v = kv_in[rows, :]
        other = pltpu.roll(v, 64, 1)
        twice = jnp.where(low128, v, other)
        kk[0, rows, :] = (twice * cosine + swap_half(twice) * sine).astype(bf16)
        vv[0, rows, :] = jnp.where(low128, other, v).astype(bf16)

    loop(blocks, rotary)
    keys = swap(kk.at[0], kk.at[1], 1)
    keys.start()
    vals = swap(vv.at[0], vv.at[1], 2)
    vals.start()

    tail.wait_recv()
    before = hist_in[8:16, :].astype(f32)
    hist[...] = jnp.where((iota((8, CH), 0) >= 5) & (c > 0), before, 0.0)
    pad[0:8, :] = hist[...]

    def fill(i):
        pad[pl.ds(pl.multiple_of(i * L + 8, 8), L), :] = cin[rows_of(i), :].astype(f32)

    loop(blocks, fill)
    ones = lower_ones()
    expand = spread()
    state[...] = jnp.zeros_like(state)

    for i in range(blocks):
        rows = pl.ds(i * L, L)
        v = taps[4:5, :] + taps[0:1, :] * pad[pl.ds(i * L + 5, L), :]
        for j in range(1, CONVW):
            v = v + taps[j : j + 1, :] * pad[pl.ds(i * L + 5 + j, L), :]
        pre[rows, :] = v
        a = v * sigmoid(v)
        act[rows, :] = a
        steps, rates = head_scalars(dt_raw[rows, :], prm)
        cum = nn(ones, rates, HI)
        tot = cum[L - 1 : L, :]
        steps_out[rows, :] = steps
        cum_out[rows, :] = cum
        tot_out[i] = jnp.broadcast_to(tot, (8, 128))
        weight = nn(jnp.exp(tot - cum) * steps, expand, HI)
        start[i] = state[...]
        add = tn(a[:, WI : WI + N].astype(bf16), (weight * a[:, :WI]).astype(bf16))
        decay = nn(jnp.broadcast_to(jnp.exp(tot), (8, 128)), expand, HI)[0:1, :]
        state[...] = decay * state[...] + add

    states = swap(state, carried, 3)
    states.start()

    keys.wait_recv()
    vals.wait_recv()
    scale = HD ** (-0.5)
    limit = length[0] - c * t

    def stacked(v):
        return jnp.concatenate([own_half(v, 0), own_half(v, 1)], axis=0)

    for i in range(blocks):
        rows = pl.ds(i * L, L)
        width = (i + 1) * L
        q2 = stacked(q_low[rows, :].astype(f32)).astype(bf16)
        s = nt(q2, kk[0, 0:width, :]) * scale
        at = iota(s.shape, 0) % L + i * L
        col = iota(s.shape, 1)
        s = jnp.where((col <= at) & (col < limit), s, FILL)
        peak = jnp.max(s, -1, keepdims=True)
        e = jnp.exp(s - peak)
        total = jnp.sum(e, -1, keepdims=True)
        o = nn(e.astype(bf16), vv[0, 0:width, :])
        scores_m[...] = jnp.broadcast_to(peak, (2 * L, 128))
        scores_l[0] = jnp.broadcast_to(total, (2 * L, 128))
        scores_l[1] = o

        @pl.when(c > 0)
        def earlier():
            s2 = nt(q2, kk[1]) * scale
            old = scores_m[:, 0:1]
            new = jnp.maximum(old, jnp.max(s2, -1, keepdims=True))
            e2 = jnp.exp(s2 - new)
            fade = jnp.exp(old - new)
            scores_m[...] = jnp.broadcast_to(new, (2 * L, 128))
            scores_l[0] = fade * scores_l[0] + jnp.sum(e2, -1, keepdims=True)
            scores_l[1] = fade * scores_l[1] + nn(e2.astype(bf16), vv[1])

        total = scores_l[0]
        o = scores_l[1] / total
        att[rows, :] = jnp.where(low128, o[:L], o[L:])
        logs = scores_m[...] + jnp.log(total)
        both = jnp.where(low128, logs[:L], logs[L:])
        lse[rows, :] = both
        turned = both.T
        lse_row[0:1, rows] = turned[0:1]
        lse_row[1:2, rows] = turned[64:65]
        lse_row[2:8, rows] = jnp.zeros((6, L), f32)

    gather.forward()
    states.wait_recv()
    carried[...] = jnp.where(c > 0, carried[...], 0.0)
    mask = iota((L, L), 0) >= iota((L, L), 1)
    for i in range(blocks):
        rows = pl.ds(i * L, L)
        if i > 0:
            decay = nn(jnp.exp(tot_out[i - 1]), expand, HI)[0:1, :]
            carried[...] = carried[...] * decay
        start[i] = start[i] + carried[...]
        s0 = start[i].astype(bf16)
        steps, cum = steps_out[rows, :], cum_out[rows, :]
        x = act[rows, 0:WI]
        xl = x.astype(bf16)
        in_map = act[rows, WI : WI + N].astype(bf16)
        out_map = act[rows, WI + N : CH].astype(bf16)
        gram = nt(out_map, in_map)
        cum_t, steps_t = cum.T, steps.T
        inner = []
        for pair in range(HL // 2):
            halves = []
            for half in range(2):
                h = 2 * pair + half
                decay = jnp.exp(jnp.where(mask, cum[:, h : h + 1] - cum_t[h : h + 1, :], FILL))
                mixing = gram * decay * steps_t[h : h + 1, :]
                halves.append(nn(mixing.astype(bf16), pair_columns(xl, pair)))
            inner.append(jnp.where(low128, halves[0], halves[1]))
        y = jnp.concatenate(inner, axis=1)
        y = y + nn(jnp.exp(cum), expand, HI) * nn(out_map, s0) + chan[1:2, :] * x
        ssd[rows, :] = y
        zz = z_in[rows, :]
        gated = y * zz * sigmoid(zz)
        gated_low[rows, :] = (gated * chan[0:1, :]).astype(bf16)
        square[:, rows] = nt(jnp.ones((8, WI), f32), gated * gated, HI)

    gather.finish()
    for copy in (tail, keys, vals, states):
        copy.wait_send()


def forward(shards, cin, q, kv, dt, z, cos, sin, wb, taps, prm, chan, length):
    t = cin.shape[0]
    out = [
        ((D, CG), bf16),
        ((t, CH), f32),
        ((8, CH), f32),
        ((t, 128), bf16),
        ((2, t, 128), bf16),
        ((2, t, 128), bf16),
        ((t, 128), f32),
        ((t, 128), f32),
        ((8, t), f32),
        ((t, WI), f32),
        ((t // L, N, WI), f32),
        ((t, 128), f32),
        ((t, 128), f32),
        ((t // L, 8, 128), f32),
        ((t, WI), bf16),
        ((8, t), f32),
    ]
    dma = pltpu.SemaphoreType.DMA
    vmem = pl.BlockSpec(memory_space=pltpu.VMEM)
    return pl.pallas_call(
        functools.partial(forward_kernel, shards),
        out_shape=[jax.ShapeDtypeStruct(*o) for o in out],
        in_specs=[vmem] * 11 + [pl.BlockSpec(memory_space=pltpu.SMEM)],
        out_specs=[vmem] * len(out),
        scratch_shapes=[
            pltpu.VMEM((t + 8, CH), f32),
            pltpu.VMEM((t, CH), f32),
            pltpu.VMEM((N, WI), f32),
            pltpu.VMEM((N, WI), f32),
            pltpu.VMEM((2 * L, 128), f32),
            pltpu.VMEM((2, 2 * L, 128), f32),
            pltpu.VMEM((16, CH), bf16),
        ]
        + Gather.sems(shards)
        + [dma((4,)), dma((4,))],
        compiler_params=pltpu.CompilerParams(
            collective_id=1, has_side_effects=True, vmem_limit_bytes=VLIMIT
        ),
        name="mix_forward",
    )(cin, q, kv, dt, z, cos, sin, wb, taps, prm, chan, length)


def ffn_kernel(
    shards,
    hid, cot, gl, att, square, wb, wm_own, gains, length,
    osend, out_own, grad_own, grads, gain_grad, total_square, ggl, grad_att, dots,
    grad_res, partial, seed, send1, recv1, low_two, grad_act, act, gg, gu, gown,
    unit, scale_keep, gsend, grecv, sqall, wm,
    zs, cs, zr, own_sem, sqs, sqr, s1, r1, ns, nr, gs, gr, hs, hr,
):
    t = hid.shape[0]
    tp, c = lax.axis_index("tp"), lax.axis_index("ctx")
    chunk = t // TP
    width = D // TP
    greet(shards, True)
    gather = Gather(shards, wm_own, wm, zs, cs, zr, own_sem)
    gather.start()

    def peer(d):
        return lax.rem(tp + d, TP)

    def crow(i):
        return rows_of(i, chunk)

    def square_to(d):
        return remote(sqall.at[tp], sqall.at[tp], sqs.at[d], sqr.at[tp], tp=peer(d))

    def square_from(d):
        return remote(sqall.at[tp], sqall.at[peer(d)], sqs.at[d], sqr.at[peer(d)], tp=peer(d))

    sqall[tp] = square[...]
    for d in range(1, TP):
        square_to(d).start()
    limit = length[0] - c * t

    def mask_seed(i):
        rows = crow(i)
        live = iota((chunk, D), 0) + i * chunk < limit
        seed[rows, :] = jnp.where(live, cot[rows, :].astype(f32), 0.0).astype(bf16)

    loop(TP, mask_seed)
    for d in range(1, TP):
        square_from(d).wait_recv()
    total_square[...] = sqall[0] + sqall[1] + sqall[2] + sqall[3]

    def first_to(d):
        return remote(send1.at[d], recv1.at[tp], s1.at[d], r1.at[tp], tp=peer(d))

    def first_from(d):
        return remote(send1.at[d], recv1.at[peer(d)], s1.at[d], r1.at[peer(d)], tp=peer(d))

    def mix(k):
        d = lax.rem(k + 1, TP)
        rows = crow(peer(d))
        scale = lax.rsqrt(total_square[:, rows] / DI + EPS)
        column = wide(tn(scale, first_row(), HI), D)
        both = nt(gl[rows, :], wb[:, CO:CW]) * column + nt(att[rows, :], wb[:, CW:CG])
        partial[rows, :] = both

        @pl.when(d > 0)
        def go():
            send1[d] = both.astype(bf16)
            first_to(d).start()

    loop(TP, mix)
    gather.forward(0, 1)
    for d in range(1, TP):
        first_from(d).wait_recv()
    own = crow(tp)
    acc = hid[own, :].astype(f32) + partial[own, :]
    for d in range(1, TP):
        acc = acc + recv1[peer(d)].astype(f32)
    scale = lax.rsqrt(jnp.mean(acc * acc, -1, keepdims=True) + EPS)
    scale_keep[...] = jnp.broadcast_to(scale, scale_keep.shape)
    unit[...] = acc * scale
    gain = gains[1:2, :]
    low_two[own, :] = (unit[...] * gain).astype(bf16)

    def norm_to(d):
        return remote(low_two.at[own], low_two.at[own], ns.at[d], nr.at[tp], tp=peer(d))

    def norm_from(d):
        there = low_two.at[crow(peer(d))]
        return remote(there, there, ns.at[d], nr.at[peer(d)], tp=peer(d))

    for d in range(1, TP):
        norm_to(d).start()
    gather.forward(1)
    gather.finish()

    def act_grad(i):
        rows = crow(i)
        grad_act[rows, :] = nn(seed[rows, :], wm[:, CD - CG : CB - CG])

    loop(TP, act_grad)

    def grad_to(d):
        return remote(gsend.at[d], grecv.at[tp], gs.at[d], gr.at[tp], tp=peer(d))

    def grad_from(d):
        return remote(gsend.at[d], grecv.at[peer(d)], gs.at[d], gr.at[peer(d)], tp=peer(d))

    def hidden_units(d):
        i = peer(d)
        rows = crow(i)

        @pl.when(d > 0)
        def arrive():
            norm_from(d).wait_recv()

        low = low_two[rows, :]
        gate, up = nn(low, wm[:, 0:FFL]), nn(low, wm[:, FFL : 2 * FFL])
        sig = sigmoid(gate)
        silu = gate * sig
        hidden_act = (silu * up).astype(bf16)
        act[rows, :] = hidden_act
        ga = grad_act[rows, :]
        g1 = (ga * up * (sig * (1.0 + gate * (1.0 - sig)))).astype(bf16)
        g2 = (ga * silu).astype(bf16)
        gg[rows, :] = g1
        gu[rows, :] = g2
        back = nt(g1, wm[:, 0:FFL]) + nt(g2, wm[:, FFL : 2 * FFL])

        @pl.when(d > 0)
        def go():
            gsend[d] = back.astype(bf16)
            grad_to(d).start()

        @pl.when(d == 0)
        def keep():
            gown[...] = back

        partial[rows, :] = partial[rows, :] + nt(hidden_act, wm[:, 2 * FFL : 3 * FFL])
        for e in range(1, TP):
            osend[e, rows, :] = partial[rows, rows_of(peer(e), width)].astype(bf16)

    loop(TP, hidden_units)

    def weight_grads(i):
        feats = rows_of(i)
        low = low_two[:, feats]
        grads[feats, CG:CU] = tn(low, gg[...]).astype(bf16)
        grads[feats, CU:CD] = tn(low, gu[...]).astype(bf16)

    loop(D // L, weight_grads)
    for d in range(1, TP):
        grad_from(d).wait_recv()
    back = gown[...]
    for d in range(1, TP):
        back = back + grecv[peer(d)].astype(f32)
    gain_grad[...] = jnp.broadcast_to(jnp.sum(back * unit[...], 0, keepdims=True), (8, D))
    weighted = back * gain
    mean = jnp.mean(weighted * unit[...], -1, keepdims=True)
    res = seed[own, :].astype(f32) + scale_keep[:, 0:1] * (weighted - unit[...] * mean)
    grad_own[...] = res
    grad_res[own, :] = res.astype(bf16)

    def res_to(d):
        return remote(grad_res.at[own], grad_res.at[own], hs.at[d], hr.at[tp], tp=peer(d))

    def res_from(d):
        there = grad_res.at[crow(peer(d))]
        return remote(there, there, hs.at[d], hr.at[peer(d)], tp=peer(d))

    for d in range(1, TP):
        res_to(d).start()

    def down_grads(i):
        feats = rows_of(i)
        grads[feats, CD:CB] = tn(seed[:, feats], act[...]).astype(bf16)

    loop(D // L, down_grads)
    mine = rows_of(tp, width)
    out_own[...] = hid[:, mine].astype(f32) + partial[:, mine]
    for d in range(1, TP):
        norm_to(d).wait_send()

    def out_back(d):
        i = peer(d)
        rows = crow(i)

        @pl.when(d > 0)
        def arrive():
            res_from(d).wait_recv()

        square_scale = lax.rsqrt(total_square[:, rows] / DI + EPS)
        column = wide(tn(square_scale, first_row(), HI), D)
        got = grad_res[rows, :]
        proj = (column * got.astype(f32)).astype(bf16)
        low_two[rows, :] = proj
        product = nn(proj, wb[:, CO:CW])
        ggl[rows, :] = product
        dots[:, rows] = nt(jnp.ones((8, WI), f32), product * gl[rows, :].astype(f32), HI)
        grad_att[rows, :] = nn(got, wb[:, CW:CG]).astype(bf16)

    loop(TP, out_back)

    def out_grads(i):
        feats = rows_of(i)
        grads[feats, CO:CW] = tn(low_two[:, feats], gl[...]).astype(bf16)
        grads[feats, CW:CG] = tn(grad_res[:, feats], att[...]).astype(bf16)

    loop(D // L, out_grads)
    for d in range(1, TP):
        square_to(d).wait_send()
        first_to(d).wait_send()
        grad_to(d).wait_send()
        res_to(d).wait_send()


def ffn(shards, hid, cot, gl, att, square, wb, wm_own, gains, length):
    t = hid.shape[0]
    chunk = t // TP
    out = [
        ((TP, t, D // TP), bf16),
        ((t, D // TP), f32),
        ((chunk, D), f32),
        ((D, CB), bf16),
        ((8, D), f32),
        ((8, t), f32),
        ((t, WI), f32),
        ((t, 128), bf16),
        ((8, t), f32),
    ]
    dma = pltpu.SemaphoreType.DMA
    vmem = pl.BlockSpec(memory_space=pltpu.VMEM)
    return pl.pallas_call(
        functools.partial(ffn_kernel, shards),
        out_shape=[jax.ShapeDtypeStruct(*o) for o in out],
        in_specs=[vmem] * 8 + [pl.BlockSpec(memory_space=pltpu.SMEM)],
        out_specs=[vmem] * len(out),
        scratch_shapes=[
            pltpu.VMEM((t, D), bf16),
            pltpu.VMEM((t, D), f32),
            pltpu.VMEM((t, D), bf16),
            pltpu.VMEM((TP, chunk, D), bf16),
            pltpu.VMEM((TP, chunk, D), bf16),
            pltpu.VMEM((t, D), bf16),
            pltpu.VMEM((t, FFL), f32),
            pltpu.VMEM((t, FFL), bf16),
            pltpu.VMEM((t, FFL), bf16),
            pltpu.VMEM((t, FFL), bf16),
            pltpu.VMEM((chunk, D), f32),
            pltpu.VMEM((chunk, D), f32),
            pltpu.VMEM((chunk, 128), f32),
            pltpu.VMEM((TP, chunk, D), bf16),
            pltpu.VMEM((TP, chunk, D), bf16),
            pltpu.VMEM((TP, 8, t), f32),
            pltpu.VMEM((D, CB - CG), bf16),
        ]
        + Gather.sems(shards)
        + [dma((TP,))] * 10,
        compiler_params=pltpu.CompilerParams(
            collective_id=2, has_side_effects=True, vmem_limit_bytes=VLIMIT
        ),
        name="feed_forward",
    )(hid, cot, gl, att, square, wb, wm_own, gains, length)


def backward_kernel(
    shards,
    ggl, grad_att, dots_in, total_square, grads, osend, out_own,
    pre, cin, hist, q_low, kk, vv, att, lse_row, ssd, start, steps_in, cum_in, tot_in, dt_raw, z_in,
    cos, sin, taps, prm, chan, length,
    output, lin, grad_b, small,
    orecv, dots, dk, dv, dy, dpre, ends, dstate, carry, kv_out, kv_in, pad, edge_out, edge_in,
    sib, stage, land, csend, crecv, zsend, zrecv, xs, xr, ts, tr, os, orr,
):
    c, tp = lax.axis_index("ctx"), lax.axis_index("tp")
    t = cin.shape[0]
    blocks = t // L
    greet(shards, True)
    scatter = Scatter(shards, grads, sib, stage, land, csend, crecv, zsend, zrecv)
    scatter.start()

    def swap(src, dst, i):
        return remote(src, dst, xs.at[i], xr.at[i], ctx=1 - c)

    def peer(d):
        return lax.rem(tp + d, TP)

    def dot_to(d):
        return remote(dots.at[tp], dots.at[tp], ts.at[d], tr.at[tp], tp=peer(d))

    def dot_from(d):
        return remote(dots.at[tp], dots.at[peer(d)], ts.at[d], tr.at[peer(d)], tp=peer(d))

    dots[tp] = dots_in[...]
    for d in range(1, TP):
        dot_to(d).start()

    def out_to(d):
        return remote(osend.at[d], orecv.at[tp], os.at[d], orr.at[tp], tp=peer(d))

    def out_from(d):
        return remote(osend.at[d], orecv.at[peer(d)], os.at[d], orr.at[peer(d)], tp=peer(d))

    for d in range(1, TP):
        out_to(d).start()
    conv_grads = small.at[:, 0:CH]
    chan_grads = small.at[:, CH : CH + WI]
    head_grads = small.at[:, CH + WI : CH + WI + 128]
    expand = spread()
    low128 = low_lanes((L, 128))
    small[...] = jnp.zeros_like(small)
    for d in range(1, TP):
        dot_from(d).wait_recv()

    def gated_back(i):
        rows = rows_of(i)
        both = dots[0, :, rows] + dots[1, :, rows] + dots[2, :, rows] + dots[3, :, rows]
        share = both / ((total_square[:, rows] / DI + EPS) * DI)
        column = wide(tn(share, first_row(), HI), WI)
        zz, y = z_in[rows, :], ssd[rows, :]
        sig = sigmoid(zz)
        silu = zz * sig
        gated = y * silu
        product = ggl[rows, :]
        chan_grads[0:1, :] += jnp.sum(product * gated, 0, keepdims=True)
        grad_gated = product * chan[0:1, :] - column * gated
        grad_y = grad_gated * silu
        dy[rows, :] = grad_y
        lin[rows, CZ:CX] = (grad_gated * y * (sig * (1.0 + zz * (1.0 - sig)))).astype(bf16)
        v = pre[rows, WI + N : CH]
        out_map = (v * sigmoid(v)).astype(bf16)
        ends[i] = tn(out_map, (nn(jnp.exp(cum_in[rows, :]), expand, HI) * grad_y).astype(bf16))

    loop(blocks, gated_back)
    dstate[...] = jnp.zeros_like(dstate)

    def chain(k):
        i = blocks - 1 - k
        add = ends[i]
        ends[i] = dstate[...]
        dstate[...] = nn(jnp.exp(tot_in[i]), expand, HI)[0:1, :] * dstate[...] + add

    loop(blocks, chain)
    states = swap(dstate, carry, 0)
    states.start()
    scatter.middle()

    scale = HD ** (-0.5)
    limit = length[0] - c * t
    dk[...] = jnp.zeros_like(dk)
    dv[...] = jnp.zeros_like(dv)
    head_of = ((iota((8, 128), 1) // HD) == iota((8, 128), 0)).astype(f32)

    def stacked(v):
        return jnp.concatenate([own_half(v, 0), own_half(v, 1)], axis=0).astype(bf16)

    def side_by_side(v):
        return jnp.concatenate([v[0:1, :], v[1:2, :]], axis=1)

    for i in range(blocks):
        rows = pl.ds(i * L, L)
        width = (i + 1) * L
        q2 = stacked(q_low[rows, :].astype(f32))
        go = grad_att[rows, :].astype(f32)
        go2 = stacked(go)
        row_dot = side_by_side(nt(head_of, go * att[rows, :], HI))
        logs = side_by_side(lse_row[:, rows])
        turn = cos[rows, :], sin[rows, :]

        def keys_of(part, size, masked):
            k, v = kk[part, 0:size, :], vv[part, 0:size, :]
            s = nt(k, q2) * scale - logs
            if masked:
                at = iota(s.shape, 1) % L + i * L
                row = iota(s.shape, 0)
                s = jnp.where((row <= at) & (row < limit), s, FILL)
            p = jnp.exp(s)
            ds = (p * (nt(v, go2) - row_dot)).astype(bf16)
            dv[part, 0:size, :] += nn(p.astype(bf16), go2)
            dk[part, 0:size, :] += nn(ds, q2)
            out = tn(ds, k) * scale
            out = jnp.where(low128, out[:L], out[L:])
            return out * turn[0] - swap_half(out) * turn[1]

        pad[rows, 0:128] = keys_of(0, width, True)

        @pl.when(c > 0)
        def earlier():
            pad[rows, 0:128] += keys_of(1, t, False)

        lin[rows, CQ:CK] = pad[rows, 0:128].astype(bf16)

    def key_values(part, rows):
        gk, gv = dk[part, rows, :] * scale, dv[part, rows, :]
        return jnp.where(low128, gk + pltpu.roll(gk, 64, 1), gv + pltpu.roll(gv, 64, 1))

    def pack(i):
        rows = rows_of(i)
        kv_out[rows, :] = key_values(1, rows).astype(bf16)

    loop(blocks, pack)
    pairs = swap(kv_out, kv_in, 1)
    pairs.start()

    pad[0:8, :] = hist[...]

    def fill(i):
        pad[pl.ds(pl.multiple_of(i * L + 8, 8), L), :] = cin[rows_of(i), :].astype(f32)

    loop(blocks, fill)
    states.wait_recv()
    carry[...] = jnp.where(c == 0, carry[...], 0.0)

    def add_carry(k):
        i = blocks - 1 - k
        ends[i] = ends[i] + carry[...]
        carry[...] = nn(jnp.exp(tot_in[i]), expand, HI)[0:1, :] * carry[...]

    loop(blocks, add_carry)
    mask = iota((L, L), 0) >= iota((L, L), 1)
    ones = lower_ones()
    lane = iota((L, 128), 1)

    def fold(v):
        return nt(v, expand, HI)

    def scan_back(i):
        rows = rows_of(i)
        v = pre[rows, :]
        sig = sigmoid(v)
        a = v * sig
        x = a[:, :WI]
        xl, bl, cl = x.astype(bf16), a[:, WI : WI + N].astype(bf16), a[:, WI + N :].astype(bf16)
        steps, cum = steps_in[rows, :], cum_in[rows, :]
        tot = cum[L - 1 : L, :]
        ecum, wend = jnp.exp(cum), jnp.exp(tot - cum)
        weight = wend * steps
        ecum_x, weight_x = nn(ecum, expand, HI), nn(weight, expand, HI)
        grad_y = dy[rows, :]
        dyl = grad_y.astype(bf16)
        s0, d1 = start[i], ends[i]
        s0l, d1l = s0.astype(bf16), d1.astype(bf16)
        bd, cs = nn(bl, d1l), nn(cl, s0l)
        dw = fold(x * bd)
        crossing = jnp.broadcast_to(jnp.sum(s0 * d1, 0, keepdims=True), (8, WI))
        dtot = jnp.sum(weight * dw, 0, keepdims=True) + jnp.exp(tot) * fold(crossing)[0:1, :]
        gram = nt(cl, bl)
        cum_t, steps_t = cum.T, steps.T
        dgram = jnp.zeros((L, L), f32)
        row_sums = jnp.zeros((L, 128), f32)
        col_sums, inner = [], []
        for pair in range(HL // 2):
            xp, dp = pair_columns(xl, pair), pair_columns(dyl, pair)
            dpf = pair_columns(grad_y, pair)
            halves = []
            for half in range(2):
                h = 2 * pair + half
                decay = jnp.exp(jnp.where(mask, cum[:, h : h + 1] - cum_t[h : h + 1, :], FILL))
                q = nt(own_half(dpf, half).astype(bf16), xp)
                mixed = gram * decay
                srow = steps_t[h : h + 1, :]
                f = mixed * q
                col_sums.append(jnp.sum(f, 0, keepdims=True))
                row_sums = jnp.where(lane == h, jnp.sum(f * srow, -1, keepdims=True), row_sums)
                dgram = dgram + decay * srow * q
                halves.append(tn((mixed * srow).astype(bf16), dp))
            inner.append(jnp.where(low128, halves[0], halves[1]))
        cols = jnp.concatenate(col_sums + [jnp.zeros((128 - HL, L), f32)], axis=0).T
        dcum = fold(grad_y * cs) * ecum - weight * dw + row_sums - steps * cols
        dcum = dcum + jnp.where(iota((L, 128), 0) == L - 1, dtot, 0.0)
        drate = tn(ones, dcum, HI)
        rate_of = prm[1:2, :]
        raw = dt_raw[rows, :] + prm[0:1, :]
        dstep = (wend * dw + cols + drate * rate_of) * sigmoid(raw)
        dstep = jnp.where(lane < HL, dstep, 0.0)
        lin[rows, CS:CA] = dstep.astype(bf16)
        head_grads[0:1, :] += jnp.sum(dstep, 0, keepdims=True)
        head_grads[1:2, :] += jnp.sum(drate * steps * rate_of, 0, keepdims=True)
        head_grads[2:3, :] += jnp.sum(fold(grad_y * x), 0, keepdims=True)
        slope = sig * (1.0 + v * (1.0 - sig))
        dx = chan[1:2, :] * grad_y + weight_x * bd + jnp.concatenate(inner, axis=1)
        dg = dgram.astype(bf16)
        db = tn(dg, cl) + nt((weight_x * x).astype(bf16), d1l)
        dc = nn(dg, bl) + nt((ecum_x * grad_y).astype(bf16), s0l)
        dpre[rows, 0:WI] = dx * slope[:, :WI]
        dpre[rows, WI : WI + N] = db * slope[:, WI : WI + N]
        dpre[rows, WI + N : CH] = dc * slope[:, WI + N :]

    loop(blocks, scan_back)
    edge_out[...] = dpre[0:8, :]
    edge = swap(edge_out, edge_in, 2)
    edge.start()
    pairs.wait_recv()

    def keys_back(i):
        rows = rows_of(i)
        v = key_values(0, rows) + kv_in[rows, :].astype(f32)
        cosine = jnp.where(low128, cos[rows, :], 1.0)
        sine = jnp.where(low128, sin[rows, :], 0.0)
        lin[rows, CK:CS] = (v * cosine - swap_half(v) * sine).astype(bf16)

    loop(blocks, keys_back)
    edge.wait_recv()
    dpre[pl.ds(t, 8), :] = jnp.where(c == 0, edge_in[...], 0.0)
    for i in range(blocks):
        rows = pl.ds(i * L, L)
        g = dpre[rows, :]
        conv_grads[4:5, :] += jnp.sum(g, 0, keepdims=True)
        back = jnp.zeros_like(g)
        for j in range(CONVW):
            back = back + taps[j : j + 1, :] * dpre[pl.ds(i * L + CONVW - 1 - j, L), :]
            conv_grads[j : j + 1, :] += jnp.sum(g * pad[pl.ds(i * L + 5 + j, L), :], 0, keepdims=True)
        lin[rows, CX:CQ] = back.astype(bf16)
    total = out_own[...]
    for d in range(1, TP):
        out_from(d).wait_recv()
        total = total + orecv[peer(d)].astype(f32)
    output[...] = total.astype(bf16)
    scatter.finish(grad_b)
    for copy in (states, pairs, edge):
        copy.wait_send()
    for d in range(1, TP):
        dot_to(d).wait_send()
        out_to(d).wait_send()


def backward(shards, *args):
    t = args[0].shape[0]
    rows = D // (2 * shards)
    out = [
        ((t, D // TP), bf16),
        ((t, CA), bf16),
        ((rows, CB), f32),
        ((8, CH + WI + 128), f32),
    ]
    dma = pltpu.SemaphoreType.DMA
    vmem = pl.BlockSpec(memory_space=pltpu.VMEM)
    return pl.pallas_call(
        functools.partial(backward_kernel, shards),
        out_shape=[jax.ShapeDtypeStruct(*o) for o in out],
        in_specs=[vmem] * (len(args) - 1) + [pl.BlockSpec(memory_space=pltpu.SMEM)],
        out_specs=[vmem] * len(out),
        scratch_shapes=[
            pltpu.VMEM((TP, t, D // TP), bf16),
            pltpu.VMEM((TP, 8, t), f32),
            pltpu.VMEM((2, t, 128), f32),
            pltpu.VMEM((2, t, 128), f32),
            pltpu.VMEM((t, WI), f32),
            pltpu.VMEM((t + 8, CH), f32),
            pltpu.VMEM((t // L, N, WI), f32),
            pltpu.VMEM((N, WI), f32),
            pltpu.VMEM((N, WI), f32),
            pltpu.VMEM((t, 128), bf16),
            pltpu.VMEM((t, 128), bf16),
            pltpu.VMEM((t + 8, CH), f32),
            pltpu.VMEM((8, CH), f32),
            pltpu.VMEM((8, CH), f32),
        ]
        + Scatter.scratch(shards, D, CB)
        + [dma((3,)), dma((3,))]
        + [dma((TP,))] * 4,
        compiler_params=pltpu.CompilerParams(
            collective_id=3, has_side_effects=True, vmem_limit_bytes=VLIMIT
        ),
        name="mix_backward",
    )(*args)


def finish_kernel(
    shards,
    lin, normed, wfull, hid, grad_own, gains, gain_two, vec,
    low, grad_a, shared, vecs,
    gsend, grecv, gown, grads, misc, misc_low, misc_sum, shsend, vec_sib, vec_z,
    sib, stage, land, csend, crecv, zsend, zrecv,
    sib2, stage2, land2, csend2, crecv2, zsend2, zrecv2,
    vcs, vcr, vzs, vzr, gs, gr, hs, hr, ss, sr, vts, vtr,
):
    tp = lax.axis_index("tp")
    t = lin.shape[0]
    chunk = t // TP
    greet(shards, True)
    scatter = Scatter(shards, grads, sib, stage, land, csend, crecv, zsend, zrecv)
    small = Scatter(shards, misc_low, sib2, stage2, land2, csend2, crecv2, zsend2, zrecv2)
    z, c = lax.axis_index("shard"), lax.axis_index("ctx")
    vec_core = remote(vec, vec_sib, vcs.at[0], vcr.at[0], ctx=1 - c)
    vec_core.start()

    def vec_to_shard(k):
        zz = lax.rem(z + k, shards)
        return remote(vec_z.at[z], vec_z.at[z], vzs.at[zz], vzr.at[z], shard=zz)

    def vec_from_shard(k):
        zz = lax.rem(z + k, shards)
        return remote(vec_z.at[z], vec_z.at[zz], vzs.at[zz], vzr.at[zz], shard=zz)

    def vec_to(d):
        return remote(vecs.at[tp], vecs.at[tp], vts.at[d], vtr.at[tp], tp=peer(d))

    def vec_from(d):
        return remote(vecs.at[tp], vecs.at[peer(d)], vts.at[d], vtr.at[peer(d)], tp=peer(d))

    def peer(d):
        return lax.rem(tp + d, TP)

    def crow(i):
        return rows_of(i, chunk)

    def grad_to(d):
        return remote(gsend.at[d], grecv.at[tp], gs.at[d], gr.at[tp], tp=peer(d))

    def grad_from(d):
        return remote(gsend.at[d], grecv.at[peer(d)], gs.at[d], gr.at[peer(d)], tp=peer(d))

    def product(k):
        d = lax.rem(k + 1, TP)
        back = nt(lin[crow(peer(d)), :], wfull[...])

        @pl.when(d > 0)
        def go():
            gsend[d] = back.astype(bf16)
            grad_to(d).start()

        @pl.when(d == 0)
        def keep():
            gown[...] = back

    loop(TP, product)
    vec_core.wait_recv()
    vec_z[z] = vec[...] + vec_sib[...]
    loop(shards - 1, lambda k: vec_to_shard(k + 1).start())

    def weight_grads(i):
        feats = rows_of(i)
        both = tn(normed[:, feats], lin[...])
        grads[feats, :] = both[:, :CS].astype(bf16)
        misc[feats, :] = both[:, CS:]

    loop(D // L, weight_grads)
    scatter.start()
    loop(shards - 1, lambda k: vec_from_shard(k + 1).wait_recv())
    vecs[tp] = lax.fori_loop(1, shards, lambda k, total: total + vec_z[k], vec_z[0])
    for d in range(1, TP):
        vec_to(d).start()
    for d in range(1, TP):
        grad_from(d).wait_recv()
    own = crow(tp)
    back = gown[...]
    for d in range(1, TP):
        back = back + grecv[peer(d)].astype(f32)
    x = hid[own, :].astype(f32)
    scale = lax.rsqrt(jnp.mean(x * x, -1, keepdims=True) + EPS)
    unit = x * scale
    gain_one = jnp.broadcast_to(jnp.sum(back * unit, 0, keepdims=True), (8, D))
    weighted = back * gains[0:1, :]
    mean = jnp.mean(weighted * unit, -1, keepdims=True)
    low[own, :] = (grad_own[...] + scale * (weighted - unit * mean)).astype(bf16)

    def low_to(d):
        return remote(low.at[own], low.at[own], hs.at[d], hr.at[tp], tp=peer(d))

    def low_from(d):
        there = low.at[crow(peer(d))]
        return remote(there, there, hs.at[d], hr.at[peer(d)], tp=peer(d))

    for d in range(1, TP):
        low_to(d).start()
    gain_rows = jnp.where(iota((8, D), 0) == 0, gain_one, gain_two[...])
    row, lane = iota((8, 128), 0), iota((8, 128), 1)
    pick = ((row < 2) & (lane == GAIN_COL + row)).astype(f32)
    misc_low[...] = (misc[...] + tn(gain_rows, pick, HI)).astype(bf16)
    small.start()
    scatter.middle()
    small.middle()
    scatter.finish(grad_a)
    small.finish(misc_sum)
    part = grad_a.shape[0] // TP
    for i in range(TP):
        shsend[i, :, 0:256] = grad_a[i * part : (i + 1) * part, CM:CQ]
        shsend[i, :, 256:384] = grad_a[i * part : (i + 1) * part, CK:CS]
        shsend[i, :, 384:512] = misc_sum[i * part : (i + 1) * part, :]

    def share_to(d):
        return remote(shsend.at[peer(d)], shared.at[tp], ss.at[d], sr.at[tp], tp=peer(d))

    def share_from(d):
        return remote(shsend.at[peer(d)], shared.at[peer(d)], ss.at[d], sr.at[peer(d)], tp=peer(d))

    for d in range(1, TP):
        share_to(d).start()
    shared[tp] = shsend[tp]
    for d in range(1, TP):
        low_from(d).wait_recv()
        share_from(d).wait_recv()
        vec_from(d).wait_recv()
    vec_core.wait_send()
    loop(shards - 1, lambda k: vec_to_shard(k + 1).wait_send())
    for d in range(1, TP):
        share_to(d).wait_send()
        grad_to(d).wait_send()
        low_to(d).wait_send()
        vec_to(d).wait_send()


def finish(shards, *args):
    t = args[0].shape[0]
    rows = D // (2 * shards)
    chunk = t // TP
    vec = args[-1].shape
    out = [
        ((t, D), bf16),
        ((rows, CS), f32),
        ((TP, rows // TP, 512), f32),
        ((TP, *vec), f32),
    ]
    dma = pltpu.SemaphoreType.DMA
    vmem = pl.BlockSpec(memory_space=pltpu.VMEM)
    return pl.pallas_call(
        functools.partial(finish_kernel, shards),
        out_shape=[jax.ShapeDtypeStruct(*o) for o in out],
        in_specs=[vmem] * len(args),
        out_specs=[vmem] * len(out),
        scratch_shapes=[
            pltpu.VMEM((TP, chunk, D), bf16),
            pltpu.VMEM((TP, chunk, D), bf16),
            pltpu.VMEM((chunk, D), f32),
            pltpu.VMEM((D, CS), bf16),
            pltpu.VMEM((D, 128), f32),
            pltpu.VMEM((D, 128), bf16),
            pltpu.VMEM((rows, 128), f32),
            pltpu.VMEM((TP, rows // TP, 512), f32),
            pltpu.VMEM(vec, f32),
            pltpu.VMEM((shards, *vec), f32),
        ]
        + Scatter.scratch(shards, D, CS)
        + Scatter.scratch(shards, D, 128)
        + [dma((1,)), dma((1,)), dma((shards,)), dma((shards,))]
        + [dma((TP,))] * 8,
        compiler_params=pltpu.CompilerParams(
            collective_id=4, has_side_effects=True, vmem_limit_bytes=VLIMIT
        ),
        name="project_backward",
    )(*args)


def rotary_tables(positions):
    index = jnp.arange(HD // 2, dtype=f32)
    inverse = rope_base ** (-2.0 * index / HD)
    angles = positions[:, None] * inverse[None, :]
    cosine, sine = jnp.cos(angles), jnp.sin(angles)
    return jnp.tile(cosine, (1, 4)), jnp.concatenate([-sine, sine, -sine, sine], axis=1)


def local(
    hidden, cotangent, lengths, norm1_gain, w_z, w_x, w_shared, w_dt, dt_bias, a_log, d_skip,
    conv_w, conv_b, gated_gain, w_out, w_q, w_o, norm2_gain, w_gate, w_up, w_down,
):
    t = hidden.shape[1]
    shards = lax.axis_size("shard")
    tp, c = lax.axis_index("tp"), lax.axis_index("ctx")
    kv_rank = tp * (NQ // TP) // (NQ // KV)
    hid, cot = hidden[0], cotangent[0]

    def cut(v, start, size, axis):
        return lax.dynamic_slice_in_dim(v, start, size, axis)

    key_start = 2 * N + kv_rank * HD
    dt_cols = cut(w_dt, tp * HL, HL, 1)
    rows = w_z.shape[0]
    misc = [
        dt_cols,
        jnp.zeros((rows, GAIN_COL - HL), bf16),
        norm1_gain[:, None],
        norm2_gain[:, None],
        jnp.zeros((rows, 128 - GAIN_COL - 2), bf16),
    ]
    wa = jnp.concatenate(
        [
            w_z,
            w_x,
            w_shared[:, : 2 * N],
            w_q,
            cut(w_shared, key_start, HD, 1),
            cut(w_shared, key_start + KV * HD, HD, 1),
        ]
        + misc,
        axis=1,
    )
    wb = jnp.concatenate([w_out.T, w_o.T], axis=1)
    wm = jnp.concatenate([w_gate, w_up, w_down.T], axis=1)
    taps = jnp.concatenate([conv_w, conv_b[None], jnp.zeros((3, DI + 2 * N), bf16)], axis=0)
    taps = jnp.concatenate([cut(taps, tp * WI, WI, 1), taps[:, DI:]], axis=1).astype(f32)
    bias = cut(dt_bias.astype(f32), tp * HL, HL, 0)
    rate = -jnp.exp(cut(a_log.astype(f32), tp * HL, HL, 0))
    prm = jnp.pad(jnp.stack([bias, rate]), ((0, 6), (0, 128 - HL)))
    skip = jnp.repeat(cut(d_skip.astype(f32), tp * HL, HL, 0), P_SIZE)
    gain_gate = cut(gated_gain.astype(f32), tp * WI, WI, 0)
    chan = jnp.pad(jnp.stack([gain_gate, skip]), ((0, 6), (0, 0)))
    cos, sin = rotary_tables((c * t + jnp.arange(t, dtype=jnp.int32)).astype(f32))

    wfull_a, normed, gains, z, cin, q, kv, dt = project(shards, hid, wa)
    (
        wfull_b, pre, hist, q_low, kk, vv, att, lse, lse_row, ssd, start, steps, cum, tot, gl, square,
    ) = forward(shards, cin, q, kv, dt, z, cos, sin, wb, taps, prm, chan, lengths)
    osend, out_own, grad_own, grads, gain_two, total_square, ggl, grad_att, dots = ffn(
        shards, hid, cot, gl, att.astype(bf16), square, wfull_b, wm, gains, lengths
    )
    output, lin, grad_b, vec = backward(
        shards, ggl, grad_att, dots, total_square, grads, osend, out_own, pre, cin, hist, q_low, kk, vv, att,
        lse_row, ssd, start, steps, cum, tot, dt, z, cos, sin, taps, prm, chan, lengths,
    )
    grad_hidden, grad_a, shared, vecs = finish(
        shards, lin, normed, wfull_a, hid, grad_own, gains, gain_two, vec
    )

    def ranks(start, width, rows):
        return jnp.concatenate([vecs[i, :rows, start : start + width] for i in range(TP)], axis=1)

    conv_all = jnp.concatenate([ranks(0, WI, 5), vecs[:, :5, WI:CH].sum(0)], axis=1)
    gate_all = ranks(CH, WI, 1)[0]
    head_all = ranks(CH + WI, HL, 3)
    maps = shared.sum(0)
    first, second = shared[0] + shared[1], shared[2] + shared[3]
    grad_shared = jnp.concatenate(
        [
            maps[:, : 2 * N],
            first[:, 256 : 256 + HD],
            second[:, 256 : 256 + HD],
            first[:, 256 + HD : 384],
            second[:, 256 + HD : 384],
        ],
        axis=1,
    )
    grad_dt = jnp.concatenate([shared[i, :, 384 : 384 + HL] for i in range(TP)], axis=1)
    return (
        output[None],
        grad_hidden[None].astype(f32),
        maps[:, 384 + GAIN_COL],
        grad_a[:, CZ:CX],
        grad_a[:, CX:CM],
        grad_shared,
        grad_dt,
        head_all[0],
        head_all[1],
        head_all[2],
        conv_all[:4],
        conv_all[4],
        gate_all,
        grad_b[:, CO:CW].T,
        grad_a[:, CQ:CK],
        grad_b[:, CW:CG].T,
        maps[:, 384 + GAIN_COL + 1],
        grad_b[:, CG:CU],
        grad_b[:, CU:CD],
        grad_b[:, CD:CB].T,
    )


def solution(mesh):
    placed = (
        P("shard", "ctx", None),
        P("shard", "ctx", None),
        P("shard"),
        P(("shard", "ctx")),
        P(("shard", "ctx"), "tp"),
        P(("shard", "ctx"), "tp"),
        P(("shard", "ctx"), None),
        P(("shard", "ctx"), None),
        P(),
        P(),
        P(),
        P(),
        P(),
        P(),
        P("tp", ("shard", "ctx")),
        P(("shard", "ctx"), "tp"),
        P("tp", ("shard", "ctx")),
        P(("shard", "ctx")),
        P(("shard", "ctx"), "tp"),
        P(("shard", "ctx"), "tp"),
        P("tp", ("shard", "ctx")),
    )
    return jax.shard_map(
        local,
        mesh=mesh,
        in_specs=placed,
        out_specs=(
            P("shard", "ctx", "tp"),
            P("shard", "ctx", None),
            P(("shard", "ctx", "tp")),
            P(("shard", "ctx"), "tp"),
            P(("shard", "ctx"), "tp"),
            P(("shard", "ctx", "tp"), None),
            P(("shard", "ctx", "tp"), None),
            P(),
            P(),
            P(),
            P(),
            P(),
            P(),
            P("tp", ("shard", "ctx")),
            P(("shard", "ctx"), "tp"),
            P("tp", ("shard", "ctx")),
            P(("shard", "ctx", "tp")),
            P(("shard", "ctx"), "tp"),
            P(("shard", "ctx"), "tp"),
            P("tp", ("shard", "ctx")),
        ),
        check_vma=False,
    )
```

```python
import functools

import jax
import jax.numpy as jnp
import numpy as np
from jax import lax
from jax.experimental import pallas as pl
from jax.experimental.pallas import tpu as pltpu
from jax.sharding import PartitionSpec as P

H = 24
P_SIZE = 64
N = 128
NQ = 8
KV = 2
HD = 64
CONVW = 4
DI = 1536
D = 1024
FFL = 512
TP = 4
HL = H // TP
WI = HL * P_SIZE
CH = WI + 2 * N
L = 256

CZ, CX, CM, CQ, CK, CS, CA = 0, 384, 768, 1024, 1152, 1280, 1408
GAIN_COL = 24
CO, CW, CG, CU, CD, CB = 0, 384, 512, 1024, 1536, 2048

EPS = 1e-05
rope_base = 10000.0
FILL = -1e30
HI = lax.Precision.HIGHEST
MESH = pl.DeviceIdType.MESH
f32 = jnp.float32
bf16 = jnp.bfloat16
VLIMIT = 60 * 1024 * 1024


def nn(a, b, precision=None):
    return lax.dot_general(
        a, b, (((1,), (0,)), ((), ())), precision=precision, preferred_element_type=f32
    )


def nt(a, b, precision=None):
    return lax.dot_general(
        a, b, (((1,), (1,)), ((), ())), precision=precision, preferred_element_type=f32
    )


def tn(a, b, precision=None):
    return lax.dot_general(
        a, b, (((0,), (0,)), ((), ())), precision=precision, preferred_element_type=f32
    )


def rows_of(index, size=L):
    return pl.ds(pl.multiple_of(index * size, size), size)


def remote(src, dst, send, recv, **where):
    return pltpu.make_async_remote_copy(
        src_ref=src,
        dst_ref=dst,
        send_sem=send,
        recv_sem=recv,
        device_id=where,
        device_id_type=MESH,
    )


def iota(shape, dim):
    return lax.broadcasted_iota(jnp.int32, shape, dim)


def loop(n, body):
    lax.fori_loop(0, n, lambda i, c: (body(i), c)[1], 0)


def greet(shards, tp_too, ctx_too=True, shard_too=True):
    barrier = pltpu.get_barrier_semaphore()
    count = 0
    z, c, t = lax.axis_index("shard"), lax.axis_index("ctx"), lax.axis_index("tp")
    if ctx_too:
        pl.semaphore_signal(barrier, inc=1, device_id={"ctx": 1 - c}, device_id_type=MESH)
        count += 1
    if shard_too:

        def one(k):
            pl.semaphore_signal(
                barrier, inc=1, device_id={"shard": lax.rem(z + 1 + k, shards)}, device_id_type=MESH
            )

        loop(shards - 1, one)
        count += shards - 1
    if tp_too:
        for d in range(1, TP):
            pl.semaphore_signal(
                barrier, inc=1, device_id={"tp": lax.rem(t + d, TP)}, device_id_type=MESH
            )
            count += 1
    pl.semaphore_wait(barrier, count)


class Gather:
    def __init__(self, shards, src, dst, zsend, csend, recv, own):
        self.s, self.src, self.dst = shards, src, dst
        self.zsend, self.csend, self.recv, self.own = zsend, csend, recv, own
        self.z, self.c = lax.axis_index("shard"), lax.axis_index("ctx")
        self.r = src.shape[0]

    def block(self, g):
        return self.dst.at[rows_of(g, self.r)]

    def to_shard(self, k):
        g = 2 * self.z + self.c
        return remote(
            self.src,
            self.block(g),
            self.zsend.at[k],
            self.recv.at[g],
            shard=lax.rem(self.z + k, self.s),
        )

    def to_core(self, k):
        zz = lax.rem(self.z + k, self.s)
        g = 2 * zz + self.c
        return remote(self.block(g), self.block(g), self.csend.at[k], self.recv.at[g], ctx=1 - self.c)

    def got(self, k, core):
        zz = lax.rem(self.z + k, self.s)
        g = 2 * zz + core
        return remote(self.block(g), self.block(g), self.csend.at[k], self.recv.at[g], ctx=1 - self.c)

    def start(self):
        keep = pltpu.make_async_copy(self.src, self.block(2 * self.z + self.c), self.own)
        keep.start()
        loop(self.s - 1, lambda k: self.to_shard(k + 1).start())
        keep.wait()
        self.to_core(0).start()

    def forward(self, first=0, last=None):
        def one(k):
            self.got(k + 1, self.c).wait_recv()
            self.to_core(k + 1).start()

        lax.fori_loop(
            first, self.s - 1 if last is None else last, lambda k, carry: (one(k), carry)[1], 0
        )

    def finish(self):
        loop(self.s, lambda k: self.got(k, 1 - self.c).wait_recv())
        loop(self.s, lambda k: self.to_core(k).wait_send())
        loop(self.s - 1, lambda k: self.to_shard(k + 1).wait_send())

    @staticmethod
    def sems(shards):
        dma = pltpu.SemaphoreType.DMA
        return [dma((shards,)), dma((shards,)), dma((2 * shards,)), dma(())]


class Scatter:
    def __init__(self, shards, src, sib, stage, land, csend, crecv, zsend, zrecv):
        self.s, self.src, self.sib, self.stage, self.land = shards, src, sib, stage, land
        self.csend, self.crecv, self.zsend, self.zrecv = csend, crecv, zsend, zrecv
        self.z, self.c = lax.axis_index("shard"), lax.axis_index("ctx")
        self.r = src.shape[0] // (2 * shards)

    def to_core(self, k):
        zz = lax.rem(self.z + k, self.s)
        return remote(
            self.src.at[rows_of(2 * zz + 1 - self.c, self.r)],
            self.sib.at[zz],
            self.csend.at[zz],
            self.crecv.at[zz],
            ctx=1 - self.c,
        )

    def to_shard(self, k):
        zz = lax.rem(self.z + k, self.s)
        return remote(
            self.stage.at[zz], self.land.at[self.z], self.zsend.at[zz], self.zrecv.at[self.z], shard=zz
        )

    def arrive(self, k):
        zz = lax.rem(self.z + k, self.s)
        return remote(
            self.stage.at[zz], self.land.at[zz], self.zsend.at[zz], self.zrecv.at[zz], shard=zz
        )

    def start(self):
        loop(self.s - 1, lambda k: self.to_core(k + 1).start())
        self.to_core(0).start()

    def middle(self):
        def one(k):
            zz = lax.rem(self.z + 1 + k, self.s)
            self.to_core(k + 1).wait_recv()
            both = self.src[rows_of(2 * zz + self.c, self.r), :].astype(f32)
            self.stage[zz] = (both + self.sib[zz].astype(f32)).astype(bf16)
            self.to_shard(k + 1).start()

        loop(self.s - 1, one)

    def finish(self, out, cols=None):
        self.to_core(0).wait_recv()
        own = self.src[rows_of(2 * self.z + self.c, self.r), :].astype(f32)
        out[...] = own + self.sib[self.z].astype(f32)

        def one(k):
            zz = lax.rem(self.z + 1 + k, self.s)
            self.arrive(k + 1).wait_recv()
            out[...] += self.land[zz].astype(f32)

        loop(self.s - 1, one)
        loop(self.s, lambda k: self.to_core(k).wait_send())
        loop(self.s - 1, lambda k: self.to_shard(k + 1).wait_send())

    @staticmethod
    def scratch(shards, rows, cols):
        dma = pltpu.SemaphoreType.DMA
        block = pltpu.VMEM((shards, rows // (2 * shards), cols), bf16)
        return [block, block, block] + [dma((shards,))] * 4


def sigmoid(v):
    return 1.0 / (1.0 + jnp.exp(-v))


def softplus(v):
    return jnp.maximum(v, 0.0) + jnp.log1p(jnp.exp(-jnp.abs(v)))


def swap_half(v):
    width = v.shape[1]
    low = iota(v.shape, 1) % HD < HD // 2
    return jnp.where(low, pltpu.roll(v, width - HD // 2, 1), pltpu.roll(v, HD // 2, 1))


def low_lanes(shape):
    return iota(shape, 1) < 64


def spread():
    return (iota((N, WI), 1) // P_SIZE == iota((N, WI), 0)).astype(f32)


def first_row():
    return (iota((8, N), 0) == 0).astype(f32)


def wide(column, width):
    return jnp.concatenate([column] * (width // column.shape[1]), axis=1)


def lower_ones():
    return (iota((L, L), 0) >= iota((L, L), 1)).astype(f32)


def head_scalars(dt_raw, prm):
    real = iota(dt_raw.shape, 1) < HL
    steps = jnp.where(real, softplus(dt_raw + prm[0:1, :]), 0.0)
    rates = steps * prm[1:2, :]
    return steps, rates


def pair_columns(v, pair):
    return v[:, 128 * pair : 128 * pair + 128]


def own_half(v, half):
    return jnp.where(low_lanes(v.shape) == (half == 0), v, jnp.zeros_like(v))


def eye(n):
    return (iota((n, n), 0) == iota((n, n), 1)).astype(bf16)


def rotary_of(table, rows):
    both = table[rows, :]
    first = iota(both.shape, 1) % HD < HD // 2
    cosine = jnp.where(first, both, pltpu.roll(both, HD // 2, 1))
    sine = jnp.where(first, -pltpu.roll(both, 128 - HD // 2, 1), both)
    return cosine, sine


def forward_kernel(
    shards,
    hid, w_z, w_x, w_shared, w_dt, w_q, w_out, w_o, gain_one, gain_two,
    conv_w, conv_b, gated_gain, head_params, table, length,
    wf1, wf2, wo, normed, gains, z_out, cin, dt_raw, taps, prm, chan,
    pre, hist, q_low, kk, vv, att, att_low, lse_row, ssd, start, steps_out, cum_out, tot_out,
    gated_low, square,
    wa1, wa2, wa3, stat, pad, act, state, carried, scores_m, scores_l, hist_in,
    zs1, cs1, zr1, own1, zs2, cs2, zr2, own2, zs3, cs3, zr3, own3, xs, xr,
):
    c, tp = lax.axis_index("ctx"), lax.axis_index("tp")
    t = hid.shape[0]
    blocks = t // L
    r = w_z.shape[0]

    kv = tp * (NQ // TP) // (NQ // KV)
    keys = w_shared[:, 2 * N : 2 * N + 128].astype(f32)
    vals = w_shared[:, 2 * N + 128 : 2 * N + 256].astype(f32)
    low_r = low_lanes((r, 128))
    other = pltpu.roll(jnp.where(kv == 0, vals, keys), 64, 1)
    wa1[:, 0:128] = w_q[...]
    wa1[:, 128:256] = jnp.where(
        kv == 0, jnp.where(low_r, keys, other), jnp.where(low_r, other, vals)
    ).astype(bf16)
    head_pick = (
        (iota((H, 128), 0) == iota((H, 128), 1) + tp * HL) & (iota((H, 128), 1) < HL)
    ).astype(bf16)
    row8, lane8 = iota((8, 128), 0), iota((8, 128), 1)
    gain_pick = ((row8 < 2) & (lane8 == GAIN_COL + row8)).astype(bf16)
    gain_rows = jnp.where(
        iota((8, r), 0) == 0, gain_one[...].astype(f32), gain_two[...].astype(f32)
    ).astype(bf16)
    wa1[:, 256:384] = (nn(w_dt[...], head_pick) + tn(gain_rows, gain_pick)).astype(bf16)
    wa2[:, 0:WI] = w_z[...]
    wa2[:, WI : 2 * WI] = w_x[...]
    wa2[:, 2 * WI : 2 * WI + 2 * N] = w_shared[:, 0 : 2 * N]
    greet(shards, False)
    gather1 = Gather(shards, wa1, wf1, zs1, cs1, zr1, own1)
    gather2 = Gather(shards, wa2, wf2, zs2, cs2, zr2, own2)
    gather3 = Gather(shards, wa3, wo, zs3, cs3, zr3, own3)
    gather1.start()
    gather2.start()
    wa3[:, CO:CW] = nt(eye(r), w_out[...]).astype(bf16)
    wa3[:, CW:CG] = nt(eye(r), w_o[...]).astype(bf16)

    expand = spread()
    mine = pl.ds(pl.multiple_of(tp * WI, 128), WI)
    taps[0:CONVW, 0:WI] = conv_w[:, mine].astype(f32)
    taps[0:CONVW, WI:CH] = conv_w[:, DI:].astype(f32)
    taps[CONVW : CONVW + 1, 0:WI] = conv_b[:, mine].astype(f32)
    taps[CONVW : CONVW + 1, WI:CH] = conv_b[:, DI:].astype(f32)
    taps[CONVW + 1 :, :] = jnp.zeros((8 - CONVW - 1, CH), f32)
    heads = pltpu.roll(head_params[...], lax.rem(128 - tp * HL, 128), 1)
    heads = jnp.where(lane8 < HL, jnp.where(row8 == 1, -jnp.exp(heads), heads), 0.0)
    prm[...] = heads
    chan[...] = jnp.zeros_like(chan)
    chan[0:1, :] = gated_gain[:, mine].astype(f32)
    chan[1:2, :] = nn(heads, expand, HI)[2:3, :]

    def swap(src, dst, i):
        return remote(src, dst, xs.at[i], xr.at[i], ctx=1 - c)

    def row_scale(i):
        rows = rows_of(i)
        x = hid[rows, :].astype(f32)
        scale = lax.rsqrt(jnp.mean(x * x, -1, keepdims=True) + EPS)
        stat[rows, :] = jnp.broadcast_to(scale, (L, 128))

    loop(blocks, row_scale)
    gather1.forward()
    gather1.finish()
    turned = wf1[:, 256:384].astype(f32).T
    gains[...] = turned[GAIN_COL : GAIN_COL + 8]
    gain = gains[0:1, :]
    low128 = low_lanes((L, 128))

    def first_projections(i):
        rows = rows_of(i)
        low = (hid[rows, :].astype(f32) * wide(stat[rows, :], D) * gain).astype(bf16)
        normed[rows, :] = low
        rest = nn(low, wf1[...])
        cosine, sine = rotary_of(table, pl.ds(pl.multiple_of(c * t + i * L, L), L))
        v = rest[:, 0:128]
        q_low[rows, :] = (v * cosine + swap_half(v) * sine).astype(bf16)
        v = rest[:, 128:256]
        other = pltpu.roll(v, 64, 1)
        twice = jnp.where(low128, v, other)
        kk[0, rows, :] = (twice * cosine + swap_half(twice) * sine).astype(bf16)
        vv[0, rows, :] = jnp.where(low128, other, v).astype(bf16)
        dt_raw[rows, :] = rest[:, 256:384]

    loop(blocks, first_projections)
    keys = swap(kk.at[0], kk.at[1], 1)
    keys.start()
    vals = swap(vv.at[0], vv.at[1], 2)
    vals.start()

    scale = HD ** (-0.5)
    limit = length[0] - c * t

    def stacked(v):
        return jnp.concatenate([own_half(v, 0), own_half(v, 1)], axis=0)

    for i in range(blocks):
        rows = pl.ds(i * L, L)
        width = (i + 1) * L
        q2 = stacked(q_low[rows, :].astype(f32)).astype(bf16)
        s = nt(q2, kk[0, 0:width, :]) * scale
        at = iota(s.shape, 0) % L + i * L
        col = iota(s.shape, 1)
        s = jnp.where((col <= at) & (col < limit), s, FILL)
        peak = jnp.max(s, -1, keepdims=True)
        e = jnp.exp(s - peak)
        total = jnp.sum(e, -1, keepdims=True)
        o = nn(e.astype(bf16), vv[0, 0:width, :])
        scores_m[...] = jnp.broadcast_to(peak, (2 * L, 128))
        scores_l[0] = jnp.broadcast_to(total, (2 * L, 128))
        scores_l[1] = o
        if i == 0:
            keys.wait_recv()
            vals.wait_recv()

        @pl.when(c > 0)
        def earlier():
            s2 = nt(q2, kk[1]) * scale
            old = scores_m[:, 0:1]
            new = jnp.maximum(old, jnp.max(s2, -1, keepdims=True))
            e2 = jnp.exp(s2 - new)
            fade = jnp.exp(old - new)
            scores_m[...] = jnp.broadcast_to(new, (2 * L, 128))
            scores_l[0] = fade * scores_l[0] + jnp.sum(e2, -1, keepdims=True)
            scores_l[1] = fade * scores_l[1] + nn(e2.astype(bf16), vv[1])

        total = scores_l[0]
        o = scores_l[1] / total
        o = jnp.where(low128, o[:L], o[L:])
        att[rows, :] = o
        att_low[rows, :] = o.astype(bf16)
        logs = scores_m[...] + jnp.log(total)
        turned = jnp.where(low128, logs[:L], logs[L:]).T
        lse_row[0:1, rows] = turned[0:1]
        lse_row[1:2, rows] = turned[64:65]
        lse_row[2:8, rows] = jnp.zeros((6, L), f32)
        if i == blocks - 2:
            gather2.forward(0, 1)
    gather2.forward(1)
    gather3.start()
    gather2.finish()

    def conv_input(k):
        i = blocks - 1 - k
        rows = rows_of(i)
        v = nn(normed[rows, :], wf2[:, WI:]).astype(bf16)
        cin[rows, :] = v
        pad[pl.ds(pl.multiple_of(i * L + 8, 8), L), :] = v.astype(f32)

    conv_input(0)
    tail = swap(cin.at[pl.ds(t - 16, 16)], hist_in, 0)
    tail.start()
    lax.fori_loop(1, blocks, lambda k, carry: (conv_input(k), carry)[1], 0)
    tail.wait_recv()
    before = hist_in[8:16, :].astype(f32)
    hist[...] = jnp.where((iota((8, CH), 0) >= 5) & (c > 0), before, 0.0)
    pad[0:8, :] = hist[...]
    ones = lower_ones()
    state[...] = jnp.zeros_like(state)

    for i in range(blocks):
        rows = pl.ds(i * L, L)
        v = taps[4:5, :] + taps[0:1, :] * pad[pl.ds(i * L + 5, L), :]
        for j in range(1, CONVW):
            v = v + taps[j : j + 1, :] * pad[pl.ds(i * L + 5 + j, L), :]
        pre[rows, :] = v
        a = v * sigmoid(v)
        act[rows, :] = a
        steps, rates = head_scalars(dt_raw[rows, :], prm)
        cum = nn(ones, rates, HI)
        tot = cum[L - 1 : L, :]
        steps_out[rows, :] = steps
        cum_out[rows, :] = cum
        tot_out[i] = jnp.broadcast_to(tot, (8, 128))
        weight = nn(jnp.exp(tot - cum) * steps, expand, HI)
        start[i] = state[...]
        add = tn(a[:, WI : WI + N].astype(bf16), (weight * a[:, :WI]).astype(bf16))
        decay = nn(jnp.broadcast_to(jnp.exp(tot), (8, 128)), expand, HI)[0:1, :]
        state[...] = decay * state[...] + add

    states = swap(state, carried, 3)
    states.start()
    gather3.forward()

    def gate_input(i):
        rows = rows_of(i)
        z_out[rows, :] = nn(normed[rows, :], wf2[:, 0:WI])

    loop(blocks, gate_input)

    states.wait_recv()
    carried[...] = jnp.where(c > 0, carried[...], 0.0)
    mask = iota((L, L), 0) >= iota((L, L), 1)
    for i in range(blocks):
        rows = pl.ds(i * L, L)
        if i > 0:
            decay = nn(jnp.exp(tot_out[i - 1]), expand, HI)[0:1, :]
            carried[...] = carried[...] * decay
        start[i] = start[i] + carried[...]
        s0 = start[i].astype(bf16)
        steps, cum = steps_out[rows, :], cum_out[rows, :]
        x = act[rows, 0:WI]
        xl = x.astype(bf16)
        in_map = act[rows, WI : WI + N].astype(bf16)
        out_map = act[rows, WI + N : CH].astype(bf16)
        gram = nt(out_map, in_map)
        cum_t, steps_t = cum.T, steps.T
        inner = []
        for pair in range(HL // 2):
            halves = []
            for half in range(2):
                h = 2 * pair + half
                decay = jnp.exp(jnp.where(mask, cum[:, h : h + 1] - cum_t[h : h + 1, :], FILL))
                mixing = gram * decay * steps_t[h : h + 1, :]
                halves.append(nn(mixing.astype(bf16), pair_columns(xl, pair)))
            inner.append(jnp.where(low128, halves[0], halves[1]))
        y = jnp.concatenate(inner, axis=1)
        y = y + nn(jnp.exp(cum), expand, HI) * nn(out_map, s0) + chan[1:2, :] * x
        ssd[rows, :] = y
        zz = z_out[rows, :]
        gated = y * zz * sigmoid(zz)
        gated_low[rows, :] = (gated * chan[0:1, :]).astype(bf16)
        square[:, rows] = nt(jnp.ones((8, WI), f32), gated * gated, HI)

    gather3.finish()
    for copy in (tail, keys, vals, states):
        copy.wait_send()


def forward(shards, *args):
    t, r = args[0].shape[0], args[1].shape[0]
    out = [
        ((D, 384), bf16),
        ((D, 1024), bf16),
        ((D, CG), bf16),
        ((t, D), bf16),
        ((8, D), f32),
        ((t, WI), f32),
        ((t, CH), bf16),
        ((t, 128), f32),
        ((8, CH), f32),
        ((8, 128), f32),
        ((8, WI), f32),
        ((t, CH), f32),
        ((8, CH), f32),
        ((t, 128), bf16),
        ((2, t, 128), bf16),
        ((2, t, 128), bf16),
        ((t, 128), f32),
        ((t, 128), bf16),
        ((8, t), f32),
        ((t, WI), f32),
        ((t // L, N, WI), f32),
        ((t, 128), f32),
        ((t, 128), f32),
        ((t // L, 8, 128), f32),
        ((t, WI), bf16),
        ((8, t), f32),
    ]
    dma = pltpu.SemaphoreType.DMA
    vmem = pl.BlockSpec(memory_space=pltpu.VMEM)
    return pl.pallas_call(
        functools.partial(forward_kernel, shards),
        out_shape=[jax.ShapeDtypeStruct(*o) for o in out],
        in_specs=[vmem] * (len(args) - 1) + [pl.BlockSpec(memory_space=pltpu.SMEM)],
        out_specs=[vmem] * len(out),
        scratch_shapes=[
            pltpu.VMEM((r, 384), bf16),
            pltpu.VMEM((r, 1024), bf16),
            pltpu.VMEM((r, CG), bf16),
            pltpu.VMEM((t, 128), f32),
            pltpu.VMEM((t + 8, CH), f32),
            pltpu.VMEM((t, CH), f32),
            pltpu.VMEM((N, WI), f32),
            pltpu.VMEM((N, WI), f32),
            pltpu.VMEM((2 * L, 128), f32),
            pltpu.VMEM((2, 2 * L, 128), f32),
            pltpu.VMEM((16, CH), bf16),
        ]
        + Gather.sems(shards) * 3
        + [dma((4,)), dma((4,))],
        compiler_params=pltpu.CompilerParams(
            collective_id=1, has_side_effects=True, vmem_limit_bytes=VLIMIT
        ),
        name="mix_forward",
    )(*args)


def ffn_kernel(
    shards,
    hid, cot, gl, att, square, wb, wm_own, gains, length,
    osend, out_own, grad_own, grads, gain_grad, total_square, ggl, grad_att, dots,
    grad_res, partial, seed, send1, recv1, low_two, grad_act, act, gg, gu, gown,
    unit, scale_keep, gsend, grecv, sqall, wm,
    zs, cs, zr, own_sem, sqs, sqr, s1, r1, ns, nr, gs, gr, hs, hr,
):
    t = hid.shape[0]
    tp, c = lax.axis_index("tp"), lax.axis_index("ctx")
    chunk = t // TP
    width = D // TP
    greet(shards, True)
    gather = Gather(shards, wm_own, wm, zs, cs, zr, own_sem)
    gather.start()

    def peer(d):
        return lax.rem(tp + d, TP)

    def crow(i):
        return rows_of(i, chunk)

    def square_to(d):
        return remote(sqall.at[tp], sqall.at[tp], sqs.at[d], sqr.at[tp], tp=peer(d))

    def square_from(d):
        return remote(sqall.at[tp], sqall.at[peer(d)], sqs.at[d], sqr.at[peer(d)], tp=peer(d))

    sqall[tp] = square[...]
    for d in range(1, TP):
        square_to(d).start()
    limit = length[0] - c * t

    def mask_seed(i):
        rows = crow(i)
        live = iota((chunk, D), 0) + i * chunk < limit
        seed[rows, :] = jnp.where(live, cot[rows, :].astype(f32), 0.0).astype(bf16)

    loop(TP, mask_seed)
    for d in range(1, TP):
        square_from(d).wait_recv()
    total_square[...] = sqall[0] + sqall[1] + sqall[2] + sqall[3]

    def first_to(d):
        return remote(send1.at[d], recv1.at[tp], s1.at[d], r1.at[tp], tp=peer(d))

    def first_from(d):
        return remote(send1.at[d], recv1.at[peer(d)], s1.at[d], r1.at[peer(d)], tp=peer(d))

    def mix(k):
        d = lax.rem(k + 1, TP)
        rows = crow(peer(d))
        scale = lax.rsqrt(total_square[:, rows] / DI + EPS)
        column = wide(tn(scale, first_row(), HI), D)
        both = nt(gl[rows, :], wb[:, CO:CW]) * column + nt(att[rows, :], wb[:, CW:CG])
        partial[rows, :] = both

        @pl.when(d > 0)
        def go():
            send1[d] = both.astype(bf16)
            first_to(d).start()

    loop(TP, mix)
    gather.forward(0, 1)
    for d in range(1, TP):
        first_from(d).wait_recv()
    own = crow(tp)
    acc = hid[own, :].astype(f32) + partial[own, :]
    for d in range(1, TP):
        acc = acc + recv1[peer(d)].astype(f32)
    scale = lax.rsqrt(jnp.mean(acc * acc, -1, keepdims=True) + EPS)
    scale_keep[...] = jnp.broadcast_to(scale, scale_keep.shape)
    unit[...] = acc * scale
    gain = gains[1:2, :]
    low_two[own, :] = (unit[...] * gain).astype(bf16)

    def norm_to(d):
        return remote(low_two.at[own], low_two.at[own], ns.at[d], nr.at[tp], tp=peer(d))

    def norm_from(d):
        there = low_two.at[crow(peer(d))]
        return remote(there, there, ns.at[d], nr.at[peer(d)], tp=peer(d))

    for d in range(1, TP):
        norm_to(d).start()
    gather.forward(1)
    gather.finish()

    def act_grad(i):
        rows = crow(i)
        grad_act[rows, :] = nn(seed[rows, :], wm[:, CD - CG : CB - CG])

    loop(TP, act_grad)

    def grad_to(d):
        return remote(gsend.at[d], grecv.at[tp], gs.at[d], gr.at[tp], tp=peer(d))

    def grad_from(d):
        return remote(gsend.at[d], grecv.at[peer(d)], gs.at[d], gr.at[peer(d)], tp=peer(d))

    def hidden_units(d):
        i = peer(d)
        rows = crow(i)

        @pl.when(d > 0)
        def arrive():
            norm_from(d).wait_recv()

        low = low_two[rows, :]
        gate, up = nn(low, wm[:, 0:FFL]), nn(low, wm[:, FFL : 2 * FFL])
        sig = sigmoid(gate)
        silu = gate * sig
        hidden_act = (silu * up).astype(bf16)
        act[rows, :] = hidden_act
        ga = grad_act[rows, :]
        g1 = (ga * up * (sig * (1.0 + gate * (1.0 - sig)))).astype(bf16)
        g2 = (ga * silu).astype(bf16)
        gg[rows, :] = g1
        gu[rows, :] = g2
        back = nt(g1, wm[:, 0:FFL]) + nt(g2, wm[:, FFL : 2 * FFL])

        @pl.when(d > 0)
        def go():
            gsend[d] = back.astype(bf16)
            grad_to(d).start()

        @pl.when(d == 0)
        def keep():
            gown[...] = back

        partial[rows, :] = partial[rows, :] + nt(hidden_act, wm[:, 2 * FFL : 3 * FFL])
        for e in range(1, TP):
            osend[e, rows, :] = partial[rows, rows_of(peer(e), width)].astype(bf16)

    loop(TP, hidden_units)

    def weight_grads(i):
        feats = rows_of(i)
        low = low_two[:, feats]
        grads[feats, CG:CU] = tn(low, gg[...]).astype(bf16)
        grads[feats, CU:CD] = tn(low, gu[...]).astype(bf16)

    loop(D // L, weight_grads)
    for d in range(1, TP):
        grad_from(d).wait_recv()
    back = gown[...]
    for d in range(1, TP):
        back = back + grecv[peer(d)].astype(f32)
    gain_grad[...] = jnp.broadcast_to(jnp.sum(back * unit[...], 0, keepdims=True), (8, D))
    weighted = back * gain
    mean = jnp.mean(weighted * unit[...], -1, keepdims=True)
    res = seed[own, :].astype(f32) + scale_keep[:, 0:1] * (weighted - unit[...] * mean)
    grad_own[...] = res
    grad_res[own, :] = res.astype(bf16)

    def res_to(d):
        return remote(grad_res.at[own], grad_res.at[own], hs.at[d], hr.at[tp], tp=peer(d))

    def res_from(d):
        there = grad_res.at[crow(peer(d))]
        return remote(there, there, hs.at[d], hr.at[peer(d)], tp=peer(d))

    for d in range(1, TP):
        res_to(d).start()

    def down_grads(i):
        feats = rows_of(i)
        grads[feats, CD:CB] = tn(seed[:, feats], act[...]).astype(bf16)

    loop(D // L, down_grads)
    mine = rows_of(tp, width)
    out_own[...] = hid[:, mine].astype(f32) + partial[:, mine]
    for d in range(1, TP):
        norm_to(d).wait_send()

    def out_back(d):
        i = peer(d)
        rows = crow(i)

        @pl.when(d > 0)
        def arrive():
            res_from(d).wait_recv()

        square_scale = lax.rsqrt(total_square[:, rows] / DI + EPS)
        column = wide(tn(square_scale, first_row(), HI), D)
        got = grad_res[rows, :]
        proj = (column * got.astype(f32)).astype(bf16)
        low_two[rows, :] = proj
        product = nn(proj, wb[:, CO:CW])
        ggl[rows, :] = product
        dots[:, rows] = nt(jnp.ones((8, WI), f32), product * gl[rows, :].astype(f32), HI)
        grad_att[rows, :] = nn(got, wb[:, CW:CG]).astype(bf16)

    loop(TP, out_back)

    def out_grads(i):
        feats = rows_of(i)
        grads[feats, CO:CW] = tn(low_two[:, feats], gl[...]).astype(bf16)
        grads[feats, CW:CG] = tn(grad_res[:, feats], att[...]).astype(bf16)

    loop(D // L, out_grads)
    for d in range(1, TP):
        square_to(d).wait_send()
        first_to(d).wait_send()
        grad_to(d).wait_send()
        res_to(d).wait_send()


def ffn(shards, hid, cot, gl, att, square, wb, wm_own, gains, length):
    t = hid.shape[0]
    chunk = t // TP
    out = [
        ((TP, t, D // TP), bf16),
        ((t, D // TP), f32),
        ((chunk, D), f32),
        ((D, CB), bf16),
        ((8, D), f32),
        ((8, t), f32),
        ((t, WI), f32),
        ((t, 128), bf16),
        ((8, t), f32),
    ]
    dma = pltpu.SemaphoreType.DMA
    vmem = pl.BlockSpec(memory_space=pltpu.VMEM)
    return pl.pallas_call(
        functools.partial(ffn_kernel, shards),
        out_shape=[jax.ShapeDtypeStruct(*o) for o in out],
        in_specs=[vmem] * 8 + [pl.BlockSpec(memory_space=pltpu.SMEM)],
        out_specs=[vmem] * len(out),
        scratch_shapes=[
            pltpu.VMEM((t, D), bf16),
            pltpu.VMEM((t, D), f32),
            pltpu.VMEM((t, D), bf16),
            pltpu.VMEM((TP, chunk, D), bf16),
            pltpu.VMEM((TP, chunk, D), bf16),
            pltpu.VMEM((t, D), bf16),
            pltpu.VMEM((t, FFL), f32),
            pltpu.VMEM((t, FFL), bf16),
            pltpu.VMEM((t, FFL), bf16),
            pltpu.VMEM((t, FFL), bf16),
            pltpu.VMEM((chunk, D), f32),
            pltpu.VMEM((chunk, D), f32),
            pltpu.VMEM((chunk, 128), f32),
            pltpu.VMEM((TP, chunk, D), bf16),
            pltpu.VMEM((TP, chunk, D), bf16),
            pltpu.VMEM((TP, 8, t), f32),
            pltpu.VMEM((D, CB - CG), bf16),
        ]
        + Gather.sems(shards)
        + [dma((TP,))] * 10,
        compiler_params=pltpu.CompilerParams(
            collective_id=2, has_side_effects=True, vmem_limit_bytes=VLIMIT
        ),
        name="feed_forward",
    )(hid, cot, gl, att, square, wb, wm_own, gains, length)


def backward_kernel(
    shards,
    ggl, grad_att, dots_in, total_square, grads, osend, out_own,
    pre, cin, hist, q_low, kk, vv, att, lse_row, ssd, start, steps_in, cum_in, tot_in, dt_raw, z_in,
    table, taps, prm, chan, length,
    output, lin, grad_b, small,
    orecv, dots, dk, dv, dy, dpre, ends, dstate, carry, kv_out, kv_in, pad, edge_out, edge_in,
    sib, stage, land, csend, crecv, zsend, zrecv, xs, xr, ts, tr, os, orr,
):
    c, tp = lax.axis_index("ctx"), lax.axis_index("tp")
    t = cin.shape[0]
    blocks = t // L
    greet(shards, True)
    scatter = Scatter(shards, grads, sib, stage, land, csend, crecv, zsend, zrecv)
    scatter.start()

    def swap(src, dst, i):
        return remote(src, dst, xs.at[i], xr.at[i], ctx=1 - c)

    def peer(d):
        return lax.rem(tp + d, TP)

    def dot_to(d):
        return remote(dots.at[tp], dots.at[tp], ts.at[d], tr.at[tp], tp=peer(d))

    def dot_from(d):
        return remote(dots.at[tp], dots.at[peer(d)], ts.at[d], tr.at[peer(d)], tp=peer(d))

    dots[tp] = dots_in[...]
    for d in range(1, TP):
        dot_to(d).start()

    def out_to(d):
        return remote(osend.at[d], orecv.at[tp], os.at[d], orr.at[tp], tp=peer(d))

    def out_from(d):
        return remote(osend.at[d], orecv.at[peer(d)], os.at[d], orr.at[peer(d)], tp=peer(d))

    for d in range(1, TP):
        out_to(d).start()
    conv_grads = small.at[:, 0:CH]
    chan_grads = small.at[:, CH : CH + WI]
    head_grads = small.at[:, CH + WI : CH + WI + 128]
    expand = spread()
    low128 = low_lanes((L, 128))
    small[...] = jnp.zeros_like(small)
    for d in range(1, TP):
        dot_from(d).wait_recv()

    def gated_back(i):
        rows = rows_of(i)
        both = dots[0, :, rows] + dots[1, :, rows] + dots[2, :, rows] + dots[3, :, rows]
        share = both / ((total_square[:, rows] / DI + EPS) * DI)
        column = wide(tn(share, first_row(), HI), WI)
        zz, y = z_in[rows, :], ssd[rows, :]
        sig = sigmoid(zz)
        silu = zz * sig
        gated = y * silu
        product = ggl[rows, :]
        chan_grads[0:1, :] += jnp.sum(product * gated, 0, keepdims=True)
        grad_gated = product * chan[0:1, :] - column * gated
        grad_y = grad_gated * silu
        dy[rows, :] = grad_y
        lin[rows, CZ:CX] = (grad_gated * y * (sig * (1.0 + zz * (1.0 - sig)))).astype(bf16)
        v = pre[rows, WI + N : CH]
        out_map = (v * sigmoid(v)).astype(bf16)
        ends[i] = tn(out_map, (nn(jnp.exp(cum_in[rows, :]), expand, HI) * grad_y).astype(bf16))

    loop(blocks, gated_back)
    dstate[...] = jnp.zeros_like(dstate)

    def chain(k):
        i = blocks - 1 - k
        add = ends[i]
        ends[i] = dstate[...]
        dstate[...] = nn(jnp.exp(tot_in[i]), expand, HI)[0:1, :] * dstate[...] + add

    loop(blocks, chain)
    states = swap(dstate, carry, 0)
    states.start()
    scatter.middle()

    scale = HD ** (-0.5)
    limit = length[0] - c * t
    dk[...] = jnp.zeros_like(dk)
    dv[...] = jnp.zeros_like(dv)
    head_of = ((iota((8, 128), 1) // HD) == iota((8, 128), 0)).astype(f32)

    def stacked(v):
        return jnp.concatenate([own_half(v, 0), own_half(v, 1)], axis=0).astype(bf16)

    def side_by_side(v):
        return jnp.concatenate([v[0:1, :], v[1:2, :]], axis=1)

    for i in range(blocks):
        rows = pl.ds(i * L, L)
        width = (i + 1) * L
        q2 = stacked(q_low[rows, :].astype(f32))
        go = grad_att[rows, :].astype(f32)
        go2 = stacked(go)
        row_dot = side_by_side(nt(head_of, go * att[rows, :], HI))
        logs = side_by_side(lse_row[:, rows])
        turn = rotary_of(table, pl.ds(pl.multiple_of(c * t + i * L, L), L))

        def keys_of(part, size, masked):
            k, v = kk[part, 0:size, :], vv[part, 0:size, :]
            s = nt(k, q2) * scale - logs
            if masked:
                at = iota(s.shape, 1) % L + i * L
                row = iota(s.shape, 0)
                s = jnp.where((row <= at) & (row < limit), s, FILL)
            p = jnp.exp(s)
            ds = (p * (nt(v, go2) - row_dot)).astype(bf16)
            dv[part, 0:size, :] += nn(p.astype(bf16), go2)
            dk[part, 0:size, :] += nn(ds, q2)
            out = tn(ds, k) * scale
            out = jnp.where(low128, out[:L], out[L:])
            return out * turn[0] - swap_half(out) * turn[1]

        pad[rows, 0:128] = keys_of(0, width, True)

        @pl.when(c > 0)
        def earlier():
            pad[rows, 0:128] += keys_of(1, t, False)

        lin[rows, CQ:CK] = pad[rows, 0:128].astype(bf16)

    def key_values(part, rows):
        gk, gv = dk[part, rows, :] * scale, dv[part, rows, :]
        return jnp.where(low128, gk + pltpu.roll(gk, 64, 1), gv + pltpu.roll(gv, 64, 1))

    def pack(i):
        rows = rows_of(i)
        kv_out[rows, :] = key_values(1, rows).astype(bf16)

    loop(blocks, pack)
    pairs = swap(kv_out, kv_in, 1)
    pairs.start()

    pad[0:8, :] = hist[...]

    def fill(i):
        pad[pl.ds(pl.multiple_of(i * L + 8, 8), L), :] = cin[rows_of(i), :].astype(f32)

    loop(blocks, fill)
    states.wait_recv()
    carry[...] = jnp.where(c == 0, carry[...], 0.0)

    def add_carry(k):
        i = blocks - 1 - k
        ends[i] = ends[i] + carry[...]
        carry[...] = nn(jnp.exp(tot_in[i]), expand, HI)[0:1, :] * carry[...]

    loop(blocks, add_carry)
    mask = iota((L, L), 0) >= iota((L, L), 1)
    ones = lower_ones()
    lane = iota((L, 128), 1)

    def fold(v):
        return nt(v, expand, HI)

    def scan_back(i):
        rows = rows_of(i)
        v = pre[rows, :]
        sig = sigmoid(v)
        a = v * sig
        x = a[:, :WI]
        xl, bl, cl = x.astype(bf16), a[:, WI : WI + N].astype(bf16), a[:, WI + N :].astype(bf16)
        steps, cum = steps_in[rows, :], cum_in[rows, :]
        tot = cum[L - 1 : L, :]
        ecum, wend = jnp.exp(cum), jnp.exp(tot - cum)
        weight = wend * steps
        ecum_x, weight_x = nn(ecum, expand, HI), nn(weight, expand, HI)
        grad_y = dy[rows, :]
        dyl = grad_y.astype(bf16)
        s0, d1 = start[i], ends[i]
        s0l, d1l = s0.astype(bf16), d1.astype(bf16)
        bd, cs = nn(bl, d1l), nn(cl, s0l)
        dw = fold(x * bd)
        crossing = jnp.broadcast_to(jnp.sum(s0 * d1, 0, keepdims=True), (8, WI))
        dtot = jnp.sum(weight * dw, 0, keepdims=True) + jnp.exp(tot) * fold(crossing)[0:1, :]
        gram = nt(cl, bl)
        cum_t, steps_t = cum.T, steps.T
        dgram = jnp.zeros((L, L), f32)
        row_sums = jnp.zeros((L, 128), f32)
        col_sums, inner = [], []
        for pair in range(HL // 2):
            xp, dp = pair_columns(xl, pair), pair_columns(dyl, pair)
            dpf = pair_columns(grad_y, pair)
            halves = []
            for half in range(2):
                h = 2 * pair + half
                decay = jnp.exp(jnp.where(mask, cum[:, h : h + 1] - cum_t[h : h + 1, :], FILL))
                q = nt(own_half(dpf, half).astype(bf16), xp)
                mixed = gram * decay
                srow = steps_t[h : h + 1, :]
                f = mixed * q
                col_sums.append(jnp.sum(f, 0, keepdims=True))
                row_sums = jnp.where(lane == h, jnp.sum(f * srow, -1, keepdims=True), row_sums)
                dgram = dgram + decay * srow * q
                halves.append(tn((mixed * srow).astype(bf16), dp))
            inner.append(jnp.where(low128, halves[0], halves[1]))
        cols = jnp.concatenate(col_sums + [jnp.zeros((128 - HL, L), f32)], axis=0).T
        dcum = fold(grad_y * cs) * ecum - weight * dw + row_sums - steps * cols
        dcum = dcum + jnp.where(iota((L, 128), 0) == L - 1, dtot, 0.0)
        drate = tn(ones, dcum, HI)
        rate_of = prm[1:2, :]
        raw = dt_raw[rows, :] + prm[0:1, :]
        dstep = (wend * dw + cols + drate * rate_of) * sigmoid(raw)
        dstep = jnp.where(lane < HL, dstep, 0.0)
        lin[rows, CS:CA] = dstep.astype(bf16)
        head_grads[0:1, :] += jnp.sum(dstep, 0, keepdims=True)
        head_grads[1:2, :] += jnp.sum(drate * steps * rate_of, 0, keepdims=True)
        head_grads[2:3, :] += jnp.sum(fold(grad_y * x), 0, keepdims=True)
        slope = sig * (1.0 + v * (1.0 - sig))
        dx = chan[1:2, :] * grad_y + weight_x * bd + jnp.concatenate(inner, axis=1)
        dg = dgram.astype(bf16)
        db = tn(dg, cl) + nt((weight_x * x).astype(bf16), d1l)
        dc = nn(dg, bl) + nt((ecum_x * grad_y).astype(bf16), s0l)
        dpre[rows, 0:WI] = dx * slope[:, :WI]
        dpre[rows, WI : WI + N] = db * slope[:, WI : WI + N]
        dpre[rows, WI + N : CH] = dc * slope[:, WI + N :]

    loop(blocks, scan_back)
    edge_out[...] = dpre[0:8, :]
    edge = swap(edge_out, edge_in, 2)
    edge.start()
    pairs.wait_recv()

    def keys_back(i):
        rows = rows_of(i)
        v = key_values(0, rows) + kv_in[rows, :].astype(f32)
        cosine, sine = rotary_of(table, pl.ds(pl.multiple_of(c * t + i * L, L), L))
        cosine = jnp.where(low128, cosine, 1.0)
        sine = jnp.where(low128, sine, 0.0)
        lin[rows, CK:CS] = (v * cosine - swap_half(v) * sine).astype(bf16)

    loop(blocks, keys_back)
    edge.wait_recv()
    dpre[pl.ds(t, 8), :] = jnp.where(c == 0, edge_in[...], 0.0)
    for i in range(blocks):
        rows = pl.ds(i * L, L)
        g = dpre[rows, :]
        conv_grads[4:5, :] += jnp.sum(g, 0, keepdims=True)
        back = jnp.zeros_like(g)
        for j in range(CONVW):
            back = back + taps[j : j + 1, :] * dpre[pl.ds(i * L + CONVW - 1 - j, L), :]
            conv_grads[j : j + 1, :] += jnp.sum(g * pad[pl.ds(i * L + 5 + j, L), :], 0, keepdims=True)
        lin[rows, CX:CQ] = back.astype(bf16)
    total = out_own[...]
    for d in range(1, TP):
        out_from(d).wait_recv()
        total = total + orecv[peer(d)].astype(f32)
    output[...] = total.astype(bf16)
    scatter.finish(grad_b)
    for copy in (states, pairs, edge):
        copy.wait_send()
    for d in range(1, TP):
        dot_to(d).wait_send()
        out_to(d).wait_send()


def backward(shards, *args):
    t = args[0].shape[0]
    rows = D // (2 * shards)
    out = [
        ((t, D // TP), bf16),
        ((t, CA), bf16),
        ((rows, CB), f32),
        ((8, CH + WI + 128), f32),
    ]
    dma = pltpu.SemaphoreType.DMA
    vmem = pl.BlockSpec(memory_space=pltpu.VMEM)
    return pl.pallas_call(
        functools.partial(backward_kernel, shards),
        out_shape=[jax.ShapeDtypeStruct(*o) for o in out],
        in_specs=[vmem] * (len(args) - 1) + [pl.BlockSpec(memory_space=pltpu.SMEM)],
        out_specs=[vmem] * len(out),
        scratch_shapes=[
            pltpu.VMEM((TP, t, D // TP), bf16),
            pltpu.VMEM((TP, 8, t), f32),
            pltpu.VMEM((2, t, 128), f32),
            pltpu.VMEM((2, t, 128), f32),
            pltpu.VMEM((t, WI), f32),
            pltpu.VMEM((t + 8, CH), f32),
            pltpu.VMEM((t // L, N, WI), f32),
            pltpu.VMEM((N, WI), f32),
            pltpu.VMEM((N, WI), f32),
            pltpu.VMEM((t, 128), bf16),
            pltpu.VMEM((t, 128), bf16),
            pltpu.VMEM((t + 8, CH), f32),
            pltpu.VMEM((8, CH), f32),
            pltpu.VMEM((8, CH), f32),
        ]
        + Scatter.scratch(shards, D, CB)
        + [dma((3,)), dma((3,))]
        + [dma((TP,))] * 4,
        compiler_params=pltpu.CompilerParams(
            collective_id=3, has_side_effects=True, vmem_limit_bytes=VLIMIT
        ),
        name="mix_backward",
    )(*args)


def finish_kernel(
    shards,
    lin, normed, wf1, wf2, hid, grad_own, gains, gain_two, vec,
    low, grad_a, shared, vecs,
    gsend, grecv, gown, grads, misc, misc_low, misc_sum, shsend, vec_sib, vec_z,
    sib, stage, land, csend, crecv, zsend, zrecv,
    sib2, stage2, land2, csend2, crecv2, zsend2, zrecv2,
    vcs, vcr, vzs, vzr, gs, gr, hs, hr, ss, sr, vts, vtr,
):
    tp = lax.axis_index("tp")
    t = lin.shape[0]
    chunk = t // TP
    greet(shards, True)
    scatter = Scatter(shards, grads, sib, stage, land, csend, crecv, zsend, zrecv)
    small = Scatter(shards, misc_low, sib2, stage2, land2, csend2, crecv2, zsend2, zrecv2)
    z, c = lax.axis_index("shard"), lax.axis_index("ctx")
    vec_core = remote(vec, vec_sib, vcs.at[0], vcr.at[0], ctx=1 - c)
    vec_core.start()

    def vec_to_shard(k):
        zz = lax.rem(z + k, shards)
        return remote(vec_z.at[z], vec_z.at[z], vzs.at[zz], vzr.at[z], shard=zz)

    def vec_from_shard(k):
        zz = lax.rem(z + k, shards)
        return remote(vec_z.at[z], vec_z.at[zz], vzs.at[zz], vzr.at[zz], shard=zz)

    def vec_to(d):
        return remote(vecs.at[tp], vecs.at[tp], vts.at[d], vtr.at[tp], tp=peer(d))

    def vec_from(d):
        return remote(vecs.at[tp], vecs.at[peer(d)], vts.at[d], vtr.at[peer(d)], tp=peer(d))

    def peer(d):
        return lax.rem(tp + d, TP)

    def crow(i):
        return rows_of(i, chunk)

    def grad_to(d):
        return remote(gsend.at[d], grecv.at[tp], gs.at[d], gr.at[tp], tp=peer(d))

    def grad_from(d):
        return remote(gsend.at[d], grecv.at[peer(d)], gs.at[d], gr.at[peer(d)], tp=peer(d))

    def product(k):
        d = lax.rem(k + 1, TP)
        rows = crow(peer(d))
        back = nt(lin[rows, CZ:CQ], wf2[...]) + nt(lin[rows, CQ:CA], wf1[...])

        @pl.when(d > 0)
        def go():
            gsend[d] = back.astype(bf16)
            grad_to(d).start()

        @pl.when(d == 0)
        def keep():
            gown[...] = back

    loop(TP, product)
    vec_core.wait_recv()
    vec_z[z] = vec[...] + vec_sib[...]
    loop(shards - 1, lambda k: vec_to_shard(k + 1).start())

    def weight_grads(i):
        feats = rows_of(i)
        both = tn(normed[:, feats], lin[...])
        grads[feats, :] = both[:, :CS].astype(bf16)
        misc[feats, :] = both[:, CS:]

    loop(D // L, weight_grads)
    scatter.start()
    scatter.middle()
    loop(shards - 1, lambda k: vec_from_shard(k + 1).wait_recv())
    vecs[tp] = lax.fori_loop(1, shards, lambda k, total: total + vec_z[k], vec_z[0])
    for d in range(1, TP):
        vec_to(d).start()
    for d in range(1, TP):
        grad_from(d).wait_recv()
    own = crow(tp)
    back = gown[...]
    for d in range(1, TP):
        back = back + grecv[peer(d)].astype(f32)
    x = hid[own, :].astype(f32)
    scale = lax.rsqrt(jnp.mean(x * x, -1, keepdims=True) + EPS)
    unit = x * scale
    gain_one = jnp.broadcast_to(jnp.sum(back * unit, 0, keepdims=True), (8, D))
    weighted = back * gains[0:1, :]
    mean = jnp.mean(weighted * unit, -1, keepdims=True)
    low[own, :] = (grad_own[...] + scale * (weighted - unit * mean)).astype(bf16)

    def low_to(d):
        return remote(low.at[own], low.at[own], hs.at[d], hr.at[tp], tp=peer(d))

    def low_from(d):
        there = low.at[crow(peer(d))]
        return remote(there, there, hs.at[d], hr.at[peer(d)], tp=peer(d))

    for d in range(1, TP):
        low_to(d).start()
    gain_rows = jnp.where(iota((8, D), 0) == 0, gain_one, gain_two[...])
    row, lane = iota((8, 128), 0), iota((8, 128), 1)
    pick = ((row < 2) & (lane == GAIN_COL + row)).astype(f32)
    misc_low[...] = (misc[...] + tn(gain_rows, pick, HI)).astype(bf16)
    small.start()
    small.middle()
    scatter.finish(grad_a)
    small.finish(misc_sum)
    part = grad_a.shape[0] // TP
    for i in range(TP):
        shsend[i, :, 0:256] = grad_a[i * part : (i + 1) * part, CM:CQ]
        shsend[i, :, 256:384] = grad_a[i * part : (i + 1) * part, CK:CS]
        shsend[i, :, 384:512] = misc_sum[i * part : (i + 1) * part, :]

    def share_to(d):
        return remote(shsend.at[peer(d)], shared.at[tp], ss.at[d], sr.at[tp], tp=peer(d))

    def share_from(d):
        return remote(shsend.at[peer(d)], shared.at[peer(d)], ss.at[d], sr.at[peer(d)], tp=peer(d))

    for d in range(1, TP):
        share_to(d).start()
    shared[tp] = shsend[tp]
    for d in range(1, TP):
        low_from(d).wait_recv()
        share_from(d).wait_recv()
        vec_from(d).wait_recv()
    vec_core.wait_send()
    loop(shards - 1, lambda k: vec_to_shard(k + 1).wait_send())
    for d in range(1, TP):
        share_to(d).wait_send()
        grad_to(d).wait_send()
        low_to(d).wait_send()
        vec_to(d).wait_send()


def finish(shards, *args):
    t = args[0].shape[0]
    rows = D // (2 * shards)
    chunk = t // TP
    vec = args[-1].shape
    out = [
        ((t, D), bf16),
        ((rows, CS), f32),
        ((TP, rows // TP, 512), f32),
        ((TP, *vec), f32),
    ]
    dma = pltpu.SemaphoreType.DMA
    vmem = pl.BlockSpec(memory_space=pltpu.VMEM)
    return pl.pallas_call(
        functools.partial(finish_kernel, shards),
        out_shape=[jax.ShapeDtypeStruct(*o) for o in out],
        in_specs=[vmem] * len(args),
        out_specs=[vmem] * len(out),
        scratch_shapes=[
            pltpu.VMEM((TP, chunk, D), bf16),
            pltpu.VMEM((TP, chunk, D), bf16),
            pltpu.VMEM((chunk, D), f32),
            pltpu.VMEM((D, CS), bf16),
            pltpu.VMEM((D, 128), f32),
            pltpu.VMEM((D, 128), bf16),
            pltpu.VMEM((rows, 128), f32),
            pltpu.VMEM((TP, rows // TP, 512), f32),
            pltpu.VMEM(vec, f32),
            pltpu.VMEM((shards, *vec), f32),
        ]
        + Scatter.scratch(shards, D, CS)
        + Scatter.scratch(shards, D, 128)
        + [dma((1,)), dma((1,)), dma((shards,)), dma((shards,))]
        + [dma((TP,))] * 8,
        compiler_params=pltpu.CompilerParams(
            collective_id=4, has_side_effects=True, vmem_limit_bytes=VLIMIT
        ),
        name="project_backward",
    )(*args)


def rotary_table(count):
    inverse = rope_base ** (-2.0 * np.arange(HD // 2, dtype=np.float32) / HD)
    angles = np.arange(count, dtype=np.float32)[:, None] * inverse.astype(np.float32)[None, :]
    both = np.concatenate([np.cos(angles), np.sin(angles)], axis=1)
    return np.tile(both, (1, 2)).astype(np.float32)


def local(
    hidden, cotangent, lengths, norm1_gain, w_z, w_x, w_shared, w_dt, dt_bias, a_log, d_skip,
    conv_w, conv_b, gated_gain, w_out, w_q, w_o, norm2_gain, w_gate, w_up, w_down,
):
    t = hidden.shape[1]
    shards = lax.axis_size("shard")
    hid, cot = hidden[0], cotangent[0]
    wm = jnp.concatenate([w_gate, w_up, w_down.T], axis=1)
    heads = jnp.pad(jnp.stack([dt_bias, a_log, d_skip]).astype(f32), ((0, 5), (0, 128 - H)))
    table = jnp.asarray(rotary_table(lax.axis_size("ctx") * t))
    (
        wf1, wf2, wo, normed, gains, z, cin, dt, taps, prm, chan,
        pre, hist, q_low, kk, vv, att, att_low, lse_row, ssd, start, steps, cum, tot, gl, square,
    ) = forward(
        shards, hid, w_z, w_x, w_shared, w_dt, w_q, w_out, w_o, norm1_gain[None], norm2_gain[None],
        conv_w, conv_b[None], gated_gain[None], heads, table, lengths,
    )
    osend, out_own, grad_own, grads, gain_two, total_square, ggl, grad_att, dots = ffn(
        shards, hid, cot, gl, att_low, square, wo, wm, gains, lengths
    )
    output, lin, grad_b, vec = backward(
        shards, ggl, grad_att, dots, total_square, grads, osend, out_own, pre, cin, hist, q_low, kk, vv, att,
        lse_row, ssd, start, steps, cum, tot, dt, z, table, taps, prm, chan, lengths,
    )
    grad_hidden, grad_a, shared, vecs = finish(
        shards, lin, normed, wf1, wf2, hid, grad_own, gains, gain_two, vec
    )

    def ranks(start, width, rows):
        return jnp.concatenate([vecs[i, :rows, start : start + width] for i in range(TP)], axis=1)

    conv_all = jnp.concatenate([ranks(0, WI, 5), vecs[:, :5, WI:CH].sum(0)], axis=1)
    gate_all = ranks(CH, WI, 1)[0]
    head_all = ranks(CH + WI, HL, 3)
    maps = shared.sum(0)
    first, second = shared[0] + shared[1], shared[2] + shared[3]
    grad_shared = jnp.concatenate(
        [
            maps[:, : 2 * N],
            first[:, 256 : 256 + HD],
            second[:, 256 : 256 + HD],
            first[:, 256 + HD : 384],
            second[:, 256 + HD : 384],
        ],
        axis=1,
    )
    grad_dt = jnp.concatenate([shared[i, :, 384 : 384 + HL] for i in range(TP)], axis=1)
    return (
        output[None],
        grad_hidden[None].astype(f32),
        maps[:, 384 + GAIN_COL],
        grad_a[:, CZ:CX],
        grad_a[:, CX:CM],
        grad_shared,
        grad_dt,
        head_all[0],
        head_all[1],
        head_all[2],
        conv_all[:4],
        conv_all[4],
        gate_all,
        grad_b[:, CO:CW].T,
        grad_a[:, CQ:CK],
        grad_b[:, CW:CG].T,
        maps[:, 384 + GAIN_COL + 1],
        grad_b[:, CG:CU],
        grad_b[:, CU:CD],
        grad_b[:, CD:CB].T,
    )


def solution(mesh):
    placed = (
        P("shard", "ctx", None),
        P("shard", "ctx", None),
        P("shard"),
        P(("shard", "ctx")),
        P(("shard", "ctx"), "tp"),
        P(("shard", "ctx"), "tp"),
        P(("shard", "ctx"), None),
        P(("shard", "ctx"), None),
        P(),
        P(),
        P(),
        P(),
        P(),
        P(),
        P("tp", ("shard", "ctx")),
        P(("shard", "ctx"), "tp"),
        P("tp", ("shard", "ctx")),
        P(("shard", "ctx")),
        P(("shard", "ctx"), "tp"),
        P(("shard", "ctx"), "tp"),
        P("tp", ("shard", "ctx")),
    )
    return jax.shard_map(
        local,
        mesh=mesh,
        in_specs=placed,
        out_specs=(
            P("shard", "ctx", "tp"),
            P("shard", "ctx", None),
            P(("shard", "ctx", "tp")),
            P(("shard", "ctx"), "tp"),
            P(("shard", "ctx"), "tp"),
            P(("shard", "ctx", "tp"), None),
            P(("shard", "ctx", "tp"), None),
            P(),
            P(),
            P(),
            P(),
            P(),
            P(),
            P("tp", ("shard", "ctx")),
            P(("shard", "ctx"), "tp"),
            P("tp", ("shard", "ctx")),
            P(("shard", "ctx", "tp")),
            P(("shard", "ctx"), "tp"),
            P(("shard", "ctx"), "tp"),
            P("tp", ("shard", "ctx")),
        ),
        check_vma=False,
    )
```

```python
import functools

import jax
import jax.numpy as jnp
import numpy as np
from jax import lax
from jax.experimental import pallas as pl
from jax.experimental.pallas import tpu as pltpu
from jax.sharding import PartitionSpec as P

H = 24
P_SIZE = 64
N = 128
NQ = 8
KV = 2
HD = 64
CONVW = 4
DI = 1536
D = 1024
FFL = 512
TP = 4
HL = H // TP
WI = HL * P_SIZE
CH = WI + 2 * N
L = 256

CZ, CX, CM, CQ, CK, CS, CA = 0, 384, 768, 1024, 1152, 1280, 1408
GAIN_COL = 24
CO, CW, CG, CU, CD, CB = 0, 384, 512, 1024, 1536, 2048

EPS = 1e-05
rope_base = 10000.0
FILL = -1e30
HI = lax.Precision.HIGHEST
MESH = pl.DeviceIdType.MESH
f32 = jnp.float32
bf16 = jnp.bfloat16
VLIMIT = 60 * 1024 * 1024


def nn(a, b, precision=None):
    return lax.dot_general(
        a, b, (((1,), (0,)), ((), ())), precision=precision, preferred_element_type=f32
    )


def nt(a, b, precision=None):
    return lax.dot_general(
        a, b, (((1,), (1,)), ((), ())), precision=precision, preferred_element_type=f32
    )


def tn(a, b, precision=None):
    return lax.dot_general(
        a, b, (((0,), (0,)), ((), ())), precision=precision, preferred_element_type=f32
    )


def rows_of(index, size=L):
    return pl.ds(pl.multiple_of(index * size, size), size)


def remote(src, dst, send, recv, **where):
    return pltpu.make_async_remote_copy(
        src_ref=src,
        dst_ref=dst,
        send_sem=send,
        recv_sem=recv,
        device_id=where,
        device_id_type=MESH,
    )


def iota(shape, dim):
    return lax.broadcasted_iota(jnp.int32, shape, dim)


def loop(n, body):
    lax.fori_loop(0, n, lambda i, c: (body(i), c)[1], 0)


def greet(shards, tp_too, ctx_too=True, shard_too=True):
    barrier = pltpu.get_barrier_semaphore()
    count = 0
    z, c, t = lax.axis_index("shard"), lax.axis_index("ctx"), lax.axis_index("tp")
    if ctx_too:
        pl.semaphore_signal(barrier, inc=1, device_id={"ctx": 1 - c}, device_id_type=MESH)
        count += 1
    if shard_too:

        def one(k):
            pl.semaphore_signal(
                barrier, inc=1, device_id={"shard": lax.rem(z + 1 + k, shards)}, device_id_type=MESH
            )

        loop(shards - 1, one)
        count += shards - 1
    if tp_too:
        for d in range(1, TP):
            pl.semaphore_signal(
                barrier, inc=1, device_id={"tp": lax.rem(t + d, TP)}, device_id_type=MESH
            )
            count += 1
    pl.semaphore_wait(barrier, count)


class Gather:
    def __init__(self, shards, src, dst, zsend, csend, recv, own):
        self.s, self.src, self.dst = shards, src, dst
        self.zsend, self.csend, self.recv, self.own = zsend, csend, recv, own
        self.z, self.c = lax.axis_index("shard"), lax.axis_index("ctx")
        self.r = src.shape[0]

    def block(self, g):
        return self.dst.at[rows_of(g, self.r)]

    def to_shard(self, k):
        g = 2 * self.z + self.c
        return remote(
            self.src,
            self.block(g),
            self.zsend.at[k],
            self.recv.at[g],
            shard=lax.rem(self.z + k, self.s),
        )

    def to_core(self, k):
        zz = lax.rem(self.z + k, self.s)
        g = 2 * zz + self.c
        return remote(self.block(g), self.block(g), self.csend.at[k], self.recv.at[g], ctx=1 - self.c)

    def got(self, k, core):
        zz = lax.rem(self.z + k, self.s)
        g = 2 * zz + core
        return remote(self.block(g), self.block(g), self.csend.at[k], self.recv.at[g], ctx=1 - self.c)

    def start(self):
        keep = pltpu.make_async_copy(self.src, self.block(2 * self.z + self.c), self.own)
        keep.start()
        loop(self.s - 1, lambda k: self.to_shard(k + 1).start())
        keep.wait()
        self.to_core(0).start()

    def forward(self, first=0, last=None):
        def one(k):
            self.got(k + 1, self.c).wait_recv()
            self.to_core(k + 1).start()

        lax.fori_loop(
            first, self.s - 1 if last is None else last, lambda k, carry: (one(k), carry)[1], 0
        )

    def finish(self):
        loop(self.s, lambda k: self.got(k, 1 - self.c).wait_recv())
        loop(self.s, lambda k: self.to_core(k).wait_send())
        loop(self.s - 1, lambda k: self.to_shard(k + 1).wait_send())

    @staticmethod
    def sems(shards):
        dma = pltpu.SemaphoreType.DMA
        return [dma((shards,)), dma((shards,)), dma((2 * shards,)), dma(())]


class Scatter:
    def __init__(self, shards, src, sib, stage, land, csend, crecv, zsend, zrecv):
        self.s, self.src, self.sib, self.stage, self.land = shards, src, sib, stage, land
        self.csend, self.crecv, self.zsend, self.zrecv = csend, crecv, zsend, zrecv
        self.z, self.c = lax.axis_index("shard"), lax.axis_index("ctx")
        self.r = src.shape[0] // (2 * shards)

    def to_core(self, k):
        zz = lax.rem(self.z + k, self.s)
        return remote(
            self.src.at[rows_of(2 * zz + 1 - self.c, self.r)],
            self.sib.at[zz],
            self.csend.at[zz],
            self.crecv.at[zz],
            ctx=1 - self.c,
        )

    def to_shard(self, k):
        zz = lax.rem(self.z + k, self.s)
        return remote(
            self.stage.at[zz], self.land.at[self.z], self.zsend.at[zz], self.zrecv.at[self.z], shard=zz
        )

    def arrive(self, k):
        zz = lax.rem(self.z + k, self.s)
        return remote(
            self.stage.at[zz], self.land.at[zz], self.zsend.at[zz], self.zrecv.at[zz], shard=zz
        )

    def start(self):
        loop(self.s - 1, lambda k: self.to_core(k + 1).start())
        self.to_core(0).start()

    def middle(self):
        def one(k):
            zz = lax.rem(self.z + 1 + k, self.s)
            self.to_core(k + 1).wait_recv()
            both = self.src[rows_of(2 * zz + self.c, self.r), :].astype(f32)
            self.stage[zz] = (both + self.sib[zz].astype(f32)).astype(bf16)
            self.to_shard(k + 1).start()

        loop(self.s - 1, one)

    def finish(self, out, cols=None):
        self.to_core(0).wait_recv()
        own = self.src[rows_of(2 * self.z + self.c, self.r), :].astype(f32)
        out[...] = own + self.sib[self.z].astype(f32)

        def one(k):
            zz = lax.rem(self.z + 1 + k, self.s)
            self.arrive(k + 1).wait_recv()
            out[...] += self.land[zz].astype(f32)

        loop(self.s - 1, one)
        loop(self.s, lambda k: self.to_core(k).wait_send())
        loop(self.s - 1, lambda k: self.to_shard(k + 1).wait_send())

    @staticmethod
    def scratch(shards, rows, cols):
        dma = pltpu.SemaphoreType.DMA
        block = pltpu.VMEM((shards, rows // (2 * shards), cols), bf16)
        return [block, block, block] + [dma((shards,))] * 4


def sigmoid(v):
    return 1.0 / (1.0 + jnp.exp(-v))


def softplus(v):
    return jnp.maximum(v, 0.0) + jnp.log1p(jnp.exp(-jnp.abs(v)))


def swap_half(v):
    width = v.shape[1]
    low = iota(v.shape, 1) % HD < HD // 2
    return jnp.where(low, pltpu.roll(v, width - HD // 2, 1), pltpu.roll(v, HD // 2, 1))


def low_lanes(shape):
    return iota(shape, 1) < 64


def spread():
    return (iota((N, WI), 1) // P_SIZE == iota((N, WI), 0)).astype(f32)


def first_row():
    return (iota((8, N), 0) == 0).astype(f32)


def wide(column, width):
    return jnp.concatenate([column] * (width // column.shape[1]), axis=1)


def lower_ones():
    return (iota((L, L), 0) >= iota((L, L), 1)).astype(f32)


def head_scalars(dt_raw, prm):
    real = iota(dt_raw.shape, 1) < HL
    steps = jnp.where(real, softplus(dt_raw + prm[0:1, :]), 0.0)
    rates = steps * prm[1:2, :]
    return steps, rates


def pair_columns(v, pair):
    return v[:, 128 * pair : 128 * pair + 128]


def own_half(v, half):
    return jnp.where(low_lanes(v.shape) == (half == 0), v, jnp.zeros_like(v))


def eye(n):
    return (iota((n, n), 0) == iota((n, n), 1)).astype(bf16)


def rotary_of(table, rows):
    both = table[rows, :]
    first = iota(both.shape, 1) % HD < HD // 2
    cosine = jnp.where(first, both, pltpu.roll(both, HD // 2, 1))
    sine = jnp.where(first, -pltpu.roll(both, 128 - HD // 2, 1), both)
    return cosine, sine


def forward_kernel(
    shards,
    hid, w_z, w_x, w_shared, w_dt, w_q, w_out, w_o, w_gate, gain_one, gain_two,
    small, table, length,
    wf1, wf2, wo, wg, normed, gains, z_out, cin, dt_raw, taps, prm, chan,
    pre, hist, q_low, kk, vv, att, att_low, lse_row, ssd, start, steps_out, cum_out, tot_out,
    gated_low, square,
    wa1, wa2, wa3, stat, pad, act, state, carried, scores_m, scores_l, hist_in,
    zs1, cs1, zr1, own1, zs2, cs2, zr2, own2, zs3, cs3, zr3, own3, zs4, cs4, zr4, own4,
    xs, xr,
):
    c, tp = lax.axis_index("ctx"), lax.axis_index("tp")
    t = hid.shape[0]
    blocks = t // L
    r = w_z.shape[0]

    kv = tp * (NQ // TP) // (NQ // KV)
    keys = w_shared[:, 2 * N : 2 * N + 128].astype(f32)
    vals = w_shared[:, 2 * N + 128 : 2 * N + 256].astype(f32)
    low_r = low_lanes((r, 128))
    other = pltpu.roll(jnp.where(kv == 0, vals, keys), 64, 1)
    wa1[:, 0:128] = w_q[...]
    wa1[:, 128:256] = jnp.where(
        kv == 0, jnp.where(low_r, keys, other), jnp.where(low_r, other, vals)
    ).astype(bf16)
    head_pick = (
        (iota((H, 128), 0) == iota((H, 128), 1) + tp * HL) & (iota((H, 128), 1) < HL)
    ).astype(bf16)
    row8, lane8 = iota((8, 128), 0), iota((8, 128), 1)
    gain_pick = ((row8 < 2) & (lane8 == GAIN_COL + row8)).astype(bf16)
    gain_rows = jnp.where(
        iota((8, r), 0) == 0, gain_one[...].astype(f32), gain_two[...].astype(f32)
    ).astype(bf16)
    wa1[:, 256:384] = (tn(w_dt[...], head_pick) + tn(gain_rows, gain_pick)).astype(bf16)
    wa2[:, 0:WI] = w_z[...]
    wa2[:, WI : 2 * WI] = w_x[...]
    wa2[:, 2 * WI : 2 * WI + 2 * N] = w_shared[:, 0 : 2 * N]
    greet(shards, False)
    gather1 = Gather(shards, wa1, wf1, zs1, cs1, zr1, own1)
    gather2 = Gather(shards, wa2, wf2, zs2, cs2, zr2, own2)
    gather3 = Gather(shards, wa3, wo, zs3, cs3, zr3, own3)
    gather4 = Gather(shards, w_gate, wg, zs4, cs4, zr4, own4)
    gather1.start()
    gather2.start()
    wa3[:, CO:CW] = nt(eye(r), w_out[...]).astype(bf16)
    wa3[:, CW:CG] = nt(eye(r), w_o[...]).astype(bf16)

    expand = spread()
    mine = pl.ds(pl.multiple_of(tp * WI, 128), WI)
    taps[0:CONVW, 0:WI] = small[0:CONVW, mine].astype(f32)
    taps[0:CONVW, WI:CH] = small[0:CONVW, DI:].astype(f32)
    taps[CONVW : CONVW + 1, 0:WI] = small[CONVW : CONVW + 1, mine].astype(f32)
    taps[CONVW : CONVW + 1, WI:CH] = small[CONVW : CONVW + 1, DI:].astype(f32)
    taps[CONVW + 1 :, :] = jnp.zeros((8 - CONVW - 1, CH), f32)
    heads = pltpu.roll(small[8:16, 0:128].astype(f32), lax.rem(128 - tp * HL, 128), 1)
    heads = jnp.where(lane8 < HL, jnp.where(row8 == 1, -jnp.exp(heads), heads), 0.0)
    prm[...] = heads
    chan[...] = jnp.zeros_like(chan)
    chan[0:1, :] = small[CONVW + 1 : CONVW + 2, mine].astype(f32)
    chan[1:2, :] = nn(heads, expand, HI)[2:3, :]

    def swap(src, dst, i):
        return remote(src, dst, xs.at[i], xr.at[i], ctx=1 - c)

    def row_scale(i):
        rows = rows_of(i)
        x = hid[rows, :].astype(f32)
        scale = lax.rsqrt(jnp.mean(x * x, -1, keepdims=True) + EPS)
        stat[rows, :] = jnp.broadcast_to(scale, (L, 128))

    loop(blocks, row_scale)
    gather1.forward()
    gather1.finish()
    turned = wf1[:, 256:384].astype(f32).T
    gains[...] = turned[GAIN_COL : GAIN_COL + 8]
    gain = gains[0:1, :]
    low128 = low_lanes((L, 128))

    def first_projections(i):
        rows = rows_of(i)
        low = (hid[rows, :].astype(f32) * wide(stat[rows, :], D) * gain).astype(bf16)
        normed[rows, :] = low
        rest = nn(low, wf1[...])
        cosine, sine = rotary_of(table, pl.ds(pl.multiple_of(c * t + i * L, L), L))
        v = rest[:, 0:128]
        q_low[rows, :] = (v * cosine + swap_half(v) * sine).astype(bf16)
        v = rest[:, 128:256]
        other = pltpu.roll(v, 64, 1)
        twice = jnp.where(low128, v, other)
        kk[0, rows, :] = (twice * cosine + swap_half(twice) * sine).astype(bf16)
        vv[0, rows, :] = jnp.where(low128, other, v).astype(bf16)
        dt_raw[rows, :] = rest[:, 256:384]

    loop(blocks, first_projections)
    keys = swap(kk.at[0], kk.at[1], 1)
    keys.start()
    vals = swap(vv.at[0], vv.at[1], 2)
    vals.start()

    scale = HD ** (-0.5)
    limit = length[0] - c * t

    def stacked(v):
        return jnp.concatenate([own_half(v, 0), own_half(v, 1)], axis=0)

    for i in range(blocks):
        rows = pl.ds(i * L, L)
        width = (i + 1) * L
        q2 = stacked(q_low[rows, :].astype(f32)).astype(bf16)
        s = nt(q2, kk[0, 0:width, :]) * scale
        at = iota(s.shape, 0) % L + i * L
        col = iota(s.shape, 1)
        s = jnp.where((col <= at) & (col < limit), s, FILL)
        peak = jnp.max(s, -1, keepdims=True)
        e = jnp.exp(s - peak)
        total = jnp.sum(e, -1, keepdims=True)
        o = nn(e.astype(bf16), vv[0, 0:width, :])
        scores_m[...] = jnp.broadcast_to(peak, (2 * L, 128))
        scores_l[0] = jnp.broadcast_to(total, (2 * L, 128))
        scores_l[1] = o
        if i == 0:
            keys.wait_recv()
            vals.wait_recv()

        @pl.when(c > 0)
        def earlier():
            s2 = nt(q2, kk[1]) * scale
            old = scores_m[:, 0:1]
            new = jnp.maximum(old, jnp.max(s2, -1, keepdims=True))
            e2 = jnp.exp(s2 - new)
            fade = jnp.exp(old - new)
            scores_m[...] = jnp.broadcast_to(new, (2 * L, 128))
            scores_l[0] = fade * scores_l[0] + jnp.sum(e2, -1, keepdims=True)
            scores_l[1] = fade * scores_l[1] + nn(e2.astype(bf16), vv[1])

        total = scores_l[0]
        o = scores_l[1] / total
        o = jnp.where(low128, o[:L], o[L:])
        att[rows, :] = o
        att_low[rows, :] = o.astype(bf16)
        logs = scores_m[...] + jnp.log(total)
        turned = jnp.where(low128, logs[:L], logs[L:]).T
        lse_row[0:1, rows] = turned[0:1]
        lse_row[1:2, rows] = turned[64:65]
        lse_row[2:8, rows] = jnp.zeros((6, L), f32)
        if i == blocks - 2:
            gather2.forward(0, 1)
    gather2.forward(1)
    gather3.start()
    gather4.start()
    gather2.finish()

    def conv_input(k):
        i = blocks - 1 - k
        rows = rows_of(i)
        v = nn(normed[rows, :], wf2[:, WI:]).astype(bf16)
        cin[rows, :] = v
        pad[pl.ds(pl.multiple_of(i * L + 8, 8), L), :] = v.astype(f32)

    conv_input(0)
    tail = swap(cin.at[pl.ds(t - 16, 16)], hist_in, 0)
    tail.start()
    lax.fori_loop(1, blocks, lambda k, carry: (conv_input(k), carry)[1], 0)
    tail.wait_recv()
    before = hist_in[8:16, :].astype(f32)
    hist[...] = jnp.where((iota((8, CH), 0) >= 5) & (c > 0), before, 0.0)
    pad[0:8, :] = hist[...]
    ones = lower_ones()
    state[...] = jnp.zeros_like(state)

    for i in range(blocks):
        rows = pl.ds(i * L, L)
        v = taps[4:5, :] + taps[0:1, :] * pad[pl.ds(i * L + 5, L), :]
        for j in range(1, CONVW):
            v = v + taps[j : j + 1, :] * pad[pl.ds(i * L + 5 + j, L), :]
        pre[rows, :] = v
        a = v * sigmoid(v)
        act[rows, :] = a
        steps, rates = head_scalars(dt_raw[rows, :], prm)
        cum = nn(ones, rates, HI)
        tot = cum[L - 1 : L, :]
        steps_out[rows, :] = steps
        cum_out[rows, :] = cum
        tot_out[i] = jnp.broadcast_to(tot, (8, 128))
        weight = nn(jnp.exp(tot - cum) * steps, expand, HI)
        start[i] = state[...]
        add = tn(a[:, WI : WI + N].astype(bf16), (weight * a[:, :WI]).astype(bf16))
        decay = nn(jnp.broadcast_to(jnp.exp(tot), (8, 128)), expand, HI)[0:1, :]
        state[...] = decay * state[...] + add

    states = swap(state, carried, 3)
    states.start()
    gather3.forward()

    def gate_input(i):
        rows = rows_of(i)
        z_out[rows, :] = nn(normed[rows, :], wf2[:, 0:WI])

    loop(blocks, gate_input)

    states.wait_recv()
    carried[...] = jnp.where(c > 0, carried[...], 0.0)
    mask = iota((L, L), 0) >= iota((L, L), 1)
    for i in range(blocks):
        rows = pl.ds(i * L, L)
        if i > 0:
            decay = nn(jnp.exp(tot_out[i - 1]), expand, HI)[0:1, :]
            carried[...] = carried[...] * decay
        start[i] = start[i] + carried[...]
        s0 = start[i].astype(bf16)
        steps, cum = steps_out[rows, :], cum_out[rows, :]
        x = act[rows, 0:WI]
        xl = x.astype(bf16)
        in_map = act[rows, WI : WI + N].astype(bf16)
        out_map = act[rows, WI + N : CH].astype(bf16)
        gram = nt(out_map, in_map)
        cum_t, steps_t = cum.T, steps.T
        inner = []
        for pair in range(HL // 2):
            halves = []
            for half in range(2):
                h = 2 * pair + half
                decay = jnp.exp(jnp.where(mask, cum[:, h : h + 1] - cum_t[h : h + 1, :], FILL))
                mixing = gram * decay * steps_t[h : h + 1, :]
                halves.append(nn(mixing.astype(bf16), pair_columns(xl, pair)))
            inner.append(jnp.where(low128, halves[0], halves[1]))
        y = jnp.concatenate(inner, axis=1)
        y = y + nn(jnp.exp(cum), expand, HI) * nn(out_map, s0) + chan[1:2, :] * x
        ssd[rows, :] = y
        zz = z_out[rows, :]
        gated = y * zz * sigmoid(zz)
        gated_low[rows, :] = (gated * chan[0:1, :]).astype(bf16)
        square[:, rows] = nt(jnp.ones((8, WI), f32), gated * gated, HI)

    gather4.forward()
    gather3.finish()
    gather4.finish()
    for copy in (tail, keys, vals, states):
        copy.wait_send()


def forward(shards, *args):
    t, r = args[0].shape[0], args[1].shape[0]
    out = [
        ((D, 384), bf16),
        ((D, 1024), bf16),
        ((D, CG), bf16),
        ((D, FFL), bf16),
        ((t, D), bf16),
        ((8, D), f32),
        ((t, WI), f32),
        ((t, CH), bf16),
        ((t, 128), f32),
        ((8, CH), f32),
        ((8, 128), f32),
        ((8, WI), f32),
        ((t, CH), f32),
        ((8, CH), f32),
        ((t, 128), bf16),
        ((2, t, 128), bf16),
        ((2, t, 128), bf16),
        ((t, 128), f32),
        ((t, 128), bf16),
        ((8, t), f32),
        ((t, WI), f32),
        ((t // L, N, WI), f32),
        ((t, 128), f32),
        ((t, 128), f32),
        ((t // L, 8, 128), f32),
        ((t, WI), bf16),
        ((8, t), f32),
    ]
    dma = pltpu.SemaphoreType.DMA
    vmem = pl.BlockSpec(memory_space=pltpu.VMEM)
    return pl.pallas_call(
        functools.partial(forward_kernel, shards),
        out_shape=[jax.ShapeDtypeStruct(*o) for o in out],
        in_specs=[vmem] * (len(args) - 1) + [pl.BlockSpec(memory_space=pltpu.SMEM)],
        out_specs=[vmem] * len(out),
        scratch_shapes=[
            pltpu.VMEM((r, 384), bf16),
            pltpu.VMEM((r, 1024), bf16),
            pltpu.VMEM((r, CG), bf16),
            pltpu.VMEM((t, 128), f32),
            pltpu.VMEM((t + 8, CH), f32),
            pltpu.VMEM((t, CH), f32),
            pltpu.VMEM((N, WI), f32),
            pltpu.VMEM((N, WI), f32),
            pltpu.VMEM((2 * L, 128), f32),
            pltpu.VMEM((2, 2 * L, 128), f32),
            pltpu.VMEM((16, CH), bf16),
        ]
        + Gather.sems(shards) * 4
        + [dma((4,)), dma((4,))],
        compiler_params=pltpu.CompilerParams(
            collective_id=1, has_side_effects=True, vmem_limit_bytes=VLIMIT
        ),
        name="mix_forward",
    )(*args)


def ffn_kernel(
    shards,
    hid, cot, gl, att, square, wb, wg, w_up, w_down, gains, length,
    osend, out_own, grad_own, grads, gain_grad, total_square, ggl, grad_att, dots,
    grad_res, partial, seed, send1, recv1, low_two, proj, grad_act, act, gg, gu, gown, back,
    unit, scale_keep, gsend, grecv, sqall, wm, wm_own,
    zs, cs, zr, own_sem, sqs, sqr, s1, r1, ns, nr, gs, gr, hs, hr,
):
    t = hid.shape[0]
    tp, c = lax.axis_index("tp"), lax.axis_index("ctx")
    blocks = t // L
    sub = L // TP
    width = D // TP
    wm_own[:, 0:FFL] = w_up[...]
    wm_own[:, FFL:] = nt(eye(w_down.shape[1]), w_down[...]).astype(bf16)
    greet(shards, True)
    gather = Gather(shards, wm_own, wm, zs, cs, zr, own_sem)
    gather.start()

    def peer(d):
        return lax.rem(tp + d, TP)

    def part(b, owner):
        return pl.ds(pl.multiple_of(b * L + owner * sub, sub), sub)

    def kept(b):
        return rows_of(b, sub)

    def square_to(d):
        return remote(sqall.at[tp], sqall.at[tp], sqs.at[d], sqr.at[tp], tp=peer(d))

    def square_from(d):
        return remote(sqall.at[tp], sqall.at[peer(d)], sqs.at[d], sqr.at[peer(d)], tp=peer(d))

    def scatter_to(send, recv, ss, rs, b, d):
        return remote(send.at[d, b], recv.at[tp, b], ss.at[d, b], rs.at[tp, b], tp=peer(d))

    def scatter_from(send, recv, ss, rs, b, d):
        return remote(send.at[d, b], recv.at[peer(d), b], ss.at[d, b], rs.at[peer(d), b], tp=peer(d))

    def gather_to(ref, ss, rs, b, d):
        there = ref.at[part(b, tp)]
        return remote(there, there, ss.at[d, b], rs.at[tp, b], tp=peer(d))

    def gather_from(ref, ss, rs, b, d):
        there = ref.at[part(b, peer(d))]
        return remote(there, there, ss.at[d, b], rs.at[peer(d), b], tp=peer(d))

    first = send1, recv1, s1, r1
    norms = low_two, ns, nr
    gradients = gsend, grecv, gs, gr
    residuals = grad_res, hs, hr

    sqall[tp] = square[...]
    for d in range(1, TP):
        square_to(d).start()
    limit = length[0] - c * t

    def mask_seed(i):
        rows = rows_of(i)
        live = iota((L, D), 0) + i * L < limit
        seed[rows, :] = jnp.where(live, cot[rows, :].astype(f32), 0.0).astype(bf16)

    loop(blocks, mask_seed)
    for d in range(1, TP):
        square_from(d).wait_recv()
    total_square[...] = sqall[0] + sqall[1] + sqall[2] + sqall[3]
    gain = gains[1:2, :]
    gain_grad[...] = jnp.zeros_like(gain_grad)

    def mix(b):
        rows = rows_of(b)
        scale = lax.rsqrt(total_square[:, rows] / DI + EPS)
        column = wide(tn(scale, first_row(), HI), D)
        partial[rows, :] = nt(gl[rows, :], wb[:, CO:CW]) * column + nt(att[rows, :], wb[:, CW:CG])
        for d in range(1, TP):
            send1[d, b] = partial[part(b, peer(d)), :].astype(bf16)
            scatter_to(*first, b, d).start()

    def norm(b):
        own = part(b, tp)
        acc = hid[own, :].astype(f32) + partial[own, :]
        for d in range(1, TP):
            scatter_from(*first, b, d).wait_recv()
            acc = acc + recv1[peer(d), b].astype(f32)
        scale = lax.rsqrt(jnp.mean(acc * acc, -1, keepdims=True) + EPS)
        scale_keep[kept(b), :] = jnp.broadcast_to(scale, (sub, 128))
        u = acc * scale
        unit[kept(b), :] = u
        low_two[own, :] = (u * gain).astype(bf16)
        for d in range(1, TP):
            gather_to(*norms, b, d).start()

    def mix_and_norm(s):
        @pl.when(s < blocks)
        def one():
            mix(s)

        @pl.when(s >= 2)
        def two():
            norm(s - 2)

    loop(blocks + 2, mix_and_norm)
    gather.forward()
    gather.finish()

    def act_grad(i):
        rows = rows_of(i)
        grad_act[rows, :] = nn(seed[rows, :], wm[:, FFL:])

    loop(blocks, act_grad)

    def hidden_units(b):
        rows = rows_of(b)
        for d in range(1, TP):
            gather_from(*norms, b, d).wait_recv()
        low = low_two[rows, :]
        gate, up = nn(low, wg[...]), nn(low, wm[:, 0:FFL])
        sig = sigmoid(gate)
        silu = gate * sig
        hidden_act = (silu * up).astype(bf16)
        act[rows, :] = hidden_act
        ga = grad_act[rows, :]
        g1 = (ga * up * (sig * (1.0 + gate * (1.0 - sig)))).astype(bf16)
        g2 = (ga * silu).astype(bf16)
        gg[rows, :] = g1
        gu[rows, :] = g2
        back[...] = nt(g1, wg[...]) + nt(g2, wm[:, 0:FFL])
        gown[kept(b), :] = back[kept(tp), :]
        for d in range(1, TP):
            gsend[d, b] = back[kept(peer(d)), :].astype(bf16)
            scatter_to(*gradients, b, d).start()
        partial[rows, :] = partial[rows, :] + nt(hidden_act, wm[:, FFL:])
        for e in range(1, TP):
            osend[e, rows, :] = partial[rows, rows_of(peer(e), width)].astype(bf16)

    def norm_back(b):
        own = part(b, tp)
        g = gown[kept(b), :]
        for d in range(1, TP):
            scatter_from(*gradients, b, d).wait_recv()
            g = g + grecv[peer(d), b].astype(f32)
        u = unit[kept(b), :]
        gain_grad[...] += jnp.broadcast_to(jnp.sum(g * u, 0, keepdims=True), (8, D))
        weighted = g * gain
        mean = jnp.mean(weighted * u, -1, keepdims=True)
        res = seed[own, :].astype(f32) + scale_keep[kept(b), 0:1] * (weighted - u * mean)
        grad_own[kept(b), :] = res
        grad_res[own, :] = res.astype(bf16)
        for d in range(1, TP):
            gather_to(*residuals, b, d).start()

    def weight_grads(i):
        feats = rows_of(i)
        low = low_two[:, feats]
        grads[feats, CG:CU] = tn(low, gg[...]).astype(bf16)
        grads[feats, CU:CD] = tn(low, gu[...]).astype(bf16)

    def down_grads(i):
        feats = rows_of(i)
        grads[feats, CD:CB] = tn(seed[:, feats], act[...]).astype(bf16)

    def out_back(b):
        rows = rows_of(b)
        for d in range(1, TP):
            gather_from(*residuals, b, d).wait_recv()
        square_scale = lax.rsqrt(total_square[:, rows] / DI + EPS)
        column = wide(tn(square_scale, first_row(), HI), D)
        got = grad_res[rows, :]
        low = (column * got.astype(f32)).astype(bf16)
        proj[rows, :] = low
        product = nn(low, wb[:, CO:CW])
        ggl[rows, :] = product
        dots[:, rows] = nt(jnp.ones((8, WI), f32), product * gl[rows, :].astype(f32), HI)
        grad_att[rows, :] = nn(got, wb[:, CW:CG]).astype(bf16)

    def there_and_back(s):
        @pl.when(s < blocks)
        def one():
            hidden_units(s)

        @pl.when(s == blocks)
        def fill():
            loop(D // L, weight_grads)

        @pl.when((s >= 1) & (s <= blocks))
        def two():
            norm_back(s - 1)

        @pl.when(s == blocks + 1)
        def more():
            loop(D // L, down_grads)

        @pl.when(s >= 2)
        def three():
            out_back(s - 2)

    loop(blocks + 2, there_and_back)

    def out_grads(i):
        feats = rows_of(i)
        grads[feats, CO:CW] = tn(proj[:, feats], gl[...]).astype(bf16)
        grads[feats, CW:CG] = tn(grad_res[:, feats], att[...]).astype(bf16)

    loop(D // L, out_grads)
    mine = rows_of(tp, width)
    out_own[...] = hid[:, mine].astype(f32) + partial[:, mine]

    def sent(b):
        for d in range(1, TP):
            scatter_to(*first, b, d).wait_send()
            gather_to(*norms, b, d).wait_send()
            scatter_to(*gradients, b, d).wait_send()
            gather_to(*residuals, b, d).wait_send()

    loop(blocks, sent)
    for d in range(1, TP):
        square_to(d).wait_send()


def ffn(shards, *args):
    t = args[0].shape[0]
    blocks, sub = t // L, L // TP
    kept = blocks * sub
    out = [
        ((TP, t, D // TP), bf16),
        ((t, D // TP), f32),
        ((kept, D), f32),
        ((D, CB), bf16),
        ((8, D), f32),
        ((8, t), f32),
        ((t, WI), f32),
        ((t, 128), bf16),
        ((8, t), f32),
    ]
    dma = pltpu.SemaphoreType.DMA
    vmem = pl.BlockSpec(memory_space=pltpu.VMEM)
    parts = pltpu.VMEM((TP, blocks, sub, D), bf16)
    return pl.pallas_call(
        functools.partial(ffn_kernel, shards),
        out_shape=[jax.ShapeDtypeStruct(*o) for o in out],
        in_specs=[vmem] * (len(args) - 1) + [pl.BlockSpec(memory_space=pltpu.SMEM)],
        out_specs=[vmem] * len(out),
        scratch_shapes=[
            pltpu.VMEM((t, D), bf16),
            pltpu.VMEM((t, D), f32),
            pltpu.VMEM((t, D), bf16),
            parts,
            parts,
            pltpu.VMEM((t, D), bf16),
            pltpu.VMEM((t, D), bf16),
            pltpu.VMEM((t, FFL), f32),
            pltpu.VMEM((t, FFL), bf16),
            pltpu.VMEM((t, FFL), bf16),
            pltpu.VMEM((t, FFL), bf16),
            pltpu.VMEM((kept, D), f32),
            pltpu.VMEM((L, D), f32),
            pltpu.VMEM((kept, D), f32),
            pltpu.VMEM((kept, 128), f32),
            parts,
            parts,
            pltpu.VMEM((TP, 8, t), f32),
            pltpu.VMEM((D, 2 * FFL), bf16),
            pltpu.VMEM((D // (2 * shards), 2 * FFL), bf16),
        ]
        + Gather.sems(shards)
        + [dma((TP,))] * 2
        + [dma((TP, blocks))] * 8,
        compiler_params=pltpu.CompilerParams(
            collective_id=2, has_side_effects=True, vmem_limit_bytes=VLIMIT
        ),
        name="feed_forward",
    )(*args)


def backward_kernel(
    shards,
    ggl, grad_att, dots_in, total_square, grads, osend, out_own,
    pre, cin, hist, q_low, kk, vv, att, lse_row, ssd, start, steps_in, cum_in, tot_in, dt_raw, z_in,
    table, taps, prm, chan, length,
    output, lin, grad_b, small,
    orecv, dots, dk, dv, dy, dpre, ends, dstate, carry, kv_out, kv_in, pad, edge_out, edge_in,
    sib, stage, land, csend, crecv, zsend, zrecv, xs, xr, ts, tr, os, orr,
):
    c, tp = lax.axis_index("ctx"), lax.axis_index("tp")
    t = cin.shape[0]
    blocks = t // L
    greet(shards, True)
    scatter = Scatter(shards, grads, sib, stage, land, csend, crecv, zsend, zrecv)
    scatter.start()

    def swap(src, dst, i):
        return remote(src, dst, xs.at[i], xr.at[i], ctx=1 - c)

    def peer(d):
        return lax.rem(tp + d, TP)

    def dot_to(d):
        return remote(dots.at[tp], dots.at[tp], ts.at[d], tr.at[tp], tp=peer(d))

    def dot_from(d):
        return remote(dots.at[tp], dots.at[peer(d)], ts.at[d], tr.at[peer(d)], tp=peer(d))

    dots[tp] = dots_in[...]
    for d in range(1, TP):
        dot_to(d).start()

    def out_to(d):
        return remote(osend.at[d], orecv.at[tp], os.at[d], orr.at[tp], tp=peer(d))

    def out_from(d):
        return remote(osend.at[d], orecv.at[peer(d)], os.at[d], orr.at[peer(d)], tp=peer(d))

    for d in range(1, TP):
        out_to(d).start()
    conv_grads = small.at[:, 0:CH]
    chan_grads = small.at[:, CH : CH + WI]
    head_grads = small.at[:, CH + WI : CH + WI + 128]
    expand = spread()
    low128 = low_lanes((L, 128))
    small[...] = jnp.zeros_like(small)
    for d in range(1, TP):
        dot_from(d).wait_recv()

    def gated_back(i):
        rows = rows_of(i)
        both = dots[0, :, rows] + dots[1, :, rows] + dots[2, :, rows] + dots[3, :, rows]
        share = both / ((total_square[:, rows] / DI + EPS) * DI)
        column = wide(tn(share, first_row(), HI), WI)
        zz, y = z_in[rows, :], ssd[rows, :]
        sig = sigmoid(zz)
        silu = zz * sig
        gated = y * silu
        product = ggl[rows, :]
        chan_grads[0:1, :] += jnp.sum(product * gated, 0, keepdims=True)
        grad_gated = product * chan[0:1, :] - column * gated
        grad_y = grad_gated * silu
        dy[rows, :] = grad_y
        lin[rows, CZ:CX] = (grad_gated * y * (sig * (1.0 + zz * (1.0 - sig)))).astype(bf16)
        v = pre[rows, WI + N : CH]
        out_map = (v * sigmoid(v)).astype(bf16)
        ends[i] = tn(out_map, (nn(jnp.exp(cum_in[rows, :]), expand, HI) * grad_y).astype(bf16))

    loop(blocks, gated_back)
    dstate[...] = jnp.zeros_like(dstate)

    def chain(k):
        i = blocks - 1 - k
        add = ends[i]
        ends[i] = dstate[...]
        dstate[...] = nn(jnp.exp(tot_in[i]), expand, HI)[0:1, :] * dstate[...] + add

    loop(blocks, chain)
    states = swap(dstate, carry, 0)
    states.start()
    scatter.middle()

    scale = HD ** (-0.5)
    limit = length[0] - c * t
    dk[...] = jnp.zeros_like(dk)
    dv[...] = jnp.zeros_like(dv)
    head_of = ((iota((8, 128), 1) // HD) == iota((8, 128), 0)).astype(f32)

    def stacked(v):
        return jnp.concatenate([own_half(v, 0), own_half(v, 1)], axis=0).astype(bf16)

    def side_by_side(v):
        return jnp.concatenate([v[0:1, :], v[1:2, :]], axis=1)

    for i in range(blocks):
        rows = pl.ds(i * L, L)
        width = (i + 1) * L
        q2 = stacked(q_low[rows, :].astype(f32))
        go = grad_att[rows, :].astype(f32)
        go2 = stacked(go)
        row_dot = side_by_side(nt(head_of, go * att[rows, :], HI))
        logs = side_by_side(lse_row[:, rows])
        turn = rotary_of(table, pl.ds(pl.multiple_of(c * t + i * L, L), L))

        def keys_of(part, size, masked):
            k, v = kk[part, 0:size, :], vv[part, 0:size, :]
            s = nt(k, q2) * scale - logs
            if masked:
                at = iota(s.shape, 1) % L + i * L
                row = iota(s.shape, 0)
                s = jnp.where((row <= at) & (row < limit), s, FILL)
            p = jnp.exp(s)
            ds = (p * (nt(v, go2) - row_dot)).astype(bf16)
            dv[part, 0:size, :] += nn(p.astype(bf16), go2)
            dk[part, 0:size, :] += nn(ds, q2)
            out = tn(ds, k) * scale
            out = jnp.where(low128, out[:L], out[L:])
            return out * turn[0] - swap_half(out) * turn[1]

        pad[rows, 0:128] = keys_of(0, width, True)

        @pl.when(c > 0)
        def earlier():
            pad[rows, 0:128] += keys_of(1, t, False)

        lin[rows, CQ:CK] = pad[rows, 0:128].astype(bf16)

    def key_values(part, rows):
        gk, gv = dk[part, rows, :] * scale, dv[part, rows, :]
        return jnp.where(low128, gk + pltpu.roll(gk, 64, 1), gv + pltpu.roll(gv, 64, 1))

    def pack(i):
        rows = rows_of(i)
        kv_out[rows, :] = key_values(1, rows).astype(bf16)

    loop(blocks, pack)
    pairs = swap(kv_out, kv_in, 1)
    pairs.start()

    pad[0:8, :] = hist[...]

    def fill(i):
        pad[pl.ds(pl.multiple_of(i * L + 8, 8), L), :] = cin[rows_of(i), :].astype(f32)

    loop(blocks, fill)
    states.wait_recv()
    carry[...] = jnp.where(c == 0, carry[...], 0.0)

    def add_carry(k):
        i = blocks - 1 - k
        ends[i] = ends[i] + carry[...]
        carry[...] = nn(jnp.exp(tot_in[i]), expand, HI)[0:1, :] * carry[...]

    loop(blocks, add_carry)
    mask = iota((L, L), 0) >= iota((L, L), 1)
    ones = lower_ones()
    lane = iota((L, 128), 1)

    def fold(v):
        return nt(v, expand, HI)

    def scan_back(i):
        rows = rows_of(i)
        v = pre[rows, :]
        sig = sigmoid(v)
        a = v * sig
        x = a[:, :WI]
        xl, bl, cl = x.astype(bf16), a[:, WI : WI + N].astype(bf16), a[:, WI + N :].astype(bf16)
        steps, cum = steps_in[rows, :], cum_in[rows, :]
        tot = cum[L - 1 : L, :]
        ecum, wend = jnp.exp(cum), jnp.exp(tot - cum)
        weight = wend * steps
        ecum_x, weight_x = nn(ecum, expand, HI), nn(weight, expand, HI)
        grad_y = dy[rows, :]
        dyl = grad_y.astype(bf16)
        s0, d1 = start[i], ends[i]
        s0l, d1l = s0.astype(bf16), d1.astype(bf16)
        bd, cs = nn(bl, d1l), nn(cl, s0l)
        dw = fold(x * bd)
        crossing = jnp.broadcast_to(jnp.sum(s0 * d1, 0, keepdims=True), (8, WI))
        dtot = jnp.sum(weight * dw, 0, keepdims=True) + jnp.exp(tot) * fold(crossing)[0:1, :]
        gram = nt(cl, bl)
        cum_t, steps_t = cum.T, steps.T
        dgram = jnp.zeros((L, L), f32)
        row_sums = jnp.zeros((L, 128), f32)
        col_sums, inner = [], []
        for pair in range(HL // 2):
            xp, dp = pair_columns(xl, pair), pair_columns(dyl, pair)
            dpf = pair_columns(grad_y, pair)
            halves = []
            for half in range(2):
                h = 2 * pair + half
                decay = jnp.exp(jnp.where(mask, cum[:, h : h + 1] - cum_t[h : h + 1, :], FILL))
                q = nt(own_half(dpf, half).astype(bf16), xp)
                mixed = gram * decay
                srow = steps_t[h : h + 1, :]
                f = mixed * q
                col_sums.append(jnp.sum(f, 0, keepdims=True))
                row_sums = jnp.where(lane == h, jnp.sum(f * srow, -1, keepdims=True), row_sums)
                dgram = dgram + decay * srow * q
                halves.append(tn((mixed * srow).astype(bf16), dp))
            inner.append(jnp.where(low128, halves[0], halves[1]))
        cols = jnp.concatenate(col_sums + [jnp.zeros((128 - HL, L), f32)], axis=0).T
        dcum = fold(grad_y * cs) * ecum - weight * dw + row_sums - steps * cols
        dcum = dcum + jnp.where(iota((L, 128), 0) == L - 1, dtot, 0.0)
        drate = tn(ones, dcum, HI)
        rate_of = prm[1:2, :]
        raw = dt_raw[rows, :] + prm[0:1, :]
        dstep = (wend * dw + cols + drate * rate_of) * sigmoid(raw)
        dstep = jnp.where(lane < HL, dstep, 0.0)
        lin[rows, CS:CA] = dstep.astype(bf16)
        head_grads[0:1, :] += jnp.sum(dstep, 0, keepdims=True)
        head_grads[1:2, :] += jnp.sum(drate * steps * rate_of, 0, keepdims=True)
        head_grads[2:3, :] += jnp.sum(fold(grad_y * x), 0, keepdims=True)
        slope = sig * (1.0 + v * (1.0 - sig))
        dx = chan[1:2, :] * grad_y + weight_x * bd + jnp.concatenate(inner, axis=1)
        dg = dgram.astype(bf16)
        db = tn(dg, cl) + nt((weight_x * x).astype(bf16), d1l)
        dc = nn(dg, bl) + nt((ecum_x * grad_y).astype(bf16), s0l)
        dpre[rows, 0:WI] = dx * slope[:, :WI]
        dpre[rows, WI : WI + N] = db * slope[:, WI : WI + N]
        dpre[rows, WI + N : CH] = dc * slope[:, WI + N :]

    loop(blocks, scan_back)
    edge_out[...] = dpre[0:8, :]
    edge = swap(edge_out, edge_in, 2)
    edge.start()
    pairs.wait_recv()

    def keys_back(i):
        rows = rows_of(i)
        v = key_values(0, rows) + kv_in[rows, :].astype(f32)
        cosine, sine = rotary_of(table, pl.ds(pl.multiple_of(c * t + i * L, L), L))
        cosine = jnp.where(low128, cosine, 1.0)
        sine = jnp.where(low128, sine, 0.0)
        lin[rows, CK:CS] = (v * cosine - swap_half(v) * sine).astype(bf16)

    loop(blocks, keys_back)
    edge.wait_recv()
    dpre[pl.ds(t, 8), :] = jnp.where(c == 0, edge_in[...], 0.0)
    for i in range(blocks):
        rows = pl.ds(i * L, L)
        g = dpre[rows, :]
        conv_grads[4:5, :] += jnp.sum(g, 0, keepdims=True)
        back = jnp.zeros_like(g)
        for j in range(CONVW):
            back = back + taps[j : j + 1, :] * dpre[pl.ds(i * L + CONVW - 1 - j, L), :]
            conv_grads[j : j + 1, :] += jnp.sum(g * pad[pl.ds(i * L + 5 + j, L), :], 0, keepdims=True)
        lin[rows, CX:CQ] = back.astype(bf16)
    total = out_own[...]
    for d in range(1, TP):
        out_from(d).wait_recv()
        total = total + orecv[peer(d)].astype(f32)
    output[...] = total.astype(bf16)
    scatter.finish(grad_b)
    for copy in (states, pairs, edge):
        copy.wait_send()
    for d in range(1, TP):
        dot_to(d).wait_send()
        out_to(d).wait_send()


def backward(shards, *args):
    t = args[0].shape[0]
    rows = D // (2 * shards)
    out = [
        ((t, D // TP), bf16),
        ((t, CA), bf16),
        ((rows, CB), f32),
        ((8, CH + WI + 128), f32),
    ]
    dma = pltpu.SemaphoreType.DMA
    vmem = pl.BlockSpec(memory_space=pltpu.VMEM)
    return pl.pallas_call(
        functools.partial(backward_kernel, shards),
        out_shape=[jax.ShapeDtypeStruct(*o) for o in out],
        in_specs=[vmem] * (len(args) - 1) + [pl.BlockSpec(memory_space=pltpu.SMEM)],
        out_specs=[vmem] * len(out),
        scratch_shapes=[
            pltpu.VMEM((TP, t, D // TP), bf16),
            pltpu.VMEM((TP, 8, t), f32),
            pltpu.VMEM((2, t, 128), f32),
            pltpu.VMEM((2, t, 128), f32),
            pltpu.VMEM((t, WI), f32),
            pltpu.VMEM((t + 8, CH), f32),
            pltpu.VMEM((t // L, N, WI), f32),
            pltpu.VMEM((N, WI), f32),
            pltpu.VMEM((N, WI), f32),
            pltpu.VMEM((t, 128), bf16),
            pltpu.VMEM((t, 128), bf16),
            pltpu.VMEM((t + 8, CH), f32),
            pltpu.VMEM((8, CH), f32),
            pltpu.VMEM((8, CH), f32),
        ]
        + Scatter.scratch(shards, D, CB)
        + [dma((3,)), dma((3,))]
        + [dma((TP,))] * 4,
        compiler_params=pltpu.CompilerParams(
            collective_id=3, has_side_effects=True, vmem_limit_bytes=VLIMIT
        ),
        name="mix_backward",
    )(*args)


def finish_kernel(
    shards,
    lin, normed, wf1, wf2, hid, grad_own, gains, gain_two, vec,
    low, grad_a, shared, vecs,
    gsend, grecv, gown, back, gain_one, grads, misc, misc_low, misc_sum, shsend, vec_sib, vec_z,
    sib, stage, land, csend, crecv, zsend, zrecv,
    sib2, stage2, land2, csend2, crecv2, zsend2, zrecv2,
    vcs, vcr, vzs, vzr, gs, gr, hs, hr, ss, sr, vts, vtr,
):
    tp = lax.axis_index("tp")
    t = lin.shape[0]
    blocks, sub = t // L, L // TP
    greet(shards, True)
    scatter = Scatter(shards, grads, sib, stage, land, csend, crecv, zsend, zrecv)
    small = Scatter(shards, misc_low, sib2, stage2, land2, csend2, crecv2, zsend2, zrecv2)
    z, c = lax.axis_index("shard"), lax.axis_index("ctx")
    vec_core = remote(vec, vec_sib, vcs.at[0], vcr.at[0], ctx=1 - c)
    vec_core.start()

    def vec_to_shard(k):
        zz = lax.rem(z + k, shards)
        return remote(vec_z.at[z], vec_z.at[z], vzs.at[zz], vzr.at[z], shard=zz)

    def vec_from_shard(k):
        zz = lax.rem(z + k, shards)
        return remote(vec_z.at[z], vec_z.at[zz], vzs.at[zz], vzr.at[zz], shard=zz)

    def vec_to(d):
        return remote(vecs.at[tp], vecs.at[tp], vts.at[d], vtr.at[tp], tp=peer(d))

    def vec_from(d):
        return remote(vecs.at[tp], vecs.at[peer(d)], vts.at[d], vtr.at[peer(d)], tp=peer(d))

    def peer(d):
        return lax.rem(tp + d, TP)

    def part(b, owner):
        return pl.ds(pl.multiple_of(b * L + owner * sub, sub), sub)

    def kept(b):
        return rows_of(b, sub)

    def grad_to(b, d):
        return remote(gsend.at[d, b], grecv.at[tp, b], gs.at[d, b], gr.at[tp, b], tp=peer(d))

    def grad_from(b, d):
        return remote(
            gsend.at[d, b], grecv.at[peer(d), b], gs.at[d, b], gr.at[peer(d), b], tp=peer(d)
        )

    def product(b):
        rows = rows_of(b)
        back[...] = nt(lin[rows, CZ:CQ], wf2[...]) + nt(lin[rows, CQ:CA], wf1[...])
        gown[kept(b), :] = back[kept(tp), :]
        for d in range(1, TP):
            gsend[d, b] = back[kept(peer(d)), :].astype(bf16)
            grad_to(b, d).start()

    loop(blocks, product)
    vec_core.wait_recv()
    vec_z[z] = vec[...] + vec_sib[...]
    loop(shards - 1, lambda k: vec_to_shard(k + 1).start())

    def weight_grads(i):
        feats = rows_of(i)
        both = tn(normed[:, feats], lin[...])
        grads[feats, :] = both[:, :CS].astype(bf16)
        misc[feats, :] = both[:, CS:]

    loop(D // L, weight_grads)
    scatter.start()
    scatter.middle()
    loop(shards - 1, lambda k: vec_from_shard(k + 1).wait_recv())
    vecs[tp] = lax.fori_loop(1, shards, lambda k, total: total + vec_z[k], vec_z[0])
    for d in range(1, TP):
        vec_to(d).start()
    gain_one[...] = jnp.zeros_like(gain_one)

    def low_to(b, d):
        there = low.at[part(b, tp)]
        return remote(there, there, hs.at[d, b], hr.at[tp, b], tp=peer(d))

    def low_from(b, d):
        there = low.at[part(b, peer(d))]
        return remote(there, there, hs.at[d, b], hr.at[peer(d), b], tp=peer(d))

    def norm_back(b):
        own = part(b, tp)
        g = gown[kept(b), :]
        for d in range(1, TP):
            grad_from(b, d).wait_recv()
            g = g + grecv[peer(d), b].astype(f32)
        x = hid[own, :].astype(f32)
        scale = lax.rsqrt(jnp.mean(x * x, -1, keepdims=True) + EPS)
        unit = x * scale
        gain_one[...] += jnp.broadcast_to(jnp.sum(g * unit, 0, keepdims=True), (8, D))
        weighted = g * gains[0:1, :]
        mean = jnp.mean(weighted * unit, -1, keepdims=True)
        low[own, :] = (grad_own[kept(b), :] + scale * (weighted - unit * mean)).astype(bf16)
        for d in range(1, TP):
            low_to(b, d).start()

    loop(blocks, norm_back)
    gain_rows = jnp.where(iota((8, D), 0) == 0, gain_one[...], gain_two[...])
    row, lane = iota((8, 128), 0), iota((8, 128), 1)
    pick = ((row < 2) & (lane == GAIN_COL + row)).astype(f32)
    misc_low[...] = (misc[...] + tn(gain_rows, pick, HI)).astype(bf16)
    small.start()
    small.middle()
    scatter.finish(grad_a)
    small.finish(misc_sum)
    few = grad_a.shape[0] // TP
    for i in range(TP):
        shsend[i, :, 0:256] = grad_a[i * few : (i + 1) * few, CM:CQ]
        shsend[i, :, 256:384] = grad_a[i * few : (i + 1) * few, CK:CS]
        shsend[i, :, 384:512] = misc_sum[i * few : (i + 1) * few, :]

    def share_to(d):
        return remote(shsend.at[peer(d)], shared.at[tp], ss.at[d], sr.at[tp], tp=peer(d))

    def share_from(d):
        return remote(shsend.at[peer(d)], shared.at[peer(d)], ss.at[d], sr.at[peer(d)], tp=peer(d))

    for d in range(1, TP):
        share_to(d).start()
    shared[tp] = shsend[tp]

    def arrived(b):
        for d in range(1, TP):
            low_from(b, d).wait_recv()
            low_to(b, d).wait_send()
            grad_to(b, d).wait_send()

    loop(blocks, arrived)
    for d in range(1, TP):
        share_from(d).wait_recv()
        vec_from(d).wait_recv()
    vec_core.wait_send()
    loop(shards - 1, lambda k: vec_to_shard(k + 1).wait_send())
    for d in range(1, TP):
        share_to(d).wait_send()
        vec_to(d).wait_send()


def finish(shards, *args):
    t = args[0].shape[0]
    rows = D // (2 * shards)
    blocks, sub = t // L, L // TP
    vec = args[-1].shape
    out = [
        ((t, D), bf16),
        ((rows, CS), f32),
        ((TP, rows // TP, 512), f32),
        ((TP, *vec), f32),
    ]
    dma = pltpu.SemaphoreType.DMA
    vmem = pl.BlockSpec(memory_space=pltpu.VMEM)
    return pl.pallas_call(
        functools.partial(finish_kernel, shards),
        out_shape=[jax.ShapeDtypeStruct(*o) for o in out],
        in_specs=[vmem] * len(args),
        out_specs=[vmem] * len(out),
        scratch_shapes=[
            pltpu.VMEM((TP, blocks, sub, D), bf16),
            pltpu.VMEM((TP, blocks, sub, D), bf16),
            pltpu.VMEM((blocks * sub, D), f32),
            pltpu.VMEM((L, D), f32),
            pltpu.VMEM((8, D), f32),
            pltpu.VMEM((D, CS), bf16),
            pltpu.VMEM((D, 128), f32),
            pltpu.VMEM((D, 128), bf16),
            pltpu.VMEM((rows, 128), f32),
            pltpu.VMEM((TP, rows // TP, 512), f32),
            pltpu.VMEM(vec, f32),
            pltpu.VMEM((shards, *vec), f32),
        ]
        + Scatter.scratch(shards, D, CS)
        + Scatter.scratch(shards, D, 128)
        + [dma((1,)), dma((1,)), dma((shards,)), dma((shards,))]
        + [dma((TP, blocks))] * 4
        + [dma((TP,))] * 4,
        compiler_params=pltpu.CompilerParams(
            collective_id=4, has_side_effects=True, vmem_limit_bytes=VLIMIT
        ),
        name="project_backward",
    )(*args)


def pack_kernel(
    low, grad_a, grad_b, shared, vecs,
    grad_hidden, g_z, g_x, g_q, g_gate, g_up, g_out, g_o, g_down, g_shared, g_dt, gains,
    g_conv, g_chan, g_heads,
):
    grad_hidden[...] = low[...].astype(f32)

    @pl.when(pl.program_id(0) == 0)
    def rest():
        g_z[...] = grad_a[:, CZ:CX]
        g_x[...] = grad_a[:, CX:CM]
        g_q[...] = grad_a[:, CQ:CK]
        g_gate[...] = grad_b[:, CG:CU]
        g_up[...] = grad_b[:, CU:CD]
        one = eye(grad_b.shape[0]).astype(f32)
        g_out[...] = tn(grad_b[:, CO:CW], one, HI)
        g_o[...] = tn(grad_b[:, CW:CG], one, HI)
        g_down[...] = tn(grad_b[:, CD:CB], one, HI)
        first, second = shared[0] + shared[1], shared[2] + shared[3]
        both = first + second
        g_shared[:, 0 : 2 * N] = both[:, 0 : 2 * N]
        kv1, kv2 = first[:, 256:384], second[:, 256:384]
        low_half = low_lanes(kv1.shape)
        g_shared[:, 2 * N : 2 * N + 128] = jnp.where(low_half, kv1, pltpu.roll(kv2, 64, 1))
        g_shared[:, 2 * N + 128 :] = jnp.where(low_half, pltpu.roll(kv1, 64, 1), kv2)
        gains[...] = tn(both[:, 384:512], eye(both.shape[0]).astype(f32), HI)[
            GAIN_COL : GAIN_COL + 8
        ]
        steps = jnp.zeros((both.shape[0], 128), f32)
        heads = jnp.zeros((8, 128), f32)
        g_chan[...] = jnp.zeros_like(g_chan)
        for i in range(TP):
            lane = iota(steps.shape, 1) // HL == i
            steps = jnp.where(lane, pltpu.roll(shared[i, :, 384:512], i * HL, 1), steps)
            lane = iota(heads.shape, 1) // HL == i
            heads = jnp.where(lane, pltpu.roll(vecs[i, :, CH + WI : CH + WI + 128], i * HL, 1), heads)
            mine = slice(i * WI, (i + 1) * WI)
            g_conv[:, mine] = vecs[i, 0:CONVW, 0:WI]
            g_chan[0:1, mine] = vecs[i, CONVW : CONVW + 1, 0:WI]
            g_chan[1:2, mine] = vecs[i, 0:1, CH : CH + WI]
        maps = vecs[0, :, WI:CH] + vecs[1, :, WI:CH] + vecs[2, :, WI:CH] + vecs[3, :, WI:CH]
        g_conv[:, DI:] = maps[0:CONVW]
        g_chan[0:1, DI:] = maps[CONVW : CONVW + 1]
        g_dt[...] = steps[:, 0:H]
        g_heads[...] = heads


def pack(low, grad_a, grad_b, shared, vecs):
    t, r, few = low.shape[0], grad_a.shape[0], shared.shape[1]
    out = [
        (t, D), (r, WI), (r, WI), (r, 128), (r, FFL), (r, FFL), (WI, r), (128, r), (FFL, r),
        (few, 512), (few, H), (8, few), (CONVW, DI + 2 * N), (8, DI + 2 * N), (8, 128),
    ]
    rows = pl.BlockSpec((L, D), lambda i: (i, 0))

    def whole(shape):
        return pl.BlockSpec(shape, lambda i: (0,) * len(shape))

    return pl.pallas_call(
        pack_kernel,
        grid=(t // L,),
        out_shape=[jax.ShapeDtypeStruct(o, f32) for o in out],
        in_specs=[rows] + [whole(v.shape) for v in (grad_a, grad_b, shared, vecs)],
        out_specs=[rows] + [whole(o) for o in out[1:]],
        compiler_params=pltpu.CompilerParams(vmem_limit_bytes=VLIMIT),
        name="lay_out",
    )(low, grad_a, grad_b, shared, vecs)


def rotary_table(count):
    inverse = rope_base ** (-2.0 * np.arange(HD // 2, dtype=np.float32) / HD)
    angles = np.arange(count, dtype=np.float32)[:, None] * inverse.astype(np.float32)[None, :]
    both = np.concatenate([np.cos(angles), np.sin(angles)], axis=1)
    return np.tile(both, (1, 2)).astype(np.float32)


def local(
    hidden, cotangent, lengths, norm1_gain, w_z, w_x, w_shared, w_dt, dt_bias, a_log, d_skip,
    conv_w, conv_b, gated_gain, w_out, w_q, w_o, norm2_gain, w_gate, w_up, w_down,
):
    t = hidden.shape[1]
    shards = lax.axis_size("shard")
    hid, cot = hidden[0], cotangent[0]
    width = conv_w.shape[1]

    def fit(v):
        return jnp.pad(v, (0, width - v.shape[0]))[None]

    nothing = jnp.zeros((2, width), bf16)
    small = jnp.concatenate(
        [conv_w, conv_b[None], fit(gated_gain), nothing]
        + [fit(v) for v in (dt_bias, a_log, d_skip)]
        + [nothing, nothing, nothing[:1]],
        axis=0,
    )
    table = jnp.asarray(rotary_table(lax.axis_size("ctx") * t))
    (
        wf1, wf2, wo, wg, normed, gains, z, cin, dt, taps, prm, chan,
        pre, hist, q_low, kk, vv, att, att_low, lse_row, ssd, start, steps, cum, tot, gl, square,
    ) = forward(
        shards, hid, w_z, w_x, w_shared, w_dt.T, w_q, w_out, w_o, w_gate,
        norm1_gain[None], norm2_gain[None], small, table, lengths,
    )
    osend, out_own, grad_own, grads, gain_two, total_square, ggl, grad_att, dots = ffn(
        shards, hid, cot, gl, att_low, square, wo, wg, w_up, w_down, gains, lengths
    )
    output, lin, grad_b, vec = backward(
        shards, ggl, grad_att, dots, total_square, grads, osend, out_own, pre, cin, hist, q_low, kk, vv, att,
        lse_row, ssd, start, steps, cum, tot, dt, z, table, taps, prm, chan, lengths,
    )
    grad_hidden, grad_a, shared, vecs = finish(
        shards, lin, normed, wf1, wf2, hid, grad_own, gains, gain_two, vec
    )

    (
        grad_full, g_z, g_x, g_q, g_gate, g_up, g_out, g_o, g_down, g_shared, g_dt, g_gains,
        g_conv, g_chan, g_heads,
    ) = pack(grad_hidden, grad_a, grad_b, shared, vecs)
    return (
        output[None],
        grad_full[None],
        g_gains[0],
        g_z,
        g_x,
        g_shared,
        g_dt,
        g_heads[0, :H],
        g_heads[1, :H],
        g_heads[2, :H],
        g_conv,
        g_chan[0],
        g_chan[1, :DI],
        g_out,
        g_q,
        g_o,
        g_gains[1],
        g_gate,
        g_up,
        g_down,
    )


def solution(mesh):
    placed = (
        P("shard", "ctx", None),
        P("shard", "ctx", None),
        P("shard"),
        P(("shard", "ctx")),
        P(("shard", "ctx"), "tp"),
        P(("shard", "ctx"), "tp"),
        P(("shard", "ctx"), None),
        P(("shard", "ctx"), None),
        P(),
        P(),
        P(),
        P(),
        P(),
        P(),
        P("tp", ("shard", "ctx")),
        P(("shard", "ctx"), "tp"),
        P("tp", ("shard", "ctx")),
        P(("shard", "ctx")),
        P(("shard", "ctx"), "tp"),
        P(("shard", "ctx"), "tp"),
        P("tp", ("shard", "ctx")),
    )
    return jax.shard_map(
        local,
        mesh=mesh,
        in_specs=placed,
        out_specs=(
            P("shard", "ctx", "tp"),
            P("shard", "ctx", None),
            P(("shard", "ctx", "tp")),
            P(("shard", "ctx"), "tp"),
            P(("shard", "ctx"), "tp"),
            P(("shard", "ctx", "tp"), None),
            P(("shard", "ctx", "tp"), None),
            P(),
            P(),
            P(),
            P(),
            P(),
            P(),
            P("tp", ("shard", "ctx")),
            P(("shard", "ctx"), "tp"),
            P("tp", ("shard", "ctx")),
            P(("shard", "ctx", "tp")),
            P(("shard", "ctx"), "tp"),
            P(("shard", "ctx"), "tp"),
            P("tp", ("shard", "ctx")),
        ),
        check_vma=False,
    )
```

```python
import functools

import jax
import jax.numpy as jnp
import numpy as np
from jax import lax
from jax.experimental import pallas as pl
from jax.experimental.pallas import tpu as pltpu
from jax.sharding import PartitionSpec as P

H = 24
P_SIZE = 64
N = 128
NQ = 8
KV = 2
HD = 64
CONVW = 4
DI = 1536
D = 1024
FFL = 512
TP = 4
HL = H // TP
WI = HL * P_SIZE
CH = WI + 2 * N
L = 256

CZ, CX, CM, CQ, CK, CS, CA = 0, 384, 768, 1024, 1152, 1280, 1408
GAIN_COL = 24
CO, CW, CG, CU, CD, CB = 0, 384, 512, 1024, 1536, 2048

EPS = 1e-05
rope_base = 10000.0
FILL = -1e30
HI = lax.Precision.HIGHEST
MESH = pl.DeviceIdType.MESH
f32 = jnp.float32
bf16 = jnp.bfloat16
VLIMIT = 60 * 1024 * 1024
VMOST = 63 * 1024 * 1024 + 512 * 1024


def nn(a, b, precision=None):
    return lax.dot_general(
        a, b, (((1,), (0,)), ((), ())), precision=precision, preferred_element_type=f32
    )


def nt(a, b, precision=None):
    return lax.dot_general(
        a, b, (((1,), (1,)), ((), ())), precision=precision, preferred_element_type=f32
    )


def tn(a, b, precision=None):
    return lax.dot_general(
        a, b, (((0,), (0,)), ((), ())), precision=precision, preferred_element_type=f32
    )


def rows_of(index, size=L):
    return pl.ds(pl.multiple_of(index * size, size), size)


def remote(src, dst, send, recv, **where):
    return pltpu.make_async_remote_copy(
        src_ref=src,
        dst_ref=dst,
        send_sem=send,
        recv_sem=recv,
        device_id=where,
        device_id_type=MESH,
    )


def iota(shape, dim):
    return lax.broadcasted_iota(jnp.int32, shape, dim)


def loop(n, body):
    lax.fori_loop(0, n, lambda i, c: (body(i), c)[1], 0)


def greet(shards, tp_too, ctx_too=True, shard_too=True):
    barrier = pltpu.get_barrier_semaphore()
    count = 0
    z, c, t = lax.axis_index("shard"), lax.axis_index("ctx"), lax.axis_index("tp")
    if ctx_too:
        pl.semaphore_signal(barrier, inc=1, device_id={"ctx": 1 - c}, device_id_type=MESH)
        count += 1
    if shard_too:

        def one(k):
            pl.semaphore_signal(
                barrier, inc=1, device_id={"shard": lax.rem(z + 1 + k, shards)}, device_id_type=MESH
            )

        loop(shards - 1, one)
        count += shards - 1
    if tp_too:
        for d in range(1, TP):
            pl.semaphore_signal(
                barrier, inc=1, device_id={"tp": lax.rem(t + d, TP)}, device_id_type=MESH
            )
            count += 1
    pl.semaphore_wait(barrier, count)


class Gather:
    def __init__(self, shards, src, dst, zsend, csend, recv, own):
        self.s, self.src, self.dst = shards, src, dst
        self.zsend, self.csend, self.recv, self.own = zsend, csend, recv, own
        self.z, self.c = lax.axis_index("shard"), lax.axis_index("ctx")
        self.r = src.shape[0]

    def block(self, g):
        return self.dst.at[rows_of(g, self.r)]

    def to_shard(self, k):
        g = 2 * self.z + self.c
        return remote(
            self.src,
            self.block(g),
            self.zsend.at[k],
            self.recv.at[g],
            shard=lax.rem(self.z + k, self.s),
        )

    def to_core(self, k):
        zz = lax.rem(self.z + k, self.s)
        g = 2 * zz + self.c
        return remote(self.block(g), self.block(g), self.csend.at[k], self.recv.at[g], ctx=1 - self.c)

    def got(self, k, core):
        zz = lax.rem(self.z + k, self.s)
        g = 2 * zz + core
        return remote(self.block(g), self.block(g), self.csend.at[k], self.recv.at[g], ctx=1 - self.c)

    def start(self):
        keep = pltpu.make_async_copy(self.src, self.block(2 * self.z + self.c), self.own)
        keep.start()
        loop(self.s - 1, lambda k: self.to_shard(k + 1).start())
        keep.wait()
        self.to_core(0).start()

    def forward(self, first=0, last=None):
        def one(k):
            self.got(k + 1, self.c).wait_recv()
            self.to_core(k + 1).start()

        lax.fori_loop(
            first, self.s - 1 if last is None else last, lambda k, carry: (one(k), carry)[1], 0
        )

    def finish(self):
        loop(self.s, lambda k: self.got(k, 1 - self.c).wait_recv())
        loop(self.s, lambda k: self.to_core(k).wait_send())
        loop(self.s - 1, lambda k: self.to_shard(k + 1).wait_send())

    @staticmethod
    def sems(shards):
        dma = pltpu.SemaphoreType.DMA
        return [dma((shards,)), dma((shards,)), dma((2 * shards,)), dma(())]


class Scatter:
    def __init__(self, shards, src, sib, land, csend, crecv, zsend, zrecv):
        self.s, self.src, self.sib, self.land = shards, src, sib, land
        self.csend, self.crecv, self.zsend, self.zrecv = csend, crecv, zsend, zrecv
        self.z, self.c = lax.axis_index("shard"), lax.axis_index("ctx")
        self.r = src.shape[0] // (2 * shards)

    def to_core(self, k):
        zz = lax.rem(self.z + k, self.s)
        return remote(
            self.src.at[rows_of(2 * zz + 1 - self.c, self.r)],
            self.sib.at[zz],
            self.csend.at[zz],
            self.crecv.at[zz],
            ctx=1 - self.c,
        )

    def to_shard(self, k):
        zz = lax.rem(self.z + k, self.s)
        return remote(
            self.sib.at[zz], self.land.at[self.z], self.zsend.at[zz], self.zrecv.at[self.z], shard=zz
        )

    def arrive(self, k):
        zz = lax.rem(self.z + k, self.s)
        return remote(
            self.sib.at[zz], self.land.at[zz], self.zsend.at[zz], self.zrecv.at[zz], shard=zz
        )

    def start(self):
        loop(self.s - 1, lambda k: self.to_core(k + 1).start())
        self.to_core(0).start()

    def middle(self):
        def one(k):
            zz = lax.rem(self.z + 1 + k, self.s)
            self.to_core(k + 1).wait_recv()
            both = self.src[rows_of(2 * zz + self.c, self.r), :].astype(f32)
            self.sib[zz] = (both + self.sib[zz].astype(f32)).astype(bf16)
            self.to_shard(k + 1).start()

        loop(self.s - 1, one)

    def finish(self, out, cols=None):
        self.to_core(0).wait_recv()
        own = self.src[rows_of(2 * self.z + self.c, self.r), :].astype(f32)
        out[...] = own + self.sib[self.z].astype(f32)

        def one(k):
            zz = lax.rem(self.z + 1 + k, self.s)
            self.arrive(k + 1).wait_recv()
            out[...] += self.land[zz].astype(f32)

        loop(self.s - 1, one)
        loop(self.s, lambda k: self.to_core(k).wait_send())
        loop(self.s - 1, lambda k: self.to_shard(k + 1).wait_send())

    @staticmethod
    def scratch(shards, rows, cols):
        dma = pltpu.SemaphoreType.DMA
        block = pltpu.VMEM((shards, rows // (2 * shards), cols), bf16)
        return [block, block] + [dma((shards,))] * 4


class ChipSum:
    def __init__(self, shards, src, sib, cols, csend, crecv):
        self.s, self.src, self.sib, self.cols = shards, src, sib, cols
        self.csend, self.crecv = csend, crecv
        self.c = lax.axis_index("ctx")
        self.r = src.shape[0] // (2 * shards)

    def to_core(self, k):
        return remote(
            self.src.at[rows_of(2 * k + 1 - self.c, self.r), self.cols],
            self.sib.at[k, :, self.cols],
            self.csend.at[k],
            self.crecv.at[k],
            ctx=1 - self.c,
        )

    def start(self):
        loop(self.s, lambda k: self.to_core(k).start())

    def finish(self):
        def one(k):
            self.to_core(k).wait_recv()
            own = self.src[rows_of(2 * k + self.c, self.r), self.cols].astype(f32)
            self.sib[k, :, self.cols] = (own + self.sib[k, :, self.cols].astype(f32)).astype(bf16)

        loop(self.s, one)
        loop(self.s, lambda k: self.to_core(k).wait_send())


class ShardSum:
    def __init__(self, shards, src, land, zsend, zrecv):
        self.s, self.src, self.land, self.zsend, self.zrecv = shards, src, land, zsend, zrecv
        self.z = lax.axis_index("shard")

    def to_shard(self, k):
        zz = lax.rem(self.z + k, self.s)
        return remote(
            self.src.at[zz], self.land.at[self.z], self.zsend.at[zz], self.zrecv.at[self.z], shard=zz
        )

    def arrive(self, k):
        zz = lax.rem(self.z + k, self.s)
        return remote(
            self.src.at[zz], self.land.at[zz], self.zsend.at[zz], self.zrecv.at[zz], shard=zz
        )

    def start(self):
        loop(self.s - 1, lambda k: self.to_shard(k + 1).start())

    def finish(self, out):
        out[...] = self.src[self.z].astype(f32)

        def one(k):
            zz = lax.rem(self.z + 1 + k, self.s)
            self.arrive(k + 1).wait_recv()
            out[...] += self.land[zz].astype(f32)

        loop(self.s - 1, one)
        loop(self.s - 1, lambda k: self.to_shard(k + 1).wait_send())


def sigmoid(v):
    return 1.0 / (1.0 + jnp.exp(-v))


def softplus(v):
    return jnp.maximum(v, 0.0) + jnp.log1p(jnp.exp(-jnp.abs(v)))


def swap_half(v):
    width = v.shape[1]
    low = iota(v.shape, 1) % HD < HD // 2
    return jnp.where(low, pltpu.roll(v, width - HD // 2, 1), pltpu.roll(v, HD // 2, 1))


def low_lanes(shape):
    return iota(shape, 1) < 64


def spread():
    return (iota((N, WI), 1) // P_SIZE == iota((N, WI), 0)).astype(f32)


def first_row():
    return (iota((8, N), 0) == 0).astype(f32)


def wide(column, width):
    return jnp.concatenate([column] * (width // column.shape[1]), axis=1)


def lower_ones():
    return (iota((L, L), 0) >= iota((L, L), 1)).astype(f32)


def head_scalars(dt_raw, prm):
    real = iota(dt_raw.shape, 1) < HL
    steps = jnp.where(real, softplus(dt_raw + prm[0:1, :]), 0.0)
    rates = steps * prm[1:2, :]
    return steps, rates


def pair_columns(v, pair):
    return v[:, 128 * pair : 128 * pair + 128]


def own_half(v, half):
    return jnp.where(low_lanes(v.shape) == (half == 0), v, jnp.zeros_like(v))


def eye(n):
    return (iota((n, n), 0) == iota((n, n), 1)).astype(bf16)


def rotary_of(table, rows):
    both = table[rows, :]
    first = iota(both.shape, 1) % HD < HD // 2
    cosine = jnp.where(first, both, pltpu.roll(both, HD // 2, 1))
    sine = jnp.where(first, -pltpu.roll(both, 128 - HD // 2, 1), both)
    return cosine, sine


def forward_kernel(
    shards,
    hid, w_z, w_x, w_shared, w_dt, w_q, w_out, w_o, w_gate, gain_one, gain_two,
    small, table, length,
    wf1, wf2, wo, wg, normed, gains, z_out, cin, dt_raw, taps, prm, chan,
    pre, hist, q_low, kk, vv, att, att_low, lse_row, ssd, start, steps_out, cum_out, tot_out,
    gated_low, square,
    wa1, wa2, wa3, stat, zf, pad, act, state, carried, scores_m, scores_l, hist_in,
    zs1, cs1, zr1, own1, zs2, cs2, zr2, own2, zs3, cs3, zr3, own3, zs4, cs4, zr4, own4,
    xs, xr,
):
    c, tp = lax.axis_index("ctx"), lax.axis_index("tp")
    t = hid.shape[0]
    blocks = t // L
    r = w_z.shape[0]

    kv = tp * (NQ // TP) // (NQ // KV)
    keys = w_shared[:, 2 * N : 2 * N + 128].astype(f32)
    vals = w_shared[:, 2 * N + 128 : 2 * N + 256].astype(f32)
    low_r = low_lanes((r, 128))
    other = pltpu.roll(jnp.where(kv == 0, vals, keys), 64, 1)
    wa1[:, 0:128] = w_q[...]
    wa1[:, 128:256] = jnp.where(
        kv == 0, jnp.where(low_r, keys, other), jnp.where(low_r, other, vals)
    ).astype(bf16)
    head_pick = (
        (iota((H, 128), 0) == iota((H, 128), 1) + tp * HL) & (iota((H, 128), 1) < HL)
    ).astype(bf16)
    row8, lane8 = iota((8, 128), 0), iota((8, 128), 1)
    gain_pick = ((row8 < 2) & (lane8 == GAIN_COL + row8)).astype(bf16)
    gain_rows = jnp.where(
        iota((8, r), 0) == 0, gain_one[...].astype(f32), gain_two[...].astype(f32)
    ).astype(bf16)
    wa1[:, 256:384] = (tn(w_dt[...], head_pick) + tn(gain_rows, gain_pick)).astype(bf16)
    wa2[:, 0:WI] = w_z[...]
    wa2[:, WI : 2 * WI] = w_x[...]
    wa2[:, 2 * WI : 2 * WI + 2 * N] = w_shared[:, 0 : 2 * N]
    greet(shards, False)
    gather1 = Gather(shards, wa1, wf1, zs1, cs1, zr1, own1)
    gather2 = Gather(shards, wa2, wf2, zs2, cs2, zr2, own2)
    gather3 = Gather(shards, wa3, wo, zs3, cs3, zr3, own3)
    gather4 = Gather(shards, w_gate, wg, zs4, cs4, zr4, own4)
    gather1.start()
    gather2.start()
    wa3[:, CO:CW] = nt(eye(r), w_out[...]).astype(bf16)
    wa3[:, CW:CG] = nt(eye(r), w_o[...]).astype(bf16)

    expand = spread()
    mine = pl.ds(pl.multiple_of(tp * WI, 128), WI)
    taps[0:CONVW, 0:WI] = small[0:CONVW, mine].astype(f32)
    taps[0:CONVW, WI:CH] = small[0:CONVW, DI:].astype(f32)
    taps[CONVW : CONVW + 1, 0:WI] = small[CONVW : CONVW + 1, mine].astype(f32)
    taps[CONVW : CONVW + 1, WI:CH] = small[CONVW : CONVW + 1, DI:].astype(f32)
    taps[CONVW + 1 :, :] = jnp.zeros((8 - CONVW - 1, CH), f32)
    heads = pltpu.roll(small[8:16, 0:128].astype(f32), lax.rem(128 - tp * HL, 128), 1)
    heads = jnp.where(lane8 < HL, jnp.where(row8 == 1, -jnp.exp(heads), heads), 0.0)
    prm[...] = heads
    chan[...] = jnp.zeros_like(chan)
    chan[0:1, :] = small[CONVW + 1 : CONVW + 2, mine].astype(f32)
    chan[1:2, :] = nn(heads, expand, HI)[2:3, :]

    def swap(src, dst, i):
        return remote(src, dst, xs.at[i], xr.at[i], ctx=1 - c)

    def row_scale(i):
        rows = rows_of(i)
        x = hid[rows, :].astype(f32)
        scale = lax.rsqrt(jnp.mean(x * x, -1, keepdims=True) + EPS)
        stat[rows, :] = jnp.broadcast_to(scale, (L, 128))

    loop(blocks, row_scale)
    gather1.forward()
    gather1.finish()
    turned = wf1[:, 256:384].astype(f32).T
    gains[...] = turned[GAIN_COL : GAIN_COL + 8]
    gain = gains[0:1, :]
    low128 = low_lanes((L, 128))

    def first_projections(i):
        rows = rows_of(i)
        low = (hid[rows, :].astype(f32) * wide(stat[rows, :], D) * gain).astype(bf16)
        normed[rows, :] = low
        rest = nn(low, wf1[...])
        cosine, sine = rotary_of(table, pl.ds(pl.multiple_of(c * t + i * L, L), L))
        v = rest[:, 0:128]
        q_low[rows, :] = (v * cosine + swap_half(v) * sine).astype(bf16)
        v = rest[:, 128:256]
        other = pltpu.roll(v, 64, 1)
        twice = jnp.where(low128, v, other)
        kk[0, rows, :] = (twice * cosine + swap_half(twice) * sine).astype(bf16)
        vv[0, rows, :] = jnp.where(low128, other, v).astype(bf16)
        dt_raw[rows, :] = rest[:, 256:384]

    loop(blocks, first_projections)
    keys = swap(kk.at[0], kk.at[1], 1)
    keys.start()
    vals = swap(vv.at[0], vv.at[1], 2)
    vals.start()

    scale = HD ** (-0.5)
    limit = length[0] - c * t

    def stacked(v):
        return jnp.concatenate([own_half(v, 0), own_half(v, 1)], axis=0)

    for i in range(blocks):
        rows = pl.ds(i * L, L)
        width = (i + 1) * L
        q2 = stacked(q_low[rows, :].astype(f32)).astype(bf16)
        s = nt(q2, kk[0, 0:width, :]) * scale
        at = iota(s.shape, 0) % L + i * L
        col = iota(s.shape, 1)
        s = jnp.where((col <= at) & (col < limit), s, FILL)
        peak = jnp.max(s, -1, keepdims=True)
        e = jnp.exp(s - peak)
        total = jnp.sum(e, -1, keepdims=True)
        o = nn(e.astype(bf16), vv[0, 0:width, :])
        scores_m[...] = jnp.broadcast_to(peak, (2 * L, 128))
        scores_l[0] = jnp.broadcast_to(total, (2 * L, 128))
        scores_l[1] = o
        if i == 0:
            keys.wait_recv()
            vals.wait_recv()

        @pl.when(c > 0)
        def earlier():
            s2 = nt(q2, kk[1]) * scale
            old = scores_m[:, 0:1]
            new = jnp.maximum(old, jnp.max(s2, -1, keepdims=True))
            e2 = jnp.exp(s2 - new)
            fade = jnp.exp(old - new)
            scores_m[...] = jnp.broadcast_to(new, (2 * L, 128))
            scores_l[0] = fade * scores_l[0] + jnp.sum(e2, -1, keepdims=True)
            scores_l[1] = fade * scores_l[1] + nn(e2.astype(bf16), vv[1])

        total = scores_l[0]
        o = scores_l[1] / total
        o = jnp.where(low128, o[:L], o[L:])
        att[rows, :] = o
        att_low[rows, :] = o.astype(bf16)
        logs = scores_m[...] + jnp.log(total)
        turned = jnp.where(low128, logs[:L], logs[L:]).T
        lse_row[0:1, rows] = turned[0:1]
        lse_row[1:2, rows] = turned[64:65]
        lse_row[2:8, rows] = jnp.zeros((6, L), f32)
        if i == blocks - 2:
            gather2.forward(0, 1)
    gather2.forward(1)
    gather3.start()
    gather4.start()
    gather2.finish()

    def conv_input(k):
        i = blocks - 1 - k
        rows = rows_of(i)
        v = nn(normed[rows, :], wf2[:, WI:]).astype(bf16)
        cin[rows, :] = v
        pad[pl.ds(pl.multiple_of(i * L + 8, 8), L), :] = v.astype(f32)

    conv_input(0)
    tail = swap(cin.at[pl.ds(t - 16, 16)], hist_in, 0)
    tail.start()
    lax.fori_loop(1, blocks, lambda k, carry: (conv_input(k), carry)[1], 0)
    tail.wait_recv()
    before = hist_in[8:16, :].astype(f32)
    hist[...] = jnp.where((iota((8, CH), 0) >= 5) & (c > 0), before, 0.0)
    pad[0:8, :] = hist[...]
    ones = lower_ones()
    state[...] = jnp.zeros_like(state)

    for i in range(blocks):
        rows = pl.ds(i * L, L)
        v = taps[4:5, :] + taps[0:1, :] * pad[pl.ds(i * L + 5, L), :]
        for j in range(1, CONVW):
            v = v + taps[j : j + 1, :] * pad[pl.ds(i * L + 5 + j, L), :]
        pre[rows, :] = v.astype(bf16)
        a = v * sigmoid(v)
        act[rows, :] = a
        steps, rates = head_scalars(dt_raw[rows, :], prm)
        cum = nn(ones, rates, HI)
        tot = cum[L - 1 : L, :]
        steps_out[rows, :] = steps
        cum_out[rows, :] = cum
        tot_out[i] = jnp.broadcast_to(tot, (8, 128))
        weight = nn(jnp.exp(tot - cum) * steps, expand, HI)
        start[i] = state[...]
        add = tn(a[:, WI : WI + N].astype(bf16), (weight * a[:, :WI]).astype(bf16))
        decay = nn(jnp.broadcast_to(jnp.exp(tot), (8, 128)), expand, HI)[0:1, :]
        state[...] = decay * state[...] + add

    states = swap(state, carried, 3)
    states.start()
    gather3.forward()

    def gate_input(i):
        rows = rows_of(i)
        zf[rows, :] = nn(normed[rows, :], wf2[:, 0:WI])
        z_out[rows, :] = zf[rows, :].astype(bf16)

    loop(blocks, gate_input)

    states.wait_recv()
    carried[...] = jnp.where(c > 0, carried[...], 0.0)
    mask = iota((L, L), 0) >= iota((L, L), 1)
    for i in range(blocks):
        rows = pl.ds(i * L, L)
        if i > 0:
            decay = nn(jnp.exp(tot_out[i - 1]), expand, HI)[0:1, :]
            carried[...] = carried[...] * decay
        start[i] = start[i] + carried[...]
        s0 = start[i].astype(bf16)
        steps, cum = steps_out[rows, :], cum_out[rows, :]
        x = act[rows, 0:WI]
        xl = x.astype(bf16)
        in_map = act[rows, WI : WI + N].astype(bf16)
        out_map = act[rows, WI + N : CH].astype(bf16)
        gram = nt(out_map, in_map)
        cum_t, steps_t = cum.T, steps.T
        inner = []
        for pair in range(HL // 2):
            halves = []
            for half in range(2):
                h = 2 * pair + half
                decay = jnp.exp(jnp.where(mask, cum[:, h : h + 1] - cum_t[h : h + 1, :], FILL))
                mixing = gram * decay * steps_t[h : h + 1, :]
                halves.append(nn(mixing.astype(bf16), pair_columns(xl, pair)))
            inner.append(jnp.where(low128, halves[0], halves[1]))
        y = jnp.concatenate(inner, axis=1)
        y = y + nn(jnp.exp(cum), expand, HI) * nn(out_map, s0) + chan[1:2, :] * x
        ssd[rows, :] = y.astype(bf16)
        zz = zf[rows, :]
        gated = y * zz * sigmoid(zz)
        gated_low[rows, :] = (gated * chan[0:1, :]).astype(bf16)
        square[:, rows] = nt(jnp.ones((8, WI), f32), gated * gated, HI)

    gather4.forward()
    gather3.finish()
    gather4.finish()
    for copy in (tail, keys, vals, states):
        copy.wait_send()


def forward(shards, *args):
    t, r = args[0].shape[0], args[1].shape[0]
    out = [
        ((D, 384), bf16),
        ((D, 1024), bf16),
        ((D, CG), bf16),
        ((D, FFL), bf16),
        ((t, D), bf16),
        ((8, D), f32),
        ((t, WI), bf16),
        ((t, CH), bf16),
        ((t, 128), f32),
        ((8, CH), f32),
        ((8, 128), f32),
        ((8, WI), f32),
        ((t, CH), bf16),
        ((8, CH), f32),
        ((t, 128), bf16),
        ((2, t, 128), bf16),
        ((2, t, 128), bf16),
        ((t, 128), f32),
        ((t, 128), bf16),
        ((8, t), f32),
        ((t, WI), bf16),
        ((t // L, N, WI), f32),
        ((t, 128), f32),
        ((t, 128), f32),
        ((t // L, 8, 128), f32),
        ((t, WI), bf16),
        ((8, t), f32),
    ]
    dma = pltpu.SemaphoreType.DMA
    vmem = pl.BlockSpec(memory_space=pltpu.VMEM)
    return pl.pallas_call(
        functools.partial(forward_kernel, shards),
        out_shape=[jax.ShapeDtypeStruct(*o) for o in out],
        in_specs=[vmem] * (len(args) - 1) + [pl.BlockSpec(memory_space=pltpu.SMEM)],
        out_specs=[vmem] * len(out),
        scratch_shapes=[
            pltpu.VMEM((r, 384), bf16),
            pltpu.VMEM((r, 1024), bf16),
            pltpu.VMEM((r, CG), bf16),
            pltpu.VMEM((t, 128), f32),
            pltpu.VMEM((t, WI), f32),
            pltpu.VMEM((t + 8, CH), f32),
            pltpu.VMEM((t, CH), f32),
            pltpu.VMEM((N, WI), f32),
            pltpu.VMEM((N, WI), f32),
            pltpu.VMEM((2 * L, 128), f32),
            pltpu.VMEM((2, 2 * L, 128), f32),
            pltpu.VMEM((16, CH), bf16),
        ]
        + Gather.sems(shards) * 4
        + [dma((4,)), dma((4,))],
        compiler_params=pltpu.CompilerParams(
            collective_id=1, has_side_effects=True, vmem_limit_bytes=VLIMIT
        ),
        name="mix_forward",
    )(*args)


def ffn_kernel(
    shards,
    hid, cot, gl, att, square, wb, wg, w_up, w_down, gains, length,
    osend, grad_own, chip, hid_own, gain_grad, total_square, ggl, grad_att, dots,
    grads, grad_res, partial, seed, send1, recv1, low_two, proj, grad_act, act, gg, gu, gown, back,
    unit, scale_keep, gsend, grecv, sqall, wm, wm_own,
    zs, cs, zr, own_sem, ms, mr, ws, wr, sqs, sqr, s1, r1, ns, nr, gs, gr, hs, hr,
):
    t = hid.shape[0]
    tp, c = lax.axis_index("tp"), lax.axis_index("ctx")
    blocks = t // L
    sub = L // TP
    width = D // TP
    wm_own[:, 0:FFL] = w_up[...]
    wm_own[:, FFL:] = nt(eye(w_down.shape[1]), w_down[...]).astype(bf16)
    greet(shards, True)
    gather = Gather(shards, wm_own, wm, zs, cs, zr, own_sem)
    gather.start()
    mlp_sum = ChipSum(shards, grads, chip, pl.ds(CG, CB - CG), ms, mr)
    out_sum = ChipSum(shards, grads, chip, pl.ds(CO, CG - CO), ws, wr)

    def peer(d):
        return lax.rem(tp + d, TP)

    def part(b, owner):
        return pl.ds(pl.multiple_of(b * L + owner * sub, sub), sub)

    def kept(b):
        return rows_of(b, sub)

    def square_to(d):
        return remote(sqall.at[tp], sqall.at[tp], sqs.at[d], sqr.at[tp], tp=peer(d))

    def square_from(d):
        return remote(sqall.at[tp], sqall.at[peer(d)], sqs.at[d], sqr.at[peer(d)], tp=peer(d))

    def scatter_to(send, recv, ss, rs, b, d):
        return remote(send.at[d, b], recv.at[tp, b], ss.at[d, b], rs.at[tp, b], tp=peer(d))

    def scatter_from(send, recv, ss, rs, b, d):
        return remote(send.at[d, b], recv.at[peer(d), b], ss.at[d, b], rs.at[peer(d), b], tp=peer(d))

    def gather_to(ref, ss, rs, b, d):
        there = ref.at[part(b, tp)]
        return remote(there, there, ss.at[d, b], rs.at[tp, b], tp=peer(d))

    def gather_from(ref, ss, rs, b, d):
        there = ref.at[part(b, peer(d))]
        return remote(there, there, ss.at[d, b], rs.at[peer(d), b], tp=peer(d))

    first = send1, recv1, s1, r1
    norms = low_two, ns, nr
    gradients = gsend, grecv, gs, gr
    residuals = grad_res, hs, hr

    sqall[tp] = square[...]
    for d in range(1, TP):
        square_to(d).start()
    limit = length[0] - c * t

    def mask_seed(i):
        rows = rows_of(i)
        live = iota((L, D), 0) + i * L < limit
        seed[rows, :] = jnp.where(live, cot[rows, :].astype(f32), 0.0).astype(bf16)

    loop(blocks, mask_seed)
    for d in range(1, TP):
        square_from(d).wait_recv()
    total_square[...] = sqall[0] + sqall[1] + sqall[2] + sqall[3]
    gain = gains[1:2, :]
    gain_grad[...] = jnp.zeros_like(gain_grad)

    def mix(b):
        rows = rows_of(b)
        scale = lax.rsqrt(total_square[:, rows] / DI + EPS)
        column = wide(tn(scale, first_row(), HI), D)
        partial[rows, :] = nt(gl[rows, :], wb[:, CO:CW]) * column + nt(att[rows, :], wb[:, CW:CG])
        for d in range(1, TP):
            send1[d, b] = partial[part(b, peer(d)), :].astype(bf16)
            scatter_to(*first, b, d).start()

    def norm(b):
        own = part(b, tp)
        hid_own[kept(b), :] = hid[own, :]
        acc = hid[own, :].astype(f32) + partial[own, :]
        for d in range(1, TP):
            scatter_from(*first, b, d).wait_recv()
            acc = acc + recv1[peer(d), b].astype(f32)
        scale = lax.rsqrt(jnp.mean(acc * acc, -1, keepdims=True) + EPS)
        scale_keep[kept(b), :] = jnp.broadcast_to(scale, (sub, 128))
        u = acc * scale
        unit[kept(b), :] = u
        low_two[own, :] = (u * gain).astype(bf16)
        for d in range(1, TP):
            gather_to(*norms, b, d).start()

    def mix_and_norm(s):
        @pl.when(s < blocks)
        def one():
            mix(s)

        @pl.when(s >= 2)
        def two():
            norm(s - 2)

    loop(blocks + 2, mix_and_norm)
    gather.forward()
    gather.finish()

    def act_grad(i):
        rows = rows_of(i)
        grad_act[rows, :] = nn(seed[rows, :], wm[:, FFL:])

    loop(blocks, act_grad)

    def hidden_units(b):
        rows = rows_of(b)
        for d in range(1, TP):
            gather_from(*norms, b, d).wait_recv()
        low = low_two[rows, :]
        gate, up = nn(low, wg[...]), nn(low, wm[:, 0:FFL])
        sig = sigmoid(gate)
        silu = gate * sig
        hidden_act = (silu * up).astype(bf16)
        act[rows, :] = hidden_act
        ga = grad_act[rows, :]
        g1 = (ga * up * (sig * (1.0 + gate * (1.0 - sig)))).astype(bf16)
        g2 = (ga * silu).astype(bf16)
        gg[rows, :] = g1
        gu[rows, :] = g2
        back[...] = nt(g1, wg[...]) + nt(g2, wm[:, 0:FFL])
        gown[kept(b), :] = back[kept(tp), :]
        for d in range(1, TP):
            gsend[d, b] = back[kept(peer(d)), :].astype(bf16)
            scatter_to(*gradients, b, d).start()
        partial[rows, :] = partial[rows, :] + nt(hidden_act, wm[:, FFL:])
        mine = rows_of(tp, width)
        osend[0, rows, :] = (partial[rows, mine] + hid[rows, mine].astype(f32)).astype(bf16)
        for e in range(1, TP):
            osend[e, rows, :] = partial[rows, rows_of(peer(e), width)].astype(bf16)

    def norm_back(b):
        own = part(b, tp)
        g = gown[kept(b), :]
        for d in range(1, TP):
            scatter_from(*gradients, b, d).wait_recv()
            g = g + grecv[peer(d), b].astype(f32)
        u = unit[kept(b), :]
        gain_grad[...] += jnp.broadcast_to(jnp.sum(g * u, 0, keepdims=True), (8, D))
        weighted = g * gain
        mean = jnp.mean(weighted * u, -1, keepdims=True)
        res = seed[own, :].astype(f32) + scale_keep[kept(b), 0:1] * (weighted - u * mean)
        grad_own[kept(b), :] = res
        grad_res[own, :] = res.astype(bf16)
        for d in range(1, TP):
            gather_to(*residuals, b, d).start()

    def weight_grads(i):
        feats = rows_of(i)
        low = low_two[:, feats]
        grads[feats, CG:CU] = tn(low, gg[...]).astype(bf16)
        grads[feats, CU:CD] = tn(low, gu[...]).astype(bf16)

    def down_grads(i):
        feats = rows_of(i)
        grads[feats, CD:CB] = tn(seed[:, feats], act[...]).astype(bf16)

    def out_back(b):
        rows = rows_of(b)
        for d in range(1, TP):
            gather_from(*residuals, b, d).wait_recv()
        square_scale = lax.rsqrt(total_square[:, rows] / DI + EPS)
        column = wide(tn(square_scale, first_row(), HI), D)
        got = grad_res[rows, :]
        low = (column * got.astype(f32)).astype(bf16)
        proj[rows, :] = low
        product = nn(low, wb[:, CO:CW])
        ggl[rows, :] = product
        dots[:, rows] = nt(jnp.ones((8, WI), f32), product * gl[rows, :].astype(f32), HI)
        grad_att[rows, :] = nn(got, wb[:, CW:CG]).astype(bf16)

    def there_and_back(s):
        @pl.when(s < blocks)
        def one():
            hidden_units(s)

        @pl.when(s == blocks)
        def fill():
            loop(D // L, weight_grads)

        @pl.when((s >= 1) & (s <= blocks))
        def two():
            norm_back(s - 1)

        @pl.when(s == blocks + 1)
        def more():
            loop(D // L, down_grads)
            mlp_sum.start()

        @pl.when(s >= 2)
        def three():
            out_back(s - 2)

    loop(blocks + 2, there_and_back)

    def out_grads(i):
        feats = rows_of(i)
        grads[feats, CO:CW] = tn(proj[:, feats], gl[...]).astype(bf16)
        grads[feats, CW:CG] = tn(grad_res[:, feats], att[...]).astype(bf16)

    loop(D // L, out_grads)
    out_sum.start()
    mlp_sum.finish()
    out_sum.finish()

    def sent(b):
        for d in range(1, TP):
            scatter_to(*first, b, d).wait_send()
            gather_to(*norms, b, d).wait_send()
            scatter_to(*gradients, b, d).wait_send()
            gather_to(*residuals, b, d).wait_send()

    loop(blocks, sent)
    for d in range(1, TP):
        square_to(d).wait_send()


def ffn(shards, *args):
    t = args[0].shape[0]
    blocks, sub = t // L, L // TP
    kept = blocks * sub
    out = [
        ((TP, t, D // TP), bf16),
        ((kept, D), f32),
        ((shards, D // (2 * shards), CB), bf16),
        ((kept, D), bf16),
        ((8, D), f32),
        ((8, t), f32),
        ((t, WI), f32),
        ((t, 128), bf16),
        ((8, t), f32),
    ]
    dma = pltpu.SemaphoreType.DMA
    vmem = pl.BlockSpec(memory_space=pltpu.VMEM)
    parts = pltpu.VMEM((TP, blocks, sub, D), bf16)
    return pl.pallas_call(
        functools.partial(ffn_kernel, shards),
        out_shape=[jax.ShapeDtypeStruct(*o) for o in out],
        in_specs=[vmem] * (len(args) - 1) + [pl.BlockSpec(memory_space=pltpu.SMEM)],
        out_specs=[vmem] * len(out),
        scratch_shapes=[
            pltpu.VMEM((D, CB), bf16),
            pltpu.VMEM((t, D), bf16),
            pltpu.VMEM((t, D), f32),
            pltpu.VMEM((t, D), bf16),
            parts,
            parts,
            pltpu.VMEM((t, D), bf16),
            pltpu.VMEM((t, D), bf16),
            pltpu.VMEM((t, FFL), f32),
            pltpu.VMEM((t, FFL), bf16),
            pltpu.VMEM((t, FFL), bf16),
            pltpu.VMEM((t, FFL), bf16),
            pltpu.VMEM((kept, D), f32),
            pltpu.VMEM((L, D), f32),
            pltpu.VMEM((kept, D), f32),
            pltpu.VMEM((kept, 128), f32),
            parts,
            parts,
            pltpu.VMEM((TP, 8, t), f32),
            pltpu.VMEM((D, 2 * FFL), bf16),
            pltpu.VMEM((D // (2 * shards), 2 * FFL), bf16),
        ]
        + Gather.sems(shards)
        + [dma((shards,))] * 4
        + [dma((TP,))] * 2
        + [dma((TP, blocks))] * 8,
        compiler_params=pltpu.CompilerParams(
            collective_id=2, has_side_effects=True, vmem_limit_bytes=VLIMIT
        ),
        name="feed_forward",
    )(*args)


def backward_kernel(
    shards,
    ggl, grad_att, dots_in, total_square, chip, osend,
    pre, cin, hist, q_low, kk, vv, att, lse_row, ssd, start, steps_in, cum_in, tot_in, dt_raw, z_in,
    taps, prm, chan, normed, wf1, wf2, hid_own, grad_own, gains, gain_two, table_all, length,
    output, low, grad_e, grad_l, grad_b, shared, vecs,
    table, lin, small, orecv, dots, dk, dv, dy, dpre, ends, dstate, carry, kv_out, kv_in, pad,
    edge_out, edge_in, gsend, grecv, gown, back, gain_one, grads_e, grads_l, misc, misc_low, misc_sum, shsend,
    vec_sib, vec_z,
    land, zsend, zrecv,
    sib0, land0, csend0, crecv0, zsend0, zrecv0,
    sib1, land1, csend1, crecv1, zsend1, zrecv1,
    sib2, land2, csend2, crecv2, zsend2, zrecv2,
    table_sem, vcs, vcr, vzs, vzr, xs, xr, ts, tr, os, orr, ss, sr, vts, vtr, gs, gr, hs, hr,
):
    z, c, tp = lax.axis_index("shard"), lax.axis_index("ctx"), lax.axis_index("tp")
    t = cin.shape[0]
    blocks, sub = t // L, L // TP
    get_table = pltpu.make_async_copy(table_all.at[rows_of(c, t)], table, table_sem)
    get_table.start()
    greet(shards, True)
    scatter = ShardSum(shards, chip, land, zsend, zrecv)
    scatter0 = Scatter(shards, grads_e, sib0, land0, csend0, crecv0, zsend0, zrecv0)
    scatter1 = Scatter(shards, grads_l, sib1, land1, csend1, crecv1, zsend1, zrecv1)
    scatter2 = Scatter(shards, misc_low, sib2, land2, csend2, crecv2, zsend2, zrecv2)
    scatter.start()

    def swap(src, dst, i):
        return remote(src, dst, xs.at[i], xr.at[i], ctx=1 - c)

    def peer(d):
        return lax.rem(tp + d, TP)

    def to_all(ref, send, recv, d):
        return remote(ref.at[tp], ref.at[tp], send.at[d], recv.at[tp], tp=peer(d))

    def from_all(ref, send, recv, d):
        return remote(ref.at[tp], ref.at[peer(d)], send.at[d], recv.at[peer(d)], tp=peer(d))

    dots[tp] = dots_in[...]
    for d in range(1, TP):
        to_all(dots, ts, tr, d).start()

    def out_to(d):
        return remote(osend.at[d], orecv.at[TP - 1 - d], os.at[d], orr.at[TP - 1 - d], tp=peer(d))

    def out_from(d):
        return remote(osend.at[d], orecv.at[d - 1], os.at[d], orr.at[d - 1], tp=peer(d))

    for d in range(1, TP):
        out_to(d).start()
    conv_grads = small.at[:, 0:CH]
    chan_grads = small.at[:, CH : CH + WI]
    head_grads = small.at[:, CH + WI : CH + WI + 128]
    expand = spread()
    low128 = low_lanes((L, 128))
    small[...] = jnp.zeros_like(small)
    for d in range(1, TP):
        from_all(dots, ts, tr, d).wait_recv()

    def gated_back(i):
        rows = rows_of(i)
        both = dots[0, :, rows] + dots[1, :, rows] + dots[2, :, rows] + dots[3, :, rows]
        share = both / ((total_square[:, rows] / DI + EPS) * DI)
        column = wide(tn(share, first_row(), HI), WI)
        zz, y = z_in[rows, :].astype(f32), ssd[rows, :].astype(f32)
        sig = sigmoid(zz)
        silu = zz * sig
        gated = y * silu
        product = ggl[rows, :]
        chan_grads[0:1, :] += jnp.sum(product * gated, 0, keepdims=True)
        grad_gated = product * chan[0:1, :] - column * gated
        grad_y = grad_gated * silu
        dy[rows, :] = grad_y
        lin[rows, CZ:CX] = (grad_gated * y * (sig * (1.0 + zz * (1.0 - sig)))).astype(bf16)
        v = pre[rows, WI + N : CH].astype(f32)
        out_map = (v * sigmoid(v)).astype(bf16)
        ends[i] = tn(out_map, (nn(jnp.exp(cum_in[rows, :]), expand, HI) * grad_y).astype(bf16))

    loop(blocks, gated_back)
    dstate[...] = jnp.zeros_like(dstate)

    def chain(k):
        i = blocks - 1 - k
        add = ends[i]
        ends[i] = dstate[...]
        dstate[...] = nn(jnp.exp(tot_in[i]), expand, HI)[0:1, :] * dstate[...] + add

    loop(blocks, chain)
    states = swap(dstate, carry, 0)
    states.start()

    scale = HD ** (-0.5)
    limit = length[0] - c * t
    dk[...] = jnp.zeros_like(dk)
    dv[...] = jnp.zeros_like(dv)
    get_table.wait()
    head_of = ((iota((8, 128), 1) // HD) == iota((8, 128), 0)).astype(f32)

    def stacked(v):
        return jnp.concatenate([own_half(v, 0), own_half(v, 1)], axis=0).astype(bf16)

    def side_by_side(v):
        return jnp.concatenate([v[0:1, :], v[1:2, :]], axis=1)

    for i in range(blocks):
        rows = pl.ds(i * L, L)
        width = (i + 1) * L
        q2 = stacked(q_low[rows, :].astype(f32))
        go = grad_att[rows, :].astype(f32)
        go2 = stacked(go)
        row_dot = side_by_side(nt(head_of, go * att[rows, :], HI))
        logs = side_by_side(lse_row[:, rows])
        turn = rotary_of(table, rows)

        def keys_of(part, size, masked):
            k, v = kk[part, 0:size, :], vv[part, 0:size, :]
            s = nt(k, q2) * scale - logs
            if masked:
                at = iota(s.shape, 1) % L + i * L
                row = iota(s.shape, 0)
                s = jnp.where((row <= at) & (row < limit), s, FILL)
            p = jnp.exp(s)
            ds = (p * (nt(v, go2) - row_dot)).astype(bf16)
            dv[part, 0:size, :] += nn(p.astype(bf16), go2)
            dk[part, 0:size, :] += nn(ds, q2)
            out = tn(ds, k) * scale
            out = jnp.where(low128, out[:L], out[L:])
            return out * turn[0] - swap_half(out) * turn[1]

        back[:, 0:128] = keys_of(0, width, True)

        @pl.when(c > 0)
        def earlier():
            back[:, 0:128] += keys_of(1, t, False)

        lin[rows, CQ:CK] = back[:, 0:128].astype(bf16)

    def key_values(part, rows):
        gk, gv = dk[part, rows, :] * scale, dv[part, rows, :]
        return jnp.where(low128, gk + pltpu.roll(gk, 64, 1), gv + pltpu.roll(gv, 64, 1))

    def pack(i):
        rows = rows_of(i)
        kv_out[rows, :] = key_values(1, rows).astype(bf16)

    loop(blocks, pack)
    pairs = swap(kv_out, kv_in, 1)
    pairs.start()

    pad[0:16, :] = jnp.concatenate([jnp.zeros((8, CH), f32), hist[...]], axis=0).astype(bf16)

    def fill(i):
        pad[pl.ds(pl.multiple_of(i * L + 16, 16), L), :] = cin[rows_of(i), :]

    loop(blocks, fill)
    states.wait_recv()
    carry[...] = jnp.where(c == 0, carry[...], 0.0)

    def add_carry(k):
        i = blocks - 1 - k
        ends[i] = ends[i] + carry[...]
        carry[...] = nn(jnp.exp(tot_in[i]), expand, HI)[0:1, :] * carry[...]

    loop(blocks, add_carry)
    mask = iota((L, L), 0) >= iota((L, L), 1)
    ones = lower_ones()
    lane = iota((L, 128), 1)

    def fold(v):
        return nt(v, expand, HI)

    def scan_back(i):
        rows = rows_of(i)
        v = pre[rows, :].astype(f32)
        sig = sigmoid(v)
        a = v * sig
        x = a[:, :WI]
        xl, bl, cl = x.astype(bf16), a[:, WI : WI + N].astype(bf16), a[:, WI + N :].astype(bf16)
        steps, cum = steps_in[rows, :], cum_in[rows, :]
        tot = cum[L - 1 : L, :]
        ecum, wend = jnp.exp(cum), jnp.exp(tot - cum)
        weight = wend * steps
        ecum_x, weight_x = nn(ecum, expand, HI), nn(weight, expand, HI)
        grad_y = dy[rows, :]
        dyl = grad_y.astype(bf16)
        s0, d1 = start[i], ends[i]
        s0l, d1l = s0.astype(bf16), d1.astype(bf16)
        bd, cs = nn(bl, d1l), nn(cl, s0l)
        dw = fold(x * bd)
        crossing = jnp.broadcast_to(jnp.sum(s0 * d1, 0, keepdims=True), (8, WI))
        dtot = jnp.sum(weight * dw, 0, keepdims=True) + jnp.exp(tot) * fold(crossing)[0:1, :]
        gram = nt(cl, bl)
        cum_t, steps_t = cum.T, steps.T
        dgram = jnp.zeros((L, L), f32)
        row_sums = jnp.zeros((L, 128), f32)
        col_sums, inner = [], []
        for pair in range(HL // 2):
            xp, dp = pair_columns(xl, pair), pair_columns(dyl, pair)
            dpf = pair_columns(grad_y, pair)
            halves = []
            for half in range(2):
                h = 2 * pair + half
                decay = jnp.exp(jnp.where(mask, cum[:, h : h + 1] - cum_t[h : h + 1, :], FILL))
                q = nt(own_half(dpf, half).astype(bf16), xp)
                mixed = gram * decay
                srow = steps_t[h : h + 1, :]
                f = mixed * q
                col_sums.append(jnp.sum(f, 0, keepdims=True))
                row_sums = jnp.where(lane == h, jnp.sum(f * srow, -1, keepdims=True), row_sums)
                dgram = dgram + decay * srow * q
                halves.append(tn((mixed * srow).astype(bf16), dp))
            inner.append(jnp.where(low128, halves[0], halves[1]))
        cols = jnp.concatenate(col_sums + [jnp.zeros((128 - HL, L), f32)], axis=0).T
        dcum = fold(grad_y * cs) * ecum - weight * dw + row_sums - steps * cols
        dcum = dcum + jnp.where(iota((L, 128), 0) == L - 1, dtot, 0.0)
        drate = tn(ones, dcum, HI)
        rate_of = prm[1:2, :]
        raw = dt_raw[rows, :] + prm[0:1, :]
        dstep = (wend * dw + cols + drate * rate_of) * sigmoid(raw)
        dstep = jnp.where(lane < HL, dstep, 0.0)
        lin[rows, CS:CA] = dstep.astype(bf16)
        head_grads[0:1, :] += jnp.sum(dstep, 0, keepdims=True)
        head_grads[1:2, :] += jnp.sum(drate * steps * rate_of, 0, keepdims=True)
        head_grads[2:3, :] += jnp.sum(fold(grad_y * x), 0, keepdims=True)
        slope = sig * (1.0 + v * (1.0 - sig))
        dx = chan[1:2, :] * grad_y + weight_x * bd + jnp.concatenate(inner, axis=1)
        dg = dgram.astype(bf16)
        db = tn(dg, cl) + nt((weight_x * x).astype(bf16), d1l)
        dc = nn(dg, bl) + nt((ecum_x * grad_y).astype(bf16), s0l)
        dpre[rows, 0:WI] = dx * slope[:, :WI]
        dpre[rows, WI : WI + N] = db * slope[:, WI : WI + N]
        dpre[rows, WI + N : CH] = dc * slope[:, WI + N :]

    edge = swap(edge_out, edge_in, 2)

    def keys_back(i):
        rows = rows_of(i)
        v = key_values(0, rows) + kv_in[rows, :].astype(f32)
        cosine, sine = rotary_of(table, rows)
        cosine = jnp.where(low128, cosine, 1.0)
        sine = jnp.where(low128, sine, 0.0)
        lin[rows, CK:CS] = (v * cosine - swap_half(v) * sine).astype(bf16)

    def conv_back(b):
        rows = rows_of(b)
        later = dpre[pl.ds(pl.multiple_of(b * L, L), L + 8), :]
        earlier = pad[pl.ds(pl.multiple_of(b * L, L), L + 16), :].astype(f32)
        g = later[0:L]
        conv_grads[4:5, :] += jnp.sum(g, 0, keepdims=True)
        total = jnp.zeros_like(g)
        for j in range(CONVW):
            total = total + taps[j : j + 1, :] * later[CONVW - 1 - j : CONVW - 1 - j + L]
            conv_grads[j : j + 1, :] += jnp.sum(g * earlier[13 + j : 13 + j + L], 0, keepdims=True)
        lin[rows, CX:CQ] = total.astype(bf16)

    def part(b, owner):
        return pl.ds(pl.multiple_of(b * L + owner * sub, sub), sub)

    def kept(b):
        return rows_of(b, sub)

    def grad_to(b, d):
        return remote(
            gsend.at[d - 1, b],
            grecv.at[TP - 1 - d, b],
            gs.at[d, b],
            gr.at[TP - 1 - d, b],
            tp=peer(d),
        )

    def grad_from(b, d):
        return remote(
            gsend.at[d - 1, b], grecv.at[d - 1, b], gs.at[d, b], gr.at[d - 1, b], tp=peer(d)
        )

    def product(b):
        rows = rows_of(b)
        back[...] = nt(lin[rows, CZ:CQ], wf2[...]) + nt(lin[rows, CQ:CA], wf1[...])
        gown[kept(b), :] = back[kept(tp), :]
        for d in range(1, TP):
            gsend[d - 1, b] = back[kept(peer(d)), :].astype(bf16)
            grad_to(b, d).start()

    def low_to(b, d):
        there = low.at[part(b, tp)]
        return remote(there, there, hs.at[d, b], hr.at[tp, b], tp=peer(d))

    def low_from(b, d):
        there = low.at[part(b, peer(d))]
        return remote(there, there, hs.at[d, b], hr.at[peer(d), b], tp=peer(d))

    gain_one[...] = jnp.zeros_like(gain_one)

    def norm_back(b):
        own = part(b, tp)
        g = gown[kept(b), :]
        for d in range(1, TP):
            grad_from(b, d).wait_recv()
            g = g + grecv[d - 1, b].astype(f32)
        x = hid_own[kept(b), :].astype(f32)
        scale = lax.rsqrt(jnp.mean(x * x, -1, keepdims=True) + EPS)
        unit = x * scale
        gain_one[...] += jnp.broadcast_to(jnp.sum(g * unit, 0, keepdims=True), (8, D))
        weighted = g * gains[0:1, :]
        mean = jnp.mean(weighted * unit, -1, keepdims=True)
        low[own, :] = (grad_own[kept(b), :] + scale * (weighted - unit * mean)).astype(bf16)
        for d in range(1, TP):
            low_to(b, d).start()

    def early_grads(i):
        feats = rows_of(i)
        grads_e[feats, 0:WI] = tn(normed[:, feats], lin[:, CZ:CX]).astype(bf16)
        grads_e[feats, WI:] = tn(normed[:, feats], lin[:, CQ:CS]).astype(bf16)

    def step(k):
        @pl.when(k < blocks)
        def scan():
            scan_back(lax.rem(2 * blocks - 1 - k + c, blocks))

        @pl.when(k == 0)
        def first():
            @pl.when(c > 0)
            def give():
                edge_out[...] = dpre[0:8, :]
                edge.start()

            pairs.wait_recv()
            loop(blocks, keys_back)
            loop(D // L, early_grads)
            scatter0.start()
            dpre[pl.ds(t, 8), :] = jnp.zeros((8, CH), f32)

            @pl.when(c == 0)
            def take():
                edge.wait_recv()
                dpre[pl.ds(t, 8), :] = edge_in[...]

        @pl.when(k >= 1)
        def there():
            conv_back(blocks - k)
            product(blocks - k)

        @pl.when(k == 1)
        def on():
            scatter0.middle()

        @pl.when(k >= 3)
        def again():
            norm_back(blocks + 2 - k)

    loop(blocks + 1, step)
    vec_core = remote(small, vec_sib, vcs.at[0], vcr.at[0], ctx=1 - c)
    vec_core.start()

    def weight_grads(i):
        feats = rows_of(i)
        grads_l[feats, :] = tn(normed[:, feats], lin[:, CX:CQ]).astype(bf16)
        misc[feats, :] = tn(normed[:, feats], lin[:, CS:CA])

    loop(D // L, weight_grads)
    scatter1.start()

    def vec_to_shard(k):
        zz = lax.rem(z + k, shards)
        return remote(vec_z.at[z], vec_z.at[z], vzs.at[zz], vzr.at[z], shard=zz)

    def vec_from_shard(k):
        zz = lax.rem(z + k, shards)
        return remote(vec_z.at[z], vec_z.at[zz], vzs.at[zz], vzr.at[zz], shard=zz)

    vec_core.wait_recv()
    vec_z[z] = small[...] + vec_sib[...]
    loop(shards - 1, lambda k: vec_to_shard(k + 1).start())
    norm_back(1)
    scatter1.middle()
    norm_back(0)
    gain_rows = jnp.where(iota((8, D), 0) == 0, gain_one[...], gain_two[...])
    row, lane8 = iota((8, 128), 0), iota((8, 128), 1)
    pick = ((row < 2) & (lane8 == GAIN_COL + row)).astype(f32)
    misc_low[...] = (misc[...] + tn(gain_rows, pick, HI)).astype(bf16)
    scatter2.start()
    total = osend[0].astype(f32)
    for d in range(1, TP):
        out_from(d).wait_recv()
        total = total + orecv[d - 1].astype(f32)
    output[...] = total.astype(bf16)
    scatter2.middle()
    loop(shards - 1, lambda k: vec_from_shard(k + 1).wait_recv())
    vecs[tp] = lax.fori_loop(1, shards, lambda k, total: total + vec_z[k], vec_z[0])
    for d in range(1, TP):
        to_all(vecs, vts, vtr, d).start()
    scatter.finish(grad_b)
    scatter0.finish(grad_e)
    scatter1.finish(grad_l)
    scatter2.finish(misc_sum)
    few = grad_e.shape[0] // TP
    for i in range(TP):
        shsend[i, :, 0:256] = grad_l[i * few : (i + 1) * few, WI:CH]
        shsend[i, :, 256:384] = grad_e[i * few : (i + 1) * few, WI + 128 : CH]
        shsend[i, :, 384:512] = misc_sum[i * few : (i + 1) * few, :]

    def share_to(d):
        return remote(shsend.at[peer(d)], shared.at[tp], ss.at[d], sr.at[tp], tp=peer(d))

    def share_from(d):
        return remote(shsend.at[peer(d)], shared.at[peer(d)], ss.at[d], sr.at[peer(d)], tp=peer(d))

    for d in range(1, TP):
        share_to(d).start()
    shared[tp] = shsend[tp]

    def arrived(b):
        for d in range(1, TP):
            low_from(b, d).wait_recv()
            low_to(b, d).wait_send()
            grad_to(b, d).wait_send()

    loop(blocks, arrived)
    for d in range(1, TP):
        share_from(d).wait_recv()
        from_all(vecs, vts, vtr, d).wait_recv()

    @pl.when(c > 0)
    def given():
        edge.wait_send()

    for copy in (states, pairs, vec_core):
        copy.wait_send()
    loop(shards - 1, lambda k: vec_to_shard(k + 1).wait_send())
    for d in range(1, TP):
        to_all(dots, ts, tr, d).wait_send()
        out_to(d).wait_send()
        share_to(d).wait_send()
        to_all(vecs, vts, vtr, d).wait_send()


def backward(shards, *args):
    t = args[0].shape[0]
    rows = D // (2 * shards)
    blocks, sub = t // L, L // TP
    vec = (8, CH + WI + 128)
    out = [
        ((t, D // TP), bf16),
        ((t, D), bf16),
        ((rows, CH), f32),
        ((rows, CH), f32),
        ((rows, CB), f32),
        ((TP, rows // TP, 512), f32),
        ((TP, *vec), f32),
    ]
    dma = pltpu.SemaphoreType.DMA
    vmem = pl.BlockSpec(memory_space=pltpu.VMEM)
    return pl.pallas_call(
        functools.partial(backward_kernel, shards),
        out_shape=[jax.ShapeDtypeStruct(*o) for o in out],
        in_specs=[vmem] * (len(args) - 2)
        + [pl.BlockSpec(memory_space=pl.ANY), pl.BlockSpec(memory_space=pltpu.SMEM)],
        out_specs=[vmem] * len(out),
        scratch_shapes=[
            pltpu.VMEM((t, 128), f32),
            pltpu.VMEM((t, CA), bf16),
            pltpu.VMEM(vec, f32),
            pltpu.VMEM((TP - 1, t, D // TP), bf16),
            pltpu.VMEM((TP, 8, t), f32),
            pltpu.VMEM((2, t, 128), f32),
            pltpu.VMEM((2, t, 128), f32),
            pltpu.VMEM((t, WI), f32),
            pltpu.VMEM((t + 8, CH), f32),
            pltpu.VMEM((t // L, N, WI), f32),
            pltpu.VMEM((N, WI), f32),
            pltpu.VMEM((N, WI), f32),
            pltpu.VMEM((t, 128), bf16),
            pltpu.VMEM((t, 128), bf16),
            pltpu.VMEM((t + 16, CH), bf16),
            pltpu.VMEM((8, CH), f32),
            pltpu.VMEM((8, CH), f32),
            pltpu.VMEM((TP - 1, blocks, sub, D), bf16),
            pltpu.VMEM((TP - 1, blocks, sub, D), bf16),
            pltpu.VMEM((blocks * sub, D), f32),
            pltpu.VMEM((L, D), f32),
            pltpu.VMEM((8, D), f32),
            pltpu.VMEM((D, CH), bf16),
            pltpu.VMEM((D, CH), bf16),
            pltpu.VMEM((D, 128), f32),
            pltpu.VMEM((D, 128), bf16),
            pltpu.VMEM((rows, 128), f32),
            pltpu.VMEM((TP, rows // TP, 512), f32),
            pltpu.VMEM(vec, f32),
            pltpu.VMEM((shards, *vec), f32),
        ]
        + [pltpu.VMEM((shards, rows, CB), bf16), dma((shards,)), dma((shards,))]
        + Scatter.scratch(shards, D, CH)
        + Scatter.scratch(shards, D, CH)
        + Scatter.scratch(shards, D, 128)
        + [dma(()), dma((1,)), dma((1,)), dma((shards,)), dma((shards,)), dma((3,)), dma((3,))]
        + [dma((TP,))] * 8
        + [dma((TP, blocks))] * 4,
        compiler_params=pltpu.CompilerParams(
            collective_id=3, has_side_effects=True, vmem_limit_bytes=VMOST
        ),
        name="mix_backward",
    )(*args)


def pack_kernel(
    low, grad_e, grad_l, grad_b, shared, vecs,
    grad_hidden, g_z, g_x, g_q, g_gate, g_up, g_out, g_o, g_down, g_shared, g_dt, gains,
    g_conv, g_chan, g_heads,
):
    grad_hidden[...] = low[...].astype(f32)

    @pl.when(pl.program_id(0) == 0)
    def rest():
        g_z[...] = grad_e[:, 0:WI]
        g_x[...] = grad_l[:, 0:WI]
        g_q[...] = grad_e[:, WI : WI + 128]
        g_gate[...] = grad_b[:, CG:CU]
        g_up[...] = grad_b[:, CU:CD]
        one = eye(grad_b.shape[0]).astype(f32)
        g_out[...] = tn(grad_b[:, CO:CW], one, HI)
        g_o[...] = tn(grad_b[:, CW:CG], one, HI)
        g_down[...] = tn(grad_b[:, CD:CB], one, HI)
        first, second = shared[0] + shared[1], shared[2] + shared[3]
        both = first + second
        g_shared[:, 0 : 2 * N] = both[:, 0 : 2 * N]
        kv1, kv2 = first[:, 256:384], second[:, 256:384]
        low_half = low_lanes(kv1.shape)
        g_shared[:, 2 * N : 2 * N + 128] = jnp.where(low_half, kv1, pltpu.roll(kv2, 64, 1))
        g_shared[:, 2 * N + 128 :] = jnp.where(low_half, pltpu.roll(kv1, 64, 1), kv2)
        gains[...] = tn(both[:, 384:512], eye(both.shape[0]).astype(f32), HI)[
            GAIN_COL : GAIN_COL + 8
        ]
        steps = jnp.zeros((both.shape[0], 128), f32)
        heads = jnp.zeros((8, 128), f32)
        g_chan[...] = jnp.zeros_like(g_chan)
        for i in range(TP):
            lane = iota(steps.shape, 1) // HL == i
            steps = jnp.where(lane, pltpu.roll(shared[i, :, 384:512], i * HL, 1), steps)
            lane = iota(heads.shape, 1) // HL == i
            heads = jnp.where(lane, pltpu.roll(vecs[i, :, CH + WI : CH + WI + 128], i * HL, 1), heads)
            mine = slice(i * WI, (i + 1) * WI)
            g_conv[:, mine] = vecs[i, 0:CONVW, 0:WI]
            g_chan[0:1, mine] = vecs[i, CONVW : CONVW + 1, 0:WI]
            g_chan[1:2, mine] = vecs[i, 0:1, CH : CH + WI]
        maps = vecs[0, :, WI:CH] + vecs[1, :, WI:CH] + vecs[2, :, WI:CH] + vecs[3, :, WI:CH]
        g_conv[:, DI:] = maps[0:CONVW]
        g_chan[0:1, DI:] = maps[CONVW : CONVW + 1]
        g_dt[...] = steps[:, 0:H]
        g_heads[...] = heads


def pack(low, grad_e, grad_l, grad_b, shared, vecs):
    t, r, few = low.shape[0], grad_e.shape[0], shared.shape[1]
    out = [
        (t, D), (r, WI), (r, WI), (r, 128), (r, FFL), (r, FFL), (WI, r), (128, r), (FFL, r),
        (few, 512), (few, H), (8, few), (CONVW, DI + 2 * N), (8, DI + 2 * N), (8, 128),
    ]
    rows = pl.BlockSpec((L, D), lambda i: (i, 0))

    def whole(shape):
        return pl.BlockSpec(shape, lambda i: (0,) * len(shape))

    return pl.pallas_call(
        pack_kernel,
        grid=(t // L,),
        out_shape=[jax.ShapeDtypeStruct(o, f32) for o in out],
        in_specs=[rows] + [whole(v.shape) for v in (grad_e, grad_l, grad_b, shared, vecs)],
        out_specs=[rows] + [whole(o) for o in out[1:]],
        compiler_params=pltpu.CompilerParams(vmem_limit_bytes=VLIMIT),
        name="lay_out",
    )(low, grad_e, grad_l, grad_b, shared, vecs)


def rotary_table(count):
    inverse = rope_base ** (-2.0 * np.arange(HD // 2, dtype=np.float32) / HD)
    angles = np.arange(count, dtype=np.float32)[:, None] * inverse.astype(np.float32)[None, :]
    both = np.concatenate([np.cos(angles), np.sin(angles)], axis=1)
    return np.tile(both, (1, 2)).astype(np.float32)


def local(
    hidden, cotangent, lengths, norm1_gain, w_z, w_x, w_shared, w_dt, dt_bias, a_log, d_skip,
    conv_w, conv_b, gated_gain, w_out, w_q, w_o, norm2_gain, w_gate, w_up, w_down,
):
    t = hidden.shape[1]
    shards = lax.axis_size("shard")
    hid, cot = hidden[0], cotangent[0]
    width = conv_w.shape[1]

    def fit(v):
        return jnp.pad(v, (0, width - v.shape[0]))[None]

    nothing = jnp.zeros((2, width), bf16)
    small = jnp.concatenate(
        [conv_w, conv_b[None], fit(gated_gain), nothing]
        + [fit(v) for v in (dt_bias, a_log, d_skip)]
        + [nothing, nothing, nothing[:1]],
        axis=0,
    )
    table = jnp.asarray(rotary_table(lax.axis_size("ctx") * t))
    (
        wf1, wf2, wo, wg, normed, gains, z, cin, dt, taps, prm, chan,
        pre, hist, q_low, kk, vv, att, att_low, lse_row, ssd, start, steps, cum, tot, gl, square,
    ) = forward(
        shards, hid, w_z, w_x, w_shared, w_dt.T, w_q, w_out, w_o, w_gate,
        norm1_gain[None], norm2_gain[None], small, table, lengths,
    )
    osend, grad_own, chip, hid_own, gain_two, total_square, ggl, grad_att, dots = ffn(
        shards, hid, cot, gl, att_low, square, wo, wg, w_up, w_down, gains, lengths
    )
    output, grad_hidden, grad_e, grad_l, grad_b, shared, vecs = backward(
        shards, ggl, grad_att, dots, total_square, chip, osend, pre, cin, hist, q_low, kk, vv, att,
        lse_row, ssd, start, steps, cum, tot, dt, z, taps, prm, chan, normed, wf1, wf2,
        hid_own, grad_own, gains, gain_two, table, lengths,
    )
    (
        grad_full, g_z, g_x, g_q, g_gate, g_up, g_out, g_o, g_down, g_shared, g_dt, g_gains,
        g_conv, g_chan, g_heads,
    ) = pack(grad_hidden, grad_e, grad_l, grad_b, shared, vecs)
    return (
        output[None],
        grad_full[None],
        g_gains[0],
        g_z,
        g_x,
        g_shared,
        g_dt,
        g_heads[0, :H],
        g_heads[1, :H],
        g_heads[2, :H],
        g_conv,
        g_chan[0],
        g_chan[1, :DI],
        g_out,
        g_q,
        g_o,
        g_gains[1],
        g_gate,
        g_up,
        g_down,
    )


def solution(mesh):
    placed = (
        P("shard", "ctx", None),
        P("shard", "ctx", None),
        P("shard"),
        P(("shard", "ctx")),
        P(("shard", "ctx"), "tp"),
        P(("shard", "ctx"), "tp"),
        P(("shard", "ctx"), None),
        P(("shard", "ctx"), None),
        P(),
        P(),
        P(),
        P(),
        P(),
        P(),
        P("tp", ("shard", "ctx")),
        P(("shard", "ctx"), "tp"),
        P("tp", ("shard", "ctx")),
        P(("shard", "ctx")),
        P(("shard", "ctx"), "tp"),
        P(("shard", "ctx"), "tp"),
        P("tp", ("shard", "ctx")),
    )
    return jax.shard_map(
        local,
        mesh=mesh,
        in_specs=placed,
        out_specs=(
            P("shard", "ctx", "tp"),
            P("shard", "ctx", None),
            P(("shard", "ctx", "tp")),
            P(("shard", "ctx"), "tp"),
            P(("shard", "ctx"), "tp"),
            P(("shard", "ctx", "tp"), None),
            P(("shard", "ctx", "tp"), None),
            P(),
            P(),
            P(),
            P(),
            P(),
            P(),
            P("tp", ("shard", "ctx")),
            P(("shard", "ctx"), "tp"),
            P("tp", ("shard", "ctx")),
            P(("shard", "ctx", "tp")),
            P(("shard", "ctx"), "tp"),
            P(("shard", "ctx"), "tp"),
            P("tp", ("shard", "ctx")),
        ),
        check_vma=False,
    )
```

```python
import functools

import jax
import jax.numpy as jnp
import numpy as np
from jax import lax
from jax.experimental import pallas as pl
from jax.experimental.pallas import tpu as pltpu
from jax.sharding import PartitionSpec as P

H = 24
P_SIZE = 64
N = 128
NQ = 8
KV = 2
HD = 64
CONVW = 4
DI = 1536
D = 1024
FFL = 512
TP = 4
HL = H // TP
WI = HL * P_SIZE
CH = WI + 2 * N
L = 256

CZ, CX, CM, CQ, CK, CS, CA = 0, 384, 768, 1024, 1152, 1280, 1408
GAIN_COL = 24
CO, CW, CG, CU, CD, CB = 0, 384, 512, 1024, 1536, 2048

EPS = 1e-05
rope_base = 10000.0
FILL = -1e30
HI = lax.Precision.HIGHEST
MESH = pl.DeviceIdType.MESH
f32 = jnp.float32
bf16 = jnp.bfloat16
VLIMIT = 60 * 1024 * 1024
VMOST = 63 * 1024 * 1024 + 512 * 1024


def nn(a, b, precision=None):
    return lax.dot_general(
        a, b, (((1,), (0,)), ((), ())), precision=precision, preferred_element_type=f32
    )


def nt(a, b, precision=None):
    return lax.dot_general(
        a, b, (((1,), (1,)), ((), ())), precision=precision, preferred_element_type=f32
    )


def tn(a, b, precision=None):
    return lax.dot_general(
        a, b, (((0,), (0,)), ((), ())), precision=precision, preferred_element_type=f32
    )


def rows_of(index, size=L):
    return pl.ds(pl.multiple_of(index * size, size), size)


def remote(src, dst, send, recv, **where):
    return pltpu.make_async_remote_copy(
        src_ref=src,
        dst_ref=dst,
        send_sem=send,
        recv_sem=recv,
        device_id=where,
        device_id_type=MESH,
    )


def iota(shape, dim):
    return lax.broadcasted_iota(jnp.int32, shape, dim)


def loop(n, body):
    lax.fori_loop(0, n, lambda i, c: (body(i), c)[1], 0)


def greet(shards, tp_too, ctx_too=True, shard_too=True):
    barrier = pltpu.get_barrier_semaphore()
    count = 0
    z, c, t = lax.axis_index("shard"), lax.axis_index("ctx"), lax.axis_index("tp")
    if ctx_too:
        pl.semaphore_signal(barrier, inc=1, device_id={"ctx": 1 - c}, device_id_type=MESH)
        count += 1
    if shard_too:

        def one(k):
            pl.semaphore_signal(
                barrier, inc=1, device_id={"shard": lax.rem(z + 1 + k, shards)}, device_id_type=MESH
            )

        loop(shards - 1, one)
        count += shards - 1
    if tp_too:
        for d in range(1, TP):
            pl.semaphore_signal(
                barrier, inc=1, device_id={"tp": lax.rem(t + d, TP)}, device_id_type=MESH
            )
            count += 1
    pl.semaphore_wait(barrier, count)


class Moves:
    def __init__(self):
        self.gets, self.puts = {}, {}

    def get(self, *names):
        for name in names:
            self.gets[name].wait()

    def put(self, *names):
        for name in names:
            self.puts[name].start()


def call_staged(kernel, args, out, late, early, scratch, left=(), **params):
    spaces = [pl.BlockSpec(memory_space=pltpu.VMEM)] * (len(args) - 1)
    spaces.append(pl.BlockSpec(memory_space=pltpu.SMEM))
    out_spaces = [pl.BlockSpec(memory_space=pltpu.VMEM)] * len(out)
    hbm = pl.BlockSpec(memory_space=pl.ANY)
    for at in (*late.values(), *left):
        spaces[at] = hbm
    for at in early.values():
        out_spaces[at] = hbm
    extra = [pltpu.VMEM(args[at].shape, args[at].dtype) for at in late.values()]
    extra += [pltpu.VMEM(*out[at]) for at in early.values()]
    dma = pltpu.SemaphoreType.DMA
    sems = [dma((len(late),)), dma((len(early),))]

    def body(*refs):
        split = len(args) + len(out)
        given, inner = list(refs[:split]), refs[split : split + len(scratch)]
        held, (get_sem, put_sem) = list(refs[split + len(scratch) : -2]), refs[-2:]
        moves = Moves()
        for n, (name, at) in enumerate(late.items()):
            buffer = held.pop(0)
            moves.gets[name] = pltpu.make_async_copy(given[at], buffer, get_sem.at[n])
            moves.gets[name].start()
            given[at] = buffer
        for n, (name, at) in enumerate(early.items()):
            buffer = held.pop(0)
            moves.puts[name] = pltpu.make_async_copy(buffer, given[len(args) + at], put_sem.at[n])
            given[len(args) + at] = buffer
        kernel(moves, *given, *inner)
        for copy in moves.puts.values():
            copy.wait()

    return pl.pallas_call(
        body,
        out_shape=[jax.ShapeDtypeStruct(*o) for o in out],
        in_specs=spaces,
        out_specs=out_spaces,
        scratch_shapes=list(scratch) + extra + sems,
        **params,
    )(*args)


class Gather:
    def __init__(self, shards, src, dst, zsend, csend, recv, own):
        self.s, self.src, self.dst = shards, src, dst
        self.zsend, self.csend, self.recv, self.own = zsend, csend, recv, own
        self.z, self.c = lax.axis_index("shard"), lax.axis_index("ctx")
        self.r = src.shape[0]

    def block(self, g):
        return self.dst.at[rows_of(g, self.r)]

    def to_shard(self, k):
        g = 2 * self.z + self.c
        return remote(
            self.src,
            self.block(g),
            self.zsend.at[k],
            self.recv.at[g],
            shard=lax.rem(self.z + k, self.s),
        )

    def to_core(self, k):
        zz = lax.rem(self.z + k, self.s)
        g = 2 * zz + self.c
        return remote(self.block(g), self.block(g), self.csend.at[k], self.recv.at[g], ctx=1 - self.c)

    def got(self, k, core):
        zz = lax.rem(self.z + k, self.s)
        g = 2 * zz + core
        return remote(self.block(g), self.block(g), self.csend.at[k], self.recv.at[g], ctx=1 - self.c)

    def start(self):
        keep = pltpu.make_async_copy(self.src, self.block(2 * self.z + self.c), self.own)
        keep.start()
        loop(self.s - 1, lambda k: self.to_shard(k + 1).start())
        keep.wait()
        self.to_core(0).start()

    def forward(self, first=0, last=None):
        def one(k):
            self.got(k + 1, self.c).wait_recv()
            self.to_core(k + 1).start()

        lax.fori_loop(
            first, self.s - 1 if last is None else last, lambda k, carry: (one(k), carry)[1], 0
        )

    def finish(self):
        loop(self.s, lambda k: self.got(k, 1 - self.c).wait_recv())
        loop(self.s, lambda k: self.to_core(k).wait_send())
        loop(self.s - 1, lambda k: self.to_shard(k + 1).wait_send())

    @staticmethod
    def sems(shards):
        dma = pltpu.SemaphoreType.DMA
        return [dma((shards,)), dma((shards,)), dma((2 * shards,)), dma(())]


class LineSum:
    def __init__(self, shards, src, hold, land, fsend, frecv, lsend, lrecv):
        self.s, self.src, self.hold, self.land = shards, src, hold, land
        self.fsend, self.frecv, self.lsend, self.lrecv = fsend, frecv, lsend, lrecv
        self.z = lax.axis_index("shard")

    def place(self, dest, way):
        return dest - 3 if way > 0 else dest

    def onward(self, src, dest, way):
        at = self.place(dest, way)
        return remote(
            src, self.hold.at[at], self.fsend.at[at], self.frecv.at[at], shard=self.z + way
        )

    def straight(self, src, steps, way):
        kind = steps - 1 + (0 if way > 0 else 2)
        return remote(
            src,
            self.land.at[kind],
            self.lsend.at[kind],
            self.lrecv.at[kind],
            shard=self.z + way * steps,
        )

    def each(self, far, two, one, waited):
        for way in (1, -1):
            first = self.z == 0 if way > 0 else self.z == self.s - 1
            now = jnp.logical_not(first) if waited else first

            def along(j, way=way, now=now):
                dest = self.s - 1 - j if way > 0 else j
                distance = (dest - self.z) * way

                @pl.when(now & (distance >= 3))
                def three():
                    far(dest, way)

                @pl.when(now & (distance == 2))
                def both():
                    two(dest, way)

            loop(self.s, along)
            if not waited:
                other = self.z + way

                @pl.when((other >= 0) & (other < self.s))
                def next_one(way=way, other=other):
                    one(other, way)

    def start(self):
        self.each(
            lambda dest, way: self.onward(self.src.at[dest], dest, way).start(),
            lambda dest, way: self.straight(self.src.at[dest], 2, way).start(),
            lambda dest, way: self.straight(self.src.at[dest], 1, way).start(),
            False,
        )

    def relay(self):
        def added(dest, way):
            at = self.place(dest, way)
            self.onward(self.src.at[dest], dest, way).wait_recv()
            own = self.src[dest].astype(f32)
            self.hold[at] = (own + self.hold[at].astype(f32)).astype(bf16)
            return self.hold.at[at]

        self.each(
            lambda dest, way: self.onward(added(dest, way), dest, way).start(),
            lambda dest, way: self.straight(added(dest, way), 2, way).start(),
            None,
            True,
        )

    def finish(self, out):
        out[...] = self.src[self.z].astype(f32)
        for steps in (1, 2):
            for way in (1, -1):
                source = self.z - way * steps

                @pl.when((source >= 0) & (source < self.s))
                def arrived(steps=steps, way=way):
                    kind = steps - 1 + (0 if way > 0 else 2)
                    remote(
                        self.land.at[kind],
                        self.land.at[kind],
                        self.lsend.at[kind],
                        self.lrecv.at[kind],
                        shard=self.z - way * steps,
                    ).wait_recv()
                    out[...] += self.land[kind].astype(f32)

        for waited in (False, True):
            self.each(
                lambda dest, way: self.onward(self.src.at[dest], dest, way).wait_send(),
                lambda dest, way: self.straight(self.src.at[dest], 2, way).wait_send(),
                lambda dest, way: self.straight(self.src.at[dest], 1, way).wait_send(),
                waited,
            )

    @staticmethod
    def scratch(shards, rows, cols):
        dma = pltpu.SemaphoreType.DMA
        far, r = max(shards - 3, 1), rows // (2 * shards)
        return [
            pltpu.VMEM((far, r, cols), bf16),
            pltpu.VMEM((4, r, cols), bf16),
            dma((far,)),
            dma((far,)),
            dma((4,)),
            dma((4,)),
        ]


class Scatter:
    def __init__(self, shards, src, sib, csend, crecv, *line):
        self.s, self.src, self.sib = shards, src, sib
        self.csend, self.crecv = csend, crecv
        self.c = lax.axis_index("ctx")
        self.r = src.shape[0] // (2 * shards)
        self.line = LineSum(shards, sib, *line)

    def to_core(self, k):
        return remote(
            self.src.at[rows_of(2 * k + 1 - self.c, self.r)],
            self.sib.at[k],
            self.csend.at[k],
            self.crecv.at[k],
            ctx=1 - self.c,
        )

    def start(self):
        loop(self.s, lambda k: self.to_core(k).start())

    def middle(self):
        def one(k):
            self.to_core(k).wait_recv()
            both = self.src[rows_of(2 * k + self.c, self.r), :].astype(f32)
            self.sib[k] = (both + self.sib[k].astype(f32)).astype(bf16)

        loop(self.s, one)
        self.line.start()

    def relay(self):
        self.line.relay()

    def finish(self, out):
        self.line.finish(out)
        loop(self.s, lambda k: self.to_core(k).wait_send())

    @staticmethod
    def scratch(shards, rows, cols):
        dma = pltpu.SemaphoreType.DMA
        block = pltpu.VMEM((shards, rows // (2 * shards), cols), bf16)
        return [block, dma((shards,)), dma((shards,))] + LineSum.scratch(shards, rows, cols)


class ChipSum:
    def __init__(self, shards, src, sib, cols, csend, crecv):
        self.s, self.src, self.sib, self.cols = shards, src, sib, cols
        self.csend, self.crecv = csend, crecv
        self.c = lax.axis_index("ctx")
        self.r = src.shape[0] // (2 * shards)

    def to_core(self, k):
        return remote(
            self.src.at[rows_of(2 * k + 1 - self.c, self.r), self.cols],
            self.sib.at[k, :, self.cols],
            self.csend.at[k],
            self.crecv.at[k],
            ctx=1 - self.c,
        )

    def start(self):
        loop(self.s, lambda k: self.to_core(k).start())

    def finish(self):
        def one(k):
            self.to_core(k).wait_recv()
            own = self.src[rows_of(2 * k + self.c, self.r), self.cols].astype(f32)
            self.sib[k, :, self.cols] = (own + self.sib[k, :, self.cols].astype(f32)).astype(bf16)

        loop(self.s, one)
        loop(self.s, lambda k: self.to_core(k).wait_send())


class Square:
    def __init__(self, kinds):
        tp = lax.axis_index("tp")
        self.me = tp
        self.x = tp + 1 - 2 * lax.rem(tp, 2)
        self.y = lax.rem(tp + 2, TP)
        self.across = TP - 1 - tp
        self.send, self.recv = kinds

    def copy(self, kind, b, src, dst):
        to = self.y if kind in (1, 2) else self.x
        return remote(src, dst, self.send.at[kind, b], self.recv.at[kind, b], tp=to)


class SquareScatter(Square):
    def __init__(self, buffers, kinds):
        super().__init__(kinds)
        self.out, self.into, self.out2, self.into2 = buffers

    def first(self, kind, b):
        return self.copy(kind, b, self.out.at[kind, b], self.into.at[kind, b])

    def second(self, kind, b):
        return self.copy(kind, b, self.out2.at[kind - 2, b], self.into2.at[kind - 2, b])

    def start(self, b, ref, rows):
        half = ref.shape[1] // 2
        left, right = pl.ds(0, half), pl.ds(half, half)
        self.out[0, b, 0] = ref[rows(self.x), left].astype(bf16)
        self.out[0, b, 1] = ref[rows(self.across), left].astype(bf16)
        self.first(0, b).start()
        self.out[1, b, 0] = ref[rows(self.y), right].astype(bf16)
        self.out[1, b, 1] = ref[rows(self.across), right].astype(bf16)
        self.first(1, b).start()
        self.out2[0, b] = ref[rows(self.y), left].astype(bf16)
        self.out2[1, b] = ref[rows(self.x), right].astype(bf16)

    def relay(self, b):
        for kind in (0, 1):
            self.first(kind, b).wait_recv()
            own = self.out2[kind, b].astype(f32)
            self.out2[kind, b] = (own + self.into[kind, b, 1].astype(f32)).astype(bf16)
            self.second(kind + 2, b).start()

    def finish(self, b):
        sums = []
        for kind in (0, 1):
            self.second(kind + 2, b).wait_recv()
            sums.append(self.into[kind, b, 0].astype(f32) + self.into2[kind, b].astype(f32))
        return jnp.concatenate(sums, axis=1)

    def sent(self, b):
        for kind in (0, 1):
            self.first(kind, b).wait_send()
            self.second(kind + 2, b).wait_send()

    @staticmethod
    def scratch(blocks, sub):
        first = pltpu.VMEM((2, blocks, 2, sub, D // 2), bf16)
        second = pltpu.VMEM((2, blocks, sub, D // 2), bf16)
        return [first, first, second, second]


class SquareGather(Square):
    def __init__(self, ref, part, kinds):
        super().__init__(kinds)
        self.ref, self.part = ref, part

    def whole(self, kind, b, owner):
        there = self.ref.at[self.part(b, owner)]
        return self.copy(kind, b, there, there)

    def half(self, kind, b, owner):
        half = self.ref.shape[1] // 2
        there = self.ref.at[self.part(b, owner), pl.ds((kind - 2) * half, half)]
        return self.copy(kind, b, there, there)

    def start(self, b):
        for kind in (0, 1):
            self.whole(kind, b, self.me).start()

    def relay(self, b):
        for kind, owner in ((0, self.x), (1, self.y)):
            self.whole(kind, b, owner).wait_recv()
            self.half(kind + 2, b, owner).start()

    def finish(self, b):
        for kind in (2, 3):
            self.half(kind, b, self.across).wait_recv()

    def sent(self, b):
        for kind, owner in ((0, self.x), (1, self.y)):
            self.whole(kind, b, self.me).wait_send()
            self.half(kind + 2, b, owner).wait_send()


def sigmoid(v):
    return 1.0 / (1.0 + jnp.exp(-v))


def softplus(v):
    return jnp.maximum(v, 0.0) + jnp.log1p(jnp.exp(-jnp.abs(v)))


def swap_half(v):
    width = v.shape[1]
    low = iota(v.shape, 1) % HD < HD // 2
    return jnp.where(low, pltpu.roll(v, width - HD // 2, 1), pltpu.roll(v, HD // 2, 1))


def low_lanes(shape):
    return iota(shape, 1) < 64


def spread():
    return (iota((N, WI), 1) // P_SIZE == iota((N, WI), 0)).astype(f32)


def first_row():
    return (iota((8, N), 0) == 0).astype(f32)


def wide(column, width):
    return jnp.concatenate([column] * (width // column.shape[1]), axis=1)


def lower_ones():
    return (iota((L, L), 0) >= iota((L, L), 1)).astype(f32)


def head_scalars(dt_raw, prm):
    real = iota(dt_raw.shape, 1) < HL
    steps = jnp.where(real, softplus(dt_raw + prm[0:1, :]), 0.0)
    rates = steps * prm[1:2, :]
    return steps, rates


def pair_columns(v, pair):
    return v[:, 128 * pair : 128 * pair + 128]


def own_half(v, half):
    return jnp.where(low_lanes(v.shape) == (half == 0), v, jnp.zeros_like(v))


def eye(n):
    return (iota((n, n), 0) == iota((n, n), 1)).astype(bf16)


def rotary_of(table, rows):
    both = table[rows, :]
    first = iota(both.shape, 1) % HD < HD // 2
    cosine = jnp.where(first, both, pltpu.roll(both, HD // 2, 1))
    sine = jnp.where(first, -pltpu.roll(both, 128 - HD // 2, 1), both)
    return cosine, sine


FORWARD_EARLY = (
    "wf1",
    "wf2",
    "normed",
    "z_out",
    "cin",
    "dt_raw",
    "pre",
    "q_low",
    "kk",
    "vv",
    "att",
    "att_low",
    "steps_out",
    "cum_out",
)
FORWARD_AT = (
    0,
    1,
    4,
    6,
    7,
    8,
    12,
    14,
    15,
    16,
    17,
    18,
    22,
    23,
)
BACKWARD_LATE = (
    "chip",
    "grad_att",
    "q_low",
    "kk",
    "vv",
    "att",
    "lse_row",
    "start",
    "steps_in",
    "dt_raw",
    "cin",
    "normed",
    "wf1",
    "wf2",
    "hid_own",
    "grad_own",
)
BACKWARD_AT = (
    4,
    1,
    9,
    10,
    11,
    12,
    13,
    15,
    16,
    19,
    7,
    24,
    25,
    26,
    27,
    28,
)


def forward_kernel(
    shards, moves,
    hid, w_z, w_x, w_shared, w_dt, w_q, w_out, w_o, w_gate, gain_one, gain_two,
    small, table, length,
    wf1, wf2, wo, wg, normed, gains, z_out, cin, dt_raw, taps, prm, chan,
    pre, hist, q_low, kk, vv, att, att_low, lse_row, ssd, start, steps_out, cum_out, tot_out,
    gated_low, square,
    wa1, wa2, wa3, stat, zf, pad, act, state, carried, scores_m, scores_l, hist_in,
    zs1, cs1, zr1, own1, zs2, cs2, zr2, own2, zs3, cs3, zr3, own3, zs4, cs4, zr4, own4,
    xs, xr,
):
    c, tp = lax.axis_index("ctx"), lax.axis_index("tp")
    t = hid.shape[0]
    blocks = t // L
    r = w_z.shape[0]

    kv = tp * (NQ // TP) // (NQ // KV)
    keys = w_shared[:, 2 * N : 2 * N + 128].astype(f32)
    vals = w_shared[:, 2 * N + 128 : 2 * N + 256].astype(f32)
    low_r = low_lanes((r, 128))
    other = pltpu.roll(jnp.where(kv == 0, vals, keys), 64, 1)
    wa1[:, 0:128] = w_q[...]
    wa1[:, 128:256] = jnp.where(
        kv == 0, jnp.where(low_r, keys, other), jnp.where(low_r, other, vals)
    ).astype(bf16)
    head_pick = (
        (iota((H, 128), 0) == iota((H, 128), 1) + tp * HL) & (iota((H, 128), 1) < HL)
    ).astype(bf16)
    row8, lane8 = iota((8, 128), 0), iota((8, 128), 1)
    gain_pick = ((row8 < 2) & (lane8 == GAIN_COL + row8)).astype(bf16)
    gain_rows = jnp.where(
        iota((8, r), 0) == 0, gain_one[...].astype(f32), gain_two[...].astype(f32)
    ).astype(bf16)
    wa1[:, 256:384] = (tn(w_dt[...], head_pick) + tn(gain_rows, gain_pick)).astype(bf16)
    wa2[:, 0:WI] = w_z[...]
    wa2[:, WI : 2 * WI] = w_x[...]
    wa2[:, 2 * WI : 2 * WI + 2 * N] = w_shared[:, 0 : 2 * N]
    greet(shards, False)
    gather1 = Gather(shards, wa1, wf1, zs1, cs1, zr1, own1)
    gather2 = Gather(shards, wa2, wf2, zs2, cs2, zr2, own2)
    gather3 = Gather(shards, wa3, wo, zs3, cs3, zr3, own3)
    gather4 = Gather(shards, w_gate, wg, zs4, cs4, zr4, own4)
    gather1.start()
    gather2.start()
    wa3[:, CO:CW] = nt(eye(r), w_out[...]).astype(bf16)
    wa3[:, CW:CG] = nt(eye(r), w_o[...]).astype(bf16)

    expand = spread()
    mine = pl.ds(pl.multiple_of(tp * WI, 128), WI)
    taps[0:CONVW, 0:WI] = small[0:CONVW, mine].astype(f32)
    taps[0:CONVW, WI:CH] = small[0:CONVW, DI:].astype(f32)
    taps[CONVW : CONVW + 1, 0:WI] = small[CONVW : CONVW + 1, mine].astype(f32)
    taps[CONVW : CONVW + 1, WI:CH] = small[CONVW : CONVW + 1, DI:].astype(f32)
    taps[CONVW + 1 :, :] = jnp.zeros((8 - CONVW - 1, CH), f32)
    heads = pltpu.roll(small[8:16, 0:128].astype(f32), lax.rem(128 - tp * HL, 128), 1)
    heads = jnp.where(lane8 < HL, jnp.where(row8 == 1, -jnp.exp(heads), heads), 0.0)
    prm[...] = heads
    chan[...] = jnp.zeros_like(chan)
    chan[0:1, :] = small[CONVW + 1 : CONVW + 2, mine].astype(f32)
    chan[1:2, :] = nn(heads, expand, HI)[2:3, :]

    def swap(src, dst, i):
        return remote(src, dst, xs.at[i], xr.at[i], ctx=1 - c)

    def row_scale(i):
        rows = rows_of(i)
        x = hid[rows, :].astype(f32)
        scale = lax.rsqrt(jnp.mean(x * x, -1, keepdims=True) + EPS)
        stat[rows, :] = jnp.broadcast_to(scale, (L, 128))

    loop(blocks, row_scale)
    gather1.forward()
    gather1.finish()
    turned = wf1[:, 256:384].astype(f32).T
    gains[...] = turned[GAIN_COL : GAIN_COL + 8]
    gain = gains[0:1, :]
    low128 = low_lanes((L, 128))
    moves.put("wf1")
    moves.get("table")

    def first_projections(i):
        rows = rows_of(i)
        low = (hid[rows, :].astype(f32) * wide(stat[rows, :], D) * gain).astype(bf16)
        normed[rows, :] = low
        rest = nn(low, wf1[...])
        cosine, sine = rotary_of(table, pl.ds(pl.multiple_of(c * t + i * L, L), L))
        v = rest[:, 0:128]
        q_low[rows, :] = (v * cosine + swap_half(v) * sine).astype(bf16)
        v = rest[:, 128:256]
        other = pltpu.roll(v, 64, 1)
        twice = jnp.where(low128, v, other)
        kk[0, rows, :] = (twice * cosine + swap_half(twice) * sine).astype(bf16)
        vv[0, rows, :] = jnp.where(low128, other, v).astype(bf16)
        dt_raw[rows, :] = rest[:, 256:384]

    loop(blocks, first_projections)
    moves.put("normed", "q_low", "dt_raw")
    keys = swap(kk.at[0], kk.at[1], 1)
    keys.start()
    vals = swap(vv.at[0], vv.at[1], 2)
    vals.start()

    scale = HD ** (-0.5)
    limit = length[0] - c * t

    def stacked(v):
        return jnp.concatenate([own_half(v, 0), own_half(v, 1)], axis=0)

    for i in range(blocks):
        rows = pl.ds(i * L, L)
        width = (i + 1) * L
        q2 = stacked(q_low[rows, :].astype(f32)).astype(bf16)
        s = nt(q2, kk[0, 0:width, :]) * scale
        at = iota(s.shape, 0) % L + i * L
        col = iota(s.shape, 1)
        s = jnp.where((col <= at) & (col < limit), s, FILL)
        peak = jnp.max(s, -1, keepdims=True)
        e = jnp.exp(s - peak)
        total = jnp.sum(e, -1, keepdims=True)
        o = nn(e.astype(bf16), vv[0, 0:width, :])
        scores_m[...] = jnp.broadcast_to(peak, (2 * L, 128))
        scores_l[0] = jnp.broadcast_to(total, (2 * L, 128))
        scores_l[1] = o
        if i == 0:
            keys.wait_recv()
            vals.wait_recv()

        @pl.when(c > 0)
        def earlier():
            s2 = nt(q2, kk[1]) * scale
            old = scores_m[:, 0:1]
            new = jnp.maximum(old, jnp.max(s2, -1, keepdims=True))
            e2 = jnp.exp(s2 - new)
            fade = jnp.exp(old - new)
            scores_m[...] = jnp.broadcast_to(new, (2 * L, 128))
            scores_l[0] = fade * scores_l[0] + jnp.sum(e2, -1, keepdims=True)
            scores_l[1] = fade * scores_l[1] + nn(e2.astype(bf16), vv[1])

        total = scores_l[0]
        o = scores_l[1] / total
        o = jnp.where(low128, o[:L], o[L:])
        att[rows, :] = o
        att_low[rows, :] = o.astype(bf16)
        logs = scores_m[...] + jnp.log(total)
        turned = jnp.where(low128, logs[:L], logs[L:]).T
        lse_row[0:1, rows] = turned[0:1]
        lse_row[1:2, rows] = turned[64:65]
        lse_row[2:8, rows] = jnp.zeros((6, L), f32)
        if i == blocks - 2:
            gather2.forward(0, 1)
    gather2.forward(1)
    moves.put("kk", "vv", "att", "att_low")
    gather3.start()
    gather4.start()
    gather2.finish()
    moves.put("wf2")

    def conv_input(k):
        i = blocks - 1 - k
        rows = rows_of(i)
        v = nn(normed[rows, :], wf2[:, WI:]).astype(bf16)
        cin[rows, :] = v
        pad[pl.ds(pl.multiple_of(i * L + 8, 8), L), :] = v.astype(f32)

    conv_input(0)
    tail = swap(cin.at[pl.ds(t - 16, 16)], hist_in, 0)
    tail.start()
    lax.fori_loop(1, blocks, lambda k, carry: (conv_input(k), carry)[1], 0)
    tail.wait_recv()
    before = hist_in[8:16, :].astype(f32)
    hist[...] = jnp.where((iota((8, CH), 0) >= 5) & (c > 0), before, 0.0)
    pad[0:8, :] = hist[...]
    ones = lower_ones()
    state[...] = jnp.zeros_like(state)

    for i in range(blocks):
        rows = pl.ds(i * L, L)
        v = taps[4:5, :] + taps[0:1, :] * pad[pl.ds(i * L + 5, L), :]
        for j in range(1, CONVW):
            v = v + taps[j : j + 1, :] * pad[pl.ds(i * L + 5 + j, L), :]
        pre[rows, :] = v
        a = v * sigmoid(v)
        act[rows, :] = a
        steps, rates = head_scalars(dt_raw[rows, :], prm)
        cum = nn(ones, rates, HI)
        tot = cum[L - 1 : L, :]
        steps_out[rows, :] = steps
        cum_out[rows, :] = cum
        tot_out[i] = jnp.broadcast_to(tot, (8, 128))
        weight = nn(jnp.exp(tot - cum) * steps, expand, HI)
        start[i] = state[...]
        add = tn(a[:, WI : WI + N].astype(bf16), (weight * a[:, :WI]).astype(bf16))
        decay = nn(jnp.broadcast_to(jnp.exp(tot), (8, 128)), expand, HI)[0:1, :]
        state[...] = decay * state[...] + add

    states = swap(state, carried, 3)
    states.start()
    moves.put("cin", "pre", "steps_out", "cum_out")
    gather3.forward()

    def gate_input(i):
        rows = rows_of(i)
        zf[rows, :] = nn(normed[rows, :], wf2[:, 0:WI])
        z_out[rows, :] = zf[rows, :].astype(bf16)

    loop(blocks, gate_input)
    moves.put("z_out")

    states.wait_recv()
    carried[...] = jnp.where(c > 0, carried[...], 0.0)
    mask = iota((L, L), 0) >= iota((L, L), 1)
    for i in range(blocks):
        rows = pl.ds(i * L, L)
        if i > 0:
            decay = nn(jnp.exp(tot_out[i - 1]), expand, HI)[0:1, :]
            carried[...] = carried[...] * decay
        start[i] = start[i] + carried[...]
        s0 = start[i].astype(bf16)
        steps, cum = steps_out[rows, :], cum_out[rows, :]
        x = act[rows, 0:WI]
        xl = x.astype(bf16)
        in_map = act[rows, WI : WI + N].astype(bf16)
        out_map = act[rows, WI + N : CH].astype(bf16)
        gram = nt(out_map, in_map)
        cum_t, steps_t = cum.T, steps.T
        inner = []
        for pair in range(HL // 2):
            halves = []
            for half in range(2):
                h = 2 * pair + half
                decay = jnp.exp(jnp.where(mask, cum[:, h : h + 1] - cum_t[h : h + 1, :], FILL))
                mixing = gram * decay * steps_t[h : h + 1, :]
                halves.append(nn(mixing.astype(bf16), pair_columns(xl, pair)))
            inner.append(jnp.where(low128, halves[0], halves[1]))
        y = jnp.concatenate(inner, axis=1)
        y = y + nn(jnp.exp(cum), expand, HI) * nn(out_map, s0) + chan[1:2, :] * x
        ssd[rows, :] = y.astype(bf16)
        zz = zf[rows, :]
        gated = y * zz * sigmoid(zz)
        gated_low[rows, :] = (gated * chan[0:1, :]).astype(bf16)
        square[:, rows] = nt(jnp.ones((8, WI), f32), gated * gated, HI)

    gather4.forward()
    gather3.finish()
    gather4.finish()
    for copy in (tail, keys, vals, states):
        copy.wait_send()


def forward(shards, *args):
    t, r = args[0].shape[0], args[1].shape[0]
    out = [
        ((D, 384), bf16),
        ((D, 1024), bf16),
        ((D, CG), bf16),
        ((D, FFL), bf16),
        ((t, D), bf16),
        ((8, D), f32),
        ((t, WI), bf16),
        ((t, CH), bf16),
        ((t, 128), f32),
        ((8, CH), f32),
        ((8, 128), f32),
        ((8, WI), f32),
        ((t, CH), f32),
        ((8, CH), f32),
        ((t, 128), bf16),
        ((2, t, 128), bf16),
        ((2, t, 128), bf16),
        ((t, 128), f32),
        ((t, 128), bf16),
        ((8, t), f32),
        ((t, WI), bf16),
        ((t // L, N, WI), f32),
        ((t, 128), f32),
        ((t, 128), f32),
        ((t // L, 8, 128), f32),
        ((t, WI), bf16),
        ((8, t), f32),
    ]
    dma = pltpu.SemaphoreType.DMA
    scratch = (
        [
            pltpu.VMEM((r, 384), bf16),
            pltpu.VMEM((r, 1024), bf16),
            pltpu.VMEM((r, CG), bf16),
            pltpu.VMEM((t, 128), f32),
            pltpu.VMEM((t, WI), f32),
            pltpu.VMEM((t + 8, CH), f32),
            pltpu.VMEM((t, CH), f32),
            pltpu.VMEM((N, WI), f32),
            pltpu.VMEM((N, WI), f32),
            pltpu.VMEM((2 * L, 128), f32),
            pltpu.VMEM((2, 2 * L, 128), f32),
            pltpu.VMEM((16, CH), bf16),
        ]
        + Gather.sems(shards) * 4
        + [dma((4,)), dma((4,))]
    )
    return call_staged(
        functools.partial(forward_kernel, shards),
        args,
        out,
        {"table": 12},
        dict(zip(FORWARD_EARLY, FORWARD_AT)),
        scratch,
        compiler_params=pltpu.CompilerParams(
            collective_id=1, has_side_effects=True, vmem_limit_bytes=VLIMIT
        ),
        name="mix_forward",
    )


def ffn_kernel(
    shards, moves,
    hid, cot, gl, att, square, wb, wg, w_up, w_down, gains, length,
    osend, grad_own, chip, hid_own, gain_grad, total_square, ggl, grad_att, dots,
    grads, grad_res, partial, seed, low_two, proj, grad_act, act, gg, gu, gown, back,
    unit, scale_keep, sqall, wm, wm_own, a1, a2, a3, a4, b1, b2, b3, b4,
    zs, cs, zr, own_sem, ms, mr, ws, wr, sqs, sqr, s1, r1, ns, nr, gs, gr, hs, hr,
):
    t = hid.shape[0]
    tp, c = lax.axis_index("tp"), lax.axis_index("ctx")
    blocks = t // L
    sub = L // TP
    width = D // TP
    wm_own[:, 0:FFL] = w_up[...]
    wm_own[:, FFL:] = nt(eye(w_down.shape[1]), w_down[...]).astype(bf16)
    greet(shards, True)
    gather = Gather(shards, wm_own, wm, zs, cs, zr, own_sem)
    gather.start()
    mlp_sum = ChipSum(shards, grads, chip, pl.ds(CG, CB - CG), ms, mr)
    out_sum = ChipSum(shards, grads, chip, pl.ds(CO, CG - CO), ws, wr)

    def peer(d):
        return lax.rem(tp + d, TP)

    def part(b, owner):
        return pl.ds(pl.multiple_of(b * L + owner * sub, sub), sub)

    def kept(b):
        return rows_of(b, sub)

    def square_to(d):
        return remote(sqall.at[tp], sqall.at[tp], sqs.at[d], sqr.at[tp], tp=peer(d))

    def square_from(d):
        return remote(sqall.at[tp], sqall.at[peer(d)], sqs.at[d], sqr.at[peer(d)], tp=peer(d))

    first = SquareScatter((a1, a2, a3, a4), (s1, r1))
    norms = SquareGather(low_two, part, (ns, nr))
    gradients = SquareScatter((b1, b2, b3, b4), (gs, gr))
    residuals = SquareGather(grad_res, part, (hs, hr))

    sqall[tp] = square[...]
    for d in range(1, TP):
        square_to(d).start()
    limit = length[0] - c * t

    def mask_seed(i):
        rows = rows_of(i)
        live = iota((L, D), 0) + i * L < limit
        seed[rows, :] = jnp.where(live, cot[rows, :].astype(f32), 0.0).astype(bf16)

    for d in range(1, TP):
        square_from(d).wait_recv()
    total_square[...] = sqall[0] + sqall[1] + sqall[2] + sqall[3]
    gain = gains[1:2, :]
    gain_grad[...] = jnp.zeros_like(gain_grad)

    def mix(b):
        rows = rows_of(b)
        scale = lax.rsqrt(total_square[:, rows] / DI + EPS)
        column = wide(tn(scale, first_row(), HI), D)
        partial[rows, :] = nt(gl[rows, :], wb[:, CO:CW]) * column + nt(att[rows, :], wb[:, CW:CG])
        first.start(b, partial, lambda owner: part(b, owner))

    def norm(b):
        own = part(b, tp)
        hid_own[kept(b), :] = hid[own, :]
        acc = hid[own, :].astype(f32) + partial[own, :] + first.finish(b)
        scale = lax.rsqrt(jnp.mean(acc * acc, -1, keepdims=True) + EPS)
        scale_keep[kept(b), :] = jnp.broadcast_to(scale, (sub, 128))
        u = acc * scale
        unit[kept(b), :] = u
        low_two[own, :] = (u * gain).astype(bf16)
        norms.start(b)

    def act_grad(i):
        rows = rows_of(i)
        grad_act[rows, :] = nn(seed[rows, :], wm[:, FFL:])

    def hidden_units(b):
        rows = rows_of(b)
        norms.finish(b)
        low = low_two[rows, :]
        gate, up = nn(low, wg[...]), nn(low, wm[:, 0:FFL])
        sig = sigmoid(gate)
        silu = gate * sig
        hidden_act = (silu * up).astype(bf16)
        act[rows, :] = hidden_act
        ga = grad_act[rows, :]
        g1 = (ga * up * (sig * (1.0 + gate * (1.0 - sig)))).astype(bf16)
        g2 = (ga * silu).astype(bf16)
        gg[rows, :] = g1
        gu[rows, :] = g2
        back[...] = nt(g1, wg[...]) + nt(g2, wm[:, 0:FFL])
        gown[kept(b), :] = back[kept(tp), :]
        gradients.start(b, back, kept)
        partial[rows, :] = partial[rows, :] + nt(hidden_act, wm[:, FFL:])
        mine = rows_of(tp, width)
        osend[0, rows, :] = (partial[rows, mine] + hid[rows, mine].astype(f32)).astype(bf16)
        for e in range(1, TP):
            osend[e, rows, :] = partial[rows, rows_of(peer(e), width)].astype(bf16)

    def norm_back(b):
        own = part(b, tp)
        g = gown[kept(b), :] + gradients.finish(b)
        u = unit[kept(b), :]
        gain_grad[...] += jnp.broadcast_to(jnp.sum(g * u, 0, keepdims=True), (8, D))
        weighted = g * gain
        mean = jnp.mean(weighted * u, -1, keepdims=True)
        res = seed[own, :].astype(f32) + scale_keep[kept(b), 0:1] * (weighted - u * mean)
        grad_own[kept(b), :] = res
        grad_res[own, :] = res.astype(bf16)
        residuals.start(b)

    def weight_grads(i):
        feats = rows_of(i)
        low = low_two[:, feats]
        grads[feats, CG:CU] = tn(low, gg[...]).astype(bf16)
        grads[feats, CU:CD] = tn(low, gu[...]).astype(bf16)

    def down_grads(i):
        feats = rows_of(i)
        grads[feats, CD:CB] = tn(seed[:, feats], act[...]).astype(bf16)

    def out_back(b):
        rows = rows_of(b)
        residuals.finish(b)
        square_scale = lax.rsqrt(total_square[:, rows] / DI + EPS)
        column = wide(tn(square_scale, first_row(), HI), D)
        got = grad_res[rows, :]
        low = (column * got.astype(f32)).astype(bf16)
        proj[rows, :] = low
        product = nn(low, wb[:, CO:CW])
        ggl[rows, :] = product
        dots[:, rows] = nt(jnp.ones((8, WI), f32), product * gl[rows, :].astype(f32), HI)
        grad_att[rows, :] = nn(got, wb[:, CW:CG]).astype(bf16)

    def stage(s, delay, act_on):
        @pl.when((s >= delay) & (s < delay + blocks))
        def go():
            act_on(s - delay)

    def step(s):
        stage(s, 0, mix)

        @pl.when(s == 1)
        def masks():
            moves.get("hid", "cot", "wg")
            loop(blocks, mask_seed)

        stage(s, 1, first.relay)
        stage(s, 2, norm)
        stage(s, 3, norms.relay)

        @pl.when(s == 3)
        def weights():
            gather.forward()
            gather.finish()
            loop(blocks, act_grad)

        stage(s, 4, hidden_units)

        @pl.when(s == blocks + 4)
        def fill():
            moves.put("osend")
            loop(D // L, weight_grads)

        stage(s, 5, gradients.relay)
        stage(s, 6, norm_back)

        @pl.when(s == blocks + 5)
        def more():
            loop(D // L, down_grads)
            mlp_sum.start()

        @pl.when(s == blocks + 6)
        def norms_done():
            moves.put("grad_own")

        stage(s, 7, residuals.relay)
        stage(s, 8, out_back)

    loop(blocks + 8, step)

    def out_grads(i):
        feats = rows_of(i)
        grads[feats, CO:CW] = tn(proj[:, feats], gl[...]).astype(bf16)
        grads[feats, CW:CG] = tn(grad_res[:, feats], att[...]).astype(bf16)

    loop(D // L, out_grads)
    out_sum.start()
    mlp_sum.finish()
    out_sum.finish()

    def sent(b):
        for exchange in (first, norms, gradients, residuals):
            exchange.sent(b)

    loop(blocks, sent)
    for d in range(1, TP):
        square_to(d).wait_send()


def ffn(shards, *args):
    t = args[0].shape[0]
    blocks, sub = t // L, L // TP
    kept = blocks * sub
    out = [
        ((TP, t, D // TP), bf16),
        ((kept, D), f32),
        ((shards, D // (2 * shards), CB), bf16),
        ((kept, D), bf16),
        ((8, D), f32),
        ((8, t), f32),
        ((t, WI), f32),
        ((t, 128), bf16),
        ((8, t), f32),
    ]
    dma = pltpu.SemaphoreType.DMA
    scratch = (
        [
            pltpu.VMEM((D, CB), bf16),
            pltpu.VMEM((t, D), bf16),
            pltpu.VMEM((t, D), f32),
            pltpu.VMEM((t, D), bf16),
            pltpu.VMEM((t, D), bf16),
            pltpu.VMEM((t, D), bf16),
            pltpu.VMEM((t, FFL), f32),
            pltpu.VMEM((t, FFL), bf16),
            pltpu.VMEM((t, FFL), bf16),
            pltpu.VMEM((t, FFL), bf16),
            pltpu.VMEM((kept, D), f32),
            pltpu.VMEM((L, D), f32),
            pltpu.VMEM((kept, D), f32),
            pltpu.VMEM((kept, 128), f32),
            pltpu.VMEM((TP, 8, t), f32),
            pltpu.VMEM((D, 2 * FFL), bf16),
            pltpu.VMEM((D // (2 * shards), 2 * FFL), bf16),
        ]
        + SquareScatter.scratch(blocks, sub) * 2
        + Gather.sems(shards)
        + [dma((shards,))] * 4
        + [dma((TP,))] * 2
        + [dma((TP, blocks))] * 8
    )
    return call_staged(
        functools.partial(ffn_kernel, shards),
        args,
        out,
        {"hid": 0, "cot": 1, "wg": 6},
        {"osend": 0, "grad_own": 1},
        scratch,
        compiler_params=pltpu.CompilerParams(
            collective_id=2, has_side_effects=True, vmem_limit_bytes=VLIMIT
        ),
        name="feed_forward",
    )


def backward_kernel(
    shards, moves,
    ggl, grad_att, dots_in, total_square, chip, osend,
    pre, cin, hist, q_low, kk, vv, att, lse_row, ssd, start, steps_in, cum_in, tot_in, dt_raw, z_in,
    taps, prm, chan, normed, wf1, wf2, hid_own, grad_own, gains, gain_two, table_all, length,
    output, low, grad_e, grad_l, grad_b, shared, vecs,
    table, own_out, lin, small, orecv, dots, dk, dv, dy, dpre, ends, dstate, carry, kv_out, kv_in, pad,
    edge_out, edge_in, gown, back, gain_one, grads_e, grads_l, misc, misc_low, misc_sum, shsend,
    vec_sib, vec_z,
    ln0, ln1, ln2, ln3, ln4, ln5,
    e0, e1, e2, e3, e4, e5, e6, e7, e8,
    l0, l1, l2, l3, l4, l5, l6, l7, l8,
    m0, m1, m2, m3, m4, m5, m6, m7, m8,
    g0, g1, g2, g3,
    table_sem, own_sem, vcs, vcr, vzs, vzr, xs, xr, ts, tr, os, orr, ss, sr, vts, vtr, gs, gr, hs, hr,
):
    z, c, tp = lax.axis_index("shard"), lax.axis_index("ctx"), lax.axis_index("tp")
    t = cin.shape[0]
    blocks, sub = t // L, L // TP
    get_table = pltpu.make_async_copy(table_all.at[rows_of(c, t)], table, table_sem)
    get_table.start()
    greet(shards, True)
    scatter = LineSum(shards, chip, ln0, ln1, ln2, ln3, ln4, ln5)
    scatter0 = Scatter(shards, grads_e, e0, e1, e2, e3, e4, e5, e6, e7, e8)
    scatter1 = Scatter(shards, grads_l, l0, l1, l2, l3, l4, l5, l6, l7, l8)
    scatter2 = Scatter(shards, misc_low, m0, m1, m2, m3, m4, m5, m6, m7, m8)
    moves.get("chip")
    scatter.start()

    def swap(src, dst, i):
        return remote(src, dst, xs.at[i], xr.at[i], ctx=1 - c)

    def peer(d):
        return lax.rem(tp + d, TP)

    def to_all(ref, send, recv, d):
        return remote(ref.at[tp], ref.at[tp], send.at[d], recv.at[tp], tp=peer(d))

    def from_all(ref, send, recv, d):
        return remote(ref.at[tp], ref.at[peer(d)], send.at[d], recv.at[peer(d)], tp=peer(d))

    dots[tp] = dots_in[...]
    for d in range(1, TP):
        to_all(dots, ts, tr, d).start()

    def out_to(d):
        return remote(osend.at[d], orecv.at[TP - 1 - d], os.at[d], orr.at[TP - 1 - d], tp=peer(d))

    def out_from(d):
        return remote(osend.at[d], orecv.at[d - 1], os.at[d], orr.at[d - 1], tp=peer(d))

    get_own = pltpu.make_async_copy(osend.at[0], own_out, own_sem)
    get_own.start()
    for d in range(1, TP):
        out_to(d).start()
    conv_grads = small.at[:, 0:CH]
    chan_grads = small.at[:, CH : CH + WI]
    head_grads = small.at[:, CH + WI : CH + WI + 128]
    expand = spread()
    low128 = low_lanes((L, 128))
    small[...] = jnp.zeros_like(small)
    for d in range(1, TP):
        from_all(dots, ts, tr, d).wait_recv()

    def gated_back(i):
        rows = rows_of(i)
        both = dots[0, :, rows] + dots[1, :, rows] + dots[2, :, rows] + dots[3, :, rows]
        share = both / ((total_square[:, rows] / DI + EPS) * DI)
        column = wide(tn(share, first_row(), HI), WI)
        zz, y = z_in[rows, :].astype(f32), ssd[rows, :].astype(f32)
        sig = sigmoid(zz)
        silu = zz * sig
        gated = y * silu
        product = ggl[rows, :]
        chan_grads[0:1, :] += jnp.sum(product * gated, 0, keepdims=True)
        grad_gated = product * chan[0:1, :] - column * gated
        grad_y = grad_gated * silu
        dy[rows, :] = grad_y
        lin[rows, CZ:CX] = (grad_gated * y * (sig * (1.0 + zz * (1.0 - sig)))).astype(bf16)
        v = pre[rows, WI + N : CH]
        out_map = (v * sigmoid(v)).astype(bf16)
        ends[i] = tn(out_map, (nn(jnp.exp(cum_in[rows, :]), expand, HI) * grad_y).astype(bf16))

    loop(blocks, gated_back)
    dstate[...] = jnp.zeros_like(dstate)

    def chain(k):
        i = blocks - 1 - k
        add = ends[i]
        ends[i] = dstate[...]
        dstate[...] = nn(jnp.exp(tot_in[i]), expand, HI)[0:1, :] * dstate[...] + add

    loop(blocks, chain)
    states = swap(dstate, carry, 0)
    states.start()

    scale = HD ** (-0.5)
    limit = length[0] - c * t
    dk[...] = jnp.zeros_like(dk)
    dv[...] = jnp.zeros_like(dv)
    get_table.wait()
    moves.get("grad_att", "q_low", "kk", "vv", "att", "lse_row")
    head_of = ((iota((8, 128), 1) // HD) == iota((8, 128), 0)).astype(f32)

    def stacked(v):
        return jnp.concatenate([own_half(v, 0), own_half(v, 1)], axis=0).astype(bf16)

    def side_by_side(v):
        return jnp.concatenate([v[0:1, :], v[1:2, :]], axis=1)

    for i in range(blocks):
        rows = pl.ds(i * L, L)
        width = (i + 1) * L
        q2 = stacked(q_low[rows, :].astype(f32))
        go = grad_att[rows, :].astype(f32)
        go2 = stacked(go)
        row_dot = side_by_side(nt(head_of, go * att[rows, :], HI))
        logs = side_by_side(lse_row[:, rows])
        turn = rotary_of(table, rows)

        def keys_of(part, size, masked):
            k, v = kk[part, 0:size, :], vv[part, 0:size, :]
            s = nt(k, q2) * scale - logs
            if masked:
                at = iota(s.shape, 1) % L + i * L
                row = iota(s.shape, 0)
                s = jnp.where((row <= at) & (row < limit), s, FILL)
            p = jnp.exp(s)
            ds = (p * (nt(v, go2) - row_dot)).astype(bf16)
            dv[part, 0:size, :] += nn(p.astype(bf16), go2)
            dk[part, 0:size, :] += nn(ds, q2)
            out = tn(ds, k) * scale
            out = jnp.where(low128, out[:L], out[L:])
            return out * turn[0] - swap_half(out) * turn[1]

        back[:, 0:128] = keys_of(0, width, True)

        @pl.when(c > 0)
        def earlier():
            back[:, 0:128] += keys_of(1, t, False)

        lin[rows, CQ:CK] = back[:, 0:128].astype(bf16)
        if i == 1:
            scatter.relay()

    def key_values(part, rows):
        gk, gv = dk[part, rows, :] * scale, dv[part, rows, :]
        return jnp.where(low128, gk + pltpu.roll(gk, 64, 1), gv + pltpu.roll(gv, 64, 1))

    def pack(i):
        rows = rows_of(i)
        kv_out[rows, :] = key_values(1, rows).astype(bf16)

    loop(blocks, pack)
    pairs = swap(kv_out, kv_in, 1)
    pairs.start()

    moves.get("start", "steps_in", "dt_raw", "cin", "normed", "wf1", "wf2", "hid_own", "grad_own")
    pad[0:16, :] = jnp.concatenate([jnp.zeros((8, CH), f32), hist[...]], axis=0).astype(bf16)

    def fill(i):
        pad[pl.ds(pl.multiple_of(i * L + 16, 16), L), :] = cin[rows_of(i), :]

    loop(blocks, fill)
    states.wait_recv()
    carry[...] = jnp.where(c == 0, carry[...], 0.0)

    def add_carry(k):
        i = blocks - 1 - k
        ends[i] = ends[i] + carry[...]
        carry[...] = nn(jnp.exp(tot_in[i]), expand, HI)[0:1, :] * carry[...]

    loop(blocks, add_carry)
    mask = iota((L, L), 0) >= iota((L, L), 1)
    ones = lower_ones()
    lane = iota((L, 128), 1)

    def fold(v):
        return nt(v, expand, HI)

    def scan_back(i):
        rows = rows_of(i)
        v = pre[rows, :]
        sig = sigmoid(v)
        a = v * sig
        x = a[:, :WI]
        xl, bl, cl = x.astype(bf16), a[:, WI : WI + N].astype(bf16), a[:, WI + N :].astype(bf16)
        steps, cum = steps_in[rows, :], cum_in[rows, :]
        tot = cum[L - 1 : L, :]
        ecum, wend = jnp.exp(cum), jnp.exp(tot - cum)
        weight = wend * steps
        ecum_x, weight_x = nn(ecum, expand, HI), nn(weight, expand, HI)
        grad_y = dy[rows, :]
        dyl = grad_y.astype(bf16)
        s0, d1 = start[i], ends[i]
        s0l, d1l = s0.astype(bf16), d1.astype(bf16)
        bd, cs = nn(bl, d1l), nn(cl, s0l)
        dw = fold(x * bd)
        crossing = jnp.broadcast_to(jnp.sum(s0 * d1, 0, keepdims=True), (8, WI))
        dtot = jnp.sum(weight * dw, 0, keepdims=True) + jnp.exp(tot) * fold(crossing)[0:1, :]
        gram = nt(cl, bl)
        cum_t, steps_t = cum.T, steps.T
        dgram = jnp.zeros((L, L), f32)
        row_sums = jnp.zeros((L, 128), f32)
        col_sums, inner = [], []
        for pair in range(HL // 2):
            xp, dp = pair_columns(xl, pair), pair_columns(dyl, pair)
            dpf = pair_columns(grad_y, pair)
            halves = []
            for half in range(2):
                h = 2 * pair + half
                decay = jnp.exp(jnp.where(mask, cum[:, h : h + 1] - cum_t[h : h + 1, :], FILL))
                q = nt(own_half(dpf, half).astype(bf16), xp)
                mixed = gram * decay
                srow = steps_t[h : h + 1, :]
                f = mixed * q
                col_sums.append(jnp.sum(f, 0, keepdims=True))
                row_sums = jnp.where(lane == h, jnp.sum(f * srow, -1, keepdims=True), row_sums)
                dgram = dgram + decay * srow * q
                halves.append(tn((mixed * srow).astype(bf16), dp))
            inner.append(jnp.where(low128, halves[0], halves[1]))
        cols = jnp.concatenate(col_sums + [jnp.zeros((128 - HL, L), f32)], axis=0).T
        dcum = fold(grad_y * cs) * ecum - weight * dw + row_sums - steps * cols
        dcum = dcum + jnp.where(iota((L, 128), 0) == L - 1, dtot, 0.0)
        drate = tn(ones, dcum, HI)
        rate_of = prm[1:2, :]
        raw = dt_raw[rows, :] + prm[0:1, :]
        dstep = (wend * dw + cols + drate * rate_of) * sigmoid(raw)
        dstep = jnp.where(lane < HL, dstep, 0.0)
        lin[rows, CS:CA] = dstep.astype(bf16)
        head_grads[0:1, :] += jnp.sum(dstep, 0, keepdims=True)
        head_grads[1:2, :] += jnp.sum(drate * steps * rate_of, 0, keepdims=True)
        head_grads[2:3, :] += jnp.sum(fold(grad_y * x), 0, keepdims=True)
        slope = sig * (1.0 + v * (1.0 - sig))
        dx = chan[1:2, :] * grad_y + weight_x * bd + jnp.concatenate(inner, axis=1)
        dg = dgram.astype(bf16)
        db = tn(dg, cl) + nt((weight_x * x).astype(bf16), d1l)
        dc = nn(dg, bl) + nt((ecum_x * grad_y).astype(bf16), s0l)
        dpre[rows, 0:WI] = dx * slope[:, :WI]
        dpre[rows, WI : WI + N] = db * slope[:, WI : WI + N]
        dpre[rows, WI + N : CH] = dc * slope[:, WI + N :]

    edge = swap(edge_out, edge_in, 2)

    def keys_back(i):
        rows = rows_of(i)
        v = key_values(0, rows) + kv_in[rows, :].astype(f32)
        cosine, sine = rotary_of(table, rows)
        cosine = jnp.where(low128, cosine, 1.0)
        sine = jnp.where(low128, sine, 0.0)
        lin[rows, CK:CS] = (v * cosine - swap_half(v) * sine).astype(bf16)

    def conv_back(b):
        rows = rows_of(b)
        later = dpre[pl.ds(pl.multiple_of(b * L, L), L + 8), :]
        earlier = pad[pl.ds(pl.multiple_of(b * L, L), L + 16), :].astype(f32)
        g = later[0:L]
        conv_grads[4:5, :] += jnp.sum(g, 0, keepdims=True)
        total = jnp.zeros_like(g)
        for j in range(CONVW):
            total = total + taps[j : j + 1, :] * later[CONVW - 1 - j : CONVW - 1 - j + L]
            conv_grads[j : j + 1, :] += jnp.sum(g * earlier[13 + j : 13 + j + L], 0, keepdims=True)
        lin[rows, CX:CQ] = total.astype(bf16)

    def part(b, owner):
        return pl.ds(pl.multiple_of(b * L + owner * sub, sub), sub)

    def kept(b):
        return rows_of(b, sub)

    grads_in = SquareScatter((g0, g1, g2, g3), (gs, gr))
    lows = SquareGather(low, part, (hs, hr))

    def product(b):
        rows = rows_of(b)
        back[...] = nt(lin[rows, CZ:CQ], wf2[...]) + nt(lin[rows, CQ:CA], wf1[...])
        gown[kept(b), :] = back[kept(tp), :]
        grads_in.start(b, back, kept)

    gain_one[...] = jnp.zeros_like(gain_one)

    def norm_back(b):
        own = part(b, tp)
        g = gown[kept(b), :] + grads_in.finish(b)
        x = hid_own[kept(b), :].astype(f32)
        scale = lax.rsqrt(jnp.mean(x * x, -1, keepdims=True) + EPS)
        unit = x * scale
        gain_one[...] += jnp.broadcast_to(jnp.sum(g * unit, 0, keepdims=True), (8, D))
        weighted = g * gains[0:1, :]
        mean = jnp.mean(weighted * unit, -1, keepdims=True)
        low[own, :] = (grad_own[kept(b), :] + scale * (weighted - unit * mean)).astype(bf16)
        lows.start(b)

    def early_grads(i):
        feats = rows_of(i)
        grads_e[feats, 0:WI] = tn(normed[:, feats], lin[:, CZ:CX]).astype(bf16)
        grads_e[feats, WI:] = tn(normed[:, feats], lin[:, CQ:CS]).astype(bf16)

    def step(k):
        @pl.when(k < blocks)
        def scan():
            scan_back(lax.rem(2 * blocks - 1 - k + c, blocks))

        @pl.when(k == 0)
        def first():
            @pl.when(c > 0)
            def give():
                edge_out[...] = dpre[0:8, :]
                edge.start()

            pairs.wait_recv()
            loop(blocks, keys_back)
            loop(D // L, early_grads)
            scatter0.start()
            dpre[pl.ds(t, 8), :] = jnp.zeros((8, CH), f32)

            @pl.when(c == 0)
            def take():
                edge.wait_recv()
                dpre[pl.ds(t, 8), :] = edge_in[...]

        @pl.when(k >= 1)
        def there():
            conv_back(blocks - k)
            product(blocks - k)

        @pl.when(k == 1)
        def on():
            scatter0.middle()

        @pl.when(k == 3)
        def further():
            scatter0.relay()

        @pl.when(k >= 2)
        def over():
            grads_in.relay(blocks + 1 - k)

        @pl.when(k >= 3)
        def again():
            norm_back(blocks + 2 - k)

        @pl.when(k >= 4)
        def last():
            lows.relay(blocks + 3 - k)

    loop(blocks + 1, step)
    vec_core = remote(small, vec_sib, vcs.at[0], vcr.at[0], ctx=1 - c)
    vec_core.start()

    def weight_grads(i):
        feats = rows_of(i)
        grads_l[feats, :] = tn(normed[:, feats], lin[:, CX:CQ]).astype(bf16)
        misc[feats, :] = tn(normed[:, feats], lin[:, CS:CA])

    loop(D // L, weight_grads)
    scatter1.start()
    grads_in.relay(0)
    norm_back(1)
    lows.relay(2)

    def vec_to_shard(k):
        zz = lax.rem(z + k, shards)
        return remote(vec_z.at[z], vec_z.at[z], vzs.at[zz], vzr.at[z], shard=zz)

    def vec_from_shard(k):
        zz = lax.rem(z + k, shards)
        return remote(vec_z.at[z], vec_z.at[zz], vzs.at[zz], vzr.at[zz], shard=zz)

    vec_core.wait_recv()
    vec_z[z] = small[...] + vec_sib[...]
    loop(shards - 1, lambda k: vec_to_shard(k + 1).start())
    scatter1.middle()
    norm_back(0)
    lows.relay(1)
    gain_rows = jnp.where(iota((8, D), 0) == 0, gain_one[...], gain_two[...])
    row, lane8 = iota((8, 128), 0), iota((8, 128), 1)
    pick = ((row < 2) & (lane8 == GAIN_COL + row)).astype(f32)
    misc_low[...] = (misc[...] + tn(gain_rows, pick, HI)).astype(bf16)
    scatter2.start()
    get_own.wait()
    total = own_out[...].astype(f32)
    for d in range(1, TP):
        out_from(d).wait_recv()
        total = total + orecv[d - 1].astype(f32)
    output[...] = total.astype(bf16)
    scatter1.relay()
    scatter2.middle()
    lows.relay(0)
    loop(shards - 1, lambda k: vec_from_shard(k + 1).wait_recv())
    vecs[tp] = lax.fori_loop(1, shards, lambda k, total: total + vec_z[k], vec_z[0])
    for d in range(1, TP):
        to_all(vecs, vts, vtr, d).start()
    scatter.finish(grad_b)
    moves.put("grad_b")
    scatter2.relay()
    scatter0.finish(grad_e)
    scatter1.finish(grad_l)
    scatter2.finish(misc_sum)
    few = grad_e.shape[0] // TP
    for i in range(TP):
        shsend[i, :, 0:256] = grad_l[i * few : (i + 1) * few, WI:CH]
        shsend[i, :, 256:384] = grad_e[i * few : (i + 1) * few, WI + 128 : CH]
        shsend[i, :, 384:512] = misc_sum[i * few : (i + 1) * few, :]

    def share_to(d):
        return remote(shsend.at[peer(d)], shared.at[tp], ss.at[d], sr.at[tp], tp=peer(d))

    def share_from(d):
        return remote(shsend.at[peer(d)], shared.at[peer(d)], ss.at[d], sr.at[peer(d)], tp=peer(d))

    for d in range(1, TP):
        share_to(d).start()
    shared[tp] = shsend[tp]

    def arrived(b):
        lows.finish(b)
        lows.sent(b)
        grads_in.sent(b)

    loop(blocks, arrived)
    for d in range(1, TP):
        share_from(d).wait_recv()
        from_all(vecs, vts, vtr, d).wait_recv()

    @pl.when(c > 0)
    def given():
        edge.wait_send()

    for copy in (states, pairs, vec_core):
        copy.wait_send()
    loop(shards - 1, lambda k: vec_to_shard(k + 1).wait_send())
    for d in range(1, TP):
        to_all(dots, ts, tr, d).wait_send()
        out_to(d).wait_send()
        share_to(d).wait_send()
        to_all(vecs, vts, vtr, d).wait_send()


def backward(shards, *args):
    t = args[0].shape[0]
    rows = D // (2 * shards)
    blocks, sub = t // L, L // TP
    vec = (8, CH + WI + 128)
    out = [
        ((t, D // TP), bf16),
        ((t, D), bf16),
        ((rows, CH), f32),
        ((rows, CH), f32),
        ((rows, CB), f32),
        ((TP, rows // TP, 512), f32),
        ((TP, *vec), f32),
    ]
    dma = pltpu.SemaphoreType.DMA
    scratch = (
        [
            pltpu.VMEM((t, 128), f32),
            pltpu.VMEM((t, D // TP), bf16),
            pltpu.VMEM((t, CA), bf16),
            pltpu.VMEM(vec, f32),
            pltpu.VMEM((TP - 1, t, D // TP), bf16),
            pltpu.VMEM((TP, 8, t), f32),
            pltpu.VMEM((2, t, 128), f32),
            pltpu.VMEM((2, t, 128), f32),
            pltpu.VMEM((t, WI), f32),
            pltpu.VMEM((t + 8, CH), f32),
            pltpu.VMEM((t // L, N, WI), f32),
            pltpu.VMEM((N, WI), f32),
            pltpu.VMEM((N, WI), f32),
            pltpu.VMEM((t, 128), bf16),
            pltpu.VMEM((t, 128), bf16),
            pltpu.VMEM((t + 16, CH), bf16),
            pltpu.VMEM((8, CH), f32),
            pltpu.VMEM((8, CH), f32),
            pltpu.VMEM((blocks * sub, D), f32),
            pltpu.VMEM((L, D), f32),
            pltpu.VMEM((8, D), f32),
            pltpu.VMEM((D, CH), bf16),
            pltpu.VMEM((D, CH), bf16),
            pltpu.VMEM((D, 128), f32),
            pltpu.VMEM((D, 128), bf16),
            pltpu.VMEM((rows, 128), f32),
            pltpu.VMEM((TP, rows // TP, 512), f32),
            pltpu.VMEM(vec, f32),
            pltpu.VMEM((shards, *vec), f32),
        ]
        + LineSum.scratch(shards, D, CB)
        + Scatter.scratch(shards, D, CH)
        + Scatter.scratch(shards, D, CH)
        + Scatter.scratch(shards, D, 128)
        + SquareScatter.scratch(blocks, sub)
        + [dma(()), dma(()), dma((1,)), dma((1,)), dma((shards,)), dma((shards,)), dma((3,)), dma((3,))]
        + [dma((TP,))] * 8
        + [dma((TP, blocks))] * 4
    )
    return call_staged(
        functools.partial(backward_kernel, shards),
        args,
        out,
        dict(zip(BACKWARD_LATE, BACKWARD_AT)),
        {"grad_b": 4},
        scratch,
        left=(5, len(args) - 2),
        compiler_params=pltpu.CompilerParams(
            collective_id=3, has_side_effects=True, vmem_limit_bytes=VMOST
        ),
        name="mix_backward",
    )


def pack_kernel(
    low, grad_e, grad_l, grad_b, shared, vecs,
    grad_hidden, g_z, g_x, g_q, g_gate, g_up, g_out, g_o, g_down, g_shared, g_dt, gains,
    g_conv, g_chan, g_heads,
):
    grad_hidden[...] = low[...].astype(f32)

    @pl.when(pl.program_id(0) == 0)
    def rest():
        g_z[...] = grad_e[:, 0:WI]
        g_x[...] = grad_l[:, 0:WI]
        g_q[...] = grad_e[:, WI : WI + 128]
        g_gate[...] = grad_b[:, CG:CU]
        g_up[...] = grad_b[:, CU:CD]
        one = eye(grad_b.shape[0]).astype(f32)
        g_out[...] = tn(grad_b[:, CO:CW], one, HI)
        g_o[...] = tn(grad_b[:, CW:CG], one, HI)
        g_down[...] = tn(grad_b[:, CD:CB], one, HI)
        first, second = shared[0] + shared[1], shared[2] + shared[3]
        both = first + second
        g_shared[:, 0 : 2 * N] = both[:, 0 : 2 * N]
        kv1, kv2 = first[:, 256:384], second[:, 256:384]
        low_half = low_lanes(kv1.shape)
        g_shared[:, 2 * N : 2 * N + 128] = jnp.where(low_half, kv1, pltpu.roll(kv2, 64, 1))
        g_shared[:, 2 * N + 128 :] = jnp.where(low_half, pltpu.roll(kv1, 64, 1), kv2)
        gains[...] = tn(both[:, 384:512], eye(both.shape[0]).astype(f32), HI)[
            GAIN_COL : GAIN_COL + 8
        ]
        steps = jnp.zeros((both.shape[0], 128), f32)
        heads = jnp.zeros((8, 128), f32)
        g_chan[...] = jnp.zeros_like(g_chan)
        for i in range(TP):
            lane = iota(steps.shape, 1) // HL == i
            steps = jnp.where(lane, pltpu.roll(shared[i, :, 384:512], i * HL, 1), steps)
            lane = iota(heads.shape, 1) // HL == i
            heads = jnp.where(lane, pltpu.roll(vecs[i, :, CH + WI : CH + WI + 128], i * HL, 1), heads)
            mine = slice(i * WI, (i + 1) * WI)
            g_conv[:, mine] = vecs[i, 0:CONVW, 0:WI]
            g_chan[0:1, mine] = vecs[i, CONVW : CONVW + 1, 0:WI]
            g_chan[1:2, mine] = vecs[i, 0:1, CH : CH + WI]
        maps = vecs[0, :, WI:CH] + vecs[1, :, WI:CH] + vecs[2, :, WI:CH] + vecs[3, :, WI:CH]
        g_conv[:, DI:] = maps[0:CONVW]
        g_chan[0:1, DI:] = maps[CONVW : CONVW + 1]
        g_dt[...] = steps[:, 0:H]
        g_heads[...] = heads


def pack(low, grad_e, grad_l, grad_b, shared, vecs):
    t, r, few = low.shape[0], grad_e.shape[0], shared.shape[1]
    out = [
        (t, D), (r, WI), (r, WI), (r, 128), (r, FFL), (r, FFL), (WI, r), (128, r), (FFL, r),
        (few, 512), (few, H), (8, few), (CONVW, DI + 2 * N), (8, DI + 2 * N), (8, 128),
    ]
    rows = pl.BlockSpec((L, D), lambda i: (i, 0))

    def whole(shape):
        return pl.BlockSpec(shape, lambda i: (0,) * len(shape))

    return pl.pallas_call(
        pack_kernel,
        grid=(t // L,),
        out_shape=[jax.ShapeDtypeStruct(o, f32) for o in out],
        in_specs=[rows] + [whole(v.shape) for v in (grad_e, grad_l, grad_b, shared, vecs)],
        out_specs=[rows] + [whole(o) for o in out[1:]],
        compiler_params=pltpu.CompilerParams(vmem_limit_bytes=VLIMIT),
        name="lay_out",
    )(low, grad_e, grad_l, grad_b, shared, vecs)


def rotary_table(count):
    inverse = rope_base ** (-2.0 * np.arange(HD // 2, dtype=np.float32) / HD)
    angles = np.arange(count, dtype=np.float32)[:, None] * inverse.astype(np.float32)[None, :]
    both = np.concatenate([np.cos(angles), np.sin(angles)], axis=1)
    return np.tile(both, (1, 2)).astype(np.float32)


def local(
    hidden, cotangent, lengths, norm1_gain, w_z, w_x, w_shared, w_dt, dt_bias, a_log, d_skip,
    conv_w, conv_b, gated_gain, w_out, w_q, w_o, norm2_gain, w_gate, w_up, w_down,
):
    t = hidden.shape[1]
    shards = lax.axis_size("shard")
    hid, cot = hidden[0], cotangent[0]
    width = conv_w.shape[1]

    def fit(v):
        return jnp.pad(v, (0, width - v.shape[0]))[None]

    nothing = jnp.zeros((2, width), bf16)
    small = jnp.concatenate(
        [conv_w, conv_b[None], fit(gated_gain), nothing]
        + [fit(v) for v in (dt_bias, a_log, d_skip)]
        + [nothing, nothing, nothing[:1]],
        axis=0,
    )
    table = jnp.asarray(rotary_table(lax.axis_size("ctx") * t))
    (
        wf1, wf2, wo, wg, normed, gains, z, cin, dt, taps, prm, chan,
        pre, hist, q_low, kk, vv, att, att_low, lse_row, ssd, start, steps, cum, tot, gl, square,
    ) = forward(
        shards, hid, w_z, w_x, w_shared, w_dt.T, w_q, w_out, w_o, w_gate,
        norm1_gain[None], norm2_gain[None], small, table, lengths,
    )
    osend, grad_own, chip, hid_own, gain_two, total_square, ggl, grad_att, dots = ffn(
        shards, hid, cot, gl, att_low, square, wo, wg, w_up, w_down, gains, lengths
    )
    output, grad_hidden, grad_e, grad_l, grad_b, shared, vecs = backward(
        shards, ggl, grad_att, dots, total_square, chip, osend, pre, cin, hist, q_low, kk, vv, att,
        lse_row, ssd, start, steps, cum, tot, dt, z, taps, prm, chan, normed, wf1, wf2,
        hid_own, grad_own, gains, gain_two, table, lengths,
    )
    (
        grad_full, g_z, g_x, g_q, g_gate, g_up, g_out, g_o, g_down, g_shared, g_dt, g_gains,
        g_conv, g_chan, g_heads,
    ) = pack(grad_hidden, grad_e, grad_l, grad_b, shared, vecs)
    return (
        output[None],
        grad_full[None],
        g_gains[0],
        g_z,
        g_x,
        g_shared,
        g_dt,
        g_heads[0, :H],
        g_heads[1, :H],
        g_heads[2, :H],
        g_conv,
        g_chan[0],
        g_chan[1, :DI],
        g_out,
        g_q,
        g_o,
        g_gains[1],
        g_gate,
        g_up,
        g_down,
    )


def solution(mesh):
    placed = (
        P("shard", "ctx", None),
        P("shard", "ctx", None),
        P("shard"),
        P(("shard", "ctx")),
        P(("shard", "ctx"), "tp"),
        P(("shard", "ctx"), "tp"),
        P(("shard", "ctx"), None),
        P(("shard", "ctx"), None),
        P(),
        P(),
        P(),
        P(),
        P(),
        P(),
        P("tp", ("shard", "ctx")),
        P(("shard", "ctx"), "tp"),
        P("tp", ("shard", "ctx")),
        P(("shard", "ctx")),
        P(("shard", "ctx"), "tp"),
        P(("shard", "ctx"), "tp"),
        P("tp", ("shard", "ctx")),
    )
    return jax.shard_map(
        local,
        mesh=mesh,
        in_specs=placed,
        out_specs=(
            P("shard", "ctx", "tp"),
            P("shard", "ctx", None),
            P(("shard", "ctx", "tp")),
            P(("shard", "ctx"), "tp"),
            P(("shard", "ctx"), "tp"),
            P(("shard", "ctx", "tp"), None),
            P(("shard", "ctx", "tp"), None),
            P(),
            P(),
            P(),
            P(),
            P(),
            P(),
            P("tp", ("shard", "ctx")),
            P(("shard", "ctx"), "tp"),
            P("tp", ("shard", "ctx")),
            P(("shard", "ctx", "tp")),
            P(("shard", "ctx"), "tp"),
            P(("shard", "ctx"), "tp"),
            P("tp", ("shard", "ctx")),
        ),
        check_vma=False,
    )
```

```python
import functools

import jax
import jax.numpy as jnp
import numpy as np
from jax import lax
from jax.experimental import pallas as pl
from jax.experimental.pallas import tpu as pltpu
from jax.sharding import PartitionSpec as P

H = 24
P_SIZE = 64
N = 128
NQ = 8
KV = 2
HD = 64
CONVW = 4
DI = 1536
D = 1024
FFL = 512
TP = 4
HL = H // TP
WI = HL * P_SIZE
CH = WI + 2 * N
L = 256

CZ, CX, CM, CQ, CK, CS, CA = 0, 384, 768, 1024, 1152, 1280, 1408
GAIN_COL = 24
CO, CW, CG, CU, CD, CB = 0, 384, 512, 1024, 1536, 2048

EPS = 1e-05
rope_base = 10000.0
FILL = -1e30
HI = lax.Precision.HIGHEST
MESH = pl.DeviceIdType.MESH
f32 = jnp.float32
bf16 = jnp.bfloat16
VLIMIT = 60 * 1024 * 1024
VMOST = 63 * 1024 * 1024 + 512 * 1024


def nn(a, b, precision=None):
    return lax.dot_general(
        a, b, (((1,), (0,)), ((), ())), precision=precision, preferred_element_type=f32
    )


def nt(a, b, precision=None):
    return lax.dot_general(
        a, b, (((1,), (1,)), ((), ())), precision=precision, preferred_element_type=f32
    )


def tn(a, b, precision=None):
    return lax.dot_general(
        a, b, (((0,), (0,)), ((), ())), precision=precision, preferred_element_type=f32
    )


def rows_of(index, size=L):
    return pl.ds(pl.multiple_of(index * size, size), size)


def remote(src, dst, send, recv, **where):
    return pltpu.make_async_remote_copy(
        src_ref=src,
        dst_ref=dst,
        send_sem=send,
        recv_sem=recv,
        device_id=where,
        device_id_type=MESH,
    )


def iota(shape, dim):
    return lax.broadcasted_iota(jnp.int32, shape, dim)


def loop(n, body):
    lax.fori_loop(0, n, lambda i, c: (body(i), c)[1], 0)


def greet(shards, tp_too, ctx_too=True, shard_too=True):
    barrier = pltpu.get_barrier_semaphore()
    count = 0
    z, c, t = lax.axis_index("shard"), lax.axis_index("ctx"), lax.axis_index("tp")
    if ctx_too:
        pl.semaphore_signal(barrier, inc=1, device_id={"ctx": 1 - c}, device_id_type=MESH)
        count += 1
    if shard_too:

        def one(k):
            pl.semaphore_signal(
                barrier, inc=1, device_id={"shard": lax.rem(z + 1 + k, shards)}, device_id_type=MESH
            )

        loop(shards - 1, one)
        count += shards - 1
    if tp_too:
        for d in range(1, TP):
            pl.semaphore_signal(
                barrier, inc=1, device_id={"tp": lax.rem(t + d, TP)}, device_id_type=MESH
            )
            count += 1
    pl.semaphore_wait(barrier, count)


class Moves:
    def __init__(self):
        self.gets, self.puts = {}, {}

    def get(self, *names):
        for name in names:
            self.gets[name].wait()

    def put(self, *names):
        for name in names:
            self.puts[name].start()


def call_staged(kernel, args, out, late, early, scratch, left=(), **params):
    spaces = [pl.BlockSpec(memory_space=pltpu.VMEM)] * (len(args) - 1)
    spaces.append(pl.BlockSpec(memory_space=pltpu.SMEM))
    out_spaces = [pl.BlockSpec(memory_space=pltpu.VMEM)] * len(out)
    hbm = pl.BlockSpec(memory_space=pl.ANY)
    for at in (*late.values(), *left):
        spaces[at] = hbm
    for at in early.values():
        out_spaces[at] = hbm
    extra = [pltpu.VMEM(args[at].shape, args[at].dtype) for at in late.values()]
    extra += [pltpu.VMEM(*out[at]) for at in early.values()]
    dma = pltpu.SemaphoreType.DMA
    sems = [dma((len(late),)), dma((len(early),))]

    def body(*refs):
        split = len(args) + len(out)
        given, inner = list(refs[:split]), refs[split : split + len(scratch)]
        held, (get_sem, put_sem) = list(refs[split + len(scratch) : -2]), refs[-2:]
        moves = Moves()
        for n, (name, at) in enumerate(late.items()):
            buffer = held.pop(0)
            moves.gets[name] = pltpu.make_async_copy(given[at], buffer, get_sem.at[n])
            moves.gets[name].start()
            given[at] = buffer
        for n, (name, at) in enumerate(early.items()):
            buffer = held.pop(0)
            moves.puts[name] = pltpu.make_async_copy(buffer, given[len(args) + at], put_sem.at[n])
            given[len(args) + at] = buffer
        kernel(moves, *given, *inner)
        for copy in moves.puts.values():
            copy.wait()

    return pl.pallas_call(
        body,
        out_shape=[jax.ShapeDtypeStruct(*o) for o in out],
        in_specs=spaces,
        out_specs=out_spaces,
        scratch_shapes=list(scratch) + extra + sems,
        **params,
    )(*args)


class Gather:
    def __init__(self, shards, src, dst, zsend, csend, recv, own):
        self.s, self.src, self.dst = shards, src, dst
        self.zsend, self.csend, self.recv, self.own = zsend, csend, recv, own
        self.z, self.c = lax.axis_index("shard"), lax.axis_index("ctx")
        self.r = src.shape[0]

    def block(self, g):
        return self.dst.at[rows_of(g, self.r)]

    def to_shard(self, k):
        g = 2 * self.z + self.c
        return remote(
            self.src,
            self.block(g),
            self.zsend.at[k],
            self.recv.at[g],
            shard=lax.rem(self.z + k, self.s),
        )

    def to_core(self, k):
        zz = lax.rem(self.z + k, self.s)
        g = 2 * zz + self.c
        return remote(self.block(g), self.block(g), self.csend.at[k], self.recv.at[g], ctx=1 - self.c)

    def got(self, k, core):
        zz = lax.rem(self.z + k, self.s)
        g = 2 * zz + core
        return remote(self.block(g), self.block(g), self.csend.at[k], self.recv.at[g], ctx=1 - self.c)

    def start(self):
        keep = pltpu.make_async_copy(self.src, self.block(2 * self.z + self.c), self.own)
        keep.start()
        loop(self.s - 1, lambda k: self.to_shard(k + 1).start())
        keep.wait()
        self.to_core(0).start()

    def forward(self, first=0, last=None):
        def one(k):
            self.got(k + 1, self.c).wait_recv()
            self.to_core(k + 1).start()

        lax.fori_loop(
            first, self.s - 1 if last is None else last, lambda k, carry: (one(k), carry)[1], 0
        )

    def finish(self):
        loop(self.s, lambda k: self.got(k, 1 - self.c).wait_recv())
        loop(self.s, lambda k: self.to_core(k).wait_send())
        loop(self.s - 1, lambda k: self.to_shard(k + 1).wait_send())

    @staticmethod
    def sems(shards):
        dma = pltpu.SemaphoreType.DMA
        return [dma((shards,)), dma((shards,)), dma((2 * shards,)), dma(())]


class LineSum:
    def __init__(self, shards, src, hold, land, fsend, frecv, lsend, lrecv):
        self.s, self.src, self.hold, self.land = shards, src, hold, land
        self.fsend, self.frecv, self.lsend, self.lrecv = fsend, frecv, lsend, lrecv
        self.z = lax.axis_index("shard")

    def place(self, dest, way):
        return dest - 3 if way > 0 else dest

    def onward(self, src, dest, way):
        at = self.place(dest, way)
        return remote(
            src, self.hold.at[at], self.fsend.at[at], self.frecv.at[at], shard=self.z + way
        )

    def straight(self, src, steps, way):
        kind = steps - 1 + (0 if way > 0 else 2)
        return remote(
            src,
            self.land.at[kind],
            self.lsend.at[kind],
            self.lrecv.at[kind],
            shard=self.z + way * steps,
        )

    def each(self, far, two, one, waited):
        for way in (1, -1):
            first = self.z == 0 if way > 0 else self.z == self.s - 1
            now = jnp.logical_not(first) if waited else first

            def along(j, way=way, now=now):
                dest = self.s - 1 - j if way > 0 else j
                distance = (dest - self.z) * way

                @pl.when(now & (distance >= 3))
                def three():
                    far(dest, way)

                @pl.when(now & (distance == 2))
                def both():
                    two(dest, way)

            loop(self.s, along)
            if not waited:
                other = self.z + way

                @pl.when((other >= 0) & (other < self.s))
                def next_one(way=way, other=other):
                    one(other, way)

    def start(self):
        self.each(
            lambda dest, way: self.onward(self.src.at[dest], dest, way).start(),
            lambda dest, way: self.straight(self.src.at[dest], 2, way).start(),
            lambda dest, way: self.straight(self.src.at[dest], 1, way).start(),
            False,
        )

    def relay(self):
        def added(dest, way):
            at = self.place(dest, way)
            self.onward(self.src.at[dest], dest, way).wait_recv()
            own = self.src[dest].astype(f32)
            self.hold[at] = (own + self.hold[at].astype(f32)).astype(bf16)
            return self.hold.at[at]

        self.each(
            lambda dest, way: self.onward(added(dest, way), dest, way).start(),
            lambda dest, way: self.straight(added(dest, way), 2, way).start(),
            None,
            True,
        )

    def finish(self, out):
        out[...] = self.src[self.z].astype(f32)
        for steps in (1, 2):
            for way in (1, -1):
                source = self.z - way * steps

                @pl.when((source >= 0) & (source < self.s))
                def arrived(steps=steps, way=way):
                    kind = steps - 1 + (0 if way > 0 else 2)
                    remote(
                        self.land.at[kind],
                        self.land.at[kind],
                        self.lsend.at[kind],
                        self.lrecv.at[kind],
                        shard=self.z - way * steps,
                    ).wait_recv()
                    out[...] += self.land[kind].astype(f32)

        for waited in (False, True):
            self.each(
                lambda dest, way: self.onward(self.src.at[dest], dest, way).wait_send(),
                lambda dest, way: self.straight(self.src.at[dest], 2, way).wait_send(),
                lambda dest, way: self.straight(self.src.at[dest], 1, way).wait_send(),
                waited,
            )

    @staticmethod
    def scratch(shards, rows, cols):
        dma = pltpu.SemaphoreType.DMA
        far, r = max(shards - 3, 1), rows // (2 * shards)
        return [
            pltpu.VMEM((far, r, cols), bf16),
            pltpu.VMEM((4, r, cols), bf16),
            dma((far,)),
            dma((far,)),
            dma((4,)),
            dma((4,)),
        ]


class Scatter:
    def __init__(self, shards, src, sib, csend, crecv, *line):
        self.s, self.src, self.sib = shards, src, sib
        self.csend, self.crecv = csend, crecv
        self.c = lax.axis_index("ctx")
        self.r = src.shape[0] // (2 * shards)
        self.line = LineSum(shards, sib, *line)

    def to_core(self, k):
        return remote(
            self.src.at[rows_of(2 * k + 1 - self.c, self.r)],
            self.sib.at[k],
            self.csend.at[k],
            self.crecv.at[k],
            ctx=1 - self.c,
        )

    def start(self):
        loop(self.s, lambda k: self.to_core(k).start())

    def middle(self):
        def one(k):
            self.to_core(k).wait_recv()
            both = self.src[rows_of(2 * k + self.c, self.r), :].astype(f32)
            self.sib[k] = (both + self.sib[k].astype(f32)).astype(bf16)

        loop(self.s, one)
        self.line.start()

    def relay(self):
        self.line.relay()

    def finish(self, out):
        self.line.finish(out)
        loop(self.s, lambda k: self.to_core(k).wait_send())

    @staticmethod
    def scratch(shards, rows, cols):
        dma = pltpu.SemaphoreType.DMA
        block = pltpu.VMEM((shards, rows // (2 * shards), cols), bf16)
        return [block, dma((shards,)), dma((shards,))] + LineSum.scratch(shards, rows, cols)


class ChipSum:
    def __init__(self, shards, src, sib, cols, csend, crecv):
        self.s, self.src, self.sib, self.cols = shards, src, sib, cols
        self.csend, self.crecv = csend, crecv
        self.c = lax.axis_index("ctx")
        self.r = src.shape[0] // (2 * shards)

    def to_core(self, k):
        return remote(
            self.src.at[rows_of(2 * k + 1 - self.c, self.r), self.cols],
            self.sib.at[k, :, self.cols],
            self.csend.at[k],
            self.crecv.at[k],
            ctx=1 - self.c,
        )

    def start(self):
        loop(self.s, lambda k: self.to_core(k).start())

    def finish(self):
        def one(k):
            self.to_core(k).wait_recv()
            own = self.src[rows_of(2 * k + self.c, self.r), self.cols].astype(f32)
            self.sib[k, :, self.cols] = (own + self.sib[k, :, self.cols].astype(f32)).astype(bf16)

        loop(self.s, one)
        loop(self.s, lambda k: self.to_core(k).wait_send())


class Square:
    def __init__(self, kinds):
        tp = lax.axis_index("tp")
        self.me = tp
        self.x = tp + 1 - 2 * lax.rem(tp, 2)
        self.y = lax.rem(tp + 2, TP)
        self.across = TP - 1 - tp
        self.send, self.recv = kinds

    def copy(self, kind, b, src, dst):
        to = self.y if kind in (1, 2) else self.x
        return remote(src, dst, self.send.at[kind, b], self.recv.at[kind, b], tp=to)


class SquareScatter(Square):
    def __init__(self, buffers, kinds):
        super().__init__(kinds)
        self.out, self.into, self.out2, self.into2 = buffers

    def first(self, kind, b):
        return self.copy(kind, b, self.out.at[kind, b], self.into.at[kind, b])

    def second(self, kind, b):
        return self.copy(kind, b, self.out2.at[kind - 2, b], self.into2.at[kind - 2, b])

    def start(self, b, ref, rows):
        half = ref.shape[1] // 2
        left, right = pl.ds(0, half), pl.ds(half, half)
        self.out[0, b, 0] = ref[rows(self.x), left].astype(bf16)
        self.out[0, b, 1] = ref[rows(self.across), left].astype(bf16)
        self.first(0, b).start()
        self.out[1, b, 0] = ref[rows(self.y), right].astype(bf16)
        self.out[1, b, 1] = ref[rows(self.across), right].astype(bf16)
        self.first(1, b).start()
        self.out2[0, b] = ref[rows(self.y), left].astype(bf16)
        self.out2[1, b] = ref[rows(self.x), right].astype(bf16)

    def relay(self, b):
        for kind in (0, 1):
            self.first(kind, b).wait_recv()
            own = self.out2[kind, b].astype(f32)
            self.out2[kind, b] = (own + self.into[kind, b, 1].astype(f32)).astype(bf16)
            self.second(kind + 2, b).start()

    def finish(self, b):
        sums = []
        for kind in (0, 1):
            self.second(kind + 2, b).wait_recv()
            sums.append(self.into[kind, b, 0].astype(f32) + self.into2[kind, b].astype(f32))
        return jnp.concatenate(sums, axis=1)

    def sent(self, b):
        for kind in (0, 1):
            self.first(kind, b).wait_send()
            self.second(kind + 2, b).wait_send()

    @staticmethod
    def scratch(blocks, sub):
        first = pltpu.VMEM((2, blocks, 2, sub, D // 2), bf16)
        second = pltpu.VMEM((2, blocks, sub, D // 2), bf16)
        return [first, first, second, second]


class SquareGather(Square):
    def __init__(self, ref, part, kinds):
        super().__init__(kinds)
        self.ref, self.part = ref, part

    def whole(self, kind, b, owner):
        there = self.ref.at[self.part(b, owner)]
        return self.copy(kind, b, there, there)

    def half(self, kind, b, owner):
        half = self.ref.shape[1] // 2
        there = self.ref.at[self.part(b, owner), pl.ds((kind - 2) * half, half)]
        return self.copy(kind, b, there, there)

    def start(self, b):
        for kind in (0, 1):
            self.whole(kind, b, self.me).start()

    def relay(self, b):
        for kind, owner in ((0, self.x), (1, self.y)):
            self.whole(kind, b, owner).wait_recv()
            self.half(kind + 2, b, owner).start()

    def finish(self, b):
        for kind in (2, 3):
            self.half(kind, b, self.across).wait_recv()

    def sent(self, b):
        for kind, owner in ((0, self.x), (1, self.y)):
            self.whole(kind, b, self.me).wait_send()
            self.half(kind + 2, b, owner).wait_send()


def sigmoid(v):
    return 1.0 / (1.0 + jnp.exp(-v))


def softplus(v):
    return jnp.maximum(v, 0.0) + jnp.log1p(jnp.exp(-jnp.abs(v)))


def swap_half(v):
    width = v.shape[1]
    low = iota(v.shape, 1) % HD < HD // 2
    return jnp.where(low, pltpu.roll(v, width - HD // 2, 1), pltpu.roll(v, HD // 2, 1))


def low_lanes(shape):
    return iota(shape, 1) < 64


def parts(v, count):
    found = []
    for _ in range(count):
        part = v.astype(bf16)
        found.append(part)
        v = v - part.astype(f32)
    return found


def packed(v):
    v = jnp.where(iota(v.shape, 1) < 8, v, 0.0)
    high, middle, low = (part.astype(f32) for part in parts(v, 3))
    return (high + pltpu.roll(middle, 8, 1) + pltpu.roll(low, 16, 1)).astype(bf16)


def unpacked(v):
    v = v + pltpu.roll(v, 120, 1) + pltpu.roll(v, 112, 1)
    return jnp.where(iota(v.shape, 1) < 8, v, 0.0)


def spread(v):
    lane, channel = iota((N, WI), 0), iota((N, WI), 1)
    pick = ((lane % 8 == channel // P_SIZE) & (lane < 24)).astype(bf16)
    return nn(packed(v), pick)


def fold(v):
    pick = (iota((WI, N), 0) // P_SIZE == iota((WI, N), 1)).astype(bf16)
    high, low = parts(v, 2)
    return nn(high, pick) + nn(low, pick)


def row_sums_of(v, pick=None):
    pick = jnp.ones((8, v.shape[1]), bf16) if pick is None else pick
    high, low = parts(v, 2)
    return nt(pick, high) + nt(pick, low)


def as_column(row):
    at = iota(row.shape, 0)
    first = jnp.broadcast_to(row[0:1, :], row.shape)
    high, middle, low = parts(first, 3)
    three = jnp.where(at == 0, high, jnp.where(at == 1, middle, low))
    return tn(three, (iota((8, N), 0) < 3).astype(bf16))


def turned_over(v):
    one = eye(v.shape[0])
    high, middle, low = parts(v, 3)
    return tn(high, one) + tn(middle, one) + tn(low, one)


def wide(column, width):
    return jnp.concatenate([column] * (width // column.shape[1]), axis=1)


def lower_ones():
    return (iota((L, L), 0) >= iota((L, L), 1)).astype(bf16)


def head_scalars(dt_raw, prm):
    real = iota(dt_raw.shape, 1) < HL
    steps = jnp.where(real, softplus(dt_raw + prm[0:1, :]), 0.0)
    rates = steps * prm[1:2, :]
    return steps, rates


def pair_columns(v, pair):
    return v[:, 128 * pair : 128 * pair + 128]


def own_half(v, half):
    return jnp.where(low_lanes(v.shape) == (half == 0), v, jnp.zeros_like(v))


def eye(n):
    return (iota((n, n), 0) == iota((n, n), 1)).astype(bf16)


def rotary_of(table, rows):
    both = table[rows, :]
    first = iota(both.shape, 1) % HD < HD // 2
    cosine = jnp.where(first, both, pltpu.roll(both, HD // 2, 1))
    sine = jnp.where(first, -pltpu.roll(both, 128 - HD // 2, 1), both)
    return cosine, sine


FORWARD_EARLY = (
    "wf1",
    "wf2",
    "normed",
    "z_out",
    "cin",
    "dt_raw",
    "pre",
    "q_low",
    "kk",
    "vv",
    "att",
    "att_low",
    "steps_out",
    "cum_out",
)
FORWARD_AT = (
    0,
    1,
    4,
    6,
    7,
    8,
    12,
    14,
    15,
    16,
    17,
    18,
    22,
    23,
)
BACKWARD_LATE = (
    "chip",
    "grad_att",
    "q_low",
    "kk",
    "vv",
    "att",
    "lse_row",
    "start",
    "steps_in",
    "dt_raw",
    "cin",
    "normed",
    "wf1",
    "wf2",
    "hid_own",
    "grad_own",
)
BACKWARD_AT = (
    4,
    1,
    9,
    10,
    11,
    12,
    13,
    15,
    16,
    19,
    7,
    24,
    25,
    26,
    27,
    28,
)


def forward_kernel(
    shards, moves,
    hid, w_z, w_x, w_shared, w_dt, w_q, w_out, w_o, w_gate, gain_one, gain_two,
    conv_w, conv_b, gated_gain, dt_bias, a_log, d_skip, table, length,
    wf1, wf2, wo, wg, normed, gains, z_out, cin, dt_raw, taps, prm, chan,
    pre, hist, q_low, kk, vv, att, att_low, lse_row, ssd, start, steps_out, cum_out, tot_out,
    gated_low, square,
    small, wa1, wa2, wa3, stat, zf, pad, act, state, carried, scores_m, scores_l, hist_in,
    zs1, cs1, zr1, own1, zs2, cs2, zr2, own2, zs3, cs3, zr3, own3, zs4, cs4, zr4, own4,
    xs, xr,
):
    c, tp = lax.axis_index("ctx"), lax.axis_index("tp")
    t = hid.shape[0]
    blocks = t // L
    r = w_z.shape[0]

    kv = tp * (NQ // TP) // (NQ // KV)
    keys = w_shared[:, 2 * N : 2 * N + 128].astype(f32)
    vals = w_shared[:, 2 * N + 128 : 2 * N + 256].astype(f32)
    low_r = low_lanes((r, 128))
    other = pltpu.roll(jnp.where(kv == 0, vals, keys), 64, 1)
    wa1[:, 0:128] = w_q[...]
    wa1[:, 128:256] = jnp.where(
        kv == 0, jnp.where(low_r, keys, other), jnp.where(low_r, other, vals)
    ).astype(bf16)
    head_pick = (
        (iota((H, 128), 0) == iota((H, 128), 1) + tp * HL) & (iota((H, 128), 1) < HL)
    ).astype(bf16)
    row8, lane8 = iota((8, 128), 0), iota((8, 128), 1)
    gain_pick = ((row8 < 2) & (lane8 == GAIN_COL + row8)).astype(bf16)
    gain_rows = jnp.where(
        iota((8, r), 0) == 0, gain_one[...].astype(f32), gain_two[...].astype(f32)
    ).astype(bf16)
    wa1[:, 256:384] = (tn(w_dt[...], head_pick) + tn(gain_rows, gain_pick)).astype(bf16)
    wa2[:, 0:WI] = w_z[...]
    wa2[:, WI : 2 * WI] = w_x[...]
    wa2[:, 2 * WI : 2 * WI + 2 * N] = w_shared[:, 0 : 2 * N]
    greet(shards, False)
    gather1 = Gather(shards, wa1, wf1, zs1, cs1, zr1, own1)
    gather2 = Gather(shards, wa2, wf2, zs2, cs2, zr2, own2)
    gather3 = Gather(shards, wa3, wo, zs3, cs3, zr3, own3)
    gather4 = Gather(shards, w_gate, wg, zs4, cs4, zr4, own4)
    gather1.start()
    gather2.start()
    wa3[:, CO:CW] = nt(eye(r), w_out[...]).astype(bf16)
    wa3[:, CW:CG] = nt(eye(r), w_o[...]).astype(bf16)

    mine = pl.ds(pl.multiple_of(tp * WI, 128), WI)
    small[...] = jnp.zeros_like(small)
    small[0:1, :] = conv_b[...].astype(f32)[None, :]
    small[1:2, 0:DI] = gated_gain[...].astype(f32)[None, :]
    small[8:9, 0:H] = dt_bias[...].astype(f32)[None, :]
    small[9:10, 0:H] = a_log[...].astype(f32)[None, :]
    small[10:11, 0:H] = d_skip[...].astype(f32)[None, :]
    taps[0:CONVW, 0:WI] = conv_w[:, mine].astype(f32)
    taps[0:CONVW, WI:CH] = conv_w[:, DI:].astype(f32)
    taps[CONVW : CONVW + 1, 0:WI] = small[0:1, mine]
    taps[CONVW : CONVW + 1, WI:CH] = small[0:1, DI:]
    taps[CONVW + 1 :, :] = jnp.zeros((8 - CONVW - 1, CH), f32)
    heads = pltpu.roll(small[8:16, 0:128], lax.rem(128 - tp * HL, 128), 1)
    heads = jnp.where(lane8 < HL, jnp.where(row8 == 1, -jnp.exp(heads), heads), 0.0)
    prm[...] = heads
    chan[...] = jnp.zeros_like(chan)
    chan[0:1, :] = small[1:2, mine]
    chan[1:2, :] = spread(heads)[2:3, :]

    def swap(src, dst, i):
        return remote(src, dst, xs.at[i], xr.at[i], ctx=1 - c)

    def row_scale(i):
        rows = rows_of(i)
        x = hid[rows, :].astype(f32)
        scale = lax.rsqrt(jnp.mean(x * x, -1, keepdims=True) + EPS)
        stat[rows, :] = jnp.broadcast_to(scale, (L, 128))

    loop(blocks, row_scale)
    gather1.forward()
    gather1.finish()
    turned = wf1[:, 256:384].astype(f32).T
    gains[...] = turned[GAIN_COL : GAIN_COL + 8]
    gain = gains[0:1, :]
    low128 = low_lanes((L, 128))
    moves.put("wf1")
    moves.get("table")

    def first_projections(i):
        rows = rows_of(i)
        low = (hid[rows, :].astype(f32) * wide(stat[rows, :], D) * gain).astype(bf16)
        normed[rows, :] = low
        rest = nn(low, wf1[...])
        cosine, sine = rotary_of(table, pl.ds(pl.multiple_of(c * t + i * L, L), L))
        v = rest[:, 0:128]
        q_low[rows, :] = (v * cosine + swap_half(v) * sine).astype(bf16)
        v = rest[:, 128:256]
        other = pltpu.roll(v, 64, 1)
        twice = jnp.where(low128, v, other)
        kk[0, rows, :] = (twice * cosine + swap_half(twice) * sine).astype(bf16)
        vv[0, rows, :] = jnp.where(low128, other, v).astype(bf16)
        dt_raw[rows, :] = rest[:, 256:384]

    loop(blocks, first_projections)
    moves.put("normed", "q_low", "dt_raw")
    keys = swap(kk.at[0], kk.at[1], 1)
    keys.start()
    vals = swap(vv.at[0], vv.at[1], 2)
    vals.start()

    scale = HD ** (-0.5)
    limit = length[0] - c * t

    def stacked(v):
        return jnp.concatenate([own_half(v, 0), own_half(v, 1)], axis=0)

    for i in range(blocks):
        rows = pl.ds(i * L, L)
        width = (i + 1) * L
        q2 = stacked(q_low[rows, :].astype(f32)).astype(bf16)
        s = nt(q2, kk[0, 0:width, :]) * scale
        at = iota(s.shape, 0) % L + i * L
        col = iota(s.shape, 1)
        s = jnp.where((col <= at) & (col < limit), s, FILL)
        peak = jnp.max(s, -1, keepdims=True)
        e = jnp.exp(s - peak)
        total = jnp.sum(e, -1, keepdims=True)
        o = nn(e.astype(bf16), vv[0, 0:width, :])
        scores_m[...] = jnp.broadcast_to(peak, (2 * L, 128))
        scores_l[0] = jnp.broadcast_to(total, (2 * L, 128))
        scores_l[1] = o
        if i == 0:
            keys.wait_recv()
            vals.wait_recv()

        @pl.when(c > 0)
        def earlier():
            s2 = nt(q2, kk[1]) * scale
            old = scores_m[:, 0:1]
            new = jnp.maximum(old, jnp.max(s2, -1, keepdims=True))
            e2 = jnp.exp(s2 - new)
            fade = jnp.exp(old - new)
            scores_m[...] = jnp.broadcast_to(new, (2 * L, 128))
            scores_l[0] = fade * scores_l[0] + jnp.sum(e2, -1, keepdims=True)
            scores_l[1] = fade * scores_l[1] + nn(e2.astype(bf16), vv[1])

        total = scores_l[0]
        o = scores_l[1] / total
        o = jnp.where(low128, o[:L], o[L:])
        att[rows, :] = o
        att_low[rows, :] = o.astype(bf16)
        logs = scores_m[...] + jnp.log(total)
        turned = jnp.where(low128, logs[:L], logs[L:]).T
        lse_row[0:1, rows] = turned[0:1]
        lse_row[1:2, rows] = turned[64:65]
        lse_row[2:8, rows] = jnp.zeros((6, L), f32)
        if i == blocks - 2:
            gather2.forward(0, 1)
    gather2.forward(1)
    moves.put("kk", "vv", "att", "att_low")
    gather3.start()
    gather4.start()
    gather2.finish()
    moves.put("wf2")

    def conv_input(k):
        i = blocks - 1 - k
        rows = rows_of(i)
        v = nn(normed[rows, :], wf2[:, WI:]).astype(bf16)
        cin[rows, :] = v
        pad[pl.ds(pl.multiple_of(i * L + 8, 8), L), :] = v.astype(f32)

    conv_input(0)
    tail = swap(cin.at[pl.ds(t - 16, 16)], hist_in, 0)
    tail.start()
    lax.fori_loop(1, blocks, lambda k, carry: (conv_input(k), carry)[1], 0)
    tail.wait_recv()
    before = hist_in[8:16, :].astype(f32)
    hist[...] = jnp.where((iota((8, CH), 0) >= 5) & (c > 0), before, 0.0)
    pad[0:8, :] = hist[...]
    ones = lower_ones()
    state[...] = jnp.zeros_like(state)

    for i in range(blocks):
        rows = pl.ds(i * L, L)
        v = taps[4:5, :] + taps[0:1, :] * pad[pl.ds(i * L + 5, L), :]
        for j in range(1, CONVW):
            v = v + taps[j : j + 1, :] * pad[pl.ds(i * L + 5 + j, L), :]
        pre[rows, :] = v
        a = v * sigmoid(v)
        act[rows, :] = a
        steps, rates = head_scalars(dt_raw[rows, :], prm)
        cum = unpacked(nn(ones, packed(rates)))
        tot = cum[L - 1 : L, :]
        steps_out[rows, :] = steps
        cum_out[rows, :] = cum
        tot_out[i] = jnp.broadcast_to(tot, (8, 128))
        weight = spread(jnp.exp(tot - cum) * steps)
        start[i] = state[...]
        add = tn(a[:, WI : WI + N].astype(bf16), (weight * a[:, :WI]).astype(bf16))
        decay = spread(jnp.broadcast_to(jnp.exp(tot), (8, 128)))[0:1, :]
        state[...] = decay * state[...] + add

    states = swap(state, carried, 3)
    states.start()
    moves.put("cin", "pre", "steps_out", "cum_out")
    gather3.forward()

    def gate_input(i):
        rows = rows_of(i)
        zf[rows, :] = nn(normed[rows, :], wf2[:, 0:WI])
        z_out[rows, :] = zf[rows, :].astype(bf16)

    loop(blocks, gate_input)
    moves.put("z_out")

    states.wait_recv()
    carried[...] = jnp.where(c > 0, carried[...], 0.0)
    mask = iota((L, L), 0) >= iota((L, L), 1)
    for i in range(blocks):
        rows = pl.ds(i * L, L)
        if i > 0:
            decay = spread(jnp.exp(tot_out[i - 1]))[0:1, :]
            carried[...] = carried[...] * decay
        start[i] = start[i] + carried[...]
        s0 = start[i].astype(bf16)
        steps, cum = steps_out[rows, :], cum_out[rows, :]
        x = act[rows, 0:WI]
        xl = x.astype(bf16)
        in_map = act[rows, WI : WI + N].astype(bf16)
        out_map = act[rows, WI + N : CH].astype(bf16)
        gram = nt(out_map, in_map)
        cum_t, steps_t = cum.T, steps.T
        inner = []
        for pair in range(HL // 2):
            halves = []
            for half in range(2):
                h = 2 * pair + half
                decay = jnp.exp(jnp.where(mask, cum[:, h : h + 1] - cum_t[h : h + 1, :], FILL))
                mixing = gram * decay * steps_t[h : h + 1, :]
                halves.append(nn(mixing.astype(bf16), pair_columns(xl, pair)))
            inner.append(jnp.where(low128, halves[0], halves[1]))
        y = jnp.concatenate(inner, axis=1)
        y = y + spread(jnp.exp(cum)) * nn(out_map, s0) + chan[1:2, :] * x
        ssd[rows, :] = y.astype(bf16)
        zz = zf[rows, :]
        gated = y * zz * sigmoid(zz)
        gated_low[rows, :] = (gated * chan[0:1, :]).astype(bf16)
        square[:, rows] = row_sums_of(gated * gated)

    gather4.forward()
    gather3.finish()
    gather4.finish()
    for copy in (tail, keys, vals, states):
        copy.wait_send()


def forward(shards, *args):
    t, r = args[0].shape[0], args[1].shape[0]
    out = [
        ((D, 384), bf16),
        ((D, 1024), bf16),
        ((D, CG), bf16),
        ((D, FFL), bf16),
        ((t, D), bf16),
        ((8, D), f32),
        ((t, WI), bf16),
        ((t, CH), bf16),
        ((t, 128), f32),
        ((8, CH), f32),
        ((8, 128), f32),
        ((8, WI), f32),
        ((t, CH), f32),
        ((8, CH), f32),
        ((t, 128), bf16),
        ((2, t, 128), bf16),
        ((2, t, 128), bf16),
        ((t, 128), f32),
        ((t, 128), bf16),
        ((8, t), f32),
        ((t, WI), bf16),
        ((t // L, N, WI), f32),
        ((t, 128), f32),
        ((t, 128), f32),
        ((t // L, 8, 128), f32),
        ((t, WI), bf16),
        ((8, t), f32),
    ]
    dma = pltpu.SemaphoreType.DMA
    scratch = (
        [
            pltpu.VMEM((16, DI + 2 * N), f32),
            pltpu.VMEM((r, 384), bf16),
            pltpu.VMEM((r, 1024), bf16),
            pltpu.VMEM((r, CG), bf16),
            pltpu.VMEM((t, 128), f32),
            pltpu.VMEM((t, WI), f32),
            pltpu.VMEM((t + 8, CH), f32),
            pltpu.VMEM((t, CH), f32),
            pltpu.VMEM((N, WI), f32),
            pltpu.VMEM((N, WI), f32),
            pltpu.VMEM((2 * L, 128), f32),
            pltpu.VMEM((2, 2 * L, 128), f32),
            pltpu.VMEM((16, CH), bf16),
        ]
        + Gather.sems(shards) * 4
        + [dma((4,)), dma((4,))]
    )
    return call_staged(
        functools.partial(forward_kernel, shards),
        args,
        out,
        {"table": 17},
        dict(zip(FORWARD_EARLY, FORWARD_AT)),
        scratch,
        compiler_params=pltpu.CompilerParams(
            collective_id=1, has_side_effects=True, vmem_limit_bytes=VLIMIT
        ),
        name="mix_forward",
    )


def ffn_kernel(
    shards, moves,
    hid, cot, gl, att, square, wb, wg, w_up, w_down, gains, length,
    osend, grad_own, chip, hid_own, gain_grad, total_square, ggl, grad_att, dots,
    grads, grad_res, partial, seed, low_two, proj, grad_act, act, gg, gu, gown, back,
    unit, scale_keep, sqall, wm, wm_own, a1, a2, a3, a4, b1, b2, b3, b4,
    zs, cs, zr, own_sem, ms, mr, ws, wr, sqs, sqr, s1, r1, ns, nr, gs, gr, hs, hr,
):
    t = hid.shape[0]
    tp, c = lax.axis_index("tp"), lax.axis_index("ctx")
    blocks = t // L
    sub = L // TP
    width = D // TP
    wm_own[:, 0:FFL] = w_up[...]
    wm_own[:, FFL:] = nt(eye(w_down.shape[1]), w_down[...]).astype(bf16)
    greet(shards, True)
    gather = Gather(shards, wm_own, wm, zs, cs, zr, own_sem)
    gather.start()
    mlp_sum = ChipSum(shards, grads, chip, pl.ds(CG, CB - CG), ms, mr)
    out_sum = ChipSum(shards, grads, chip, pl.ds(CO, CG - CO), ws, wr)

    def peer(d):
        return lax.rem(tp + d, TP)

    def part(b, owner):
        return pl.ds(pl.multiple_of(b * L + owner * sub, sub), sub)

    def kept(b):
        return rows_of(b, sub)

    def square_to(d):
        return remote(sqall.at[tp], sqall.at[tp], sqs.at[d], sqr.at[tp], tp=peer(d))

    def square_from(d):
        return remote(sqall.at[tp], sqall.at[peer(d)], sqs.at[d], sqr.at[peer(d)], tp=peer(d))

    first = SquareScatter((a1, a2, a3, a4), (s1, r1))
    norms = SquareGather(low_two, part, (ns, nr))
    gradients = SquareScatter((b1, b2, b3, b4), (gs, gr))
    residuals = SquareGather(grad_res, part, (hs, hr))

    sqall[tp] = square[...]
    for d in range(1, TP):
        square_to(d).start()
    limit = length[0] - c * t

    def mask_seed(i):
        rows = rows_of(i)
        live = iota((L, D), 0) + i * L < limit
        seed[rows, :] = jnp.where(live, cot[rows, :].astype(f32), 0.0).astype(bf16)

    for d in range(1, TP):
        square_from(d).wait_recv()
    total_square[...] = sqall[0] + sqall[1] + sqall[2] + sqall[3]
    gain = gains[1:2, :]
    gain_grad[...] = jnp.zeros_like(gain_grad)

    def mix(b):
        rows = rows_of(b)
        scale = lax.rsqrt(total_square[:, rows] / DI + EPS)
        column = wide(as_column(scale), D)
        partial[rows, :] = nt(gl[rows, :], wb[:, CO:CW]) * column + nt(att[rows, :], wb[:, CW:CG])
        first.start(b, partial, lambda owner: part(b, owner))

    def norm(b):
        own = part(b, tp)
        hid_own[kept(b), :] = hid[own, :]
        acc = hid[own, :].astype(f32) + partial[own, :] + first.finish(b)
        scale = lax.rsqrt(jnp.mean(acc * acc, -1, keepdims=True) + EPS)
        scale_keep[kept(b), :] = jnp.broadcast_to(scale, (sub, 128))
        u = acc * scale
        unit[kept(b), :] = u
        low_two[own, :] = (u * gain).astype(bf16)
        norms.start(b)

    def act_grad(i):
        rows = rows_of(i)
        grad_act[rows, :] = nn(seed[rows, :], wm[:, FFL:])

    def hidden_units(b):
        rows = rows_of(b)
        norms.finish(b)
        low = low_two[rows, :]
        gate, up = nn(low, wg[...]), nn(low, wm[:, 0:FFL])
        sig = sigmoid(gate)
        silu = gate * sig
        hidden_act = (silu * up).astype(bf16)
        act[rows, :] = hidden_act
        ga = grad_act[rows, :]
        g1 = (ga * up * (sig * (1.0 + gate * (1.0 - sig)))).astype(bf16)
        g2 = (ga * silu).astype(bf16)
        gg[rows, :] = g1
        gu[rows, :] = g2
        back[...] = nt(g1, wg[...]) + nt(g2, wm[:, 0:FFL])
        gown[kept(b), :] = back[kept(tp), :]
        gradients.start(b, back, kept)
        partial[rows, :] = partial[rows, :] + nt(hidden_act, wm[:, FFL:])
        mine = rows_of(tp, width)
        osend[0, rows, :] = (partial[rows, mine] + hid[rows, mine].astype(f32)).astype(bf16)
        for e in range(1, TP):
            osend[e, rows, :] = partial[rows, rows_of(peer(e), width)].astype(bf16)

    def norm_back(b):
        own = part(b, tp)
        g = gown[kept(b), :] + gradients.finish(b)
        u = unit[kept(b), :]
        gain_grad[...] += jnp.broadcast_to(jnp.sum(g * u, 0, keepdims=True), (8, D))
        weighted = g * gain
        mean = jnp.mean(weighted * u, -1, keepdims=True)
        res = seed[own, :].astype(f32) + scale_keep[kept(b), 0:1] * (weighted - u * mean)
        grad_own[kept(b), :] = res
        grad_res[own, :] = res.astype(bf16)
        residuals.start(b)

    def weight_grads(i):
        feats = rows_of(i)
        low = low_two[:, feats]
        grads[feats, CG:CU] = tn(low, gg[...]).astype(bf16)
        grads[feats, CU:CD] = tn(low, gu[...]).astype(bf16)

    def down_grads(i):
        feats = rows_of(i)
        grads[feats, CD:CB] = tn(seed[:, feats], act[...]).astype(bf16)

    def out_back(b):
        rows = rows_of(b)
        residuals.finish(b)
        square_scale = lax.rsqrt(total_square[:, rows] / DI + EPS)
        column = wide(as_column(square_scale), D)
        got = grad_res[rows, :]
        low = (column * got.astype(f32)).astype(bf16)
        proj[rows, :] = low
        product = nn(low, wb[:, CO:CW])
        ggl[rows, :] = product
        dots[:, rows] = row_sums_of(product * gl[rows, :].astype(f32))
        grad_att[rows, :] = nn(got, wb[:, CW:CG]).astype(bf16)

    def stage(s, delay, act_on):
        @pl.when((s >= delay) & (s < delay + blocks))
        def go():
            act_on(s - delay)

    def step(s):
        stage(s, 0, mix)

        @pl.when(s == 1)
        def masks():
            moves.get("hid", "cot", "wg")
            loop(blocks, mask_seed)

        stage(s, 1, first.relay)
        stage(s, 2, norm)
        stage(s, 3, norms.relay)

        @pl.when(s == 3)
        def weights():
            gather.forward()
            gather.finish()
            loop(blocks, act_grad)

        stage(s, 4, hidden_units)

        @pl.when(s == blocks + 4)
        def fill():
            moves.put("osend")
            loop(D // L, weight_grads)

        stage(s, 5, gradients.relay)
        stage(s, 6, norm_back)

        @pl.when(s == blocks + 5)
        def more():
            loop(D // L, down_grads)
            mlp_sum.start()

        @pl.when(s == blocks + 6)
        def norms_done():
            moves.put("grad_own")

        stage(s, 7, residuals.relay)
        stage(s, 8, out_back)

    loop(blocks + 8, step)

    def out_grads(i):
        feats = rows_of(i)
        grads[feats, CO:CW] = tn(proj[:, feats], gl[...]).astype(bf16)
        grads[feats, CW:CG] = tn(grad_res[:, feats], att[...]).astype(bf16)

    loop(D // L, out_grads)
    out_sum.start()
    mlp_sum.finish()
    out_sum.finish()

    def sent(b):
        for exchange in (first, norms, gradients, residuals):
            exchange.sent(b)

    loop(blocks, sent)
    for d in range(1, TP):
        square_to(d).wait_send()


def ffn(shards, *args):
    t = args[0].shape[0]
    blocks, sub = t // L, L // TP
    kept = blocks * sub
    out = [
        ((TP, t, D // TP), bf16),
        ((kept, D), f32),
        ((shards, D // (2 * shards), CB), bf16),
        ((kept, D), bf16),
        ((8, D), f32),
        ((8, t), f32),
        ((t, WI), f32),
        ((t, 128), bf16),
        ((8, t), f32),
    ]
    dma = pltpu.SemaphoreType.DMA
    scratch = (
        [
            pltpu.VMEM((D, CB), bf16),
            pltpu.VMEM((t, D), bf16),
            pltpu.VMEM((t, D), f32),
            pltpu.VMEM((t, D), bf16),
            pltpu.VMEM((t, D), bf16),
            pltpu.VMEM((t, D), bf16),
            pltpu.VMEM((t, FFL), f32),
            pltpu.VMEM((t, FFL), bf16),
            pltpu.VMEM((t, FFL), bf16),
            pltpu.VMEM((t, FFL), bf16),
            pltpu.VMEM((kept, D), f32),
            pltpu.VMEM((L, D), f32),
            pltpu.VMEM((kept, D), f32),
            pltpu.VMEM((kept, 128), f32),
            pltpu.VMEM((TP, 8, t), f32),
            pltpu.VMEM((D, 2 * FFL), bf16),
            pltpu.VMEM((D // (2 * shards), 2 * FFL), bf16),
        ]
        + SquareScatter.scratch(blocks, sub) * 2
        + Gather.sems(shards)
        + [dma((shards,))] * 4
        + [dma((TP,))] * 2
        + [dma((TP, blocks))] * 8
    )
    return call_staged(
        functools.partial(ffn_kernel, shards),
        args,
        out,
        {"hid": 0, "cot": 1, "wg": 6},
        {"osend": 0, "grad_own": 1},
        scratch,
        compiler_params=pltpu.CompilerParams(
            collective_id=2, has_side_effects=True, vmem_limit_bytes=VLIMIT
        ),
        name="feed_forward",
    )


def backward_kernel(
    shards, moves,
    ggl, grad_att, dots_in, total_square, chip, osend,
    pre, cin, hist, q_low, kk, vv, att, lse_row, ssd, start, steps_in, cum_in, tot_in, dt_raw, z_in,
    taps, prm, chan, normed, wf1, wf2, hid_own, grad_own, gains, gain_two, table_all, length,
    output, low, grad_e, grad_l, grad_b, shared, vecs,
    table, own_out, lin, small, orecv, dots, dk, dv, dy, dpre, ends, dstate, carry, kv_out, kv_in, pad,
    edge_out, edge_in, gown, back, gain_one, grads_e, grads_l, misc, misc_low, misc_sum, shsend,
    vec_sib, vec_z,
    ln0, ln1, ln2, ln3, ln4, ln5,
    e0, e1, e2, e3, e4, e5, e6, e7, e8,
    l0, l1, l2, l3, l4, l5, l6, l7, l8,
    m0, m1, m2, m3, m4, m5, m6, m7, m8,
    g0, g1, g2, g3,
    table_sem, own_sem, vcs, vcr, vzs, vzr, xs, xr, ts, tr, os, orr, ss, sr, vts, vtr, gs, gr, hs, hr,
):
    z, c, tp = lax.axis_index("shard"), lax.axis_index("ctx"), lax.axis_index("tp")
    t = cin.shape[0]
    blocks, sub = t // L, L // TP
    get_table = pltpu.make_async_copy(table_all.at[rows_of(c, t)], table, table_sem)
    get_table.start()
    greet(shards, True)
    scatter = LineSum(shards, chip, ln0, ln1, ln2, ln3, ln4, ln5)
    scatter0 = Scatter(shards, grads_e, e0, e1, e2, e3, e4, e5, e6, e7, e8)
    scatter1 = Scatter(shards, grads_l, l0, l1, l2, l3, l4, l5, l6, l7, l8)
    scatter2 = Scatter(shards, misc_low, m0, m1, m2, m3, m4, m5, m6, m7, m8)
    moves.get("chip")
    scatter.start()

    def swap(src, dst, i):
        return remote(src, dst, xs.at[i], xr.at[i], ctx=1 - c)

    def peer(d):
        return lax.rem(tp + d, TP)

    def to_all(ref, send, recv, d):
        return remote(ref.at[tp], ref.at[tp], send.at[d], recv.at[tp], tp=peer(d))

    def from_all(ref, send, recv, d):
        return remote(ref.at[tp], ref.at[peer(d)], send.at[d], recv.at[peer(d)], tp=peer(d))

    dots[tp] = dots_in[...]
    for d in range(1, TP):
        to_all(dots, ts, tr, d).start()

    def out_to(d):
        return remote(osend.at[d], orecv.at[TP - 1 - d], os.at[d], orr.at[TP - 1 - d], tp=peer(d))

    def out_from(d):
        return remote(osend.at[d], orecv.at[d - 1], os.at[d], orr.at[d - 1], tp=peer(d))

    get_own = pltpu.make_async_copy(osend.at[0], own_out, own_sem)
    get_own.start()
    for d in range(1, TP):
        out_to(d).start()
    conv_grads = small.at[:, 0:CH]
    chan_grads = small.at[:, CH : CH + WI]
    head_grads = small.at[:, CH + WI : CH + WI + 128]
    low128 = low_lanes((L, 128))
    small[...] = jnp.zeros_like(small)
    for d in range(1, TP):
        from_all(dots, ts, tr, d).wait_recv()

    def gated_back(i):
        rows = rows_of(i)
        both = dots[0, :, rows] + dots[1, :, rows] + dots[2, :, rows] + dots[3, :, rows]
        share = both / ((total_square[:, rows] / DI + EPS) * DI)
        column = wide(as_column(share), WI)
        zz, y = z_in[rows, :].astype(f32), ssd[rows, :].astype(f32)
        sig = sigmoid(zz)
        silu = zz * sig
        gated = y * silu
        product = ggl[rows, :]
        chan_grads[0:1, :] += jnp.sum(product * gated, 0, keepdims=True)
        grad_gated = product * chan[0:1, :] - column * gated
        grad_y = grad_gated * silu
        dy[rows, :] = grad_y
        lin[rows, CZ:CX] = (grad_gated * y * (sig * (1.0 + zz * (1.0 - sig)))).astype(bf16)
        v = pre[rows, WI + N : CH]
        out_map = (v * sigmoid(v)).astype(bf16)
        ends[i] = tn(out_map, (spread(jnp.exp(cum_in[rows, :])) * grad_y).astype(bf16))

    loop(blocks, gated_back)
    dstate[...] = jnp.zeros_like(dstate)

    def chain(k):
        i = blocks - 1 - k
        add = ends[i]
        ends[i] = dstate[...]
        dstate[...] = spread(jnp.exp(tot_in[i]))[0:1, :] * dstate[...] + add

    loop(blocks, chain)
    states = swap(dstate, carry, 0)
    states.start()

    scale = HD ** (-0.5)
    limit = length[0] - c * t
    dk[...] = jnp.zeros_like(dk)
    dv[...] = jnp.zeros_like(dv)
    get_table.wait()
    moves.get("grad_att", "q_low", "kk", "vv", "att", "lse_row")
    head_of = ((iota((8, 128), 1) // HD) == iota((8, 128), 0)).astype(bf16)

    def stacked(v):
        return jnp.concatenate([own_half(v, 0), own_half(v, 1)], axis=0).astype(bf16)

    def side_by_side(v):
        return jnp.concatenate([v[0:1, :], v[1:2, :]], axis=1)

    for i in range(blocks):
        rows = pl.ds(i * L, L)
        width = (i + 1) * L
        q2 = stacked(q_low[rows, :].astype(f32))
        go = grad_att[rows, :].astype(f32)
        go2 = stacked(go)
        row_dot = side_by_side(row_sums_of(go * att[rows, :], head_of))
        logs = side_by_side(lse_row[:, rows])
        turn = rotary_of(table, rows)

        def keys_of(part, size, masked):
            k, v = kk[part, 0:size, :], vv[part, 0:size, :]
            s = nt(k, q2) * scale - logs
            if masked:
                at = iota(s.shape, 1) % L + i * L
                row = iota(s.shape, 0)
                s = jnp.where((row <= at) & (row < limit), s, FILL)
            p = jnp.exp(s)
            ds = (p * (nt(v, go2) - row_dot)).astype(bf16)
            dv[part, 0:size, :] += nn(p.astype(bf16), go2)
            dk[part, 0:size, :] += nn(ds, q2)
            out = tn(ds, k) * scale
            out = jnp.where(low128, out[:L], out[L:])
            return out * turn[0] - swap_half(out) * turn[1]

        back[:, 0:128] = keys_of(0, width, True)

        @pl.when(c > 0)
        def earlier():
            back[:, 0:128] += keys_of(1, t, False)

        lin[rows, CQ:CK] = back[:, 0:128].astype(bf16)
        if i == 1:
            scatter.relay()

    def key_values(part, rows):
        gk, gv = dk[part, rows, :] * scale, dv[part, rows, :]
        return jnp.where(low128, gk + pltpu.roll(gk, 64, 1), gv + pltpu.roll(gv, 64, 1))

    def pack(i):
        rows = rows_of(i)
        kv_out[rows, :] = key_values(1, rows).astype(bf16)

    loop(blocks, pack)
    pairs = swap(kv_out, kv_in, 1)
    pairs.start()

    moves.get("start", "steps_in", "dt_raw", "cin", "normed", "wf1", "wf2", "hid_own", "grad_own")
    pad[0:16, :] = jnp.concatenate([jnp.zeros((8, CH), f32), hist[...]], axis=0).astype(bf16)

    def fill(i):
        pad[pl.ds(pl.multiple_of(i * L + 16, 16), L), :] = cin[rows_of(i), :]

    loop(blocks, fill)
    states.wait_recv()
    carry[...] = jnp.where(c == 0, carry[...], 0.0)

    def add_carry(k):
        i = blocks - 1 - k
        ends[i] = ends[i] + carry[...]
        carry[...] = spread(jnp.exp(tot_in[i]))[0:1, :] * carry[...]

    loop(blocks, add_carry)
    mask = iota((L, L), 0) >= iota((L, L), 1)
    ones = lower_ones()
    lane = iota((L, 128), 1)

    def scan_back(i):
        rows = rows_of(i)
        v = pre[rows, :]
        sig = sigmoid(v)
        a = v * sig
        x = a[:, :WI]
        xl, bl, cl = x.astype(bf16), a[:, WI : WI + N].astype(bf16), a[:, WI + N :].astype(bf16)
        steps, cum = steps_in[rows, :], cum_in[rows, :]
        tot = cum[L - 1 : L, :]
        ecum, wend = jnp.exp(cum), jnp.exp(tot - cum)
        weight = wend * steps
        ecum_x, weight_x = spread(ecum), spread(weight)
        grad_y = dy[rows, :]
        dyl = grad_y.astype(bf16)
        s0, d1 = start[i], ends[i]
        s0l, d1l = s0.astype(bf16), d1.astype(bf16)
        bd, cs = nn(bl, d1l), nn(cl, s0l)
        dw = fold(x * bd)
        crossing = jnp.broadcast_to(jnp.sum(s0 * d1, 0, keepdims=True), (8, WI))
        dtot = jnp.sum(weight * dw, 0, keepdims=True) + jnp.exp(tot) * fold(crossing)[0:1, :]
        gram = nt(cl, bl)
        cum_t, steps_t = cum.T, steps.T
        dgram = jnp.zeros((L, L), f32)
        row_sums = jnp.zeros((L, 128), f32)
        col_sums, inner = [], []
        for pair in range(HL // 2):
            xp, dp = pair_columns(xl, pair), pair_columns(dyl, pair)
            dpf = pair_columns(grad_y, pair)
            halves = []
            for half in range(2):
                h = 2 * pair + half
                decay = jnp.exp(jnp.where(mask, cum[:, h : h + 1] - cum_t[h : h + 1, :], FILL))
                q = nt(own_half(dpf, half).astype(bf16), xp)
                mixed = gram * decay
                srow = steps_t[h : h + 1, :]
                f = mixed * q
                col_sums.append(jnp.sum(f, 0, keepdims=True))
                row_sums = jnp.where(lane == h, jnp.sum(f * srow, -1, keepdims=True), row_sums)
                dgram = dgram + decay * srow * q
                halves.append(tn((mixed * srow).astype(bf16), dp))
            inner.append(jnp.where(low128, halves[0], halves[1]))
        cols = jnp.concatenate(col_sums + [jnp.zeros((128 - HL, L), f32)], axis=0).T
        dcum = fold(grad_y * cs) * ecum - weight * dw + row_sums - steps * cols
        dcum = dcum + jnp.where(iota((L, 128), 0) == L - 1, dtot, 0.0)
        drate = unpacked(tn(ones, packed(dcum)))
        rate_of = prm[1:2, :]
        raw = dt_raw[rows, :] + prm[0:1, :]
        dstep = (wend * dw + cols + drate * rate_of) * sigmoid(raw)
        dstep = jnp.where(lane < HL, dstep, 0.0)
        lin[rows, CS:CA] = dstep.astype(bf16)
        head_grads[0:1, :] += jnp.sum(dstep, 0, keepdims=True)
        head_grads[1:2, :] += jnp.sum(drate * steps * rate_of, 0, keepdims=True)
        head_grads[2:3, :] += jnp.sum(fold(grad_y * x), 0, keepdims=True)
        slope = sig * (1.0 + v * (1.0 - sig))
        dx = chan[1:2, :] * grad_y + weight_x * bd + jnp.concatenate(inner, axis=1)
        dg = dgram.astype(bf16)
        db = tn(dg, cl) + nt((weight_x * x).astype(bf16), d1l)
        dc = nn(dg, bl) + nt((ecum_x * grad_y).astype(bf16), s0l)
        dpre[rows, 0:WI] = dx * slope[:, :WI]
        dpre[rows, WI : WI + N] = db * slope[:, WI : WI + N]
        dpre[rows, WI + N : CH] = dc * slope[:, WI + N :]

    edge = swap(edge_out, edge_in, 2)

    def keys_back(i):
        rows = rows_of(i)
        v = key_values(0, rows) + kv_in[rows, :].astype(f32)
        cosine, sine = rotary_of(table, rows)
        cosine = jnp.where(low128, cosine, 1.0)
        sine = jnp.where(low128, sine, 0.0)
        lin[rows, CK:CS] = (v * cosine - swap_half(v) * sine).astype(bf16)

    def conv_back(b):
        rows = rows_of(b)
        later = dpre[pl.ds(pl.multiple_of(b * L, L), L + 8), :]
        earlier = pad[pl.ds(pl.multiple_of(b * L, L), L + 16), :].astype(f32)
        g = later[0:L]
        conv_grads[4:5, :] += jnp.sum(g, 0, keepdims=True)
        total = jnp.zeros_like(g)
        for j in range(CONVW):
            total = total + taps[j : j + 1, :] * later[CONVW - 1 - j : CONVW - 1 - j + L]
            conv_grads[j : j + 1, :] += jnp.sum(g * earlier[13 + j : 13 + j + L], 0, keepdims=True)
        lin[rows, CX:CQ] = total.astype(bf16)

    def part(b, owner):
        return pl.ds(pl.multiple_of(b * L + owner * sub, sub), sub)

    def kept(b):
        return rows_of(b, sub)

    grads_in = SquareScatter((g0, g1, g2, g3), (gs, gr))
    lows = SquareGather(low, part, (hs, hr))

    def product(b):
        rows = rows_of(b)
        back[...] = nt(lin[rows, CZ:CQ], wf2[...]) + nt(lin[rows, CQ:CA], wf1[...])
        gown[kept(b), :] = back[kept(tp), :]
        grads_in.start(b, back, kept)

    gain_one[...] = jnp.zeros_like(gain_one)

    def norm_back(b):
        own = part(b, tp)
        g = gown[kept(b), :] + grads_in.finish(b)
        x = hid_own[kept(b), :].astype(f32)
        scale = lax.rsqrt(jnp.mean(x * x, -1, keepdims=True) + EPS)
        unit = x * scale
        gain_one[...] += jnp.broadcast_to(jnp.sum(g * unit, 0, keepdims=True), (8, D))
        weighted = g * gains[0:1, :]
        mean = jnp.mean(weighted * unit, -1, keepdims=True)
        low[own, :] = (grad_own[kept(b), :] + scale * (weighted - unit * mean)).astype(bf16)
        lows.start(b)

    def early_grads(i):
        feats = rows_of(i)
        grads_e[feats, 0:WI] = tn(normed[:, feats], lin[:, CZ:CX]).astype(bf16)
        grads_e[feats, WI:] = tn(normed[:, feats], lin[:, CQ:CS]).astype(bf16)

    def step(k):
        @pl.when(k < blocks)
        def scan():
            scan_back(lax.rem(2 * blocks - 1 - k + c, blocks))

        @pl.when(k == 0)
        def first():
            @pl.when(c > 0)
            def give():
                edge_out[...] = dpre[0:8, :]
                edge.start()

            pairs.wait_recv()
            loop(blocks, keys_back)
            loop(D // L, early_grads)
            scatter0.start()
            dpre[pl.ds(t, 8), :] = jnp.zeros((8, CH), f32)

            @pl.when(c == 0)
            def take():
                edge.wait_recv()
                dpre[pl.ds(t, 8), :] = edge_in[...]

        @pl.when(k >= 1)
        def there():
            conv_back(blocks - k)
            product(blocks - k)

        @pl.when(k == 1)
        def on():
            scatter0.middle()

        @pl.when(k == 3)
        def further():
            scatter0.relay()

        @pl.when(k >= 2)
        def over():
            grads_in.relay(blocks + 1 - k)

        @pl.when(k >= 3)
        def again():
            norm_back(blocks + 2 - k)

        @pl.when(k >= 4)
        def last():
            lows.relay(blocks + 3 - k)

    loop(blocks + 1, step)
    vec_core = remote(small, vec_sib, vcs.at[0], vcr.at[0], ctx=1 - c)
    vec_core.start()

    def weight_grads(i):
        feats = rows_of(i)
        grads_l[feats, :] = tn(normed[:, feats], lin[:, CX:CQ]).astype(bf16)
        misc[feats, :] = tn(normed[:, feats], lin[:, CS:CA])

    loop(D // L, weight_grads)
    scatter1.start()
    grads_in.relay(0)
    norm_back(1)
    lows.relay(2)

    def vec_to_shard(k):
        zz = lax.rem(z + k, shards)
        return remote(vec_z.at[z], vec_z.at[z], vzs.at[zz], vzr.at[z], shard=zz)

    def vec_from_shard(k):
        zz = lax.rem(z + k, shards)
        return remote(vec_z.at[z], vec_z.at[zz], vzs.at[zz], vzr.at[zz], shard=zz)

    vec_core.wait_recv()
    vec_z[z] = small[...] + vec_sib[...]
    loop(shards - 1, lambda k: vec_to_shard(k + 1).start())
    scatter1.middle()
    norm_back(0)
    lows.relay(1)
    gain_rows = jnp.where(iota((8, D), 0) == 0, gain_one[...], gain_two[...])
    row, lane8 = iota((8, 128), 0), iota((8, 128), 1)
    pick = ((row < 2) & (lane8 == GAIN_COL + row)).astype(f32)
    misc_low[...] = (misc[...] + tn(gain_rows, pick, HI)).astype(bf16)
    scatter2.start()
    get_own.wait()
    total = own_out[...].astype(f32)
    for d in range(1, TP):
        out_from(d).wait_recv()
        total = total + orecv[d - 1].astype(f32)
    output[...] = total.astype(bf16)
    scatter1.relay()
    scatter2.middle()
    lows.relay(0)
    loop(shards - 1, lambda k: vec_from_shard(k + 1).wait_recv())
    vecs[tp] = lax.fori_loop(1, shards, lambda k, total: total + vec_z[k], vec_z[0])
    for d in range(1, TP):
        to_all(vecs, vts, vtr, d).start()
    scatter.finish(grad_b)
    moves.put("grad_b")
    scatter2.relay()
    scatter0.finish(grad_e)
    scatter1.finish(grad_l)
    scatter2.finish(misc_sum)
    few = grad_e.shape[0] // TP
    for i in range(TP):
        shsend[i, :, 0:256] = grad_l[i * few : (i + 1) * few, WI:CH]
        shsend[i, :, 256:384] = grad_e[i * few : (i + 1) * few, WI + 128 : CH]
        shsend[i, :, 384:512] = misc_sum[i * few : (i + 1) * few, :]

    def share_to(d):
        return remote(shsend.at[peer(d)], shared.at[tp], ss.at[d], sr.at[tp], tp=peer(d))

    def share_from(d):
        return remote(shsend.at[peer(d)], shared.at[peer(d)], ss.at[d], sr.at[peer(d)], tp=peer(d))

    for d in range(1, TP):
        share_to(d).start()
    shared[tp] = shsend[tp]

    def arrived(b):
        lows.finish(b)
        lows.sent(b)
        grads_in.sent(b)

    loop(blocks, arrived)
    for d in range(1, TP):
        share_from(d).wait_recv()
        from_all(vecs, vts, vtr, d).wait_recv()

    @pl.when(c > 0)
    def given():
        edge.wait_send()

    for copy in (states, pairs, vec_core):
        copy.wait_send()
    loop(shards - 1, lambda k: vec_to_shard(k + 1).wait_send())
    for d in range(1, TP):
        to_all(dots, ts, tr, d).wait_send()
        out_to(d).wait_send()
        share_to(d).wait_send()
        to_all(vecs, vts, vtr, d).wait_send()


def backward(shards, *args):
    t = args[0].shape[0]
    rows = D // (2 * shards)
    blocks, sub = t // L, L // TP
    vec = (8, CH + WI + 128)
    out = [
        ((t, D // TP), bf16),
        ((t, D), bf16),
        ((rows, CH), f32),
        ((rows, CH), f32),
        ((rows, CB), f32),
        ((TP, rows // TP, 512), f32),
        ((TP, *vec), f32),
    ]
    dma = pltpu.SemaphoreType.DMA
    scratch = (
        [
            pltpu.VMEM((t, 128), f32),
            pltpu.VMEM((t, D // TP), bf16),
            pltpu.VMEM((t, CA), bf16),
            pltpu.VMEM(vec, f32),
            pltpu.VMEM((TP - 1, t, D // TP), bf16),
            pltpu.VMEM((TP, 8, t), f32),
            pltpu.VMEM((2, t, 128), f32),
            pltpu.VMEM((2, t, 128), f32),
            pltpu.VMEM((t, WI), f32),
            pltpu.VMEM((t + 8, CH), f32),
            pltpu.VMEM((t // L, N, WI), f32),
            pltpu.VMEM((N, WI), f32),
            pltpu.VMEM((N, WI), f32),
            pltpu.VMEM((t, 128), bf16),
            pltpu.VMEM((t, 128), bf16),
            pltpu.VMEM((t + 16, CH), bf16),
            pltpu.VMEM((8, CH), f32),
            pltpu.VMEM((8, CH), f32),
            pltpu.VMEM((blocks * sub, D), f32),
            pltpu.VMEM((L, D), f32),
            pltpu.VMEM((8, D), f32),
            pltpu.VMEM((D, CH), bf16),
            pltpu.VMEM((D, CH), bf16),
            pltpu.VMEM((D, 128), f32),
            pltpu.VMEM((D, 128), bf16),
            pltpu.VMEM((rows, 128), f32),
            pltpu.VMEM((TP, rows // TP, 512), f32),
            pltpu.VMEM(vec, f32),
            pltpu.VMEM((shards, *vec), f32),
        ]
        + LineSum.scratch(shards, D, CB)
        + Scatter.scratch(shards, D, CH)
        + Scatter.scratch(shards, D, CH)
        + Scatter.scratch(shards, D, 128)
        + SquareScatter.scratch(blocks, sub)
        + [dma(()), dma(()), dma((1,)), dma((1,)), dma((shards,)), dma((shards,)), dma((3,)), dma((3,))]
        + [dma((TP,))] * 8
        + [dma((TP, blocks))] * 4
    )
    return call_staged(
        functools.partial(backward_kernel, shards),
        args,
        out,
        dict(zip(BACKWARD_LATE, BACKWARD_AT)),
        {"grad_b": 4},
        scratch,
        left=(5, len(args) - 2),
        compiler_params=pltpu.CompilerParams(
            collective_id=3, has_side_effects=True, vmem_limit_bytes=VMOST
        ),
        name="mix_backward",
    )


def pack_kernel(
    low, output, grad_e, grad_l, grad_b, shared, vecs,
    grad_hidden, out, g_z, g_x, g_q, g_gate, g_up, g_out, g_o, g_down, g_shared, g_dt, g_one,
    g_two, g_conv, g_conv_b, g_gate_gain, g_bias, g_decay, g_skip, g_chan,
):
    grad_hidden[...] = low[...].astype(f32)
    out[...] = output[...]

    @pl.when(pl.program_id(0) == 0)
    def rest():
        g_z[...] = grad_e[:, 0:WI]
        g_x[...] = grad_l[:, 0:WI]
        g_q[...] = grad_e[:, WI : WI + 128]
        g_gate[...] = grad_b[:, CG:CU]
        g_up[...] = grad_b[:, CU:CD]
        g_out[...] = turned_over(grad_b[:, CO:CW])
        g_o[...] = turned_over(grad_b[:, CW:CG])
        g_down[...] = turned_over(grad_b[:, CD:CB])
        first, second = shared[0] + shared[1], shared[2] + shared[3]
        both = first + second
        g_shared[:, 0 : 2 * N] = both[:, 0 : 2 * N]
        kv1, kv2 = first[:, 256:384], second[:, 256:384]
        low_half = low_lanes(kv1.shape)
        g_shared[:, 2 * N : 2 * N + 128] = jnp.where(low_half, kv1, pltpu.roll(kv2, 64, 1))
        g_shared[:, 2 * N + 128 :] = jnp.where(low_half, pltpu.roll(kv1, 64, 1), kv2)
        gains = turned_over(both[:, 384:512])[GAIN_COL : GAIN_COL + 8]
        g_one[...] = gains[0]
        g_two[...] = gains[1]
        steps = jnp.zeros((both.shape[0], 128), f32)
        heads = jnp.zeros((8, 128), f32)
        g_chan[...] = jnp.zeros_like(g_chan)
        for i in range(TP):
            lane = iota(steps.shape, 1) // HL == i
            steps = jnp.where(lane, pltpu.roll(shared[i, :, 384:512], i * HL, 1), steps)
            lane = iota(heads.shape, 1) // HL == i
            heads = jnp.where(lane, pltpu.roll(vecs[i, :, CH + WI : CH + WI + 128], i * HL, 1), heads)
            mine = slice(i * WI, (i + 1) * WI)
            g_conv[:, mine] = vecs[i, 0:CONVW, 0:WI]
            g_chan[0:1, mine] = vecs[i, CONVW : CONVW + 1, 0:WI]
            g_chan[1:2, mine] = vecs[i, 0:1, CH : CH + WI]
        maps = vecs[0, :, WI:CH] + vecs[1, :, WI:CH] + vecs[2, :, WI:CH] + vecs[3, :, WI:CH]
        g_conv[:, DI:] = maps[0:CONVW]
        g_chan[0:1, DI:] = maps[CONVW : CONVW + 1]
        g_dt[...] = turned_over(steps)[0:H]
        g_bias[...] = heads[0, 0:H]
        g_decay[...] = heads[1, 0:H]
        g_skip[...] = heads[2, 0:H]
        g_conv_b[...] = g_chan[0, :]
        g_gate_gain[...] = g_chan[1, 0:DI]


def pack(low, output, grad_e, grad_l, grad_b, shared, vecs):
    t, r, few = low.shape[0], grad_e.shape[0], shared.shape[1]
    out = [
        (t, D), output.shape, (r, WI), (r, WI), (r, 128), (r, FFL), (r, FFL), (WI, r), (128, r), (FFL, r),
        (few, 512), (H, few), (few,), (few,), (CONVW, DI + 2 * N), (DI + 2 * N,), (DI,), (H,), (H,),
        (H,),
    ]
    rows = pl.BlockSpec((L, D), lambda i: (i, 0))
    few_rows = pl.BlockSpec((L, output.shape[1]), lambda i: (i, 0))
    kinds = [f32, bf16] + [f32] * (len(out) - 2)

    def whole(shape):
        return pl.BlockSpec(shape, lambda i: (0,) * len(shape))

    return pl.pallas_call(
        pack_kernel,
        grid=(t // L,),
        out_shape=[jax.ShapeDtypeStruct(o, k) for o, k in zip(out, kinds)],
        in_specs=[rows, few_rows] + [whole(v.shape) for v in (grad_e, grad_l, grad_b, shared, vecs)],
        out_specs=[rows, few_rows] + [whole(o) for o in out[2:]],
        scratch_shapes=[pltpu.VMEM((8, DI + 2 * N), f32)],
        compiler_params=pltpu.CompilerParams(vmem_limit_bytes=VLIMIT),
        name="lay_out",
    )(low, output, grad_e, grad_l, grad_b, shared, vecs)


def rotary_table(count):
    inverse = rope_base ** (-2.0 * np.arange(HD // 2, dtype=np.float32) / HD)
    angles = np.arange(count, dtype=np.float32)[:, None] * inverse.astype(np.float32)[None, :]
    both = np.concatenate([np.cos(angles), np.sin(angles)], axis=1)
    return np.tile(both, (1, 2)).astype(np.float32)


def local(
    hidden, cotangent, lengths, norm1_gain, w_z, w_x, w_shared, w_dt, dt_bias, a_log, d_skip,
    conv_w, conv_b, gated_gain, w_out, w_q, w_o, norm2_gain, w_gate, w_up, w_down,
):
    t = hidden.shape[1]
    shards = lax.axis_size("shard")
    hid, cot = hidden[0], cotangent[0]
    table = jnp.asarray(rotary_table(lax.axis_size("ctx") * t))
    (
        wf1, wf2, wo, wg, normed, gains, z, cin, dt, taps, prm, chan,
        pre, hist, q_low, kk, vv, att, att_low, lse_row, ssd, start, steps, cum, tot, gl, square,
    ) = forward(
        shards, hid, w_z, w_x, w_shared, w_dt.T, w_q, w_out, w_o, w_gate,
        norm1_gain[None], norm2_gain[None], conv_w, conv_b, gated_gain, dt_bias, a_log, d_skip,
        table, lengths,
    )
    osend, grad_own, chip, hid_own, gain_two, total_square, ggl, grad_att, dots = ffn(
        shards, hid, cot, gl, att_low, square, wo, wg, w_up, w_down, gains, lengths
    )
    output, grad_hidden, grad_e, grad_l, grad_b, shared, vecs = backward(
        shards, ggl, grad_att, dots, total_square, chip, osend, pre, cin, hist, q_low, kk, vv, att,
        lse_row, ssd, start, steps, cum, tot, dt, z, taps, prm, chan, normed, wf1, wf2,
        hid_own, grad_own, gains, gain_two, table, lengths,
    )
    (
        grad_full, output_full, g_z, g_x, g_q, g_gate, g_up, g_out, g_o, g_down, g_shared, g_dt, g_one,
        g_two, g_conv, g_conv_b, g_gate_gain, g_bias, g_decay, g_skip,
    ) = pack(grad_hidden, output, grad_e, grad_l, grad_b, shared, vecs)
    return (
        output_full[None],
        grad_full[None],
        g_one,
        g_z,
        g_x,
        g_shared,
        g_dt.T,
        g_bias,
        g_decay,
        g_skip,
        g_conv,
        g_conv_b,
        g_gate_gain,
        g_out,
        g_q,
        g_o,
        g_two,
        g_gate,
        g_up,
        g_down,
    )


def solution(mesh):
    placed = (
        P("shard", "ctx", None),
        P("shard", "ctx", None),
        P("shard"),
        P(("shard", "ctx")),
        P(("shard", "ctx"), "tp"),
        P(("shard", "ctx"), "tp"),
        P(("shard", "ctx"), None),
        P(("shard", "ctx"), None),
        P(),
        P(),
        P(),
        P(),
        P(),
        P(),
        P("tp", ("shard", "ctx")),
        P(("shard", "ctx"), "tp"),
        P("tp", ("shard", "ctx")),
        P(("shard", "ctx")),
        P(("shard", "ctx"), "tp"),
        P(("shard", "ctx"), "tp"),
        P("tp", ("shard", "ctx")),
    )
    return jax.shard_map(
        local,
        mesh=mesh,
        in_specs=placed,
        out_specs=(
            P("shard", "ctx", "tp"),
            P("shard", "ctx", None),
            P(("shard", "ctx", "tp")),
            P(("shard", "ctx"), "tp"),
            P(("shard", "ctx"), "tp"),
            P(("shard", "ctx", "tp"), None),
            P(("shard", "ctx", "tp"), None),
            P(),
            P(),
            P(),
            P(),
            P(),
            P(),
            P("tp", ("shard", "ctx")),
            P(("shard", "ctx"), "tp"),
            P("tp", ("shard", "ctx")),
            P(("shard", "ctx", "tp")),
            P(("shard", "ctx"), "tp"),
            P(("shard", "ctx"), "tp"),
            P("tp", ("shard", "ctx")),
        ),
        check_vma=False,
    )
```

```python
import functools

import jax
import jax.numpy as jnp
import numpy as np
from jax import lax
from jax.experimental import pallas as pl
from jax.experimental.pallas import tpu as pltpu
from jax.sharding import PartitionSpec as P

H = 24
P_SIZE = 64
N = 128
NQ = 8
KV = 2
HD = 64
CONVW = 4
DI = 1536
D = 1024
FFL = 512
TP = 4
HL = H // TP
WI = HL * P_SIZE
CH = WI + 2 * N
L = 256

CZ, CX, CM, CQ, CK, CS, CA = 0, 384, 768, 1024, 1152, 1280, 1408
GAIN_COL = 24
CO, CW, CG, CU, CD, CB = 0, 384, 512, 1024, 1536, 2048

EPS = 1e-05
rope_base = 10000.0
FILL = -1e30
HI = lax.Precision.HIGHEST
MESH = pl.DeviceIdType.MESH
f32 = jnp.float32
bf16 = jnp.bfloat16
VLIMIT = 60 * 1024 * 1024
VMOST = 63 * 1024 * 1024 + 512 * 1024


def nn(a, b, precision=None):
    return lax.dot_general(
        a, b, (((1,), (0,)), ((), ())), precision=precision, preferred_element_type=f32
    )


def nt(a, b, precision=None):
    return lax.dot_general(
        a, b, (((1,), (1,)), ((), ())), precision=precision, preferred_element_type=f32
    )


def tn(a, b, precision=None):
    return lax.dot_general(
        a, b, (((0,), (0,)), ((), ())), precision=precision, preferred_element_type=f32
    )


def rows_of(index, size=L):
    return pl.ds(pl.multiple_of(index * size, size), size)


def remote(src, dst, send, recv, **where):
    return pltpu.make_async_remote_copy(
        src_ref=src,
        dst_ref=dst,
        send_sem=send,
        recv_sem=recv,
        device_id=where,
        device_id_type=MESH,
    )


def iota(shape, dim):
    return lax.broadcasted_iota(jnp.int32, shape, dim)


def loop(n, body):
    lax.fori_loop(0, n, lambda i, c: (body(i), c)[1], 0)


def greet(shards, tp_too, ctx_too=True, shard_too=True):
    barrier = pltpu.get_barrier_semaphore()
    count = 0
    z, c, t = lax.axis_index("shard"), lax.axis_index("ctx"), lax.axis_index("tp")
    if ctx_too:
        pl.semaphore_signal(barrier, inc=1, device_id={"ctx": 1 - c}, device_id_type=MESH)
        count += 1
    if shard_too:

        def one(k):
            pl.semaphore_signal(
                barrier, inc=1, device_id={"shard": lax.rem(z + 1 + k, shards)}, device_id_type=MESH
            )

        loop(shards - 1, one)
        count += shards - 1
    if tp_too:
        for d in range(1, TP):
            pl.semaphore_signal(
                barrier, inc=1, device_id={"tp": lax.rem(t + d, TP)}, device_id_type=MESH
            )
            count += 1
    pl.semaphore_wait(barrier, count)


class Moves:
    def __init__(self):
        self.gets, self.puts = {}, {}

    def get(self, *names):
        for name in names:
            self.gets[name].wait()

    def put(self, *names):
        for name in names:
            self.puts[name].start()


def call_staged(kernel, args, out, late, early, scratch, left=(), **params):
    spaces = [pl.BlockSpec(memory_space=pltpu.VMEM)] * (len(args) - 1)
    spaces.append(pl.BlockSpec(memory_space=pltpu.SMEM))
    out_spaces = [pl.BlockSpec(memory_space=pltpu.VMEM)] * len(out)
    hbm = pl.BlockSpec(memory_space=pl.ANY)
    for at in (*late.values(), *left):
        spaces[at] = hbm
    for at in early.values():
        out_spaces[at] = hbm
    extra = [pltpu.VMEM(args[at].shape, args[at].dtype) for at in late.values()]
    extra += [pltpu.VMEM(*out[at]) for at in early.values()]
    dma = pltpu.SemaphoreType.DMA
    sems = [dma((len(late),)), dma((len(early),))]

    def body(*refs):
        split = len(args) + len(out)
        given, inner = list(refs[:split]), refs[split : split + len(scratch)]
        held, (get_sem, put_sem) = list(refs[split + len(scratch) : -2]), refs[-2:]
        moves = Moves()
        for n, (name, at) in enumerate(late.items()):
            buffer = held.pop(0)
            moves.gets[name] = pltpu.make_async_copy(given[at], buffer, get_sem.at[n])
            moves.gets[name].start()
            given[at] = buffer
        for n, (name, at) in enumerate(early.items()):
            buffer = held.pop(0)
            moves.puts[name] = pltpu.make_async_copy(buffer, given[len(args) + at], put_sem.at[n])
            given[len(args) + at] = buffer
        kernel(moves, *given, *inner)
        for copy in moves.puts.values():
            copy.wait()

    return pl.pallas_call(
        body,
        out_shape=[jax.ShapeDtypeStruct(*o) for o in out],
        in_specs=spaces,
        out_specs=out_spaces,
        scratch_shapes=list(scratch) + extra + sems,
        **params,
    )(*args)


class Gather:
    def __init__(self, shards, src, dst, zsend, fsend, csend, recv, own, cols=None):
        self.s, self.dst, self.cols = shards, dst, cols
        self.src = src if cols is None else src.at[:, cols]
        self.zsend, self.fsend, self.csend, self.recv, self.own = zsend, fsend, csend, recv, own
        self.z, self.c = lax.axis_index("shard"), lax.axis_index("ctx")
        self.r = src.shape[0]

    def block(self, g):
        rows = rows_of(g, self.r)
        return self.dst.at[rows] if self.cols is None else self.dst.at[rows, self.cols]

    def inside(self, zz):
        return (zz >= 0) & (zz < self.s)

    def straight(self, steps, way):
        g = 2 * self.z + self.c
        kind = steps - 1 + (0 if way > 0 else 2)
        return remote(
            self.src, self.block(g), self.zsend.at[kind], self.recv.at[g], shard=self.z + way * steps
        )

    def onward(self, zz, way):
        there = self.block(2 * zz + self.c)
        return remote(
            there, there, self.fsend.at[zz], self.recv.at[2 * zz + self.c], shard=self.z + way
        )

    def to_core(self, zz, core):
        there = self.block(2 * zz + core)
        return remote(
            there, there, self.csend.at[zz], self.recv.at[2 * zz + core], ctx=1 - self.c
        )

    def straight_ones(self, act_on):
        for steps in (2, 1):
            for way in (1, -1):

                @pl.when(self.inside(self.z + way * steps))
                def go(steps=steps, way=way):
                    act_on(self.straight(steps, way))

    def start(self):
        keep = pltpu.make_async_copy(self.src, self.block(2 * self.z + self.c), self.own)
        keep.start()
        self.straight_ones(lambda copy: copy.start())
        keep.wait()
        self.to_core(self.z, self.c).start()

    def forward(self, first=0, last=None):
        def one(k):
            for way in (1, -1):
                zz = self.z - way * (k + 1)

                @pl.when(self.inside(zz))
                def came(way=way, zz=zz):
                    self.to_core(zz, self.c).wait_recv()
                    self.to_core(zz, self.c).start()

                    @pl.when((k >= 1) & self.inside(self.z + way))
                    def pass_on():
                        self.onward(zz, way).start()

        lax.fori_loop(
            first, self.s - 1 if last is None else last, lambda k, carry: (one(k), carry)[1], 0
        )

    def finish(self):
        loop(self.s, lambda zz: self.to_core(zz, 1 - self.c).wait_recv())
        loop(self.s, lambda zz: self.to_core(zz, self.c).wait_send())
        self.straight_ones(lambda copy: copy.wait_send())

        def passed(k):
            for way in (1, -1):
                zz = self.z - way * (k + 1)

                @pl.when(self.inside(zz) & self.inside(self.z + way))
                def on(way=way, zz=zz):
                    self.onward(zz, way).wait_send()

        lax.fori_loop(1, self.s - 1, lambda k, carry: (passed(k), carry)[1], 0)

    @staticmethod
    def sems(shards):
        dma = pltpu.SemaphoreType.DMA
        return [dma((4,)), dma((shards,)), dma((shards,)), dma((2 * shards,)), dma(())]


class LineSum:
    def __init__(self, shards, src, hold, land, fsend, frecv, lsend, lrecv):
        self.s, self.src, self.hold, self.land = shards, src, hold, land
        self.fsend, self.frecv, self.lsend, self.lrecv = fsend, frecv, lsend, lrecv
        self.z = lax.axis_index("shard")

    def place(self, dest, way):
        return dest - 3 if way > 0 else dest

    def onward(self, src, dest, way):
        at = self.place(dest, way)
        return remote(
            src, self.hold.at[at], self.fsend.at[at], self.frecv.at[at], shard=self.z + way
        )

    def straight(self, src, steps, way):
        kind = steps - 1 + (0 if way > 0 else 2)
        return remote(
            src,
            self.land.at[kind],
            self.lsend.at[kind],
            self.lrecv.at[kind],
            shard=self.z + way * steps,
        )

    def each(self, far, two, one, waited):
        for way in (1, -1):
            first = self.z == 0 if way > 0 else self.z == self.s - 1
            now = jnp.logical_not(first) if waited else first

            def along(j, way=way, now=now):
                dest = self.s - 1 - j if way > 0 else j
                distance = (dest - self.z) * way

                @pl.when(now & (distance >= 3))
                def three():
                    far(dest, way)

                @pl.when(now & (distance == 2))
                def both():
                    two(dest, way)

            loop(self.s, along)
            if not waited:
                other = self.z + way

                @pl.when((other >= 0) & (other < self.s))
                def next_one(way=way, other=other):
                    one(other, way)

    def start(self):
        self.each(
            lambda dest, way: self.onward(self.src.at[dest], dest, way).start(),
            lambda dest, way: self.straight(self.src.at[dest], 2, way).start(),
            lambda dest, way: self.straight(self.src.at[dest], 1, way).start(),
            False,
        )

    def relay(self):
        def added(dest, way):
            at = self.place(dest, way)
            self.onward(self.src.at[dest], dest, way).wait_recv()
            own = self.src[dest].astype(f32)
            self.hold[at] = (own + self.hold[at].astype(f32)).astype(bf16)
            return self.hold.at[at]

        self.each(
            lambda dest, way: self.onward(added(dest, way), dest, way).start(),
            lambda dest, way: self.straight(added(dest, way), 2, way).start(),
            None,
            True,
        )

    def finish(self, out):
        out[...] = self.src[self.z].astype(f32)
        for steps in (1, 2):
            for way in (1, -1):
                source = self.z - way * steps

                @pl.when((source >= 0) & (source < self.s))
                def arrived(steps=steps, way=way):
                    kind = steps - 1 + (0 if way > 0 else 2)
                    remote(
                        self.land.at[kind],
                        self.land.at[kind],
                        self.lsend.at[kind],
                        self.lrecv.at[kind],
                        shard=self.z - way * steps,
                    ).wait_recv()
                    out[...] += self.land[kind].astype(f32)

        for waited in (False, True):
            self.each(
                lambda dest, way: self.onward(self.src.at[dest], dest, way).wait_send(),
                lambda dest, way: self.straight(self.src.at[dest], 2, way).wait_send(),
                lambda dest, way: self.straight(self.src.at[dest], 1, way).wait_send(),
                waited,
            )

    @staticmethod
    def scratch(shards, rows, cols):
        dma = pltpu.SemaphoreType.DMA
        far, r = max(shards - 3, 1), rows // (2 * shards)
        return [
            pltpu.VMEM((far, r, cols), bf16),
            pltpu.VMEM((4, r, cols), bf16),
            dma((far,)),
            dma((far,)),
            dma((4,)),
            dma((4,)),
        ]


class Scatter:
    def __init__(self, shards, src, sib, csend, crecv, *line):
        self.s, self.src, self.sib = shards, src, sib
        self.csend, self.crecv = csend, crecv
        self.c = lax.axis_index("ctx")
        self.r = src.shape[0] // (2 * shards)
        self.line = LineSum(shards, sib, *line)

    def to_core(self, k):
        return remote(
            self.src.at[rows_of(2 * k + 1 - self.c, self.r)],
            self.sib.at[k],
            self.csend.at[k],
            self.crecv.at[k],
            ctx=1 - self.c,
        )

    def start(self):
        loop(self.s, lambda k: self.to_core(k).start())

    def middle(self):
        def one(k):
            self.to_core(k).wait_recv()
            both = self.src[rows_of(2 * k + self.c, self.r), :].astype(f32)
            self.sib[k] = (both + self.sib[k].astype(f32)).astype(bf16)

        loop(self.s, one)
        self.line.start()

    def relay(self):
        self.line.relay()

    def finish(self, out):
        self.line.finish(out)
        loop(self.s, lambda k: self.to_core(k).wait_send())

    @staticmethod
    def scratch(shards, rows, cols):
        dma = pltpu.SemaphoreType.DMA
        block = pltpu.VMEM((shards, rows // (2 * shards), cols), bf16)
        return [block, dma((shards,)), dma((shards,))] + LineSum.scratch(shards, rows, cols)


class ChipSum:
    def __init__(self, shards, src, sib, cols, csend, crecv):
        self.s, self.src, self.sib, self.cols = shards, src, sib, cols
        self.csend, self.crecv = csend, crecv
        self.c = lax.axis_index("ctx")
        self.r = src.shape[0] // (2 * shards)

    def to_core(self, k):
        return remote(
            self.src.at[rows_of(2 * k + 1 - self.c, self.r), self.cols],
            self.sib.at[k, :, self.cols],
            self.csend.at[k],
            self.crecv.at[k],
            ctx=1 - self.c,
        )

    def start(self):
        loop(self.s, lambda k: self.to_core(k).start())

    def finish(self):
        def one(k):
            self.to_core(k).wait_recv()
            own = self.src[rows_of(2 * k + self.c, self.r), self.cols].astype(f32)
            self.sib[k, :, self.cols] = (own + self.sib[k, :, self.cols].astype(f32)).astype(bf16)

        loop(self.s, one)
        loop(self.s, lambda k: self.to_core(k).wait_send())


class Square:
    def __init__(self, kinds):
        tp = lax.axis_index("tp")
        self.me = tp
        self.x = tp + 1 - 2 * lax.rem(tp, 2)
        self.y = lax.rem(tp + 2, TP)
        self.across = TP - 1 - tp
        self.send, self.recv = kinds

    def copy(self, kind, b, src, dst):
        to = self.y if kind in (1, 2) else self.x
        return remote(src, dst, self.send.at[kind, b], self.recv.at[kind, b], tp=to)


class SquareScatter(Square):
    def __init__(self, buffers, kinds):
        super().__init__(kinds)
        self.out, self.into, self.out2, self.into2 = buffers

    def first(self, kind, b):
        return self.copy(kind, b, self.out.at[kind, b], self.into.at[kind, b])

    def second(self, kind, b):
        return self.copy(kind, b, self.out2.at[kind - 2, b], self.into2.at[kind - 2, b])

    def start(self, b, ref, rows):
        half = ref.shape[1] // 2
        left, right = pl.ds(0, half), pl.ds(half, half)
        self.out[0, b, 0] = ref[rows(self.x), left].astype(bf16)
        self.out[0, b, 1] = ref[rows(self.across), left].astype(bf16)
        self.first(0, b).start()
        self.out[1, b, 0] = ref[rows(self.y), right].astype(bf16)
        self.out[1, b, 1] = ref[rows(self.across), right].astype(bf16)
        self.first(1, b).start()
        self.out2[0, b] = ref[rows(self.y), left].astype(bf16)
        self.out2[1, b] = ref[rows(self.x), right].astype(bf16)

    def relay(self, b):
        for kind in (0, 1):
            self.first(kind, b).wait_recv()
            own = self.out2[kind, b].astype(f32)
            self.out2[kind, b] = (own + self.into[kind, b, 1].astype(f32)).astype(bf16)
            self.second(kind + 2, b).start()

    def finish(self, b):
        sums = []
        for kind in (0, 1):
            self.second(kind + 2, b).wait_recv()
            sums.append(self.into[kind, b, 0].astype(f32) + self.into2[kind, b].astype(f32))
        return jnp.concatenate(sums, axis=1)

    def sent(self, b):
        for kind in (0, 1):
            self.first(kind, b).wait_send()
            self.second(kind + 2, b).wait_send()

    @staticmethod
    def scratch(blocks, sub):
        first = pltpu.VMEM((2, blocks, 2, sub, D // 2), bf16)
        second = pltpu.VMEM((2, blocks, sub, D // 2), bf16)
        return [first, first, second, second]


class SquareGather(Square):
    def __init__(self, ref, part, kinds):
        super().__init__(kinds)
        self.ref, self.part = ref, part

    def whole(self, kind, b, owner):
        there = self.ref.at[self.part(b, owner)]
        return self.copy(kind, b, there, there)

    def half(self, kind, b, owner):
        half = self.ref.shape[1] // 2
        there = self.ref.at[self.part(b, owner), pl.ds((kind - 2) * half, half)]
        return self.copy(kind, b, there, there)

    def start(self, b):
        for kind in (0, 1):
            self.whole(kind, b, self.me).start()

    def relay(self, b):
        for kind, owner in ((0, self.x), (1, self.y)):
            self.whole(kind, b, owner).wait_recv()
            self.half(kind + 2, b, owner).start()

    def finish(self, b):
        for kind in (2, 3):
            self.half(kind, b, self.across).wait_recv()

    def sent(self, b):
        for kind, owner in ((0, self.x), (1, self.y)):
            self.whole(kind, b, self.me).wait_send()
            self.half(kind + 2, b, owner).wait_send()


def sigmoid(v):
    return 1.0 / (1.0 + jnp.exp(-v))


def softplus(v):
    return jnp.maximum(v, 0.0) + jnp.log1p(jnp.exp(-jnp.abs(v)))


def swap_half(v):
    width = v.shape[1]
    low = iota(v.shape, 1) % HD < HD // 2
    return jnp.where(low, pltpu.roll(v, width - HD // 2, 1), pltpu.roll(v, HD // 2, 1))


def low_lanes(shape):
    return iota(shape, 1) < 64


def parts(v, count):
    found = []
    for _ in range(count):
        part = v.astype(bf16)
        found.append(part)
        v = v - part.astype(f32)
    return found


def packed(v):
    v = jnp.where(iota(v.shape, 1) < 8, v, 0.0)
    high, middle, low = (part.astype(f32) for part in parts(v, 3))
    return (high + pltpu.roll(middle, 8, 1) + pltpu.roll(low, 16, 1)).astype(bf16)


def unpacked(v):
    v = v + pltpu.roll(v, 120, 1) + pltpu.roll(v, 112, 1)
    return jnp.where(iota(v.shape, 1) < 8, v, 0.0)


def spread(v):
    lane, channel = iota((N, WI), 0), iota((N, WI), 1)
    pick = ((lane % 8 == channel // P_SIZE) & (lane < 24)).astype(bf16)
    return nn(packed(v), pick)


def fold(v):
    pick = (iota((WI, N), 0) // P_SIZE == iota((WI, N), 1)).astype(bf16)
    high, low = parts(v, 2)
    return nn(high, pick) + nn(low, pick)


def row_sums_of(v, pick=None):
    pick = jnp.ones((8, v.shape[1]), bf16) if pick is None else pick
    high, low = parts(v, 2)
    return nt(pick, high) + nt(pick, low)


def as_column(row):
    at = iota(row.shape, 0)
    first = jnp.broadcast_to(row[0:1, :], row.shape)
    high, middle, low = parts(first, 3)
    three = jnp.where(at == 0, high, jnp.where(at == 1, middle, low))
    return tn(three, (iota((8, N), 0) < 3).astype(bf16))


def turned_over(v):
    one = eye(v.shape[0])
    high, middle, low = parts(v, 3)
    return tn(high, one) + tn(middle, one) + tn(low, one)


def wide(column, width):
    return jnp.concatenate([column] * (width // column.shape[1]), axis=1)


def lower_ones():
    return (iota((L, L), 0) >= iota((L, L), 1)).astype(bf16)


def head_scalars(dt_raw, prm):
    real = iota(dt_raw.shape, 1) < HL
    steps = jnp.where(real, softplus(dt_raw + prm[0:1, :]), 0.0)
    rates = steps * prm[1:2, :]
    return steps, rates


def pair_columns(v, pair):
    return v[:, 128 * pair : 128 * pair + 128]


def own_half(v, half):
    return jnp.where(low_lanes(v.shape) == (half == 0), v, jnp.zeros_like(v))


def eye(n):
    return (iota((n, n), 0) == iota((n, n), 1)).astype(bf16)


def rotary_of(table, rows):
    both = table[rows, :]
    first = iota(both.shape, 1) % HD < HD // 2
    cosine = jnp.where(first, both, pltpu.roll(both, HD // 2, 1))
    sine = jnp.where(first, -pltpu.roll(both, 128 - HD // 2, 1), both)
    return cosine, sine


FORWARD_EARLY = (
    "wf1",
    "wf2",
    "normed",
    "z_out",
    "cin",
    "dt_raw",
    "pre",
    "q_low",
    "kk",
    "vv",
    "att",
    "att_low",
    "steps_out",
    "cum_out",
)
FORWARD_AT = (
    0,
    1,
    4,
    6,
    7,
    8,
    12,
    14,
    15,
    16,
    17,
    18,
    22,
    23,
)
BACKWARD_LATE = (
    "chip",
    "grad_att",
    "q_low",
    "kk",
    "vv",
    "att",
    "lse_row",
    "start",
    "steps_in",
    "dt_raw",
    "cin",
    "normed",
    "wf1",
    "wf2",
    "hid_own",
    "grad_own",
)
BACKWARD_AT = (
    4,
    1,
    9,
    10,
    11,
    12,
    13,
    15,
    16,
    19,
    7,
    24,
    25,
    26,
    27,
    28,
)


def forward_kernel(
    shards, moves,
    hid, w_z, w_x, w_shared, w_dt, w_q, w_out, w_o, w_gate, gain_one, gain_two,
    conv_w, conv_b, gated_gain, dt_bias, a_log, d_skip, table, length,
    wf1, wf2, wo, wg, normed, gains, z_out, cin, dt_raw, taps, prm, chan,
    pre, hist, q_low, kk, vv, att, att_low, lse_row, ssd, start, steps_out, cum_out, tot_out,
    gated_low, square,
    small, wa1, wa2, wa3, stat, zf, pad, act, state, carried, scores_m, scores_l, hist_in,
    zs1, fs1, cs1, zr1, own1, zs2, fs2, cs2, zr2, own2, zs3, fs3, cs3, zr3, own3,
    zs4, fs4, cs4, zr4, own4, zs5, fs5, cs5, zr5, own5,
    xs, xr,
):
    c, tp = lax.axis_index("ctx"), lax.axis_index("tp")
    t = hid.shape[0]
    blocks = t // L
    r = w_z.shape[0]

    kv = tp * (NQ // TP) // (NQ // KV)
    keys = w_shared[:, 2 * N : 2 * N + 128].astype(f32)
    vals = w_shared[:, 2 * N + 128 : 2 * N + 256].astype(f32)
    low_r = low_lanes((r, 128))
    other = pltpu.roll(jnp.where(kv == 0, vals, keys), 64, 1)
    wa1[:, 0:128] = w_q[...]
    wa1[:, 128:256] = jnp.where(
        kv == 0, jnp.where(low_r, keys, other), jnp.where(low_r, other, vals)
    ).astype(bf16)
    head_pick = (
        (iota((H, 128), 0) == iota((H, 128), 1) + tp * HL) & (iota((H, 128), 1) < HL)
    ).astype(bf16)
    row8, lane8 = iota((8, 128), 0), iota((8, 128), 1)
    gain_pick = ((row8 < 2) & (lane8 == GAIN_COL + row8)).astype(bf16)
    gain_rows = jnp.where(
        iota((8, r), 0) == 0, gain_one[...].astype(f32), gain_two[...].astype(f32)
    ).astype(bf16)
    wa1[:, 256:384] = (tn(w_dt[...], head_pick) + tn(gain_rows, gain_pick)).astype(bf16)
    wa2[:, 0:WI] = w_z[...]
    wa2[:, WI : 2 * WI] = w_x[...]
    wa2[:, 2 * WI : 2 * WI + 2 * N] = w_shared[:, 0 : 2 * N]
    greet(shards, False)
    gather1 = Gather(shards, wa1, wf1, zs1, fs1, cs1, zr1, own1)
    gather2 = Gather(shards, wa2, wf2, zs2, fs2, cs2, zr2, own2, pl.ds(WI, CH))
    gather5 = Gather(shards, wa2, wf2, zs5, fs5, cs5, zr5, own5, pl.ds(0, WI))
    gather3 = Gather(shards, wa3, wo, zs3, fs3, cs3, zr3, own3)
    gather4 = Gather(shards, w_gate, wg, zs4, fs4, cs4, zr4, own4)
    gather1.start()
    gather2.start()
    wa3[:, CO:CW] = nt(eye(r), w_out[...]).astype(bf16)
    wa3[:, CW:CG] = nt(eye(r), w_o[...]).astype(bf16)

    mine = pl.ds(pl.multiple_of(tp * WI, 128), WI)
    small[...] = jnp.zeros_like(small)
    small[0:1, :] = conv_b[...].astype(f32)[None, :]
    small[1:2, 0:DI] = gated_gain[...].astype(f32)[None, :]
    small[8:9, 0:H] = dt_bias[...].astype(f32)[None, :]
    small[9:10, 0:H] = a_log[...].astype(f32)[None, :]
    small[10:11, 0:H] = d_skip[...].astype(f32)[None, :]
    taps[0:CONVW, 0:WI] = conv_w[:, mine].astype(f32)
    taps[0:CONVW, WI:CH] = conv_w[:, DI:].astype(f32)
    taps[CONVW : CONVW + 1, 0:WI] = small[0:1, mine]
    taps[CONVW : CONVW + 1, WI:CH] = small[0:1, DI:]
    taps[CONVW + 1 :, :] = jnp.zeros((8 - CONVW - 1, CH), f32)
    heads = pltpu.roll(small[8:16, 0:128], lax.rem(128 - tp * HL, 128), 1)
    heads = jnp.where(lane8 < HL, jnp.where(row8 == 1, -jnp.exp(heads), heads), 0.0)
    prm[...] = heads
    chan[...] = jnp.zeros_like(chan)
    chan[0:1, :] = small[1:2, mine]
    chan[1:2, :] = spread(heads)[2:3, :]

    def swap(src, dst, i):
        return remote(src, dst, xs.at[i], xr.at[i], ctx=1 - c)

    def row_scale(i):
        rows = rows_of(i)
        x = hid[rows, :].astype(f32)
        scale = lax.rsqrt(jnp.mean(x * x, -1, keepdims=True) + EPS)
        stat[rows, :] = jnp.broadcast_to(scale, (L, 128))

    loop(blocks, row_scale)
    gather1.forward()
    gather1.finish()
    gather5.start()
    turned = wf1[:, 256:384].astype(f32).T
    gains[...] = turned[GAIN_COL : GAIN_COL + 8]
    gain = gains[0:1, :]
    low128 = low_lanes((L, 128))
    moves.put("wf1")
    moves.get("table")

    def first_projections(i):
        rows = rows_of(i)
        low = (hid[rows, :].astype(f32) * wide(stat[rows, :], D) * gain).astype(bf16)
        normed[rows, :] = low
        rest = nn(low, wf1[...])
        cosine, sine = rotary_of(table, pl.ds(pl.multiple_of(c * t + i * L, L), L))
        v = rest[:, 0:128]
        q_low[rows, :] = (v * cosine + swap_half(v) * sine).astype(bf16)
        v = rest[:, 128:256]
        other = pltpu.roll(v, 64, 1)
        twice = jnp.where(low128, v, other)
        kk[0, rows, :] = (twice * cosine + swap_half(twice) * sine).astype(bf16)
        vv[0, rows, :] = jnp.where(low128, other, v).astype(bf16)
        dt_raw[rows, :] = rest[:, 256:384]

    loop(blocks, first_projections)
    moves.put("normed", "q_low", "dt_raw")
    keys = swap(kk.at[0], kk.at[1], 1)
    keys.start()
    vals = swap(vv.at[0], vv.at[1], 2)
    vals.start()

    scale = HD ** (-0.5)
    limit = length[0] - c * t

    def stacked(v):
        return jnp.concatenate([own_half(v, 0), own_half(v, 1)], axis=0)

    for i in range(blocks):
        rows = pl.ds(i * L, L)
        width = (i + 1) * L
        q2 = stacked(q_low[rows, :].astype(f32)).astype(bf16)
        s = nt(q2, kk[0, 0:width, :]) * scale
        at = iota(s.shape, 0) % L + i * L
        col = iota(s.shape, 1)
        s = jnp.where((col <= at) & (col < limit), s, FILL)
        peak = jnp.max(s, -1, keepdims=True)
        e = jnp.exp(s - peak)
        total = jnp.sum(e, -1, keepdims=True)
        o = nn(e.astype(bf16), vv[0, 0:width, :])
        scores_m[...] = jnp.broadcast_to(peak, (2 * L, 128))
        scores_l[0] = jnp.broadcast_to(total, (2 * L, 128))
        scores_l[1] = o
        if i == 0:
            keys.wait_recv()
            vals.wait_recv()

        @pl.when(c > 0)
        def earlier():
            s2 = nt(q2, kk[1]) * scale
            old = scores_m[:, 0:1]
            new = jnp.maximum(old, jnp.max(s2, -1, keepdims=True))
            e2 = jnp.exp(s2 - new)
            fade = jnp.exp(old - new)
            scores_m[...] = jnp.broadcast_to(new, (2 * L, 128))
            scores_l[0] = fade * scores_l[0] + jnp.sum(e2, -1, keepdims=True)
            scores_l[1] = fade * scores_l[1] + nn(e2.astype(bf16), vv[1])

        total = scores_l[0]
        o = scores_l[1] / total
        o = jnp.where(low128, o[:L], o[L:])
        att[rows, :] = o
        att_low[rows, :] = o.astype(bf16)
        logs = scores_m[...] + jnp.log(total)
        turned = jnp.where(low128, logs[:L], logs[L:]).T
        lse_row[0:1, rows] = turned[0:1]
        lse_row[1:2, rows] = turned[64:65]
        lse_row[2:8, rows] = jnp.zeros((6, L), f32)
        if i == blocks - 3:
            gather2.forward(0, 2)
        if i == blocks - 2:
            gather2.forward(2)
            gather3.start()
    moves.put("kk", "vv", "att", "att_low")
    gather5.forward(0, 2)
    gather2.finish()

    def conv_input(k):
        i = blocks - 1 - k
        rows = rows_of(i)
        v = nn(normed[rows, :], wf2[:, WI:]).astype(bf16)
        cin[rows, :] = v
        pad[pl.ds(pl.multiple_of(i * L + 8, 8), L), :] = v.astype(f32)

    conv_input(0)
    tail = swap(cin.at[pl.ds(t - 16, 16)], hist_in, 0)
    tail.start()
    lax.fori_loop(1, blocks, lambda k, carry: (conv_input(k), carry)[1], 0)
    gather5.forward(2)
    gather4.start()
    tail.wait_recv()
    before = hist_in[8:16, :].astype(f32)
    hist[...] = jnp.where((iota((8, CH), 0) >= 5) & (c > 0), before, 0.0)
    pad[0:8, :] = hist[...]
    ones = lower_ones()
    state[...] = jnp.zeros_like(state)

    for i in range(blocks):
        rows = pl.ds(i * L, L)
        v = taps[4:5, :] + taps[0:1, :] * pad[pl.ds(i * L + 5, L), :]
        for j in range(1, CONVW):
            v = v + taps[j : j + 1, :] * pad[pl.ds(i * L + 5 + j, L), :]
        pre[rows, :] = v
        a = v * sigmoid(v)
        act[rows, :] = a
        steps, rates = head_scalars(dt_raw[rows, :], prm)
        cum = unpacked(nn(ones, packed(rates)))
        tot = cum[L - 1 : L, :]
        steps_out[rows, :] = steps
        cum_out[rows, :] = cum
        tot_out[i] = jnp.broadcast_to(tot, (8, 128))
        weight = spread(jnp.exp(tot - cum) * steps)
        start[i] = state[...]
        add = tn(a[:, WI : WI + N].astype(bf16), (weight * a[:, :WI]).astype(bf16))
        decay = spread(jnp.broadcast_to(jnp.exp(tot), (8, 128)))[0:1, :]
        state[...] = decay * state[...] + add

    states = swap(state, carried, 3)
    states.start()
    moves.put("cin", "pre", "steps_out", "cum_out")
    gather3.forward(0, 2)

    gather5.finish()
    moves.put("wf2")

    def gate_input(i):
        rows = rows_of(i)
        zf[rows, :] = nn(normed[rows, :], wf2[:, 0:WI])
        z_out[rows, :] = zf[rows, :].astype(bf16)

    loop(blocks, gate_input)
    moves.put("z_out")

    states.wait_recv()
    gather3.forward(2)
    carried[...] = jnp.where(c > 0, carried[...], 0.0)
    mask = iota((L, L), 0) >= iota((L, L), 1)
    for i in range(blocks):
        rows = pl.ds(i * L, L)
        if i > 0:
            decay = spread(jnp.exp(tot_out[i - 1]))[0:1, :]
            carried[...] = carried[...] * decay
        start[i] = start[i] + carried[...]
        s0 = start[i].astype(bf16)
        steps, cum = steps_out[rows, :], cum_out[rows, :]
        x = act[rows, 0:WI]
        xl = x.astype(bf16)
        in_map = act[rows, WI : WI + N].astype(bf16)
        out_map = act[rows, WI + N : CH].astype(bf16)
        gram = nt(out_map, in_map)
        cum_t, steps_t = cum.T, steps.T
        inner = []
        for pair in range(HL // 2):
            halves = []
            for half in range(2):
                h = 2 * pair + half
                decay = jnp.exp(jnp.where(mask, cum[:, h : h + 1] - cum_t[h : h + 1, :], FILL))
                mixing = gram * decay * steps_t[h : h + 1, :]
                halves.append(nn(mixing.astype(bf16), pair_columns(xl, pair)))
            inner.append(jnp.where(low128, halves[0], halves[1]))
        y = jnp.concatenate(inner, axis=1)
        y = y + spread(jnp.exp(cum)) * nn(out_map, s0) + chan[1:2, :] * x
        ssd[rows, :] = y.astype(bf16)
        zz = zf[rows, :]
        gated = y * zz * sigmoid(zz)
        gated_low[rows, :] = (gated * chan[0:1, :]).astype(bf16)
        square[:, rows] = row_sums_of(gated * gated)
        if i == 1:
            gather4.forward(0, 2)

    gather4.forward(2)
    gather3.finish()
    gather4.finish()
    for copy in (tail, keys, vals, states):
        copy.wait_send()


def forward(shards, *args):
    t, r = args[0].shape[0], args[1].shape[0]
    out = [
        ((D, 384), bf16),
        ((D, 1024), bf16),
        ((D, CG), bf16),
        ((D, FFL), bf16),
        ((t, D), bf16),
        ((8, D), f32),
        ((t, WI), bf16),
        ((t, CH), bf16),
        ((t, 128), f32),
        ((8, CH), f32),
        ((8, 128), f32),
        ((8, WI), f32),
        ((t, CH), f32),
        ((8, CH), f32),
        ((t, 128), bf16),
        ((2, t, 128), bf16),
        ((2, t, 128), bf16),
        ((t, 128), f32),
        ((t, 128), bf16),
        ((8, t), f32),
        ((t, WI), bf16),
        ((t // L, N, WI), f32),
        ((t, 128), f32),
        ((t, 128), f32),
        ((t // L, 8, 128), f32),
        ((t, WI), bf16),
        ((8, t), f32),
    ]
    dma = pltpu.SemaphoreType.DMA
    scratch = (
        [
            pltpu.VMEM((16, DI + 2 * N), f32),
            pltpu.VMEM((r, 384), bf16),
            pltpu.VMEM((r, 1024), bf16),
            pltpu.VMEM((r, CG), bf16),
            pltpu.VMEM((t, 128), f32),
            pltpu.VMEM((t, WI), f32),
            pltpu.VMEM((t + 8, CH), f32),
            pltpu.VMEM((t, CH), f32),
            pltpu.VMEM((N, WI), f32),
            pltpu.VMEM((N, WI), f32),
            pltpu.VMEM((2 * L, 128), f32),
            pltpu.VMEM((2, 2 * L, 128), f32),
            pltpu.VMEM((16, CH), bf16),
        ]
        + Gather.sems(shards) * 5
        + [dma((4,)), dma((4,))]
    )
    return call_staged(
        functools.partial(forward_kernel, shards),
        args,
        out,
        {"table": 17},
        dict(zip(FORWARD_EARLY, FORWARD_AT)),
        scratch,
        compiler_params=pltpu.CompilerParams(
            collective_id=1, has_side_effects=True, vmem_limit_bytes=VLIMIT
        ),
        name="mix_forward",
    )


def ffn_kernel(
    shards, moves,
    hid, cot, gl, att, square, wb, wg, w_up, w_down, gains, length,
    osend, grad_own, chip, hid_own, gain_grad, total_square, ggl, grad_att, dots,
    grads, grad_res, partial, seed, low_two, proj, grad_act, act, gg, gu, gown, back,
    unit, scale_keep, sqall, wm, wm_own, a1, a2, a3, a4, b1, b2, b3, b4,
    zs, fs, cs, zr, own_sem, ms, mr, ws, wr, sqs, sqr, s1, r1, ns, nr, gs, gr, hs, hr,
):
    t = hid.shape[0]
    tp, c = lax.axis_index("tp"), lax.axis_index("ctx")
    blocks = t // L
    sub = L // TP
    width = D // TP
    wm_own[:, 0:FFL] = w_up[...]
    wm_own[:, FFL:] = nt(eye(w_down.shape[1]), w_down[...]).astype(bf16)
    greet(shards, True)
    gather = Gather(shards, wm_own, wm, zs, fs, cs, zr, own_sem)
    gather.start()
    mlp_sum = ChipSum(shards, grads, chip, pl.ds(CG, CB - CG), ms, mr)
    out_sum = ChipSum(shards, grads, chip, pl.ds(CO, CG - CO), ws, wr)

    def peer(d):
        return lax.rem(tp + d, TP)

    def part(b, owner):
        return pl.ds(pl.multiple_of(b * L + owner * sub, sub), sub)

    def kept(b):
        return rows_of(b, sub)

    def square_to(d):
        return remote(sqall.at[tp], sqall.at[tp], sqs.at[d], sqr.at[tp], tp=peer(d))

    def square_from(d):
        return remote(sqall.at[tp], sqall.at[peer(d)], sqs.at[d], sqr.at[peer(d)], tp=peer(d))

    first = SquareScatter((a1, a2, a3, a4), (s1, r1))
    norms = SquareGather(low_two, part, (ns, nr))
    gradients = SquareScatter((b1, b2, b3, b4), (gs, gr))
    residuals = SquareGather(grad_res, part, (hs, hr))

    sqall[tp] = square[...]
    for d in range(1, TP):
        square_to(d).start()
    limit = length[0] - c * t

    def mask_seed(i):
        rows = rows_of(i)
        live = iota((L, D), 0) + i * L < limit
        seed[rows, :] = jnp.where(live, cot[rows, :].astype(f32), 0.0).astype(bf16)

    for d in range(1, TP):
        square_from(d).wait_recv()
    total_square[...] = sqall[0] + sqall[1] + sqall[2] + sqall[3]
    gain = gains[1:2, :]
    gain_grad[...] = jnp.zeros_like(gain_grad)

    def mix(b):
        rows = rows_of(b)
        scale = lax.rsqrt(total_square[:, rows] / DI + EPS)
        column = wide(as_column(scale), D)
        partial[rows, :] = nt(gl[rows, :], wb[:, CO:CW]) * column + nt(att[rows, :], wb[:, CW:CG])
        first.start(b, partial, lambda owner: part(b, owner))

    def norm(b):
        own = part(b, tp)
        hid_own[kept(b), :] = hid[own, :]
        acc = hid[own, :].astype(f32) + partial[own, :] + first.finish(b)
        scale = lax.rsqrt(jnp.mean(acc * acc, -1, keepdims=True) + EPS)
        scale_keep[kept(b), :] = jnp.broadcast_to(scale, (sub, 128))
        u = acc * scale
        unit[kept(b), :] = u
        low_two[own, :] = (u * gain).astype(bf16)
        norms.start(b)

    def act_grad(i):
        rows = rows_of(i)
        grad_act[rows, :] = nn(seed[rows, :], wm[:, FFL:])

    def hidden_units(b):
        rows = rows_of(b)
        norms.finish(b)
        low = low_two[rows, :]
        gate, up = nn(low, wg[...]), nn(low, wm[:, 0:FFL])
        sig = sigmoid(gate)
        silu = gate * sig
        hidden_act = (silu * up).astype(bf16)
        act[rows, :] = hidden_act
        ga = grad_act[rows, :]
        g1 = (ga * up * (sig * (1.0 + gate * (1.0 - sig)))).astype(bf16)
        g2 = (ga * silu).astype(bf16)
        gg[rows, :] = g1
        gu[rows, :] = g2
        back[...] = nt(g1, wg[...]) + nt(g2, wm[:, 0:FFL])
        gown[kept(b), :] = back[kept(tp), :]
        gradients.start(b, back, kept)
        partial[rows, :] = partial[rows, :] + nt(hidden_act, wm[:, FFL:])
        mine = rows_of(tp, width)
        osend[0, rows, :] = (partial[rows, mine] + hid[rows, mine].astype(f32)).astype(bf16)
        for e in range(1, TP):
            osend[e, rows, :] = partial[rows, rows_of(peer(e), width)].astype(bf16)

    def norm_back(b):
        own = part(b, tp)
        g = gown[kept(b), :] + gradients.finish(b)
        u = unit[kept(b), :]
        gain_grad[...] += jnp.broadcast_to(jnp.sum(g * u, 0, keepdims=True), (8, D))
        weighted = g * gain
        mean = jnp.mean(weighted * u, -1, keepdims=True)
        res = seed[own, :].astype(f32) + scale_keep[kept(b), 0:1] * (weighted - u * mean)
        grad_own[kept(b), :] = res
        grad_res[own, :] = res.astype(bf16)
        residuals.start(b)

    def weight_grads(i):
        feats = rows_of(i)
        low = low_two[:, feats]
        grads[feats, CG:CU] = tn(low, gg[...]).astype(bf16)
        grads[feats, CU:CD] = tn(low, gu[...]).astype(bf16)

    def down_grads(i):
        feats = rows_of(i)
        grads[feats, CD:CB] = tn(seed[:, feats], act[...]).astype(bf16)

    def out_back(b):
        rows = rows_of(b)
        residuals.finish(b)
        square_scale = lax.rsqrt(total_square[:, rows] / DI + EPS)
        column = wide(as_column(square_scale), D)
        got = grad_res[rows, :]
        low = (column * got.astype(f32)).astype(bf16)
        proj[rows, :] = low
        product = nn(low, wb[:, CO:CW])
        ggl[rows, :] = product
        dots[:, rows] = row_sums_of(product * gl[rows, :].astype(f32))
        grad_att[rows, :] = nn(got, wb[:, CW:CG]).astype(bf16)

    def stage(s, delay, act_on):
        @pl.when((s >= delay) & (s < delay + blocks))
        def go():
            act_on(s - delay)

    def step(s):
        stage(s, 0, mix)

        @pl.when(s == 1)
        def masks():
            moves.get("hid", "cot", "wg")
            loop(blocks, mask_seed)

        @pl.when(s == 2)
        def pieces():
            gather.forward(0, 2)

        stage(s, 1, first.relay)
        stage(s, 2, norm)
        stage(s, 3, norms.relay)

        @pl.when(s == 3)
        def weights():
            gather.forward(2)
            gather.finish()
            loop(blocks, act_grad)

        stage(s, 4, hidden_units)

        @pl.when(s == blocks + 4)
        def fill():
            moves.put("osend")
            loop(D // L, weight_grads)

        stage(s, 5, gradients.relay)
        stage(s, 6, norm_back)

        @pl.when(s == blocks + 5)
        def more():
            loop(D // L, down_grads)
            mlp_sum.start()

        @pl.when(s == blocks + 6)
        def norms_done():
            moves.put("grad_own")

        stage(s, 7, residuals.relay)
        stage(s, 8, out_back)

    loop(blocks + 8, step)

    def out_grads(i):
        feats = rows_of(i)
        grads[feats, CO:CW] = tn(proj[:, feats], gl[...]).astype(bf16)
        grads[feats, CW:CG] = tn(grad_res[:, feats], att[...]).astype(bf16)

    loop(D // L, out_grads)
    out_sum.start()
    mlp_sum.finish()
    out_sum.finish()

    def sent(b):
        for exchange in (first, norms, gradients, residuals):
            exchange.sent(b)

    loop(blocks, sent)
    for d in range(1, TP):
        square_to(d).wait_send()


def ffn(shards, *args):
    t = args[0].shape[0]
    blocks, sub = t // L, L // TP
    kept = blocks * sub
    out = [
        ((TP, t, D // TP), bf16),
        ((kept, D), f32),
        ((shards, D // (2 * shards), CB), bf16),
        ((kept, D), bf16),
        ((8, D), f32),
        ((8, t), f32),
        ((t, WI), f32),
        ((t, 128), bf16),
        ((8, t), f32),
    ]
    dma = pltpu.SemaphoreType.DMA
    scratch = (
        [
            pltpu.VMEM((D, CB), bf16),
            pltpu.VMEM((t, D), bf16),
            pltpu.VMEM((t, D), f32),
            pltpu.VMEM((t, D), bf16),
            pltpu.VMEM((t, D), bf16),
            pltpu.VMEM((t, D), bf16),
            pltpu.VMEM((t, FFL), f32),
            pltpu.VMEM((t, FFL), bf16),
            pltpu.VMEM((t, FFL), bf16),
            pltpu.VMEM((t, FFL), bf16),
            pltpu.VMEM((kept, D), f32),
            pltpu.VMEM((L, D), f32),
            pltpu.VMEM((kept, D), f32),
            pltpu.VMEM((kept, 128), f32),
            pltpu.VMEM((TP, 8, t), f32),
            pltpu.VMEM((D, 2 * FFL), bf16),
            pltpu.VMEM((D // (2 * shards), 2 * FFL), bf16),
        ]
        + SquareScatter.scratch(blocks, sub) * 2
        + Gather.sems(shards)
        + [dma((shards,))] * 4
        + [dma((TP,))] * 2
        + [dma((TP, blocks))] * 8
    )
    return call_staged(
        functools.partial(ffn_kernel, shards),
        args,
        out,
        {"hid": 0, "cot": 1, "wg": 6},
        {"osend": 0, "grad_own": 1},
        scratch,
        compiler_params=pltpu.CompilerParams(
            collective_id=2, has_side_effects=True, vmem_limit_bytes=VLIMIT
        ),
        name="feed_forward",
    )


def backward_kernel(
    shards, moves,
    ggl, grad_att, dots_in, total_square, chip, osend,
    pre, cin, hist, q_low, kk, vv, att, lse_row, ssd, start, steps_in, cum_in, tot_in, dt_raw, z_in,
    taps, prm, chan, normed, wf1, wf2, hid_own, grad_own, gains, gain_two, table_all, length,
    output, low, grad_e, grad_l, grad_b, shared, vecs,
    table, own_out, lin, small, orecv, dots, dk, dv, dy, dpre, ends, dstate, carry, kv_out, kv_in, pad,
    edge_out, edge_in, gown, back, gain_one, grads_e, grads_l, misc, misc_low, misc_sum, shsend,
    vec_sib, vec_z,
    ln0, ln1, ln2, ln3, ln4, ln5,
    e0, e1, e2, e3, e4, e5, e6, e7, e8,
    l0, l1, l2, l3, l4, l5, l6, l7, l8,
    m0, m1, m2, m3, m4, m5, m6, m7, m8,
    g0, g1, g2, g3,
    table_sem, own_sem, vcs, vcr, vzs, vzr, xs, xr, ts, tr, os, orr, ss, sr, vts, vtr, gs, gr, hs, hr,
):
    z, c, tp = lax.axis_index("shard"), lax.axis_index("ctx"), lax.axis_index("tp")
    t = cin.shape[0]
    blocks, sub = t // L, L // TP
    get_table = pltpu.make_async_copy(table_all.at[rows_of(c, t)], table, table_sem)
    get_table.start()
    greet(shards, True)
    scatter = LineSum(shards, chip, ln0, ln1, ln2, ln3, ln4, ln5)
    scatter0 = Scatter(shards, grads_e, e0, e1, e2, e3, e4, e5, e6, e7, e8)
    scatter1 = Scatter(shards, grads_l, l0, l1, l2, l3, l4, l5, l6, l7, l8)
    scatter2 = Scatter(shards, misc_low, m0, m1, m2, m3, m4, m5, m6, m7, m8)
    moves.get("chip")
    scatter.start()

    def swap(src, dst, i):
        return remote(src, dst, xs.at[i], xr.at[i], ctx=1 - c)

    def peer(d):
        return lax.rem(tp + d, TP)

    def to_all(ref, send, recv, d):
        return remote(ref.at[tp], ref.at[tp], send.at[d], recv.at[tp], tp=peer(d))

    def from_all(ref, send, recv, d):
        return remote(ref.at[tp], ref.at[peer(d)], send.at[d], recv.at[peer(d)], tp=peer(d))

    dots[tp] = dots_in[...]
    for d in range(1, TP):
        to_all(dots, ts, tr, d).start()

    def out_to(d):
        return remote(osend.at[d], orecv.at[TP - 1 - d], os.at[d], orr.at[TP - 1 - d], tp=peer(d))

    def out_from(d):
        return remote(osend.at[d], orecv.at[d - 1], os.at[d], orr.at[d - 1], tp=peer(d))

    get_own = pltpu.make_async_copy(osend.at[0], own_out, own_sem)
    get_own.start()
    for d in range(1, TP):
        out_to(d).start()
    conv_grads = small.at[:, 0:CH]
    chan_grads = small.at[:, CH : CH + WI]
    head_grads = small.at[:, CH + WI : CH + WI + 128]
    low128 = low_lanes((L, 128))
    small[...] = jnp.zeros_like(small)
    for d in range(1, TP):
        from_all(dots, ts, tr, d).wait_recv()

    def gated_back(i):
        rows = rows_of(i)
        both = dots[0, :, rows] + dots[1, :, rows] + dots[2, :, rows] + dots[3, :, rows]
        share = both / ((total_square[:, rows] / DI + EPS) * DI)
        column = wide(as_column(share), WI)
        zz, y = z_in[rows, :].astype(f32), ssd[rows, :].astype(f32)
        sig = sigmoid(zz)
        silu = zz * sig
        gated = y * silu
        product = ggl[rows, :]
        chan_grads[0:1, :] += jnp.sum(product * gated, 0, keepdims=True)
        grad_gated = product * chan[0:1, :] - column * gated
        grad_y = grad_gated * silu
        dy[rows, :] = grad_y
        lin[rows, CZ:CX] = (grad_gated * y * (sig * (1.0 + zz * (1.0 - sig)))).astype(bf16)
        v = pre[rows, WI + N : CH]
        out_map = (v * sigmoid(v)).astype(bf16)
        ends[i] = tn(out_map, (spread(jnp.exp(cum_in[rows, :])) * grad_y).astype(bf16))

    loop(blocks, gated_back)
    dstate[...] = jnp.zeros_like(dstate)

    def chain(k):
        i = blocks - 1 - k
        add = ends[i]
        ends[i] = dstate[...]
        dstate[...] = spread(jnp.exp(tot_in[i]))[0:1, :] * dstate[...] + add

    loop(blocks, chain)
    states = swap(dstate, carry, 0)
    states.start()

    scale = HD ** (-0.5)
    limit = length[0] - c * t
    dk[...] = jnp.zeros_like(dk)
    dv[...] = jnp.zeros_like(dv)
    get_table.wait()
    moves.get("grad_att", "q_low", "kk", "vv", "att", "lse_row")
    head_of = ((iota((8, 128), 1) // HD) == iota((8, 128), 0)).astype(bf16)

    def stacked(v):
        return jnp.concatenate([own_half(v, 0), own_half(v, 1)], axis=0).astype(bf16)

    def side_by_side(v):
        return jnp.concatenate([v[0:1, :], v[1:2, :]], axis=1)

    for i in range(blocks):
        rows = pl.ds(i * L, L)
        width = (i + 1) * L
        q2 = stacked(q_low[rows, :].astype(f32))
        go = grad_att[rows, :].astype(f32)
        go2 = stacked(go)
        row_dot = side_by_side(row_sums_of(go * att[rows, :], head_of))
        logs = side_by_side(lse_row[:, rows])
        turn = rotary_of(table, rows)

        def keys_of(part, size, masked):
            k, v = kk[part, 0:size, :], vv[part, 0:size, :]
            s = nt(k, q2) * scale - logs
            if masked:
                at = iota(s.shape, 1) % L + i * L
                row = iota(s.shape, 0)
                s = jnp.where((row <= at) & (row < limit), s, FILL)
            p = jnp.exp(s)
            ds = (p * (nt(v, go2) - row_dot)).astype(bf16)
            dv[part, 0:size, :] += nn(p.astype(bf16), go2)
            dk[part, 0:size, :] += nn(ds, q2)
            out = tn(ds, k) * scale
            out = jnp.where(low128, out[:L], out[L:])
            return out * turn[0] - swap_half(out) * turn[1]

        back[:, 0:128] = keys_of(0, width, True)

        @pl.when(c > 0)
        def earlier():
            back[:, 0:128] += keys_of(1, t, False)

        lin[rows, CQ:CK] = back[:, 0:128].astype(bf16)
        if i == 1:
            scatter.relay()

    def key_values(part, rows):
        gk, gv = dk[part, rows, :] * scale, dv[part, rows, :]
        return jnp.where(low128, gk + pltpu.roll(gk, 64, 1), gv + pltpu.roll(gv, 64, 1))

    def pack(i):
        rows = rows_of(i)
        kv_out[rows, :] = key_values(1, rows).astype(bf16)

    loop(blocks, pack)
    pairs = swap(kv_out, kv_in, 1)
    pairs.start()

    moves.get("start", "steps_in", "dt_raw", "cin", "normed", "wf1", "wf2", "hid_own", "grad_own")
    pad[0:16, :] = jnp.concatenate([jnp.zeros((8, CH), f32), hist[...]], axis=0).astype(bf16)

    def fill(i):
        pad[pl.ds(pl.multiple_of(i * L + 16, 16), L), :] = cin[rows_of(i), :]

    loop(blocks, fill)
    states.wait_recv()
    carry[...] = jnp.where(c == 0, carry[...], 0.0)

    def add_carry(k):
        i = blocks - 1 - k
        ends[i] = ends[i] + carry[...]
        carry[...] = spread(jnp.exp(tot_in[i]))[0:1, :] * carry[...]

    loop(blocks, add_carry)
    mask = iota((L, L), 0) >= iota((L, L), 1)
    ones = lower_ones()
    lane = iota((L, 128), 1)

    def scan_back(i):
        rows = rows_of(i)
        v = pre[rows, :]
        sig = sigmoid(v)
        a = v * sig
        x = a[:, :WI]
        xl, bl, cl = x.astype(bf16), a[:, WI : WI + N].astype(bf16), a[:, WI + N :].astype(bf16)
        steps, cum = steps_in[rows, :], cum_in[rows, :]
        tot = cum[L - 1 : L, :]
        ecum, wend = jnp.exp(cum), jnp.exp(tot - cum)
        weight = wend * steps
        ecum_x, weight_x = spread(ecum), spread(weight)
        grad_y = dy[rows, :]
        dyl = grad_y.astype(bf16)
        s0, d1 = start[i], ends[i]
        s0l, d1l = s0.astype(bf16), d1.astype(bf16)
        bd, cs = nn(bl, d1l), nn(cl, s0l)
        dw = fold(x * bd)
        crossing = jnp.broadcast_to(jnp.sum(s0 * d1, 0, keepdims=True), (8, WI))
        dtot = jnp.sum(weight * dw, 0, keepdims=True) + jnp.exp(tot) * fold(crossing)[0:1, :]
        gram = nt(cl, bl)
        cum_t, steps_t = cum.T, steps.T
        dgram = jnp.zeros((L, L), f32)
        row_sums = jnp.zeros((L, 128), f32)
        col_sums, inner = [], []
        for pair in range(HL // 2):
            xp, dp = pair_columns(xl, pair), pair_columns(dyl, pair)
            dpf = pair_columns(grad_y, pair)
            halves = []
            for half in range(2):
                h = 2 * pair + half
                decay = jnp.exp(jnp.where(mask, cum[:, h : h + 1] - cum_t[h : h + 1, :], FILL))
                q = nt(own_half(dpf, half).astype(bf16), xp)
                mixed = gram * decay
                srow = steps_t[h : h + 1, :]
                f = mixed * q
                col_sums.append(jnp.sum(f, 0, keepdims=True))
                row_sums = jnp.where(lane == h, jnp.sum(f * srow, -1, keepdims=True), row_sums)
                dgram = dgram + decay * srow * q
                halves.append(tn((mixed * srow).astype(bf16), dp))
            inner.append(jnp.where(low128, halves[0], halves[1]))
        cols = jnp.concatenate(col_sums + [jnp.zeros((128 - HL, L), f32)], axis=0).T
        dcum = fold(grad_y * cs) * ecum - weight * dw + row_sums - steps * cols
        dcum = dcum + jnp.where(iota((L, 128), 0) == L - 1, dtot, 0.0)
        drate = unpacked(tn(ones, packed(dcum)))
        rate_of = prm[1:2, :]
        raw = dt_raw[rows, :] + prm[0:1, :]
        dstep = (wend * dw + cols + drate * rate_of) * sigmoid(raw)
        dstep = jnp.where(lane < HL, dstep, 0.0)
        lin[rows, CS:CA] = dstep.astype(bf16)
        head_grads[0:1, :] += jnp.sum(dstep, 0, keepdims=True)
        head_grads[1:2, :] += jnp.sum(drate * steps * rate_of, 0, keepdims=True)
        head_grads[2:3, :] += jnp.sum(fold(grad_y * x), 0, keepdims=True)
        slope = sig * (1.0 + v * (1.0 - sig))
        dx = chan[1:2, :] * grad_y + weight_x * bd + jnp.concatenate(inner, axis=1)
        dg = dgram.astype(bf16)
        db = tn(dg, cl) + nt((weight_x * x).astype(bf16), d1l)
        dc = nn(dg, bl) + nt((ecum_x * grad_y).astype(bf16), s0l)
        dpre[rows, 0:WI] = dx * slope[:, :WI]
        dpre[rows, WI : WI + N] = db * slope[:, WI : WI + N]
        dpre[rows, WI + N : CH] = dc * slope[:, WI + N :]

    edge = swap(edge_out, edge_in, 2)

    def keys_back(i):
        rows = rows_of(i)
        v = key_values(0, rows) + kv_in[rows, :].astype(f32)
        cosine, sine = rotary_of(table, rows)
        cosine = jnp.where(low128, cosine, 1.0)
        sine = jnp.where(low128, sine, 0.0)
        lin[rows, CK:CS] = (v * cosine - swap_half(v) * sine).astype(bf16)

    def conv_back(b):
        rows = rows_of(b)
        later = dpre[pl.ds(pl.multiple_of(b * L, L), L + 8), :]
        earlier = pad[pl.ds(pl.multiple_of(b * L, L), L + 16), :].astype(f32)
        g = later[0:L]
        conv_grads[4:5, :] += jnp.sum(g, 0, keepdims=True)
        total = jnp.zeros_like(g)
        for j in range(CONVW):
            total = total + taps[j : j + 1, :] * later[CONVW - 1 - j : CONVW - 1 - j + L]
            conv_grads[j : j + 1, :] += jnp.sum(g * earlier[13 + j : 13 + j + L], 0, keepdims=True)
        lin[rows, CX:CQ] = total.astype(bf16)

    def part(b, owner):
        return pl.ds(pl.multiple_of(b * L + owner * sub, sub), sub)

    def kept(b):
        return rows_of(b, sub)

    grads_in = SquareScatter((g0, g1, g2, g3), (gs, gr))
    lows = SquareGather(low, part, (hs, hr))

    def product(b):
        rows = rows_of(b)
        back[...] = nt(lin[rows, CZ:CQ], wf2[...]) + nt(lin[rows, CQ:CA], wf1[...])
        gown[kept(b), :] = back[kept(tp), :]
        grads_in.start(b, back, kept)

    gain_one[...] = jnp.zeros_like(gain_one)

    def norm_back(b):
        own = part(b, tp)
        g = gown[kept(b), :] + grads_in.finish(b)
        x = hid_own[kept(b), :].astype(f32)
        scale = lax.rsqrt(jnp.mean(x * x, -1, keepdims=True) + EPS)
        unit = x * scale
        gain_one[...] += jnp.broadcast_to(jnp.sum(g * unit, 0, keepdims=True), (8, D))
        weighted = g * gains[0:1, :]
        mean = jnp.mean(weighted * unit, -1, keepdims=True)
        low[own, :] = (grad_own[kept(b), :] + scale * (weighted - unit * mean)).astype(bf16)
        lows.start(b)

    def early_grads(i):
        feats = rows_of(i)
        grads_e[feats, 0:WI] = tn(normed[:, feats], lin[:, CZ:CX]).astype(bf16)
        grads_e[feats, WI:] = tn(normed[:, feats], lin[:, CQ:CS]).astype(bf16)

    def step(k):
        @pl.when(k < blocks)
        def scan():
            scan_back(lax.rem(2 * blocks - 1 - k + c, blocks))

        @pl.when(k == 0)
        def first():
            @pl.when(c > 0)
            def give():
                edge_out[...] = dpre[0:8, :]
                edge.start()

            pairs.wait_recv()
            loop(blocks, keys_back)
            loop(D // L, early_grads)
            scatter0.start()
            dpre[pl.ds(t, 8), :] = jnp.zeros((8, CH), f32)

            @pl.when(c == 0)
            def take():
                edge.wait_recv()
                dpre[pl.ds(t, 8), :] = edge_in[...]

        @pl.when(k >= 1)
        def there():
            conv_back(blocks - k)
            product(blocks - k)

        @pl.when(k == 1)
        def on():
            scatter0.middle()

        @pl.when(k == 3)
        def further():
            scatter0.relay()

        @pl.when(k >= 2)
        def over():
            grads_in.relay(blocks + 1 - k)

        @pl.when(k >= 3)
        def again():
            norm_back(blocks + 2 - k)

        @pl.when(k >= 4)
        def last():
            lows.relay(blocks + 3 - k)

    loop(blocks + 1, step)
    vec_core = remote(small, vec_sib, vcs.at[0], vcr.at[0], ctx=1 - c)
    vec_core.start()

    def weight_grads(i):
        feats = rows_of(i)
        grads_l[feats, :] = tn(normed[:, feats], lin[:, CX:CQ]).astype(bf16)
        misc[feats, :] = tn(normed[:, feats], lin[:, CS:CA])

    loop(D // L, weight_grads)
    scatter1.start()
    grads_in.relay(0)
    norm_back(1)
    lows.relay(2)

    def vec_to_shard(k):
        zz = lax.rem(z + k, shards)
        return remote(vec_z.at[z], vec_z.at[z], vzs.at[zz], vzr.at[z], shard=zz)

    def vec_from_shard(k):
        zz = lax.rem(z + k, shards)
        return remote(vec_z.at[z], vec_z.at[zz], vzs.at[zz], vzr.at[zz], shard=zz)

    vec_core.wait_recv()
    vec_z[z] = small[...] + vec_sib[...]
    loop(shards - 1, lambda k: vec_to_shard(k + 1).start())
    scatter1.middle()
    norm_back(0)
    lows.relay(1)
    gain_rows = jnp.where(iota((8, D), 0) == 0, gain_one[...], gain_two[...])
    row, lane8 = iota((8, 128), 0), iota((8, 128), 1)
    pick = ((row < 2) & (lane8 == GAIN_COL + row)).astype(f32)
    misc_low[...] = (misc[...] + tn(gain_rows, pick, HI)).astype(bf16)
    scatter2.start()
    get_own.wait()
    total = own_out[...].astype(f32)
    for d in range(1, TP):
        out_from(d).wait_recv()
        total = total + orecv[d - 1].astype(f32)
    output[...] = total.astype(bf16)
    scatter1.relay()
    scatter2.middle()
    lows.relay(0)
    loop(shards - 1, lambda k: vec_from_shard(k + 1).wait_recv())
    vecs[tp] = lax.fori_loop(1, shards, lambda k, total: total + vec_z[k], vec_z[0])
    for d in range(1, TP):
        to_all(vecs, vts, vtr, d).start()
    scatter.finish(grad_b)
    moves.put("grad_b")
    scatter2.relay()
    scatter0.finish(grad_e)
    scatter1.finish(grad_l)
    scatter2.finish(misc_sum)
    few = grad_e.shape[0] // TP
    for i in range(TP):
        shsend[i, :, 0:256] = grad_l[i * few : (i + 1) * few, WI:CH]
        shsend[i, :, 256:384] = grad_e[i * few : (i + 1) * few, WI + 128 : CH]
        shsend[i, :, 384:512] = misc_sum[i * few : (i + 1) * few, :]

    def share_to(d):
        return remote(shsend.at[peer(d)], shared.at[tp], ss.at[d], sr.at[tp], tp=peer(d))

    def share_from(d):
        return remote(shsend.at[peer(d)], shared.at[peer(d)], ss.at[d], sr.at[peer(d)], tp=peer(d))

    for d in range(1, TP):
        share_to(d).start()
    shared[tp] = shsend[tp]

    def arrived(b):
        lows.finish(b)
        lows.sent(b)
        grads_in.sent(b)

    loop(blocks, arrived)
    for d in range(1, TP):
        share_from(d).wait_recv()
        from_all(vecs, vts, vtr, d).wait_recv()

    @pl.when(c > 0)
    def given():
        edge.wait_send()

    for copy in (states, pairs, vec_core):
        copy.wait_send()
    loop(shards - 1, lambda k: vec_to_shard(k + 1).wait_send())
    for d in range(1, TP):
        to_all(dots, ts, tr, d).wait_send()
        out_to(d).wait_send()
        share_to(d).wait_send()
        to_all(vecs, vts, vtr, d).wait_send()


def backward(shards, *args):
    t = args[0].shape[0]
    rows = D // (2 * shards)
    blocks, sub = t // L, L // TP
    vec = (8, CH + WI + 128)
    out = [
        ((t, D // TP), bf16),
        ((t, D), bf16),
        ((rows, CH), f32),
        ((rows, CH), f32),
        ((rows, CB), f32),
        ((TP, rows // TP, 512), f32),
        ((TP, *vec), f32),
    ]
    dma = pltpu.SemaphoreType.DMA
    scratch = (
        [
            pltpu.VMEM((t, 128), f32),
            pltpu.VMEM((t, D // TP), bf16),
            pltpu.VMEM((t, CA), bf16),
            pltpu.VMEM(vec, f32),
            pltpu.VMEM((TP - 1, t, D // TP), bf16),
            pltpu.VMEM((TP, 8, t), f32),
            pltpu.VMEM((2, t, 128), f32),
            pltpu.VMEM((2, t, 128), f32),
            pltpu.VMEM((t, WI), f32),
            pltpu.VMEM((t + 8, CH), f32),
            pltpu.VMEM((t // L, N, WI), f32),
            pltpu.VMEM((N, WI), f32),
            pltpu.VMEM((N, WI), f32),
            pltpu.VMEM((t, 128), bf16),
            pltpu.VMEM((t, 128), bf16),
            pltpu.VMEM((t + 16, CH), bf16),
            pltpu.VMEM((8, CH), f32),
            pltpu.VMEM((8, CH), f32),
            pltpu.VMEM((blocks * sub, D), f32),
            pltpu.VMEM((L, D), f32),
            pltpu.VMEM((8, D), f32),
            pltpu.VMEM((D, CH), bf16),
            pltpu.VMEM((D, CH), bf16),
            pltpu.VMEM((D, 128), f32),
            pltpu.VMEM((D, 128), bf16),
            pltpu.VMEM((rows, 128), f32),
            pltpu.VMEM((TP, rows // TP, 512), f32),
            pltpu.VMEM(vec, f32),
            pltpu.VMEM((shards, *vec), f32),
        ]
        + LineSum.scratch(shards, D, CB)
        + Scatter.scratch(shards, D, CH)
        + Scatter.scratch(shards, D, CH)
        + Scatter.scratch(shards, D, 128)
        + SquareScatter.scratch(blocks, sub)
        + [dma(()), dma(()), dma((1,)), dma((1,)), dma((shards,)), dma((shards,)), dma((3,)), dma((3,))]
        + [dma((TP,))] * 8
        + [dma((TP, blocks))] * 4
    )
    return call_staged(
        functools.partial(backward_kernel, shards),
        args,
        out,
        dict(zip(BACKWARD_LATE, BACKWARD_AT)),
        {"grad_b": 4},
        scratch,
        left=(5, len(args) - 2),
        compiler_params=pltpu.CompilerParams(
            collective_id=3, has_side_effects=True, vmem_limit_bytes=VMOST
        ),
        name="mix_backward",
    )


def pack_kernel(
    low, output, grad_e, grad_l, grad_b, shared, vecs,
    grad_hidden, out, g_z, g_x, g_q, g_gate, g_up, g_out, g_o, g_down, g_shared, g_dt, g_one,
    g_two, g_conv, g_conv_b, g_gate_gain, g_bias, g_decay, g_skip, g_chan,
):
    grad_hidden[...] = low[...].astype(f32)
    out[...] = output[...]

    @pl.when(pl.program_id(0) == 0)
    def rest():
        g_z[...] = grad_e[:, 0:WI]
        g_x[...] = grad_l[:, 0:WI]
        g_q[...] = grad_e[:, WI : WI + 128]
        g_gate[...] = grad_b[:, CG:CU]
        g_up[...] = grad_b[:, CU:CD]
        g_out[...] = turned_over(grad_b[:, CO:CW])
        g_o[...] = turned_over(grad_b[:, CW:CG])
        g_down[...] = turned_over(grad_b[:, CD:CB])
        first, second = shared[0] + shared[1], shared[2] + shared[3]
        both = first + second
        g_shared[:, 0 : 2 * N] = both[:, 0 : 2 * N]
        kv1, kv2 = first[:, 256:384], second[:, 256:384]
        low_half = low_lanes(kv1.shape)
        g_shared[:, 2 * N : 2 * N + 128] = jnp.where(low_half, kv1, pltpu.roll(kv2, 64, 1))
        g_shared[:, 2 * N + 128 :] = jnp.where(low_half, pltpu.roll(kv1, 64, 1), kv2)
        gains = turned_over(both[:, 384:512])[GAIN_COL : GAIN_COL + 8]
        g_one[...] = gains[0]
        g_two[...] = gains[1]
        steps = jnp.zeros((both.shape[0], 128), f32)
        heads = jnp.zeros((8, 128), f32)
        g_chan[...] = jnp.zeros_like(g_chan)
        for i in range(TP):
            lane = iota(steps.shape, 1) // HL == i
            steps = jnp.where(lane, pltpu.roll(shared[i, :, 384:512], i * HL, 1), steps)
            lane = iota(heads.shape, 1) // HL == i
            heads = jnp.where(lane, pltpu.roll(vecs[i, :, CH + WI : CH + WI + 128], i * HL, 1), heads)
            mine = slice(i * WI, (i + 1) * WI)
            g_conv[:, mine] = vecs[i, 0:CONVW, 0:WI]
            g_chan[0:1, mine] = vecs[i, CONVW : CONVW + 1, 0:WI]
            g_chan[1:2, mine] = vecs[i, 0:1, CH : CH + WI]
        maps = vecs[0, :, WI:CH] + vecs[1, :, WI:CH] + vecs[2, :, WI:CH] + vecs[3, :, WI:CH]
        g_conv[:, DI:] = maps[0:CONVW]
        g_chan[0:1, DI:] = maps[CONVW : CONVW + 1]
        g_dt[...] = turned_over(steps)[0:H]
        g_bias[...] = heads[0, 0:H]
        g_decay[...] = heads[1, 0:H]
        g_skip[...] = heads[2, 0:H]
        g_conv_b[...] = g_chan[0, :]
        g_gate_gain[...] = g_chan[1, 0:DI]


def pack(low, output, grad_e, grad_l, grad_b, shared, vecs):
    t, r, few = low.shape[0], grad_e.shape[0], shared.shape[1]
    out = [
        (t, D), output.shape, (r, WI), (r, WI), (r, 128), (r, FFL), (r, FFL), (WI, r), (128, r), (FFL, r),
        (few, 512), (H, few), (few,), (few,), (CONVW, DI + 2 * N), (DI + 2 * N,), (DI,), (H,), (H,),
        (H,),
    ]
    rows = pl.BlockSpec((L, D), lambda i: (i, 0))
    few_rows = pl.BlockSpec((L, output.shape[1]), lambda i: (i, 0))
    kinds = [f32, bf16] + [f32] * (len(out) - 2)

    def whole(shape):
        return pl.BlockSpec(shape, lambda i: (0,) * len(shape))

    return pl.pallas_call(
        pack_kernel,
        grid=(t // L,),
        out_shape=[jax.ShapeDtypeStruct(o, k) for o, k in zip(out, kinds)],
        in_specs=[rows, few_rows] + [whole(v.shape) for v in (grad_e, grad_l, grad_b, shared, vecs)],
        out_specs=[rows, few_rows] + [whole(o) for o in out[2:]],
        scratch_shapes=[pltpu.VMEM((8, DI + 2 * N), f32)],
        compiler_params=pltpu.CompilerParams(vmem_limit_bytes=VLIMIT),
        name="lay_out",
    )(low, output, grad_e, grad_l, grad_b, shared, vecs)


def rotary_table(count):
    inverse = rope_base ** (-2.0 * np.arange(HD // 2, dtype=np.float32) / HD)
    angles = np.arange(count, dtype=np.float32)[:, None] * inverse.astype(np.float32)[None, :]
    both = np.concatenate([np.cos(angles), np.sin(angles)], axis=1)
    return np.tile(both, (1, 2)).astype(np.float32)


def local(
    hidden, cotangent, lengths, norm1_gain, w_z, w_x, w_shared, w_dt, dt_bias, a_log, d_skip,
    conv_w, conv_b, gated_gain, w_out, w_q, w_o, norm2_gain, w_gate, w_up, w_down,
):
    t = hidden.shape[1]
    shards = lax.axis_size("shard")
    hid, cot = hidden[0], cotangent[0]
    table = jnp.asarray(rotary_table(lax.axis_size("ctx") * t))
    (
        wf1, wf2, wo, wg, normed, gains, z, cin, dt, taps, prm, chan,
        pre, hist, q_low, kk, vv, att, att_low, lse_row, ssd, start, steps, cum, tot, gl, square,
    ) = forward(
        shards, hid, w_z, w_x, w_shared, w_dt.T, w_q, w_out, w_o, w_gate,
        norm1_gain[None], norm2_gain[None], conv_w, conv_b, gated_gain, dt_bias, a_log, d_skip,
        table, lengths,
    )
    osend, grad_own, chip, hid_own, gain_two, total_square, ggl, grad_att, dots = ffn(
        shards, hid, cot, gl, att_low, square, wo, wg, w_up, w_down, gains, lengths
    )
    output, grad_hidden, grad_e, grad_l, grad_b, shared, vecs = backward(
        shards, ggl, grad_att, dots, total_square, chip, osend, pre, cin, hist, q_low, kk, vv, att,
        lse_row, ssd, start, steps, cum, tot, dt, z, taps, prm, chan, normed, wf1, wf2,
        hid_own, grad_own, gains, gain_two, table, lengths,
    )
    (
        grad_full, output_full, g_z, g_x, g_q, g_gate, g_up, g_out, g_o, g_down, g_shared, g_dt, g_one,
        g_two, g_conv, g_conv_b, g_gate_gain, g_bias, g_decay, g_skip,
    ) = pack(grad_hidden, output, grad_e, grad_l, grad_b, shared, vecs)
    return (
        output_full[None],
        grad_full[None],
        g_one,
        g_z,
        g_x,
        g_shared,
        g_dt.T,
        g_bias,
        g_decay,
        g_skip,
        g_conv,
        g_conv_b,
        g_gate_gain,
        g_out,
        g_q,
        g_o,
        g_two,
        g_gate,
        g_up,
        g_down,
    )


def solution(mesh):
    placed = (
        P("shard", "ctx", None),
        P("shard", "ctx", None),
        P("shard"),
        P(("shard", "ctx")),
        P(("shard", "ctx"), "tp"),
        P(("shard", "ctx"), "tp"),
        P(("shard", "ctx"), None),
        P(("shard", "ctx"), None),
        P(),
        P(),
        P(),
        P(),
        P(),
        P(),
        P("tp", ("shard", "ctx")),
        P(("shard", "ctx"), "tp"),
        P("tp", ("shard", "ctx")),
        P(("shard", "ctx")),
        P(("shard", "ctx"), "tp"),
        P(("shard", "ctx"), "tp"),
        P("tp", ("shard", "ctx")),
    )
    return jax.shard_map(
        local,
        mesh=mesh,
        in_specs=placed,
        out_specs=(
            P("shard", "ctx", "tp"),
            P("shard", "ctx", None),
            P(("shard", "ctx", "tp")),
            P(("shard", "ctx"), "tp"),
            P(("shard", "ctx"), "tp"),
            P(("shard", "ctx", "tp"), None),
            P(("shard", "ctx", "tp"), None),
            P(),
            P(),
            P(),
            P(),
            P(),
            P(),
            P("tp", ("shard", "ctx")),
            P(("shard", "ctx"), "tp"),
            P("tp", ("shard", "ctx")),
            P(("shard", "ctx", "tp")),
            P(("shard", "ctx"), "tp"),
            P(("shard", "ctx"), "tp"),
            P("tp", ("shard", "ctx")),
        ),
        check_vma=False,
    )
```

```python
import functools

import jax
import jax.numpy as jnp
import numpy as np
from jax import lax
from jax.experimental import pallas as pl
from jax.experimental.pallas import tpu as pltpu
from jax.sharding import PartitionSpec as P

H = 24
P_SIZE = 64
N = 128
NQ = 8
KV = 2
HD = 64
CONVW = 4
DI = 1536
D = 1024
FFL = 512
TP = 4
HL = H // TP
WI = HL * P_SIZE
CH = WI + 2 * N
L = 256

CZ, CX, CM, CQ, CK, CS, CA = 0, 384, 768, 1024, 1152, 1280, 1408
GAIN_COL = 24
CO, CW, CG, CU, CD, CB = 0, 384, 512, 1024, 1536, 2048

EPS = 1e-05
rope_base = 10000.0
FILL = -1e30
HI = lax.Precision.HIGHEST
MESH = pl.DeviceIdType.MESH
f32 = jnp.float32
bf16 = jnp.bfloat16
VLIMIT = 60 * 1024 * 1024
VMOST = 63 * 1024 * 1024 + 512 * 1024


def nn(a, b, precision=None):
    return lax.dot_general(
        a, b, (((1,), (0,)), ((), ())), precision=precision, preferred_element_type=f32
    )


def nt(a, b, precision=None):
    return lax.dot_general(
        a, b, (((1,), (1,)), ((), ())), precision=precision, preferred_element_type=f32
    )


def tn(a, b, precision=None):
    return lax.dot_general(
        a, b, (((0,), (0,)), ((), ())), precision=precision, preferred_element_type=f32
    )


def rows_of(index, size=L):
    return pl.ds(pl.multiple_of(index * size, size), size)


def remote(src, dst, send, recv, **where):
    return pltpu.make_async_remote_copy(
        src_ref=src,
        dst_ref=dst,
        send_sem=send,
        recv_sem=recv,
        device_id=where,
        device_id_type=MESH,
    )


def iota(shape, dim):
    return lax.broadcasted_iota(jnp.int32, shape, dim)


def loop(n, body):
    lax.fori_loop(0, n, lambda i, c: (body(i), c)[1], 0)


def greet(shards, tp_too, ctx_too=True, shard_too=True):
    barrier = pltpu.get_barrier_semaphore()
    count = 0
    z, c, t = lax.axis_index("shard"), lax.axis_index("ctx"), lax.axis_index("tp")
    if ctx_too:
        pl.semaphore_signal(barrier, inc=1, device_id={"ctx": 1 - c}, device_id_type=MESH)
        count += 1
    if shard_too:

        def one(k):
            pl.semaphore_signal(
                barrier, inc=1, device_id={"shard": lax.rem(z + 1 + k, shards)}, device_id_type=MESH
            )

        loop(shards - 1, one)
        count += shards - 1
    if tp_too:
        for d in range(1, TP):
            pl.semaphore_signal(
                barrier, inc=1, device_id={"tp": lax.rem(t + d, TP)}, device_id_type=MESH
            )
            count += 1
    pl.semaphore_wait(barrier, count)


class Moves:
    def __init__(self):
        self.gets, self.puts = {}, {}

    def get(self, *names):
        for name in names:
            self.gets[name].wait()

    def put(self, *names):
        for name in names:
            self.puts[name].start()


def call_staged(kernel, args, out, late, early, scratch, left=(), **params):
    spaces = [pl.BlockSpec(memory_space=pltpu.VMEM)] * (len(args) - 1)
    spaces.append(pl.BlockSpec(memory_space=pltpu.SMEM))
    out_spaces = [pl.BlockSpec(memory_space=pltpu.VMEM)] * len(out)
    hbm = pl.BlockSpec(memory_space=pl.ANY)
    for at in (*late.values(), *left):
        spaces[at] = hbm
    for at in early.values():
        out_spaces[at] = hbm
    extra = [pltpu.VMEM(args[at].shape, args[at].dtype) for at in late.values()]
    extra += [pltpu.VMEM(*out[at]) for at in early.values()]
    dma = pltpu.SemaphoreType.DMA
    sems = [dma((len(late),)), dma((len(early),))]

    def body(*refs):
        split = len(args) + len(out)
        given, inner = list(refs[:split]), refs[split : split + len(scratch)]
        held, (get_sem, put_sem) = list(refs[split + len(scratch) : -2]), refs[-2:]
        moves = Moves()
        for n, (name, at) in enumerate(late.items()):
            buffer = held.pop(0)
            moves.gets[name] = pltpu.make_async_copy(given[at], buffer, get_sem.at[n])
            moves.gets[name].start()
            given[at] = buffer
        for n, (name, at) in enumerate(early.items()):
            buffer = held.pop(0)
            moves.puts[name] = pltpu.make_async_copy(buffer, given[len(args) + at], put_sem.at[n])
            given[len(args) + at] = buffer
        kernel(moves, *given, *inner)
        for copy in moves.puts.values():
            copy.wait()

    return pl.pallas_call(
        body,
        out_shape=[jax.ShapeDtypeStruct(*o) for o in out],
        in_specs=spaces,
        out_specs=out_spaces,
        scratch_shapes=list(scratch) + extra + sems,
        **params,
    )(*args)


class Gather:
    def __init__(self, shards, src, dst, zsend, fsend, csend, recv, own, cols=None):
        self.s, self.dst, self.cols = shards, dst, cols
        self.src = src if cols is None else src.at[:, cols]
        self.zsend, self.fsend, self.csend, self.recv, self.own = zsend, fsend, csend, recv, own
        self.z, self.c = lax.axis_index("shard"), lax.axis_index("ctx")
        self.r = src.shape[0]

    def block(self, g):
        rows = rows_of(g, self.r)
        return self.dst.at[rows] if self.cols is None else self.dst.at[rows, self.cols]

    def inside(self, zz):
        return (zz >= 0) & (zz < self.s)

    def straight(self, steps, way):
        g = 2 * self.z + self.c
        kind = steps - 1 + (0 if way > 0 else 2)
        return remote(
            self.src, self.block(g), self.zsend.at[kind], self.recv.at[g], shard=self.z + way * steps
        )

    def onward(self, zz, way):
        there = self.block(2 * zz + self.c)
        return remote(
            there, there, self.fsend.at[zz], self.recv.at[2 * zz + self.c], shard=self.z + way
        )

    def to_core(self, zz, core):
        there = self.block(2 * zz + core)
        return remote(
            there, there, self.csend.at[zz], self.recv.at[2 * zz + core], ctx=1 - self.c
        )

    def straight_ones(self, act_on):
        for steps in (2, 1):
            for way in (1, -1):

                @pl.when(self.inside(self.z + way * steps))
                def go(steps=steps, way=way):
                    act_on(self.straight(steps, way))

    def start(self):
        keep = pltpu.make_async_copy(self.src, self.block(2 * self.z + self.c), self.own)
        keep.start()
        self.straight_ones(lambda copy: copy.start())
        keep.wait()
        self.to_core(self.z, self.c).start()

    def forward(self, first=0, last=None):
        def one(k):
            for way in (1, -1):
                zz = self.z - way * (k + 1)

                @pl.when(self.inside(zz))
                def came(way=way, zz=zz):
                    self.to_core(zz, self.c).wait_recv()
                    self.to_core(zz, self.c).start()

                    @pl.when((k >= 1) & self.inside(self.z + way))
                    def pass_on():
                        self.onward(zz, way).start()

        lax.fori_loop(
            first, self.s - 1 if last is None else last, lambda k, carry: (one(k), carry)[1], 0
        )

    def finish(self):
        loop(self.s, lambda zz: self.to_core(zz, 1 - self.c).wait_recv())
        loop(self.s, lambda zz: self.to_core(zz, self.c).wait_send())
        self.straight_ones(lambda copy: copy.wait_send())

        def passed(k):
            for way in (1, -1):
                zz = self.z - way * (k + 1)

                @pl.when(self.inside(zz) & self.inside(self.z + way))
                def on(way=way, zz=zz):
                    self.onward(zz, way).wait_send()

        lax.fori_loop(1, self.s - 1, lambda k, carry: (passed(k), carry)[1], 0)

    @staticmethod
    def sems(shards):
        dma = pltpu.SemaphoreType.DMA
        return [dma((4,)), dma((shards,)), dma((shards,)), dma((2 * shards,)), dma(())]


class LineSum:
    def __init__(self, shards, src, hold, land, fsend, frecv, lsend, lrecv):
        self.s, self.src, self.hold, self.land = shards, src, hold, land
        self.fsend, self.frecv, self.lsend, self.lrecv = fsend, frecv, lsend, lrecv
        self.z = lax.axis_index("shard")

    def place(self, dest, way):
        return dest - 3 if way > 0 else dest

    def onward(self, src, dest, way):
        at = self.place(dest, way)
        return remote(
            src, self.hold.at[at], self.fsend.at[at], self.frecv.at[at], shard=self.z + way
        )

    def straight(self, src, steps, way):
        kind = steps - 1 + (0 if way > 0 else 2)
        return remote(
            src,
            self.land.at[kind],
            self.lsend.at[kind],
            self.lrecv.at[kind],
            shard=self.z + way * steps,
        )

    def each(self, far, two, one, waited):
        for way in (1, -1):
            first = self.z == 0 if way > 0 else self.z == self.s - 1
            now = jnp.logical_not(first) if waited else first

            def along(j, way=way, now=now):
                dest = self.s - 1 - j if way > 0 else j
                distance = (dest - self.z) * way

                @pl.when(now & (distance >= 3))
                def three():
                    far(dest, way)

                @pl.when(now & (distance == 2))
                def both():
                    two(dest, way)

            loop(self.s, along)
            if not waited:
                other = self.z + way

                @pl.when((other >= 0) & (other < self.s))
                def next_one(way=way, other=other):
                    one(other, way)

    def start(self):
        self.each(
            lambda dest, way: self.onward(self.src.at[dest], dest, way).start(),
            lambda dest, way: self.straight(self.src.at[dest], 2, way).start(),
            lambda dest, way: self.straight(self.src.at[dest], 1, way).start(),
            False,
        )

    def relay(self):
        def added(dest, way):
            at = self.place(dest, way)
            self.onward(self.src.at[dest], dest, way).wait_recv()
            own = self.src[dest].astype(f32)
            self.hold[at] = (own + self.hold[at].astype(f32)).astype(bf16)
            return self.hold.at[at]

        self.each(
            lambda dest, way: self.onward(added(dest, way), dest, way).start(),
            lambda dest, way: self.straight(added(dest, way), 2, way).start(),
            None,
            True,
        )

    def finish(self, out):
        out[...] = self.src[self.z].astype(f32)
        for steps in (1, 2):
            for way in (1, -1):
                source = self.z - way * steps

                @pl.when((source >= 0) & (source < self.s))
                def arrived(steps=steps, way=way):
                    kind = steps - 1 + (0 if way > 0 else 2)
                    remote(
                        self.land.at[kind],
                        self.land.at[kind],
                        self.lsend.at[kind],
                        self.lrecv.at[kind],
                        shard=self.z - way * steps,
                    ).wait_recv()
                    out[...] += self.land[kind].astype(f32)

        for waited in (False, True):
            self.each(
                lambda dest, way: self.onward(self.src.at[dest], dest, way).wait_send(),
                lambda dest, way: self.straight(self.src.at[dest], 2, way).wait_send(),
                lambda dest, way: self.straight(self.src.at[dest], 1, way).wait_send(),
                waited,
            )

    @staticmethod
    def scratch(shards, rows, cols):
        dma = pltpu.SemaphoreType.DMA
        far, r = max(shards - 3, 1), rows // (2 * shards)
        return [
            pltpu.VMEM((far, r, cols), bf16),
            pltpu.VMEM((4, r, cols), bf16),
            dma((far,)),
            dma((far,)),
            dma((4,)),
            dma((4,)),
        ]


class Scatter:
    def __init__(self, shards, src, sib, csend, crecv, *line):
        self.s, self.src, self.sib = shards, src, sib
        self.csend, self.crecv = csend, crecv
        self.c = lax.axis_index("ctx")
        self.r = src.shape[0] // (2 * shards)
        self.line = LineSum(shards, sib, *line)

    def to_core(self, k):
        return remote(
            self.src.at[rows_of(2 * k + 1 - self.c, self.r)],
            self.sib.at[k],
            self.csend.at[k],
            self.crecv.at[k],
            ctx=1 - self.c,
        )

    def start(self):
        loop(self.s, lambda k: self.to_core(k).start())

    def middle(self):
        def one(k):
            self.to_core(k).wait_recv()
            both = self.src[rows_of(2 * k + self.c, self.r), :].astype(f32)
            self.sib[k] = (both + self.sib[k].astype(f32)).astype(bf16)

        loop(self.s, one)
        self.line.start()

    def relay(self):
        self.line.relay()

    def finish(self, out):
        self.line.finish(out)
        loop(self.s, lambda k: self.to_core(k).wait_send())

    @staticmethod
    def scratch(shards, rows, cols):
        dma = pltpu.SemaphoreType.DMA
        block = pltpu.VMEM((shards, rows // (2 * shards), cols), bf16)
        return [block, dma((shards,)), dma((shards,))] + LineSum.scratch(shards, rows, cols)


class ChipSum:
    def __init__(self, shards, src, sib, cols, csend, crecv):
        self.s, self.src, self.sib, self.cols = shards, src, sib, cols
        self.csend, self.crecv = csend, crecv
        self.c = lax.axis_index("ctx")
        self.r = src.shape[0] // (2 * shards)

    def to_core(self, k):
        return remote(
            self.src.at[rows_of(2 * k + 1 - self.c, self.r), self.cols],
            self.sib.at[k, :, self.cols],
            self.csend.at[k],
            self.crecv.at[k],
            ctx=1 - self.c,
        )

    def start(self):
        loop(self.s, lambda k: self.to_core(k).start())

    def finish(self):
        def one(k):
            self.to_core(k).wait_recv()
            own = self.src[rows_of(2 * k + self.c, self.r), self.cols].astype(f32)
            self.sib[k, :, self.cols] = (own + self.sib[k, :, self.cols].astype(f32)).astype(bf16)

        loop(self.s, one)
        loop(self.s, lambda k: self.to_core(k).wait_send())


class Square:
    def __init__(self, kinds):
        tp = lax.axis_index("tp")
        self.me = tp
        self.x = tp + 1 - 2 * lax.rem(tp, 2)
        self.y = lax.rem(tp + 2, TP)
        self.across = TP - 1 - tp
        self.send, self.recv = kinds

    def copy(self, kind, b, src, dst):
        to = self.y if kind in (1, 2) else self.x
        return remote(src, dst, self.send.at[kind, b], self.recv.at[kind, b], tp=to)


class SquareScatter(Square):
    def __init__(self, buffers, kinds):
        super().__init__(kinds)
        self.out, self.into, self.out2, self.into2 = buffers

    def first(self, kind, b):
        return self.copy(kind, b, self.out.at[kind, b], self.into.at[kind, b])

    def second(self, kind, b):
        return self.copy(kind, b, self.out2.at[kind - 2, b], self.into2.at[kind - 2, b])

    def start(self, b, ref, rows):
        half = ref.shape[1] // 2
        left, right = pl.ds(0, half), pl.ds(half, half)
        self.out[0, b, 0] = ref[rows(self.x), left].astype(bf16)
        self.out[0, b, 1] = ref[rows(self.across), left].astype(bf16)
        self.first(0, b).start()
        self.out[1, b, 0] = ref[rows(self.y), right].astype(bf16)
        self.out[1, b, 1] = ref[rows(self.across), right].astype(bf16)
        self.first(1, b).start()
        self.out2[0, b] = ref[rows(self.y), left].astype(bf16)
        self.out2[1, b] = ref[rows(self.x), right].astype(bf16)

    def relay(self, b):
        for kind in (0, 1):
            self.first(kind, b).wait_recv()
            own = self.out2[kind, b].astype(f32)
            self.out2[kind, b] = (own + self.into[kind, b, 1].astype(f32)).astype(bf16)
            self.second(kind + 2, b).start()

    def finish(self, b):
        sums = []
        for kind in (0, 1):
            self.second(kind + 2, b).wait_recv()
            sums.append(self.into[kind, b, 0].astype(f32) + self.into2[kind, b].astype(f32))
        return jnp.concatenate(sums, axis=1)

    def sent(self, b):
        for kind in (0, 1):
            self.first(kind, b).wait_send()
            self.second(kind + 2, b).wait_send()

    @staticmethod
    def scratch(blocks, sub):
        first = pltpu.VMEM((2, blocks, 2, sub, D // 2), bf16)
        second = pltpu.VMEM((2, blocks, sub, D // 2), bf16)
        return [first, first, second, second]


class SquareGather(Square):
    def __init__(self, ref, part, kinds):
        super().__init__(kinds)
        self.ref, self.part = ref, part

    def whole(self, kind, b, owner):
        there = self.ref.at[self.part(b, owner)]
        return self.copy(kind, b, there, there)

    def half(self, kind, b, owner):
        half = self.ref.shape[1] // 2
        there = self.ref.at[self.part(b, owner), pl.ds((kind - 2) * half, half)]
        return self.copy(kind, b, there, there)

    def start(self, b):
        for kind in (0, 1):
            self.whole(kind, b, self.me).start()

    def relay(self, b):
        for kind, owner in ((0, self.x), (1, self.y)):
            self.whole(kind, b, owner).wait_recv()
            self.half(kind + 2, b, owner).start()

    def finish(self, b):
        for kind in (2, 3):
            self.half(kind, b, self.across).wait_recv()

    def sent(self, b):
        for kind, owner in ((0, self.x), (1, self.y)):
            self.whole(kind, b, self.me).wait_send()
            self.half(kind + 2, b, owner).wait_send()


class RowTotal:
    def __init__(self, slots, send, recv):
        self.slots, self.send, self.recv = slots, send, recv
        self.tp = lax.axis_index("tp")

    def to(self, d):
        there = self.slots.at[self.tp]
        return remote(
            there, there, self.send.at[d], self.recv.at[self.tp], tp=lax.rem(self.tp + d, TP)
        )

    def came(self, d):
        peer = lax.rem(self.tp + d, TP)
        there = self.slots.at[peer]
        return remote(there, there, self.send.at[d], self.recv.at[peer], tp=peer)

    def start(self, rows):
        self.slots[self.tp] = rows
        for d in range(1, TP):
            self.to(d).start()

    def finish(self):
        for d in range(1, TP):
            self.came(d).wait_recv()
            self.to(d).wait_send()
        return self.slots[0] + self.slots[1] + self.slots[2] + self.slots[3]


def sigmoid(v):
    return 1.0 / (1.0 + jnp.exp(-v))


def softplus(v):
    return jnp.maximum(v, 0.0) + jnp.log1p(jnp.exp(-jnp.abs(v)))


def swap_half(v):
    width = v.shape[1]
    low = iota(v.shape, 1) % HD < HD // 2
    return jnp.where(low, pltpu.roll(v, width - HD // 2, 1), pltpu.roll(v, HD // 2, 1))


def low_lanes(shape):
    return iota(shape, 1) < 64


def parts(v, count):
    found = []
    for _ in range(count):
        part = v.astype(bf16)
        found.append(part)
        v = v - part.astype(f32)
    return found


def packed(v):
    v = jnp.where(iota(v.shape, 1) < 8, v, 0.0)
    high, middle, low = (part.astype(f32) for part in parts(v, 3))
    return (high + pltpu.roll(middle, 8, 1) + pltpu.roll(low, 16, 1)).astype(bf16)


def unpacked(v):
    v = v + pltpu.roll(v, 120, 1) + pltpu.roll(v, 112, 1)
    return jnp.where(iota(v.shape, 1) < 8, v, 0.0)


def spread(v):
    lane, channel = iota((N, WI), 0), iota((N, WI), 1)
    pick = ((lane % 8 == channel // P_SIZE) & (lane < 24)).astype(bf16)
    return nn(packed(v), pick)


def fold(v):
    pick = (iota((WI, N), 0) // P_SIZE == iota((WI, N), 1)).astype(bf16)
    high, low = parts(v, 2)
    return nn(high, pick) + nn(low, pick)


def row_sums_of(v, pick=None):
    pick = jnp.ones((8, v.shape[1]), bf16) if pick is None else pick
    high, low = parts(v, 2)
    return nt(pick, high) + nt(pick, low)


def as_column(row):
    at = iota(row.shape, 0)
    first = jnp.broadcast_to(row[0:1, :], row.shape)
    high, middle, low = parts(first, 3)
    three = jnp.where(at == 0, high, jnp.where(at == 1, middle, low))
    return tn(three, (iota((8, N), 0) < 3).astype(bf16))


def turned_over(v):
    one = eye(v.shape[0])
    high, middle, low = parts(v, 3)
    return tn(high, one) + tn(middle, one) + tn(low, one)


def wide(column, width):
    return jnp.concatenate([column] * (width // column.shape[1]), axis=1)


def lower_ones():
    return (iota((L, L), 0) >= iota((L, L), 1)).astype(bf16)


def head_scalars(dt_raw, prm):
    real = iota(dt_raw.shape, 1) < HL
    steps = jnp.where(real, softplus(dt_raw + prm[0:1, :]), 0.0)
    rates = steps * prm[1:2, :]
    return steps, rates


def pair_columns(v, pair):
    return v[:, 128 * pair : 128 * pair + 128]


def own_half(v, half):
    return jnp.where(low_lanes(v.shape) == (half == 0), v, jnp.zeros_like(v))


def eye(n):
    return (iota((n, n), 0) == iota((n, n), 1)).astype(bf16)


def rotary_of(table, rows):
    both = table[rows, :]
    first = iota(both.shape, 1) % HD < HD // 2
    cosine = jnp.where(first, both, pltpu.roll(both, HD // 2, 1))
    sine = jnp.where(first, -pltpu.roll(both, 128 - HD // 2, 1), both)
    return cosine, sine


FORWARD_EARLY = (
    "wf1",
    "wf2",
    "normed",
    "z_out",
    "cin",
    "dt_raw",
    "pre",
    "q_low",
    "kk",
    "vv",
    "att",
    "att_low",
    "steps_out",
    "cum_out",
)
FORWARD_AT = (
    0,
    1,
    4,
    6,
    7,
    8,
    12,
    14,
    15,
    16,
    17,
    18,
    22,
    23,
)
BACKWARD_LATE = (
    "chip",
    "grad_att",
    "q_low",
    "kk",
    "vv",
    "att",
    "lse_row",
    "start",
    "steps_in",
    "dt_raw",
    "cin",
    "normed",
    "wf1",
    "wf2",
    "hid_own",
    "grad_own",
)
BACKWARD_AT = (
    4,
    1,
    9,
    10,
    11,
    12,
    13,
    15,
    16,
    19,
    7,
    24,
    25,
    26,
    27,
    28,
)


def forward_kernel(
    shards, moves,
    hid, w_z, w_x, w_shared, w_dt, w_q, w_out, w_o, w_gate, gain_one, gain_two,
    conv_w, conv_b, gated_gain, dt_bias, a_log, d_skip, table, length,
    wf1, wf2, wo, wg, normed, gains, z_out, cin, dt_raw, taps, prm, chan,
    pre, hist, q_low, kk, vv, att, att_low, lse_row, ssd, start, steps_out, cum_out, tot_out,
    gated_low, square,
    slots, small, wa1, wa2, wa3, stat, zf, pad, act, state, carried, scores_m, scores_l, hist_in,
    zs1, fs1, cs1, zr1, own1, zs2, fs2, cs2, zr2, own2, zs3, fs3, cs3, zr3, own3,
    zs4, fs4, cs4, zr4, own4, zs5, fs5, cs5, zr5, own5,
    xs, xr, qs, qr,
):
    c, tp = lax.axis_index("ctx"), lax.axis_index("tp")
    t = hid.shape[0]
    blocks = t // L
    r = w_z.shape[0]

    kv = tp * (NQ // TP) // (NQ // KV)
    keys = w_shared[:, 2 * N : 2 * N + 128].astype(f32)
    vals = w_shared[:, 2 * N + 128 : 2 * N + 256].astype(f32)
    low_r = low_lanes((r, 128))
    other = pltpu.roll(jnp.where(kv == 0, vals, keys), 64, 1)
    wa1[:, 0:128] = w_q[...]
    wa1[:, 128:256] = jnp.where(
        kv == 0, jnp.where(low_r, keys, other), jnp.where(low_r, other, vals)
    ).astype(bf16)
    head_pick = (
        (iota((H, 128), 0) == iota((H, 128), 1) + tp * HL) & (iota((H, 128), 1) < HL)
    ).astype(bf16)
    row8, lane8 = iota((8, 128), 0), iota((8, 128), 1)
    gain_pick = ((row8 < 2) & (lane8 == GAIN_COL + row8)).astype(bf16)
    gain_rows = jnp.where(
        iota((8, r), 0) == 0, gain_one[...].astype(f32), gain_two[...].astype(f32)
    ).astype(bf16)
    wa1[:, 256:384] = (tn(w_dt[...], head_pick) + tn(gain_rows, gain_pick)).astype(bf16)
    wa2[:, 0:WI] = w_z[...]
    wa2[:, WI : 2 * WI] = w_x[...]
    wa2[:, 2 * WI : 2 * WI + 2 * N] = w_shared[:, 0 : 2 * N]
    greet(shards, True)
    gather1 = Gather(shards, wa1, wf1, zs1, fs1, cs1, zr1, own1)
    gather2 = Gather(shards, wa2, wf2, zs2, fs2, cs2, zr2, own2, pl.ds(WI, CH))
    gather5 = Gather(shards, wa2, wf2, zs5, fs5, cs5, zr5, own5, pl.ds(0, WI))
    gather3 = Gather(shards, wa3, wo, zs3, fs3, cs3, zr3, own3)
    gather4 = Gather(shards, w_gate, wg, zs4, fs4, cs4, zr4, own4)
    gather1.start()
    gather2.start()
    wa3[:, CO:CW] = nt(eye(r), w_out[...]).astype(bf16)
    wa3[:, CW:CG] = nt(eye(r), w_o[...]).astype(bf16)

    mine = pl.ds(pl.multiple_of(tp * WI, 128), WI)
    small[...] = jnp.zeros_like(small)
    small[0:1, :] = conv_b[...].astype(f32)[None, :]
    small[1:2, 0:DI] = gated_gain[...].astype(f32)[None, :]
    small[8:9, 0:H] = dt_bias[...].astype(f32)[None, :]
    small[9:10, 0:H] = a_log[...].astype(f32)[None, :]
    small[10:11, 0:H] = d_skip[...].astype(f32)[None, :]
    taps[0:CONVW, 0:WI] = conv_w[:, mine].astype(f32)
    taps[0:CONVW, WI:CH] = conv_w[:, DI:].astype(f32)
    taps[CONVW : CONVW + 1, 0:WI] = small[0:1, mine]
    taps[CONVW : CONVW + 1, WI:CH] = small[0:1, DI:]
    taps[CONVW + 1 :, :] = jnp.zeros((8 - CONVW - 1, CH), f32)
    heads = pltpu.roll(small[8:16, 0:128], lax.rem(128 - tp * HL, 128), 1)
    heads = jnp.where(lane8 < HL, jnp.where(row8 == 1, -jnp.exp(heads), heads), 0.0)
    prm[...] = heads
    chan[...] = jnp.zeros_like(chan)
    chan[0:1, :] = small[1:2, mine]
    chan[1:2, :] = spread(heads)[2:3, :]

    def swap(src, dst, i):
        return remote(src, dst, xs.at[i], xr.at[i], ctx=1 - c)

    def row_scale(i):
        rows = rows_of(i)
        x = hid[rows, :].astype(f32)
        scale = lax.rsqrt(jnp.mean(x * x, -1, keepdims=True) + EPS)
        stat[rows, :] = jnp.broadcast_to(scale, (L, 128))

    loop(blocks, row_scale)
    gather1.forward()
    gather1.finish()
    gather5.start()
    turned = wf1[:, 256:384].astype(f32).T
    gains[...] = turned[GAIN_COL : GAIN_COL + 8]
    gain = gains[0:1, :]
    low128 = low_lanes((L, 128))
    moves.put("wf1")
    moves.get("table")

    def first_projections(i):
        rows = rows_of(i)
        low = (hid[rows, :].astype(f32) * wide(stat[rows, :], D) * gain).astype(bf16)
        normed[rows, :] = low
        rest = nn(low, wf1[...])
        cosine, sine = rotary_of(table, pl.ds(pl.multiple_of(c * t + i * L, L), L))
        v = rest[:, 0:128]
        q_low[rows, :] = (v * cosine + swap_half(v) * sine).astype(bf16)
        v = rest[:, 128:256]
        other = pltpu.roll(v, 64, 1)
        twice = jnp.where(low128, v, other)
        kk[0, rows, :] = (twice * cosine + swap_half(twice) * sine).astype(bf16)
        vv[0, rows, :] = jnp.where(low128, other, v).astype(bf16)
        dt_raw[rows, :] = rest[:, 256:384]

    loop(blocks, first_projections)
    moves.put("normed", "q_low", "dt_raw")
    keys = swap(kk.at[0], kk.at[1], 1)
    keys.start()
    vals = swap(vv.at[0], vv.at[1], 2)
    vals.start()

    scale = HD ** (-0.5)
    limit = length[0] - c * t

    def stacked(v):
        return jnp.concatenate([own_half(v, 0), own_half(v, 1)], axis=0)

    for i in range(blocks):
        rows = pl.ds(i * L, L)
        width = (i + 1) * L
        q2 = stacked(q_low[rows, :].astype(f32)).astype(bf16)
        s = nt(q2, kk[0, 0:width, :]) * scale
        at = iota(s.shape, 0) % L + i * L
        col = iota(s.shape, 1)
        s = jnp.where((col <= at) & (col < limit), s, FILL)
        peak = jnp.max(s, -1, keepdims=True)
        e = jnp.exp(s - peak)
        total = jnp.sum(e, -1, keepdims=True)
        o = nn(e.astype(bf16), vv[0, 0:width, :])
        scores_m[...] = jnp.broadcast_to(peak, (2 * L, 128))
        scores_l[0] = jnp.broadcast_to(total, (2 * L, 128))
        scores_l[1] = o
        if i == 0:
            keys.wait_recv()
            vals.wait_recv()

        @pl.when(c > 0)
        def earlier():
            s2 = nt(q2, kk[1]) * scale
            old = scores_m[:, 0:1]
            new = jnp.maximum(old, jnp.max(s2, -1, keepdims=True))
            e2 = jnp.exp(s2 - new)
            fade = jnp.exp(old - new)
            scores_m[...] = jnp.broadcast_to(new, (2 * L, 128))
            scores_l[0] = fade * scores_l[0] + jnp.sum(e2, -1, keepdims=True)
            scores_l[1] = fade * scores_l[1] + nn(e2.astype(bf16), vv[1])

        total = scores_l[0]
        o = scores_l[1] / total
        o = jnp.where(low128, o[:L], o[L:])
        att[rows, :] = o
        att_low[rows, :] = o.astype(bf16)
        logs = scores_m[...] + jnp.log(total)
        turned = jnp.where(low128, logs[:L], logs[L:]).T
        lse_row[0:1, rows] = turned[0:1]
        lse_row[1:2, rows] = turned[64:65]
        lse_row[2:8, rows] = jnp.zeros((6, L), f32)
        if i == blocks - 3:
            gather2.forward(0, 2)
        if i == blocks - 2:
            gather2.forward(2)
            gather3.start()
    moves.put("kk", "vv", "att", "att_low")
    gather5.forward(0, 2)
    gather2.finish()

    def conv_input(k):
        i = blocks - 1 - k
        rows = rows_of(i)
        v = nn(normed[rows, :], wf2[:, WI:]).astype(bf16)
        cin[rows, :] = v
        pad[pl.ds(pl.multiple_of(i * L + 8, 8), L), :] = v.astype(f32)

    conv_input(0)
    tail = swap(cin.at[pl.ds(t - 16, 16)], hist_in, 0)
    tail.start()
    lax.fori_loop(1, blocks, lambda k, carry: (conv_input(k), carry)[1], 0)
    gather5.forward(2)
    gather4.start()
    tail.wait_recv()
    before = hist_in[8:16, :].astype(f32)
    hist[...] = jnp.where((iota((8, CH), 0) >= 5) & (c > 0), before, 0.0)
    pad[0:8, :] = hist[...]
    ones = lower_ones()
    state[...] = jnp.zeros_like(state)

    for i in range(blocks):
        rows = pl.ds(i * L, L)
        v = taps[4:5, :] + taps[0:1, :] * pad[pl.ds(i * L + 5, L), :]
        for j in range(1, CONVW):
            v = v + taps[j : j + 1, :] * pad[pl.ds(i * L + 5 + j, L), :]
        pre[rows, :] = v
        a = v * sigmoid(v)
        act[rows, :] = a
        steps, rates = head_scalars(dt_raw[rows, :], prm)
        cum = unpacked(nn(ones, packed(rates)))
        tot = cum[L - 1 : L, :]
        steps_out[rows, :] = steps
        cum_out[rows, :] = cum
        tot_out[i] = jnp.broadcast_to(tot, (8, 128))
        weight = spread(jnp.exp(tot - cum) * steps)
        start[i] = state[...]
        add = tn(a[:, WI : WI + N].astype(bf16), (weight * a[:, :WI]).astype(bf16))
        decay = spread(jnp.broadcast_to(jnp.exp(tot), (8, 128)))[0:1, :]
        state[...] = decay * state[...] + add

    states = swap(state, carried, 3)
    states.start()
    moves.put("cin", "pre", "steps_out", "cum_out")
    gather3.forward(0, 2)

    gather5.finish()
    moves.put("wf2")

    def gate_input(i):
        rows = rows_of(i)
        zf[rows, :] = nn(normed[rows, :], wf2[:, 0:WI])
        z_out[rows, :] = zf[rows, :].astype(bf16)

    loop(blocks, gate_input)
    moves.put("z_out")

    states.wait_recv()
    gather3.forward(2)
    carried[...] = jnp.where(c > 0, carried[...], 0.0)
    mask = iota((L, L), 0) >= iota((L, L), 1)
    for i in range(blocks):
        rows = pl.ds(i * L, L)
        if i > 0:
            decay = spread(jnp.exp(tot_out[i - 1]))[0:1, :]
            carried[...] = carried[...] * decay
        start[i] = start[i] + carried[...]
        s0 = start[i].astype(bf16)
        steps, cum = steps_out[rows, :], cum_out[rows, :]
        x = act[rows, 0:WI]
        xl = x.astype(bf16)
        in_map = act[rows, WI : WI + N].astype(bf16)
        out_map = act[rows, WI + N : CH].astype(bf16)
        gram = nt(out_map, in_map)
        cum_t, steps_t = cum.T, steps.T
        inner = []
        for pair in range(HL // 2):
            halves = []
            for half in range(2):
                h = 2 * pair + half
                decay = jnp.exp(jnp.where(mask, cum[:, h : h + 1] - cum_t[h : h + 1, :], FILL))
                mixing = gram * decay * steps_t[h : h + 1, :]
                halves.append(nn(mixing.astype(bf16), pair_columns(xl, pair)))
            inner.append(jnp.where(low128, halves[0], halves[1]))
        y = jnp.concatenate(inner, axis=1)
        y = y + spread(jnp.exp(cum)) * nn(out_map, s0) + chan[1:2, :] * x
        ssd[rows, :] = y.astype(bf16)
        zz = zf[rows, :]
        gated = y * zz * sigmoid(zz)
        gated_low[rows, :] = (gated * chan[0:1, :]).astype(bf16)
        square[:, rows] = row_sums_of(gated * gated)
        if i == 1:
            gather4.forward(0, 2)

    squares = RowTotal(slots, qs, qr)
    squares.start(square[...])
    gather4.forward(2)
    gather3.finish()
    gather4.finish()
    square[...] = squares.finish()
    for copy in (tail, keys, vals, states):
        copy.wait_send()


def forward(shards, *args):
    t, r = args[0].shape[0], args[1].shape[0]
    out = [
        ((D, 384), bf16),
        ((D, 1024), bf16),
        ((D, CG), bf16),
        ((D, FFL), bf16),
        ((t, D), bf16),
        ((8, D), f32),
        ((t, WI), bf16),
        ((t, CH), bf16),
        ((t, 128), f32),
        ((8, CH), f32),
        ((8, 128), f32),
        ((8, WI), f32),
        ((t, CH), f32),
        ((8, CH), f32),
        ((t, 128), bf16),
        ((2, t, 128), bf16),
        ((2, t, 128), bf16),
        ((t, 128), f32),
        ((t, 128), bf16),
        ((8, t), f32),
        ((t, WI), bf16),
        ((t // L, N, WI), f32),
        ((t, 128), f32),
        ((t, 128), f32),
        ((t // L, 8, 128), f32),
        ((t, WI), bf16),
        ((8, t), f32),
    ]
    dma = pltpu.SemaphoreType.DMA
    scratch = (
        [
            pltpu.VMEM((TP, 8, t), f32),
            pltpu.VMEM((16, DI + 2 * N), f32),
            pltpu.VMEM((r, 384), bf16),
            pltpu.VMEM((r, 1024), bf16),
            pltpu.VMEM((r, CG), bf16),
            pltpu.VMEM((t, 128), f32),
            pltpu.VMEM((t, WI), f32),
            pltpu.VMEM((t + 8, CH), f32),
            pltpu.VMEM((t, CH), f32),
            pltpu.VMEM((N, WI), f32),
            pltpu.VMEM((N, WI), f32),
            pltpu.VMEM((2 * L, 128), f32),
            pltpu.VMEM((2, 2 * L, 128), f32),
            pltpu.VMEM((16, CH), bf16),
        ]
        + Gather.sems(shards) * 5
        + [dma((4,)), dma((4,)), dma((TP,)), dma((TP,))]
    )
    return call_staged(
        functools.partial(forward_kernel, shards),
        args,
        out,
        {"table": 17},
        dict(zip(FORWARD_EARLY, FORWARD_AT)),
        scratch,
        compiler_params=pltpu.CompilerParams(
            collective_id=1, has_side_effects=True, vmem_limit_bytes=VLIMIT
        ),
        name="mix_forward",
    )


def ffn_kernel(
    shards, moves,
    hid, cot, gl, att, total_square, wb, wg, w_up, w_down, gains, length,
    osend, grad_own, chip, hid_own, gain_grad, ggl, grad_att, dots,
    grads, grad_res, partial, seed, low_two, proj, act, gg, gu, gown, back,
    unit, scale_keep, sqall, wm, wm_own, a1, a2, a3, a4, b1, b2, b3, b4,
    zs, fs, cs, zr, own_sem, ms, mr, ws, wr, sqs, sqr, s1, r1, ns, nr, gs, gr, hs, hr,
):
    t = hid.shape[0]
    tp, c = lax.axis_index("tp"), lax.axis_index("ctx")
    blocks = t // L
    sub = L // TP
    width = D // TP
    wm_own[:, 0:FFL] = w_up[...]
    wm_own[:, FFL:] = nt(eye(w_down.shape[1]), w_down[...]).astype(bf16)
    greet(shards, True)
    gather = Gather(shards, wm_own, wm, zs, fs, cs, zr, own_sem)
    gather.start()
    mlp_sum = ChipSum(shards, grads, chip, pl.ds(CG, CB - CG), ms, mr)
    out_sum = ChipSum(shards, grads, chip, pl.ds(CO, CG - CO), ws, wr)

    def peer(d):
        return lax.rem(tp + d, TP)

    def part(b, owner):
        return pl.ds(pl.multiple_of(b * L + owner * sub, sub), sub)

    def kept(b):
        return rows_of(b, sub)

    first = SquareScatter((a1, a2, a3, a4), (s1, r1))
    norms = SquareGather(low_two, part, (ns, nr))
    gradients = SquareScatter((b1, b2, b3, b4), (gs, gr))
    residuals = SquareGather(grad_res, part, (hs, hr))

    limit = length[0] - c * t

    def mask_seed(i):
        rows = rows_of(i)
        live = iota((L, D), 0) + i * L < limit
        seed[rows, :] = jnp.where(live, cot[rows, :].astype(f32), 0.0).astype(bf16)

    gain = gains[1:2, :]
    gain_grad[...] = jnp.zeros_like(gain_grad)

    def mix(b):
        rows = rows_of(b)
        scale = lax.rsqrt(total_square[:, rows] / DI + EPS)
        column = wide(as_column(scale), D)
        partial[rows, :] = nt(gl[rows, :], wb[:, CO:CW]) * column + nt(att[rows, :], wb[:, CW:CG])
        first.start(b, partial, lambda owner: part(b, owner))

    def norm(b):
        own = part(b, tp)
        hid_own[kept(b), :] = hid[own, :]
        acc = hid[own, :].astype(f32) + partial[own, :] + first.finish(b)
        scale = lax.rsqrt(jnp.mean(acc * acc, -1, keepdims=True) + EPS)
        scale_keep[kept(b), :] = jnp.broadcast_to(scale, (sub, 128))
        u = acc * scale
        unit[kept(b), :] = u
        low_two[own, :] = (u * gain).astype(bf16)
        norms.start(b)

    def hidden_units(b):
        rows = rows_of(b)
        norms.finish(b)
        low = low_two[rows, :]
        gate, up = nn(low, wg[...]), nn(low, wm[:, 0:FFL])
        sig = sigmoid(gate)
        silu = gate * sig
        hidden_act = (silu * up).astype(bf16)
        act[rows, :] = hidden_act
        ga = nn(seed[rows, :], wm[:, FFL:])
        g1 = (ga * up * (sig * (1.0 + gate * (1.0 - sig)))).astype(bf16)
        g2 = (ga * silu).astype(bf16)
        gg[rows, :] = g1
        gu[rows, :] = g2
        back[...] = nt(g1, wg[...]) + nt(g2, wm[:, 0:FFL])
        gown[kept(b), :] = back[kept(tp), :]
        gradients.start(b, back, kept)
        partial[rows, :] = partial[rows, :] + nt(hidden_act, wm[:, FFL:])
        mine = rows_of(tp, width)
        osend[0, rows, :] = (partial[rows, mine] + hid[rows, mine].astype(f32)).astype(bf16)
        for e in range(1, TP):
            osend[e, rows, :] = partial[rows, rows_of(peer(e), width)].astype(bf16)

    def norm_back(b):
        own = part(b, tp)
        g = gown[kept(b), :] + gradients.finish(b)
        u = unit[kept(b), :]
        gain_grad[...] += jnp.broadcast_to(jnp.sum(g * u, 0, keepdims=True), (8, D))
        weighted = g * gain
        mean = jnp.mean(weighted * u, -1, keepdims=True)
        res = seed[own, :].astype(f32) + scale_keep[kept(b), 0:1] * (weighted - u * mean)
        grad_own[kept(b), :] = res
        grad_res[own, :] = res.astype(bf16)
        residuals.start(b)

    def weight_grads(i):
        feats = rows_of(i)
        low = low_two[:, feats]
        grads[feats, CG:CU] = tn(low, gg[...]).astype(bf16)
        grads[feats, CU:CD] = tn(low, gu[...]).astype(bf16)

    def down_grads(i):
        feats = rows_of(i)
        grads[feats, CD:CB] = tn(seed[:, feats], act[...]).astype(bf16)

    def out_back(b):
        rows = rows_of(b)
        residuals.finish(b)
        square_scale = lax.rsqrt(total_square[:, rows] / DI + EPS)
        column = wide(as_column(square_scale), D)
        got = grad_res[rows, :]
        low = (column * got.astype(f32)).astype(bf16)
        proj[rows, :] = low
        product = nn(low, wb[:, CO:CW])
        ggl[rows, :] = product
        dots[:, rows] = row_sums_of(product * gl[rows, :].astype(f32))
        grad_att[rows, :] = nn(got, wb[:, CW:CG]).astype(bf16)

    def stage(s, delay, act_on):
        @pl.when((s >= delay) & (s < delay + blocks))
        def go():
            act_on(s - delay)

    def step(s):
        stage(s, 0, mix)

        @pl.when(s == 1)
        def masks():
            moves.get("hid", "cot", "wg")
            loop(blocks, mask_seed)

        @pl.when(s == 2)
        def pieces():
            gather.forward(0, 2)

        stage(s, 1, first.relay)
        stage(s, 2, norm)
        stage(s, 3, norms.relay)

        @pl.when(s == 3)
        def weights():
            gather.forward(2)
            gather.finish()

        stage(s, 4, hidden_units)

        @pl.when(s == blocks + 4)
        def fill():
            moves.put("osend")
            loop(D // L, weight_grads)

        stage(s, 5, gradients.relay)
        stage(s, 6, norm_back)

        @pl.when(s == blocks + 5)
        def more():
            loop(D // L, down_grads)
            mlp_sum.start()

        @pl.when(s == blocks + 6)
        def norms_done():
            moves.put("grad_own")

        stage(s, 7, residuals.relay)
        stage(s, 8, out_back)

    loop(blocks + 8, step)

    def out_grads(i):
        feats = rows_of(i)
        grads[feats, CO:CW] = tn(proj[:, feats], gl[...]).astype(bf16)
        grads[feats, CW:CG] = tn(grad_res[:, feats], att[...]).astype(bf16)

    totals = RowTotal(sqall, sqs, sqr)
    totals.start(dots[...])
    loop(D // L, out_grads)
    out_sum.start()
    mlp_sum.finish()
    dots[...] = totals.finish()
    out_sum.finish()

    def sent(b):
        for exchange in (first, norms, gradients, residuals):
            exchange.sent(b)

    loop(blocks, sent)


def ffn(shards, *args):
    t = args[0].shape[0]
    blocks, sub = t // L, L // TP
    kept = blocks * sub
    out = [
        ((TP, t, D // TP), bf16),
        ((kept, D), f32),
        ((shards, D // (2 * shards), CB), bf16),
        ((kept, D), bf16),
        ((8, D), f32),
        ((t, WI), f32),
        ((t, 128), bf16),
        ((8, t), f32),
    ]
    dma = pltpu.SemaphoreType.DMA
    scratch = (
        [
            pltpu.VMEM((D, CB), bf16),
            pltpu.VMEM((t, D), bf16),
            pltpu.VMEM((t, D), f32),
            pltpu.VMEM((t, D), bf16),
            pltpu.VMEM((t, D), bf16),
            pltpu.VMEM((t, D), bf16),
            pltpu.VMEM((t, FFL), bf16),
            pltpu.VMEM((t, FFL), bf16),
            pltpu.VMEM((t, FFL), bf16),
            pltpu.VMEM((kept, D), f32),
            pltpu.VMEM((L, D), f32),
            pltpu.VMEM((kept, D), f32),
            pltpu.VMEM((kept, 128), f32),
            pltpu.VMEM((TP, 8, t), f32),
            pltpu.VMEM((D, 2 * FFL), bf16),
            pltpu.VMEM((D // (2 * shards), 2 * FFL), bf16),
        ]
        + SquareScatter.scratch(blocks, sub) * 2
        + Gather.sems(shards)
        + [dma((shards,))] * 4
        + [dma((TP,))] * 2
        + [dma((TP, blocks))] * 8
    )
    return call_staged(
        functools.partial(ffn_kernel, shards),
        args,
        out,
        {"hid": 0, "cot": 1, "wg": 6},
        {"osend": 0, "grad_own": 1},
        scratch,
        compiler_params=pltpu.CompilerParams(
            collective_id=2, has_side_effects=True, vmem_limit_bytes=VLIMIT
        ),
        name="feed_forward",
    )


def backward_kernel(
    shards, moves,
    ggl, grad_att, dots_in, total_square, chip, osend,
    pre, cin, hist, q_low, kk, vv, att, lse_row, ssd, start, steps_in, cum_in, tot_in, dt_raw, z_in,
    taps, prm, chan, normed, wf1, wf2, hid_own, grad_own, gains, gain_two, table_all, length,
    output, low, grad_e, grad_l, grad_b, shared, vecs,
    table, own_out, lin, small, orecv, dk, dv, dy, dpre, ends, dstate, carry, kv_out, kv_in, pad,
    edge_out, edge_in, gown, back, gain_one, grads_e, grads_l, misc, misc_low, misc_sum, shsend,
    vec_sib, vec_z,
    ln0, ln1, ln2, ln3, ln4, ln5,
    e0, e1, e2, e3, e4, e5, e6, e7, e8,
    l0, l1, l2, l3, l4, l5, l6, l7, l8,
    m0, m1, m2, m3, m4, m5, m6, m7, m8,
    g0, g1, g2, g3,
    table_sem, own_sem, vcs, vcr, vzs, vzr, xs, xr, os, orr, ss, sr, vts, vtr, gs, gr, hs, hr,
):
    z, c, tp = lax.axis_index("shard"), lax.axis_index("ctx"), lax.axis_index("tp")
    t = cin.shape[0]
    blocks, sub = t // L, L // TP
    get_table = pltpu.make_async_copy(table_all.at[rows_of(c, t)], table, table_sem)
    get_table.start()
    greet(shards, True)
    scatter = LineSum(shards, chip, ln0, ln1, ln2, ln3, ln4, ln5)
    scatter0 = Scatter(shards, grads_e, e0, e1, e2, e3, e4, e5, e6, e7, e8)
    scatter1 = Scatter(shards, grads_l, l0, l1, l2, l3, l4, l5, l6, l7, l8)
    scatter2 = Scatter(shards, misc_low, m0, m1, m2, m3, m4, m5, m6, m7, m8)
    moves.get("chip")
    scatter.start()

    def swap(src, dst, i):
        return remote(src, dst, xs.at[i], xr.at[i], ctx=1 - c)

    def peer(d):
        return lax.rem(tp + d, TP)

    def to_all(ref, send, recv, d):
        return remote(ref.at[tp], ref.at[tp], send.at[d], recv.at[tp], tp=peer(d))

    def from_all(ref, send, recv, d):
        return remote(ref.at[tp], ref.at[peer(d)], send.at[d], recv.at[peer(d)], tp=peer(d))


    def out_to(d):
        return remote(osend.at[d], orecv.at[TP - 1 - d], os.at[d], orr.at[TP - 1 - d], tp=peer(d))

    def out_from(d):
        return remote(osend.at[d], orecv.at[d - 1], os.at[d], orr.at[d - 1], tp=peer(d))

    get_own = pltpu.make_async_copy(osend.at[0], own_out, own_sem)
    get_own.start()
    for d in range(1, TP):
        out_to(d).start()
    conv_grads = small.at[:, 0:CH]
    chan_grads = small.at[:, CH : CH + WI]
    head_grads = small.at[:, CH + WI : CH + WI + 128]
    low128 = low_lanes((L, 128))
    small[...] = jnp.zeros_like(small)

    def gated_back(i):
        rows = rows_of(i)
        share = dots_in[:, rows] / ((total_square[:, rows] / DI + EPS) * DI)
        column = wide(as_column(share), WI)
        zz, y = z_in[rows, :].astype(f32), ssd[rows, :].astype(f32)
        sig = sigmoid(zz)
        silu = zz * sig
        gated = y * silu
        product = ggl[rows, :]
        chan_grads[0:1, :] += jnp.sum(product * gated, 0, keepdims=True)
        grad_gated = product * chan[0:1, :] - column * gated
        grad_y = grad_gated * silu
        dy[rows, :] = grad_y
        lin[rows, CZ:CX] = (grad_gated * y * (sig * (1.0 + zz * (1.0 - sig)))).astype(bf16)
        v = pre[rows, WI + N : CH]
        out_map = (v * sigmoid(v)).astype(bf16)
        ends[i] = tn(out_map, (spread(jnp.exp(cum_in[rows, :])) * grad_y).astype(bf16))

    loop(blocks, gated_back)
    dstate[...] = jnp.zeros_like(dstate)

    def chain(k):
        i = blocks - 1 - k
        add = ends[i]
        ends[i] = dstate[...]
        dstate[...] = spread(jnp.exp(tot_in[i]))[0:1, :] * dstate[...] + add

    loop(blocks, chain)
    states = swap(dstate, carry, 0)
    states.start()

    scale = HD ** (-0.5)
    limit = length[0] - c * t
    dk[...] = jnp.zeros_like(dk)
    dv[...] = jnp.zeros_like(dv)
    get_table.wait()
    moves.get("grad_att", "q_low", "kk", "vv", "att", "lse_row")
    head_of = ((iota((8, 128), 1) // HD) == iota((8, 128), 0)).astype(bf16)

    def stacked(v):
        return jnp.concatenate([own_half(v, 0), own_half(v, 1)], axis=0).astype(bf16)

    def side_by_side(v):
        return jnp.concatenate([v[0:1, :], v[1:2, :]], axis=1)

    for i in range(blocks):
        rows = pl.ds(i * L, L)
        width = (i + 1) * L
        q2 = stacked(q_low[rows, :].astype(f32))
        go = grad_att[rows, :].astype(f32)
        go2 = stacked(go)
        row_dot = side_by_side(row_sums_of(go * att[rows, :], head_of))
        logs = side_by_side(lse_row[:, rows])
        turn = rotary_of(table, rows)

        def keys_of(part, size, masked):
            k, v = kk[part, 0:size, :], vv[part, 0:size, :]
            s = nt(k, q2) * scale - logs
            if masked:
                at = iota(s.shape, 1) % L + i * L
                row = iota(s.shape, 0)
                s = jnp.where((row <= at) & (row < limit), s, FILL)
            p = jnp.exp(s)
            ds = (p * (nt(v, go2) - row_dot)).astype(bf16)
            dv[part, 0:size, :] += nn(p.astype(bf16), go2)
            dk[part, 0:size, :] += nn(ds, q2)
            out = tn(ds, k) * scale
            out = jnp.where(low128, out[:L], out[L:])
            return out * turn[0] - swap_half(out) * turn[1]

        back[:, 0:128] = keys_of(0, width, True)

        @pl.when(c > 0)
        def earlier():
            back[:, 0:128] += keys_of(1, t, False)

        lin[rows, CQ:CK] = back[:, 0:128].astype(bf16)
        if i == 1:
            scatter.relay()

    def key_values(part, rows):
        gk, gv = dk[part, rows, :] * scale, dv[part, rows, :]
        return jnp.where(low128, gk + pltpu.roll(gk, 64, 1), gv + pltpu.roll(gv, 64, 1))

    def pack(i):
        rows = rows_of(i)
        kv_out[rows, :] = key_values(1, rows).astype(bf16)

    loop(blocks, pack)
    pairs = swap(kv_out, kv_in, 1)
    pairs.start()

    moves.get("start", "steps_in", "dt_raw", "cin", "normed", "wf1", "wf2", "hid_own", "grad_own")
    pad[0:16, :] = jnp.concatenate([jnp.zeros((8, CH), f32), hist[...]], axis=0).astype(bf16)

    def fill(i):
        pad[pl.ds(pl.multiple_of(i * L + 16, 16), L), :] = cin[rows_of(i), :]

    loop(blocks, fill)
    states.wait_recv()
    carry[...] = jnp.where(c == 0, carry[...], 0.0)

    def add_carry(k):
        i = blocks - 1 - k
        ends[i] = ends[i] + carry[...]
        carry[...] = spread(jnp.exp(tot_in[i]))[0:1, :] * carry[...]

    loop(blocks, add_carry)
    mask = iota((L, L), 0) >= iota((L, L), 1)
    ones = lower_ones()
    lane = iota((L, 128), 1)

    def scan_back(i):
        rows = rows_of(i)
        v = pre[rows, :]
        sig = sigmoid(v)
        a = v * sig
        x = a[:, :WI]
        xl, bl, cl = x.astype(bf16), a[:, WI : WI + N].astype(bf16), a[:, WI + N :].astype(bf16)
        steps, cum = steps_in[rows, :], cum_in[rows, :]
        tot = cum[L - 1 : L, :]
        ecum, wend = jnp.exp(cum), jnp.exp(tot - cum)
        weight = wend * steps
        ecum_x, weight_x = spread(ecum), spread(weight)
        grad_y = dy[rows, :]
        dyl = grad_y.astype(bf16)
        s0, d1 = start[i], ends[i]
        s0l, d1l = s0.astype(bf16), d1.astype(bf16)
        bd, cs = nn(bl, d1l), nn(cl, s0l)
        dw = fold(x * bd)
        crossing = jnp.broadcast_to(jnp.sum(s0 * d1, 0, keepdims=True), (8, WI))
        dtot = jnp.sum(weight * dw, 0, keepdims=True) + jnp.exp(tot) * fold(crossing)[0:1, :]
        gram = nt(cl, bl)
        cum_t, steps_t = cum.T, steps.T
        dgram = jnp.zeros((L, L), f32)
        row_sums = jnp.zeros((L, 128), f32)
        col_sums, inner = [], []
        for pair in range(HL // 2):
            xp, dp = pair_columns(xl, pair), pair_columns(dyl, pair)
            dpf = pair_columns(grad_y, pair)
            halves = []
            for half in range(2):
                h = 2 * pair + half
                decay = jnp.exp(jnp.where(mask, cum[:, h : h + 1] - cum_t[h : h + 1, :], FILL))
                q = nt(own_half(dpf, half).astype(bf16), xp)
                mixed = gram * decay
                srow = steps_t[h : h + 1, :]
                f = mixed * q
                col_sums.append(jnp.sum(f, 0, keepdims=True))
                row_sums = jnp.where(lane == h, jnp.sum(f * srow, -1, keepdims=True), row_sums)
                dgram = dgram + decay * srow * q
                halves.append(tn((mixed * srow).astype(bf16), dp))
            inner.append(jnp.where(low128, halves[0], halves[1]))
        cols = jnp.concatenate(col_sums + [jnp.zeros((128 - HL, L), f32)], axis=0).T
        dcum = fold(grad_y * cs) * ecum - weight * dw + row_sums - steps * cols
        dcum = dcum + jnp.where(iota((L, 128), 0) == L - 1, dtot, 0.0)
        drate = unpacked(tn(ones, packed(dcum)))
        rate_of = prm[1:2, :]
        raw = dt_raw[rows, :] + prm[0:1, :]
        dstep = (wend * dw + cols + drate * rate_of) * sigmoid(raw)
        dstep = jnp.where(lane < HL, dstep, 0.0)
        lin[rows, CS:CA] = dstep.astype(bf16)
        head_grads[0:1, :] += jnp.sum(dstep, 0, keepdims=True)
        head_grads[1:2, :] += jnp.sum(drate * steps * rate_of, 0, keepdims=True)
        head_grads[2:3, :] += jnp.sum(fold(grad_y * x), 0, keepdims=True)
        slope = sig * (1.0 + v * (1.0 - sig))
        dx = chan[1:2, :] * grad_y + weight_x * bd + jnp.concatenate(inner, axis=1)
        dg = dgram.astype(bf16)
        db = tn(dg, cl) + nt((weight_x * x).astype(bf16), d1l)
        dc = nn(dg, bl) + nt((ecum_x * grad_y).astype(bf16), s0l)
        dpre[rows, 0:WI] = dx * slope[:, :WI]
        dpre[rows, WI : WI + N] = db * slope[:, WI : WI + N]
        dpre[rows, WI + N : CH] = dc * slope[:, WI + N :]

    edge = swap(edge_out, edge_in, 2)

    def keys_back(i):
        rows = rows_of(i)
        v = key_values(0, rows) + kv_in[rows, :].astype(f32)
        cosine, sine = rotary_of(table, rows)
        cosine = jnp.where(low128, cosine, 1.0)
        sine = jnp.where(low128, sine, 0.0)
        lin[rows, CK:CS] = (v * cosine - swap_half(v) * sine).astype(bf16)

    def conv_back(b):
        rows = rows_of(b)
        later = dpre[pl.ds(pl.multiple_of(b * L, L), L + 8), :]
        earlier = pad[pl.ds(pl.multiple_of(b * L, L), L + 16), :].astype(f32)
        g = later[0:L]
        conv_grads[4:5, :] += jnp.sum(g, 0, keepdims=True)
        total = jnp.zeros_like(g)
        for j in range(CONVW):
            total = total + taps[j : j + 1, :] * later[CONVW - 1 - j : CONVW - 1 - j + L]
            conv_grads[j : j + 1, :] += jnp.sum(g * earlier[13 + j : 13 + j + L], 0, keepdims=True)
        lin[rows, CX:CQ] = total.astype(bf16)

    def part(b, owner):
        return pl.ds(pl.multiple_of(b * L + owner * sub, sub), sub)

    def kept(b):
        return rows_of(b, sub)

    grads_in = SquareScatter((g0, g1, g2, g3), (gs, gr))
    lows = SquareGather(low, part, (hs, hr))

    def product(b):
        rows = rows_of(b)
        back[...] = nt(lin[rows, CZ:CQ], wf2[...]) + nt(lin[rows, CQ:CA], wf1[...])
        gown[kept(b), :] = back[kept(tp), :]
        grads_in.start(b, back, kept)

    gain_one[...] = jnp.zeros_like(gain_one)

    def norm_back(b):
        own = part(b, tp)
        g = gown[kept(b), :] + grads_in.finish(b)
        x = hid_own[kept(b), :].astype(f32)
        scale = lax.rsqrt(jnp.mean(x * x, -1, keepdims=True) + EPS)
        unit = x * scale
        gain_one[...] += jnp.broadcast_to(jnp.sum(g * unit, 0, keepdims=True), (8, D))
        weighted = g * gains[0:1, :]
        mean = jnp.mean(weighted * unit, -1, keepdims=True)
        low[own, :] = (grad_own[kept(b), :] + scale * (weighted - unit * mean)).astype(bf16)
        lows.start(b)

    def early_grads(i):
        feats = rows_of(i)
        grads_e[feats, 0:WI] = tn(normed[:, feats], lin[:, CZ:CX]).astype(bf16)
        grads_e[feats, WI:] = tn(normed[:, feats], lin[:, CQ:CS]).astype(bf16)

    def step(k):
        @pl.when(k < blocks)
        def scan():
            scan_back(lax.rem(2 * blocks - 1 - k + c, blocks))

        @pl.when(k == 0)
        def first():
            @pl.when(c > 0)
            def give():
                edge_out[...] = dpre[0:8, :]
                edge.start()

            pairs.wait_recv()
            loop(blocks, keys_back)
            loop(D // L, early_grads)
            scatter0.start()
            dpre[pl.ds(t, 8), :] = jnp.zeros((8, CH), f32)

            @pl.when(c == 0)
            def take():
                edge.wait_recv()
                dpre[pl.ds(t, 8), :] = edge_in[...]

        @pl.when(k >= 1)
        def there():
            conv_back(blocks - k)
            product(blocks - k)

        @pl.when(k == 1)
        def on():
            scatter0.middle()

        @pl.when(k == 3)
        def further():
            scatter0.relay()

        @pl.when(k >= 2)
        def over():
            grads_in.relay(blocks + 1 - k)

        @pl.when(k >= 3)
        def again():
            norm_back(blocks + 2 - k)

        @pl.when(k >= 4)
        def last():
            lows.relay(blocks + 3 - k)

    loop(blocks + 1, step)
    vec_core = remote(small, vec_sib, vcs.at[0], vcr.at[0], ctx=1 - c)
    vec_core.start()

    def weight_grads(i):
        feats = rows_of(i)
        grads_l[feats, :] = tn(normed[:, feats], lin[:, CX:CQ]).astype(bf16)
        misc[feats, :] = tn(normed[:, feats], lin[:, CS:CA])

    loop(D // L, weight_grads)
    scatter1.start()
    grads_in.relay(0)
    norm_back(1)
    lows.relay(2)

    def vec_to_shard(k):
        zz = lax.rem(z + k, shards)
        return remote(vec_z.at[z], vec_z.at[z], vzs.at[zz], vzr.at[z], shard=zz)

    def vec_from_shard(k):
        zz = lax.rem(z + k, shards)
        return remote(vec_z.at[z], vec_z.at[zz], vzs.at[zz], vzr.at[zz], shard=zz)

    vec_core.wait_recv()
    vec_z[z] = small[...] + vec_sib[...]
    loop(shards - 1, lambda k: vec_to_shard(k + 1).start())
    scatter1.middle()
    norm_back(0)
    lows.relay(1)
    gain_rows = jnp.where(iota((8, D), 0) == 0, gain_one[...], gain_two[...])
    row, lane8 = iota((8, 128), 0), iota((8, 128), 1)
    pick = ((row < 2) & (lane8 == GAIN_COL + row)).astype(f32)
    misc_low[...] = (misc[...] + tn(gain_rows, pick, HI)).astype(bf16)
    scatter2.start()
    get_own.wait()
    total = own_out[...].astype(f32)
    for d in range(1, TP):
        out_from(d).wait_recv()
        total = total + orecv[d - 1].astype(f32)
    output[...] = total.astype(bf16)
    scatter1.relay()
    scatter2.middle()
    lows.relay(0)
    loop(shards - 1, lambda k: vec_from_shard(k + 1).wait_recv())
    vecs[tp] = lax.fori_loop(1, shards, lambda k, total: total + vec_z[k], vec_z[0])
    for d in range(1, TP):
        to_all(vecs, vts, vtr, d).start()
    scatter.finish(grad_b)
    moves.put("grad_b")
    scatter2.relay()
    scatter0.finish(grad_e)
    scatter1.finish(grad_l)
    scatter2.finish(misc_sum)
    few = grad_e.shape[0] // TP
    for i in range(TP):
        shsend[i, :, 0:256] = grad_l[i * few : (i + 1) * few, WI:CH]
        shsend[i, :, 256:384] = grad_e[i * few : (i + 1) * few, WI + 128 : CH]
        shsend[i, :, 384:512] = misc_sum[i * few : (i + 1) * few, :]

    def share_to(d):
        return remote(shsend.at[peer(d)], shared.at[tp], ss.at[d], sr.at[tp], tp=peer(d))

    def share_from(d):
        return remote(shsend.at[peer(d)], shared.at[peer(d)], ss.at[d], sr.at[peer(d)], tp=peer(d))

    for d in range(1, TP):
        share_to(d).start()
    shared[tp] = shsend[tp]

    def arrived(b):
        lows.finish(b)
        lows.sent(b)
        grads_in.sent(b)

    loop(blocks, arrived)
    for d in range(1, TP):
        share_from(d).wait_recv()
        from_all(vecs, vts, vtr, d).wait_recv()

    @pl.when(c > 0)
    def given():
        edge.wait_send()

    for copy in (states, pairs, vec_core):
        copy.wait_send()
    loop(shards - 1, lambda k: vec_to_shard(k + 1).wait_send())
    for d in range(1, TP):
        out_to(d).wait_send()
        share_to(d).wait_send()
        to_all(vecs, vts, vtr, d).wait_send()


def backward(shards, *args):
    t = args[0].shape[0]
    rows = D // (2 * shards)
    blocks, sub = t // L, L // TP
    vec = (8, CH + WI + 128)
    out = [
        ((t, D // TP), bf16),
        ((t, D), bf16),
        ((rows, CH), f32),
        ((rows, CH), f32),
        ((rows, CB), f32),
        ((TP, rows // TP, 512), f32),
        ((TP, *vec), f32),
    ]
    dma = pltpu.SemaphoreType.DMA
    scratch = (
        [
            pltpu.VMEM((t, 128), f32),
            pltpu.VMEM((t, D // TP), bf16),
            pltpu.VMEM((t, CA), bf16),
            pltpu.VMEM(vec, f32),
            pltpu.VMEM((TP - 1, t, D // TP), bf16),
            pltpu.VMEM((2, t, 128), f32),
            pltpu.VMEM((2, t, 128), f32),
            pltpu.VMEM((t, WI), f32),
            pltpu.VMEM((t + 8, CH), f32),
            pltpu.VMEM((t // L, N, WI), f32),
            pltpu.VMEM((N, WI), f32),
            pltpu.VMEM((N, WI), f32),
            pltpu.VMEM((t, 128), bf16),
            pltpu.VMEM((t, 128), bf16),
            pltpu.VMEM((t + 16, CH), bf16),
            pltpu.VMEM((8, CH), f32),
            pltpu.VMEM((8, CH), f32),
            pltpu.VMEM((blocks * sub, D), f32),
            pltpu.VMEM((L, D), f32),
            pltpu.VMEM((8, D), f32),
            pltpu.VMEM((D, CH), bf16),
            pltpu.VMEM((D, CH), bf16),
            pltpu.VMEM((D, 128), f32),
            pltpu.VMEM((D, 128), bf16),
            pltpu.VMEM((rows, 128), f32),
            pltpu.VMEM((TP, rows // TP, 512), f32),
            pltpu.VMEM(vec, f32),
            pltpu.VMEM((shards, *vec), f32),
        ]
        + LineSum.scratch(shards, D, CB)
        + Scatter.scratch(shards, D, CH)
        + Scatter.scratch(shards, D, CH)
        + Scatter.scratch(shards, D, 128)
        + SquareScatter.scratch(blocks, sub)
        + [dma(()), dma(()), dma((1,)), dma((1,)), dma((shards,)), dma((shards,)), dma((3,)), dma((3,))]
        + [dma((TP,))] * 6
        + [dma((TP, blocks))] * 4
    )
    return call_staged(
        functools.partial(backward_kernel, shards),
        args,
        out,
        dict(zip(BACKWARD_LATE, BACKWARD_AT)),
        {"grad_b": 4},
        scratch,
        left=(5, len(args) - 2),
        compiler_params=pltpu.CompilerParams(
            collective_id=3, has_side_effects=True, vmem_limit_bytes=VMOST
        ),
        name="mix_backward",
    )


def pack_kernel(
    low, output, grad_e, grad_l, grad_b, shared, vecs,
    grad_hidden, out, g_z, g_x, g_q, g_gate, g_up, g_out, g_o, g_down, g_shared, g_dt, g_one,
    g_two, g_conv, g_conv_b, g_gate_gain, g_bias, g_decay, g_skip, g_chan,
):
    grad_hidden[...] = low[...].astype(f32)
    out[...] = output[...]

    @pl.when(pl.program_id(0) == 0)
    def rest():
        g_z[...] = grad_e[:, 0:WI]
        g_x[...] = grad_l[:, 0:WI]
        g_q[...] = grad_e[:, WI : WI + 128]
        g_gate[...] = grad_b[:, CG:CU]
        g_up[...] = grad_b[:, CU:CD]
        g_out[...] = turned_over(grad_b[:, CO:CW])
        g_o[...] = turned_over(grad_b[:, CW:CG])
        g_down[...] = turned_over(grad_b[:, CD:CB])
        first, second = shared[0] + shared[1], shared[2] + shared[3]
        both = first + second
        g_shared[:, 0 : 2 * N] = both[:, 0 : 2 * N]
        kv1, kv2 = first[:, 256:384], second[:, 256:384]
        low_half = low_lanes(kv1.shape)
        g_shared[:, 2 * N : 2 * N + 128] = jnp.where(low_half, kv1, pltpu.roll(kv2, 64, 1))
        g_shared[:, 2 * N + 128 :] = jnp.where(low_half, pltpu.roll(kv1, 64, 1), kv2)
        gains = turned_over(both[:, 384:512])[GAIN_COL : GAIN_COL + 8]
        g_one[...] = gains[0]
        g_two[...] = gains[1]
        steps = jnp.zeros((both.shape[0], 128), f32)
        heads = jnp.zeros((8, 128), f32)
        g_chan[...] = jnp.zeros_like(g_chan)
        for i in range(TP):
            lane = iota(steps.shape, 1) // HL == i
            steps = jnp.where(lane, pltpu.roll(shared[i, :, 384:512], i * HL, 1), steps)
            lane = iota(heads.shape, 1) // HL == i
            heads = jnp.where(lane, pltpu.roll(vecs[i, :, CH + WI : CH + WI + 128], i * HL, 1), heads)
            mine = slice(i * WI, (i + 1) * WI)
            g_conv[:, mine] = vecs[i, 0:CONVW, 0:WI]
            g_chan[0:1, mine] = vecs[i, CONVW : CONVW + 1, 0:WI]
            g_chan[1:2, mine] = vecs[i, 0:1, CH : CH + WI]
        maps = vecs[0, :, WI:CH] + vecs[1, :, WI:CH] + vecs[2, :, WI:CH] + vecs[3, :, WI:CH]
        g_conv[:, DI:] = maps[0:CONVW]
        g_chan[0:1, DI:] = maps[CONVW : CONVW + 1]
        g_dt[...] = turned_over(steps)[0:H]
        g_bias[...] = heads[0, 0:H]
        g_decay[...] = heads[1, 0:H]
        g_skip[...] = heads[2, 0:H]
        g_conv_b[...] = g_chan[0, :]
        g_gate_gain[...] = g_chan[1, 0:DI]


def pack(low, output, grad_e, grad_l, grad_b, shared, vecs):
    t, r, few = low.shape[0], grad_e.shape[0], shared.shape[1]
    out = [
        (t, D), output.shape, (r, WI), (r, WI), (r, 128), (r, FFL), (r, FFL), (WI, r), (128, r), (FFL, r),
        (few, 512), (H, few), (few,), (few,), (CONVW, DI + 2 * N), (DI + 2 * N,), (DI,), (H,), (H,),
        (H,),
    ]
    rows = pl.BlockSpec((L, D), lambda i: (i, 0))
    few_rows = pl.BlockSpec((L, output.shape[1]), lambda i: (i, 0))
    kinds = [f32, bf16] + [f32] * (len(out) - 2)

    def whole(shape):
        return pl.BlockSpec(shape, lambda i: (0,) * len(shape))

    return pl.pallas_call(
        pack_kernel,
        grid=(t // L,),
        out_shape=[jax.ShapeDtypeStruct(o, k) for o, k in zip(out, kinds)],
        in_specs=[rows, few_rows] + [whole(v.shape) for v in (grad_e, grad_l, grad_b, shared, vecs)],
        out_specs=[rows, few_rows] + [whole(o) for o in out[2:]],
        scratch_shapes=[pltpu.VMEM((8, DI + 2 * N), f32)],
        compiler_params=pltpu.CompilerParams(vmem_limit_bytes=VLIMIT),
        name="lay_out",
    )(low, output, grad_e, grad_l, grad_b, shared, vecs)


def rotary_table(count):
    inverse = rope_base ** (-2.0 * np.arange(HD // 2, dtype=np.float32) / HD)
    angles = np.arange(count, dtype=np.float32)[:, None] * inverse.astype(np.float32)[None, :]
    both = np.concatenate([np.cos(angles), np.sin(angles)], axis=1)
    return np.tile(both, (1, 2)).astype(np.float32)


def local(
    hidden, cotangent, lengths, norm1_gain, w_z, w_x, w_shared, w_dt, dt_bias, a_log, d_skip,
    conv_w, conv_b, gated_gain, w_out, w_q, w_o, norm2_gain, w_gate, w_up, w_down,
):
    t = hidden.shape[1]
    shards = lax.axis_size("shard")
    hid, cot = hidden[0], cotangent[0]
    table = jnp.asarray(rotary_table(lax.axis_size("ctx") * t))
    (
        wf1, wf2, wo, wg, normed, gains, z, cin, dt, taps, prm, chan,
        pre, hist, q_low, kk, vv, att, att_low, lse_row, ssd, start, steps, cum, tot, gl, square,
    ) = forward(
        shards, hid, w_z, w_x, w_shared, w_dt.T, w_q, w_out, w_o, w_gate,
        norm1_gain[None], norm2_gain[None], conv_w, conv_b, gated_gain, dt_bias, a_log, d_skip,
        table, lengths,
    )
    osend, grad_own, chip, hid_own, gain_two, ggl, grad_att, dots = ffn(
        shards, hid, cot, gl, att_low, square, wo, wg, w_up, w_down, gains, lengths
    )
    output, grad_hidden, grad_e, grad_l, grad_b, shared, vecs = backward(
        shards, ggl, grad_att, dots, square, chip, osend, pre, cin, hist, q_low, kk, vv, att,
        lse_row, ssd, start, steps, cum, tot, dt, z, taps, prm, chan, normed, wf1, wf2,
        hid_own, grad_own, gains, gain_two, table, lengths,
    )
    (
        grad_full, output_full, g_z, g_x, g_q, g_gate, g_up, g_out, g_o, g_down, g_shared, g_dt, g_one,
        g_two, g_conv, g_conv_b, g_gate_gain, g_bias, g_decay, g_skip,
    ) = pack(grad_hidden, output, grad_e, grad_l, grad_b, shared, vecs)
    return (
        output_full[None],
        grad_full[None],
        g_one,
        g_z,
        g_x,
        g_shared,
        g_dt.T,
        g_bias,
        g_decay,
        g_skip,
        g_conv,
        g_conv_b,
        g_gate_gain,
        g_out,
        g_q,
        g_o,
        g_two,
        g_gate,
        g_up,
        g_down,
    )


def solution(mesh):
    placed = (
        P("shard", "ctx", None),
        P("shard", "ctx", None),
        P("shard"),
        P(("shard", "ctx")),
        P(("shard", "ctx"), "tp"),
        P(("shard", "ctx"), "tp"),
        P(("shard", "ctx"), None),
        P(("shard", "ctx"), None),
        P(),
        P(),
        P(),
        P(),
        P(),
        P(),
        P("tp", ("shard", "ctx")),
        P(("shard", "ctx"), "tp"),
        P("tp", ("shard", "ctx")),
        P(("shard", "ctx")),
        P(("shard", "ctx"), "tp"),
        P(("shard", "ctx"), "tp"),
        P("tp", ("shard", "ctx")),
    )
    return jax.shard_map(
        local,
        mesh=mesh,
        in_specs=placed,
        out_specs=(
            P("shard", "ctx", "tp"),
            P("shard", "ctx", None),
            P(("shard", "ctx", "tp")),
            P(("shard", "ctx"), "tp"),
            P(("shard", "ctx"), "tp"),
            P(("shard", "ctx", "tp"), None),
            P(("shard", "ctx", "tp"), None),
            P(),
            P(),
            P(),
            P(),
            P(),
            P(),
            P("tp", ("shard", "ctx")),
            P(("shard", "ctx"), "tp"),
            P("tp", ("shard", "ctx")),
            P(("shard", "ctx", "tp")),
            P(("shard", "ctx"), "tp"),
            P(("shard", "ctx"), "tp"),
            P("tp", ("shard", "ctx")),
        ),
        check_vma=False,
    )
```

```python
import functools

import jax
import jax.numpy as jnp
import numpy as np
from jax import lax
from jax.experimental import pallas as pl
from jax.experimental.pallas import tpu as pltpu
from jax.sharding import PartitionSpec as P

H = 24
P_SIZE = 64
N = 128
NQ = 8
KV = 2
HD = 64
CONVW = 4
DI = 1536
D = 1024
FFL = 512
TP = 4
HL = H // TP
WI = HL * P_SIZE
CH = WI + 2 * N
L = 256

CZ, CX, CM, CQ, CK, CS, CA = 0, 384, 768, 1024, 1152, 1280, 1408
GAIN_COL = 24
CO, CW, CG, CU, CD, CB = 0, 384, 512, 1024, 1536, 2048

EPS = 1e-05
rope_base = 10000.0
FILL = -1e30
HI = lax.Precision.HIGHEST
MESH = pl.DeviceIdType.MESH
f32 = jnp.float32
bf16 = jnp.bfloat16
VLIMIT = 60 * 1024 * 1024
VMOST = 63 * 1024 * 1024 + 512 * 1024


def nn(a, b, precision=None):
    return lax.dot_general(
        a, b, (((1,), (0,)), ((), ())), precision=precision, preferred_element_type=f32
    )


def nt(a, b, precision=None):
    return lax.dot_general(
        a, b, (((1,), (1,)), ((), ())), precision=precision, preferred_element_type=f32
    )


def tn(a, b, precision=None):
    return lax.dot_general(
        a, b, (((0,), (0,)), ((), ())), precision=precision, preferred_element_type=f32
    )


def rows_of(index, size=L):
    return pl.ds(pl.multiple_of(index * size, size), size)


def remote(src, dst, send, recv, **where):
    return pltpu.make_async_remote_copy(
        src_ref=src,
        dst_ref=dst,
        send_sem=send,
        recv_sem=recv,
        device_id=where,
        device_id_type=MESH,
    )


def iota(shape, dim):
    return lax.broadcasted_iota(jnp.int32, shape, dim)


def loop(n, body):
    lax.fori_loop(0, n, lambda i, c: (body(i), c)[1], 0)


def greet(shards, tp_too, ctx_too=True, shard_too=True):
    barrier = pltpu.get_barrier_semaphore()
    count = 0
    z, c, t = lax.axis_index("shard"), lax.axis_index("ctx"), lax.axis_index("tp")
    if ctx_too:
        pl.semaphore_signal(barrier, inc=1, device_id={"ctx": 1 - c}, device_id_type=MESH)
        count += 1
    if shard_too:

        def one(k):
            pl.semaphore_signal(
                barrier, inc=1, device_id={"shard": lax.rem(z + 1 + k, shards)}, device_id_type=MESH
            )

        loop(shards - 1, one)
        count += shards - 1
    if tp_too:
        for d in range(1, TP):
            pl.semaphore_signal(
                barrier, inc=1, device_id={"tp": lax.rem(t + d, TP)}, device_id_type=MESH
            )
            count += 1
    pl.semaphore_wait(barrier, count)


class Moves:
    def __init__(self):
        self.gets, self.puts = {}, {}

    def get(self, *names):
        for name in names:
            self.gets[name].wait()

    def put(self, *names):
        for name in names:
            self.puts[name].start()


def call_staged(kernel, args, out, late, early, scratch, left=(), **params):
    spaces = [pl.BlockSpec(memory_space=pltpu.VMEM)] * (len(args) - 1)
    spaces.append(pl.BlockSpec(memory_space=pltpu.SMEM))
    out_spaces = [pl.BlockSpec(memory_space=pltpu.VMEM)] * len(out)
    hbm = pl.BlockSpec(memory_space=pl.ANY)
    for at in (*late.values(), *left):
        spaces[at] = hbm
    for at in early.values():
        out_spaces[at] = hbm
    extra = [pltpu.VMEM(args[at].shape, args[at].dtype) for at in late.values()]
    extra += [pltpu.VMEM(*out[at]) for at in early.values()]
    dma = pltpu.SemaphoreType.DMA
    sems = [dma((len(late),)), dma((len(early),))]

    def body(*refs):
        split = len(args) + len(out)
        given, inner = list(refs[:split]), refs[split : split + len(scratch)]
        held, (get_sem, put_sem) = list(refs[split + len(scratch) : -2]), refs[-2:]
        moves = Moves()
        for n, (name, at) in enumerate(late.items()):
            buffer = held.pop(0)
            moves.gets[name] = pltpu.make_async_copy(given[at], buffer, get_sem.at[n])
            moves.gets[name].start()
            given[at] = buffer
        for n, (name, at) in enumerate(early.items()):
            buffer = held.pop(0)
            moves.puts[name] = pltpu.make_async_copy(buffer, given[len(args) + at], put_sem.at[n])
            given[len(args) + at] = buffer
        kernel(moves, *given, *inner)
        for copy in moves.puts.values():
            copy.wait()

    return pl.pallas_call(
        body,
        out_shape=[jax.ShapeDtypeStruct(*o) for o in out],
        in_specs=spaces,
        out_specs=out_spaces,
        scratch_shapes=list(scratch) + extra + sems,
        **params,
    )(*args)


class Gather:
    def __init__(self, shards, src, dst, zsend, fsend, csend, recv, own, cols=None):
        self.s, self.dst, self.cols = shards, dst, cols
        self.src = src if cols is None else src.at[:, cols]
        self.zsend, self.fsend, self.csend, self.recv, self.own = zsend, fsend, csend, recv, own
        self.z, self.c = lax.axis_index("shard"), lax.axis_index("ctx")
        self.r = src.shape[0]

    def block(self, g):
        rows = rows_of(g, self.r)
        return self.dst.at[rows] if self.cols is None else self.dst.at[rows, self.cols]

    def inside(self, zz):
        return (zz >= 0) & (zz < self.s)

    def straight(self, steps, way):
        g = 2 * self.z + self.c
        kind = steps - 1 + (0 if way > 0 else 2)
        return remote(
            self.src, self.block(g), self.zsend.at[kind], self.recv.at[g], shard=self.z + way * steps
        )

    def onward(self, zz, way):
        there = self.block(2 * zz + self.c)
        return remote(
            there, there, self.fsend.at[zz], self.recv.at[2 * zz + self.c], shard=self.z + way
        )

    def to_core(self, zz, core):
        there = self.block(2 * zz + core)
        return remote(
            there, there, self.csend.at[zz], self.recv.at[2 * zz + core], ctx=1 - self.c
        )

    def straight_ones(self, act_on):
        for steps in (2, 1):
            for way in (1, -1):

                @pl.when(self.inside(self.z + way * steps))
                def go(steps=steps, way=way):
                    act_on(self.straight(steps, way))

    def start(self):
        keep = pltpu.make_async_copy(self.src, self.block(2 * self.z + self.c), self.own)
        keep.start()
        self.straight_ones(lambda copy: copy.start())
        keep.wait()
        self.to_core(self.z, self.c).start()

    def forward(self, first=0, last=None):
        def one(k):
            for way in (1, -1):
                zz = self.z - way * (k + 1)

                @pl.when(self.inside(zz))
                def came(way=way, zz=zz):
                    self.to_core(zz, self.c).wait_recv()
                    self.to_core(zz, self.c).start()

                    @pl.when((k >= 1) & self.inside(self.z + way))
                    def pass_on():
                        self.onward(zz, way).start()

        lax.fori_loop(
            first, self.s - 1 if last is None else last, lambda k, carry: (one(k), carry)[1], 0
        )

    def finish(self):
        loop(self.s, lambda zz: self.to_core(zz, 1 - self.c).wait_recv())
        loop(self.s, lambda zz: self.to_core(zz, self.c).wait_send())
        self.straight_ones(lambda copy: copy.wait_send())

        def passed(k):
            for way in (1, -1):
                zz = self.z - way * (k + 1)

                @pl.when(self.inside(zz) & self.inside(self.z + way))
                def on(way=way, zz=zz):
                    self.onward(zz, way).wait_send()

        lax.fori_loop(1, self.s - 1, lambda k, carry: (passed(k), carry)[1], 0)

    @staticmethod
    def sems(shards):
        dma = pltpu.SemaphoreType.DMA
        return [dma((4,)), dma((shards,)), dma((shards,)), dma((2 * shards,)), dma(())]


class LineSum:
    def __init__(self, shards, src, hold, land, fsend, frecv, lsend, lrecv):
        self.s, self.src, self.hold, self.land = shards, src, hold, land
        self.fsend, self.frecv, self.lsend, self.lrecv = fsend, frecv, lsend, lrecv
        self.z = lax.axis_index("shard")

    def place(self, dest, way):
        return dest - 3 if way > 0 else dest

    def onward(self, src, dest, way):
        at = self.place(dest, way)
        return remote(
            src, self.hold.at[at], self.fsend.at[at], self.frecv.at[at], shard=self.z + way
        )

    def straight(self, src, steps, way):
        kind = steps - 1 + (0 if way > 0 else 2)
        return remote(
            src,
            self.land.at[kind],
            self.lsend.at[kind],
            self.lrecv.at[kind],
            shard=self.z + way * steps,
        )

    def each(self, far, two, one, waited):
        for way in (1, -1):
            first = self.z == 0 if way > 0 else self.z == self.s - 1
            now = jnp.logical_not(first) if waited else first

            def along(j, way=way, now=now):
                dest = self.s - 1 - j if way > 0 else j
                distance = (dest - self.z) * way

                @pl.when(now & (distance >= 3))
                def three():
                    far(dest, way)

                @pl.when(now & (distance == 2))
                def both():
                    two(dest, way)

            loop(self.s, along)
            if not waited:
                other = self.z + way

                @pl.when((other >= 0) & (other < self.s))
                def next_one(way=way, other=other):
                    one(other, way)

    def start(self):
        self.each(
            lambda dest, way: self.onward(self.src.at[dest], dest, way).start(),
            lambda dest, way: self.straight(self.src.at[dest], 2, way).start(),
            lambda dest, way: self.straight(self.src.at[dest], 1, way).start(),
            False,
        )

    def relay(self):
        def added(dest, way):
            at = self.place(dest, way)
            self.onward(self.src.at[dest], dest, way).wait_recv()
            own = self.src[dest].astype(f32)
            self.hold[at] = (own + self.hold[at].astype(f32)).astype(bf16)
            return self.hold.at[at]

        self.each(
            lambda dest, way: self.onward(added(dest, way), dest, way).start(),
            lambda dest, way: self.straight(added(dest, way), 2, way).start(),
            None,
            True,
        )

    def finish(self, out):
        out[...] = self.src[self.z].astype(f32)
        for steps in (1, 2):
            for way in (1, -1):
                source = self.z - way * steps

                @pl.when((source >= 0) & (source < self.s))
                def arrived(steps=steps, way=way):
                    kind = steps - 1 + (0 if way > 0 else 2)
                    remote(
                        self.land.at[kind],
                        self.land.at[kind],
                        self.lsend.at[kind],
                        self.lrecv.at[kind],
                        shard=self.z - way * steps,
                    ).wait_recv()
                    out[...] += self.land[kind].astype(f32)

        for waited in (False, True):
            self.each(
                lambda dest, way: self.onward(self.src.at[dest], dest, way).wait_send(),
                lambda dest, way: self.straight(self.src.at[dest], 2, way).wait_send(),
                lambda dest, way: self.straight(self.src.at[dest], 1, way).wait_send(),
                waited,
            )

    @staticmethod
    def scratch(shards, rows, cols):
        dma = pltpu.SemaphoreType.DMA
        far, r = max(shards - 3, 1), rows // (2 * shards)
        return [
            pltpu.VMEM((far, r, cols), bf16),
            pltpu.VMEM((4, r, cols), bf16),
            dma((far,)),
            dma((far,)),
            dma((4,)),
            dma((4,)),
        ]


class Scatter:
    def __init__(self, shards, src, sib, csend, crecv, *line):
        self.s, self.src, self.sib = shards, src, sib
        self.csend, self.crecv = csend, crecv
        self.c = lax.axis_index("ctx")
        self.r = src.shape[0] // (2 * shards)
        self.line = LineSum(shards, sib, *line)

    def to_core(self, k):
        return remote(
            self.src.at[rows_of(2 * k + 1 - self.c, self.r)],
            self.sib.at[k],
            self.csend.at[k],
            self.crecv.at[k],
            ctx=1 - self.c,
        )

    def start(self):
        loop(self.s, lambda k: self.to_core(k).start())

    def middle(self):
        def one(k):
            self.to_core(k).wait_recv()
            both = self.src[rows_of(2 * k + self.c, self.r), :].astype(f32)
            self.sib[k] = (both + self.sib[k].astype(f32)).astype(bf16)

        loop(self.s, one)
        self.line.start()

    def relay(self):
        self.line.relay()

    def finish(self, out):
        self.line.finish(out)
        loop(self.s, lambda k: self.to_core(k).wait_send())

    @staticmethod
    def scratch(shards, rows, cols):
        dma = pltpu.SemaphoreType.DMA
        block = pltpu.VMEM((shards, rows // (2 * shards), cols), bf16)
        return [block, dma((shards,)), dma((shards,))] + LineSum.scratch(shards, rows, cols)


class ChipSum:
    def __init__(self, shards, src, sib, cols, csend, crecv):
        self.s, self.src, self.sib, self.cols = shards, src, sib, cols
        self.csend, self.crecv = csend, crecv
        self.c = lax.axis_index("ctx")
        self.r = src.shape[0] // (2 * shards)

    def to_core(self, k):
        return remote(
            self.src.at[rows_of(2 * k + 1 - self.c, self.r), self.cols],
            self.sib.at[k, :, self.cols],
            self.csend.at[k],
            self.crecv.at[k],
            ctx=1 - self.c,
        )

    def start(self):
        loop(self.s, lambda k: self.to_core(k).start())

    def finish(self):
        def one(k):
            self.to_core(k).wait_recv()
            own = self.src[rows_of(2 * k + self.c, self.r), self.cols].astype(f32)
            self.sib[k, :, self.cols] = (own + self.sib[k, :, self.cols].astype(f32)).astype(bf16)

        loop(self.s, one)
        loop(self.s, lambda k: self.to_core(k).wait_send())


class Square:
    def __init__(self, kinds):
        tp = lax.axis_index("tp")
        self.me = tp
        self.x = tp + 1 - 2 * lax.rem(tp, 2)
        self.y = lax.rem(tp + 2, TP)
        self.across = TP - 1 - tp
        self.send, self.recv = kinds

    def copy(self, kind, b, src, dst):
        to = self.y if kind in (1, 2) else self.x
        return remote(src, dst, self.send.at[kind, b], self.recv.at[kind, b], tp=to)


class SquareScatter(Square):
    def __init__(self, buffers, kinds):
        super().__init__(kinds)
        self.out, self.into, self.out2, self.into2 = buffers

    def first(self, kind, b):
        return self.copy(kind, b, self.out.at[kind, b], self.into.at[kind, b])

    def second(self, kind, b):
        return self.copy(kind, b, self.out2.at[kind - 2, b], self.into2.at[kind - 2, b])

    def start(self, b, ref, rows):
        half = ref.shape[1] // 2
        left, right = pl.ds(0, half), pl.ds(half, half)
        self.out[0, b, 0] = ref[rows(self.x), left].astype(bf16)
        self.out[0, b, 1] = ref[rows(self.across), left].astype(bf16)
        self.first(0, b).start()
        self.out[1, b, 0] = ref[rows(self.y), right].astype(bf16)
        self.out[1, b, 1] = ref[rows(self.across), right].astype(bf16)
        self.first(1, b).start()
        self.out2[0, b] = ref[rows(self.y), left].astype(bf16)
        self.out2[1, b] = ref[rows(self.x), right].astype(bf16)

    def relay(self, b):
        for kind in (0, 1):
            self.first(kind, b).wait_recv()
            own = self.out2[kind, b].astype(f32)
            self.out2[kind, b] = (own + self.into[kind, b, 1].astype(f32)).astype(bf16)
            self.second(kind + 2, b).start()

    def finish(self, b):
        sums = []
        for kind in (0, 1):
            self.second(kind + 2, b).wait_recv()
            sums.append(self.into[kind, b, 0].astype(f32) + self.into2[kind, b].astype(f32))
        return jnp.concatenate(sums, axis=1)

    def sent(self, b):
        for kind in (0, 1):
            self.first(kind, b).wait_send()
            self.second(kind + 2, b).wait_send()

    @staticmethod
    def scratch(blocks, sub):
        first = pltpu.VMEM((2, blocks, 2, sub, D // 2), bf16)
        second = pltpu.VMEM((2, blocks, sub, D // 2), bf16)
        return [first, first, second, second]


class SquareGather(Square):
    def __init__(self, ref, part, kinds):
        super().__init__(kinds)
        self.ref, self.part = ref, part

    def whole(self, kind, b, owner):
        there = self.ref.at[self.part(b, owner)]
        return self.copy(kind, b, there, there)

    def half(self, kind, b, owner):
        half = self.ref.shape[1] // 2
        there = self.ref.at[self.part(b, owner), pl.ds((kind - 2) * half, half)]
        return self.copy(kind, b, there, there)

    def start(self, b):
        for kind in (0, 1):
            self.whole(kind, b, self.me).start()

    def relay(self, b):
        for kind, owner in ((0, self.x), (1, self.y)):
            self.whole(kind, b, owner).wait_recv()
            self.half(kind + 2, b, owner).start()

    def finish(self, b):
        for kind in (2, 3):
            self.half(kind, b, self.across).wait_recv()

    def sent(self, b):
        for kind, owner in ((0, self.x), (1, self.y)):
            self.whole(kind, b, self.me).wait_send()
            self.half(kind + 2, b, owner).wait_send()


class RowTotal:
    def __init__(self, slots, send, recv):
        self.slots, self.send, self.recv = slots, send, recv
        self.tp = lax.axis_index("tp")

    def to(self, d):
        there = self.slots.at[self.tp]
        return remote(
            there, there, self.send.at[d], self.recv.at[self.tp], tp=lax.rem(self.tp + d, TP)
        )

    def came(self, d):
        peer = lax.rem(self.tp + d, TP)
        there = self.slots.at[peer]
        return remote(there, there, self.send.at[d], self.recv.at[peer], tp=peer)

    def start(self, rows):
        self.slots[self.tp] = rows
        for d in range(1, TP):
            self.to(d).start()

    def finish(self):
        for d in range(1, TP):
            self.came(d).wait_recv()
            self.to(d).wait_send()
        return self.slots[0] + self.slots[1] + self.slots[2] + self.slots[3]


def sigmoid(v):
    return 1.0 / (1.0 + jnp.exp(-v))


def softplus(v):
    return jnp.maximum(v, 0.0) + jnp.log1p(jnp.exp(-jnp.abs(v)))


def swap_half(v):
    width = v.shape[1]
    low = iota(v.shape, 1) % HD < HD // 2
    return jnp.where(low, pltpu.roll(v, width - HD // 2, 1), pltpu.roll(v, HD // 2, 1))


def low_lanes(shape):
    return iota(shape, 1) < 64


def parts(v, count):
    found = []
    for _ in range(count):
        part = v.astype(bf16)
        found.append(part)
        v = v - part.astype(f32)
    return found


def packed(v):
    v = jnp.where(iota(v.shape, 1) < 8, v, 0.0)
    high, middle, low = (part.astype(f32) for part in parts(v, 3))
    return (high + pltpu.roll(middle, 8, 1) + pltpu.roll(low, 16, 1)).astype(bf16)


def unpacked(v):
    v = v + pltpu.roll(v, 120, 1) + pltpu.roll(v, 112, 1)
    return jnp.where(iota(v.shape, 1) < 8, v, 0.0)


def spread(v):
    lane, channel = iota((N, WI), 0), iota((N, WI), 1)
    pick = ((lane % 8 == channel // P_SIZE) & (lane < 24)).astype(bf16)
    return nn(packed(v), pick)


def fold(v):
    pick = (iota((WI, N), 0) // P_SIZE == iota((WI, N), 1)).astype(bf16)
    high, low = parts(v, 2)
    return nn(high, pick) + nn(low, pick)


def row_sums_of(v, pick=None):
    pick = jnp.ones((8, v.shape[1]), bf16) if pick is None else pick
    high, low = parts(v, 2)
    return nt(pick, high) + nt(pick, low)


def as_column(row):
    at = iota(row.shape, 0)
    first = jnp.broadcast_to(row[0:1, :], row.shape)
    high, middle, low = parts(first, 3)
    three = jnp.where(at == 0, high, jnp.where(at == 1, middle, low))
    return tn(three, (iota((8, N), 0) < 3).astype(bf16))


def turned_over(v):
    one = eye(v.shape[0])
    high, middle, low = parts(v, 3)
    return tn(high, one) + tn(middle, one) + tn(low, one)


def wide(column, width):
    return jnp.concatenate([column] * (width // column.shape[1]), axis=1)


def lower_ones():
    return (iota((L, L), 0) >= iota((L, L), 1)).astype(bf16)


def head_scalars(dt_raw, prm):
    real = iota(dt_raw.shape, 1) < HL
    steps = jnp.where(real, softplus(dt_raw + prm[0:1, :]), 0.0)
    rates = steps * prm[1:2, :]
    return steps, rates


def pair_columns(v, pair):
    return v[:, 128 * pair : 128 * pair + 128]


def own_half(v, half):
    return jnp.where(low_lanes(v.shape) == (half == 0), v, jnp.zeros_like(v))


def eye(n):
    return (iota((n, n), 0) == iota((n, n), 1)).astype(bf16)


def rotary_of(table, rows):
    both = table[rows, :]
    first = iota(both.shape, 1) % HD < HD // 2
    cosine = jnp.where(first, both, pltpu.roll(both, HD // 2, 1))
    sine = jnp.where(first, -pltpu.roll(both, 128 - HD // 2, 1), both)
    return cosine, sine


FORWARD_EARLY = (
    "wf1",
    "wf2",
    "normed",
    "z_out",
    "cin",
    "dt_raw",
    "pre",
    "q_low",
    "kk",
    "vv",
    "att",
    "att_low",
    "steps_out",
    "cum_out",
)
FORWARD_AT = (
    0,
    1,
    4,
    6,
    7,
    8,
    12,
    14,
    15,
    16,
    17,
    18,
    22,
    23,
)
BACKWARD_LATE = (
    "chip",
    "grad_att",
    "q_low",
    "kk",
    "vv",
    "att",
    "lse_row",
    "start",
    "steps_in",
    "dt_raw",
    "cin",
    "normed",
    "wf1",
    "wf2",
    "hid_own",
    "grad_own",
)
BACKWARD_AT = (
    4,
    1,
    9,
    10,
    11,
    12,
    13,
    15,
    16,
    19,
    7,
    24,
    25,
    26,
    27,
    28,
)


def forward_kernel(
    shards, moves,
    hid, w_z, w_x, w_shared, w_dt, w_q, w_out, w_o, w_gate, gain_one, gain_two,
    conv_w, conv_b, gated_gain, dt_bias, a_log, d_skip, table, length,
    wf1, wf2, wo, wg, normed, gains, z_out, cin, dt_raw, taps, prm, chan,
    pre, hist, q_low, kk, vv, att, att_low, lse_row, ssd, start, steps_out, cum_out, tot_out,
    gated_low, square,
    slots, small, wa1, wa2, wa3, stat, zf, pad, act, state, carried, scores_m, scores_l, hist_in,
    zs1, fs1, cs1, zr1, own1, zs2, fs2, cs2, zr2, own2, zs3, fs3, cs3, zr3, own3,
    zs4, fs4, cs4, zr4, own4, zs5, fs5, cs5, zr5, own5,
    xs, xr, qs, qr,
):
    c, tp = lax.axis_index("ctx"), lax.axis_index("tp")
    t = hid.shape[0]
    blocks = t // L
    r = w_z.shape[0]

    kv = tp * (NQ // TP) // (NQ // KV)
    keys = w_shared[:, 2 * N : 2 * N + 128].astype(f32)
    vals = w_shared[:, 2 * N + 128 : 2 * N + 256].astype(f32)
    low_r = low_lanes((r, 128))
    other = pltpu.roll(jnp.where(kv == 0, vals, keys), 64, 1)
    wa1[:, 0:128] = w_q[...]
    wa1[:, 128:256] = jnp.where(
        kv == 0, jnp.where(low_r, keys, other), jnp.where(low_r, other, vals)
    ).astype(bf16)
    head_pick = (
        (iota((H, 128), 0) == iota((H, 128), 1) + tp * HL) & (iota((H, 128), 1) < HL)
    ).astype(bf16)
    row8, lane8 = iota((8, 128), 0), iota((8, 128), 1)
    gain_pick = ((row8 < 2) & (lane8 == GAIN_COL + row8)).astype(bf16)
    gain_rows = jnp.where(
        iota((8, r), 0) == 0, gain_one[...].astype(f32), gain_two[...].astype(f32)
    ).astype(bf16)
    wa1[:, 256:384] = (tn(w_dt[...], head_pick) + tn(gain_rows, gain_pick)).astype(bf16)
    wa2[:, 0:WI] = w_z[...]
    wa2[:, WI : 2 * WI] = w_x[...]
    wa2[:, 2 * WI : 2 * WI + 2 * N] = w_shared[:, 0 : 2 * N]
    greet(shards, True)
    gather1 = Gather(shards, wa1, wf1, zs1, fs1, cs1, zr1, own1)
    gather2 = Gather(shards, wa2, wf2, zs2, fs2, cs2, zr2, own2, pl.ds(WI, CH))
    gather5 = Gather(shards, wa2, wf2, zs5, fs5, cs5, zr5, own5, pl.ds(0, WI))
    gather3 = Gather(shards, wa3, wo, zs3, fs3, cs3, zr3, own3)
    gather4 = Gather(shards, w_gate, wg, zs4, fs4, cs4, zr4, own4)
    gather1.start()
    gather2.start()
    wa3[:, CO:CW] = nt(eye(r), w_out[...]).astype(bf16)
    wa3[:, CW:CG] = nt(eye(r), w_o[...]).astype(bf16)

    mine = pl.ds(pl.multiple_of(tp * WI, 128), WI)
    small[...] = jnp.zeros_like(small)
    small[0:1, :] = conv_b[...].astype(f32)[None, :]
    small[1:2, 0:DI] = gated_gain[...].astype(f32)[None, :]
    small[8:9, 0:H] = dt_bias[...].astype(f32)[None, :]
    small[9:10, 0:H] = a_log[...].astype(f32)[None, :]
    small[10:11, 0:H] = d_skip[...].astype(f32)[None, :]
    taps[0:CONVW, 0:WI] = conv_w[:, mine].astype(f32)
    taps[0:CONVW, WI:CH] = conv_w[:, DI:].astype(f32)
    taps[CONVW : CONVW + 1, 0:WI] = small[0:1, mine]
    taps[CONVW : CONVW + 1, WI:CH] = small[0:1, DI:]
    taps[CONVW + 1 :, :] = jnp.zeros((8 - CONVW - 1, CH), f32)
    heads = pltpu.roll(small[8:16, 0:128], lax.rem(128 - tp * HL, 128), 1)
    heads = jnp.where(lane8 < HL, jnp.where(row8 == 1, -jnp.exp(heads), heads), 0.0)
    prm[...] = heads
    chan[...] = jnp.zeros_like(chan)
    chan[0:1, :] = small[1:2, mine]
    chan[1:2, :] = spread(heads)[2:3, :]

    def swap(src, dst, i):
        return remote(src, dst, xs.at[i], xr.at[i], ctx=1 - c)

    def row_scale(i):
        rows = rows_of(i)
        x = hid[rows, :].astype(f32)
        scale = lax.rsqrt(jnp.mean(x * x, -1, keepdims=True) + EPS)
        stat[rows, :] = jnp.broadcast_to(scale, (L, 128))

    loop(blocks, row_scale)
    gather1.forward()
    gather1.finish()
    gather5.start()
    turned = wf1[:, 256:384].astype(f32).T
    gains[...] = turned[GAIN_COL : GAIN_COL + 8]
    gain = gains[0:1, :]
    low128 = low_lanes((L, 128))
    moves.put("wf1")
    moves.get("table")

    def first_projections(i):
        rows = rows_of(i)
        low = (hid[rows, :].astype(f32) * wide(stat[rows, :], D) * gain).astype(bf16)
        normed[rows, :] = low
        rest = nn(low, wf1[...])
        cosine, sine = rotary_of(table, pl.ds(pl.multiple_of(c * t + i * L, L), L))
        v = rest[:, 0:128]
        q_low[rows, :] = (v * cosine + swap_half(v) * sine).astype(bf16)
        v = rest[:, 128:256]
        other = pltpu.roll(v, 64, 1)
        twice = jnp.where(low128, v, other)
        kk[0, rows, :] = (twice * cosine + swap_half(twice) * sine).astype(bf16)
        vv[0, rows, :] = jnp.where(low128, other, v).astype(bf16)
        dt_raw[rows, :] = rest[:, 256:384]

    loop(blocks, first_projections)
    moves.put("normed", "q_low", "dt_raw")
    keys = swap(kk.at[0], kk.at[1], 1)
    keys.start()
    vals = swap(vv.at[0], vv.at[1], 2)
    vals.start()

    scale = HD ** (-0.5)
    limit = length[0] - c * t

    def stacked(v):
        return jnp.concatenate([own_half(v, 0), own_half(v, 1)], axis=0)

    for i in range(blocks):
        rows = pl.ds(i * L, L)
        width = (i + 1) * L
        q2 = stacked(q_low[rows, :].astype(f32)).astype(bf16)
        s = nt(q2, kk[0, 0:width, :]) * scale
        at = iota(s.shape, 0) % L + i * L
        col = iota(s.shape, 1)
        s = jnp.where((col <= at) & (col < limit), s, FILL)
        peak = jnp.max(s, -1, keepdims=True)
        e = jnp.exp(s - peak)
        total = jnp.sum(e, -1, keepdims=True)
        o = nn(e.astype(bf16), vv[0, 0:width, :])
        scores_m[...] = jnp.broadcast_to(peak, (2 * L, 128))
        scores_l[0] = jnp.broadcast_to(total, (2 * L, 128))
        scores_l[1] = o
        if i == 0:
            keys.wait_recv()
            vals.wait_recv()

        @pl.when(c > 0)
        def earlier():
            s2 = nt(q2, kk[1]) * scale
            old = scores_m[:, 0:1]
            new = jnp.maximum(old, jnp.max(s2, -1, keepdims=True))
            e2 = jnp.exp(s2 - new)
            fade = jnp.exp(old - new)
            scores_m[...] = jnp.broadcast_to(new, (2 * L, 128))
            scores_l[0] = fade * scores_l[0] + jnp.sum(e2, -1, keepdims=True)
            scores_l[1] = fade * scores_l[1] + nn(e2.astype(bf16), vv[1])

        total = scores_l[0]
        o = scores_l[1] / total
        o = jnp.where(low128, o[:L], o[L:])
        att[rows, :] = o
        att_low[rows, :] = o.astype(bf16)
        logs = scores_m[...] + jnp.log(total)
        turned = jnp.where(low128, logs[:L], logs[L:]).T
        lse_row[0:1, rows] = turned[0:1]
        lse_row[1:2, rows] = turned[64:65]
        lse_row[2:8, rows] = jnp.zeros((6, L), f32)
        if i == blocks - 3:
            gather2.forward(0, 2)
        if i == blocks - 2:
            gather2.forward(2)
            gather3.start()
    moves.put("kk", "vv", "att", "att_low")
    gather5.forward(0, 2)
    gather2.finish()

    def conv_input(k):
        i = blocks - 1 - k
        rows = rows_of(i)
        v = nn(normed[rows, :], wf2[:, WI:]).astype(bf16)
        cin[rows, :] = v
        pad[pl.ds(pl.multiple_of(i * L + 8, 8), L), :] = v.astype(f32)

    conv_input(0)
    tail = swap(cin.at[pl.ds(t - 16, 16)], hist_in, 0)
    tail.start()
    lax.fori_loop(1, blocks, lambda k, carry: (conv_input(k), carry)[1], 0)
    gather5.forward(2)
    gather4.start()
    tail.wait_recv()
    before = hist_in[8:16, :].astype(f32)
    hist[...] = jnp.where((iota((8, CH), 0) >= 5) & (c > 0), before, 0.0)
    pad[0:8, :] = hist[...]
    ones = lower_ones()
    state[...] = jnp.zeros_like(state)

    for i in range(blocks):
        rows = pl.ds(i * L, L)
        v = taps[4:5, :] + taps[0:1, :] * pad[pl.ds(i * L + 5, L), :]
        for j in range(1, CONVW):
            v = v + taps[j : j + 1, :] * pad[pl.ds(i * L + 5 + j, L), :]
        pre[rows, :] = v
        a = v * sigmoid(v)
        act[rows, :] = a
        steps, rates = head_scalars(dt_raw[rows, :], prm)
        cum = unpacked(nn(ones, packed(rates)))
        tot = cum[L - 1 : L, :]
        steps_out[rows, :] = steps
        cum_out[rows, :] = cum
        tot_out[i] = jnp.broadcast_to(tot, (8, 128))
        weight = spread(jnp.exp(tot - cum) * steps)
        start[i] = state[...]
        add = tn(a[:, WI : WI + N].astype(bf16), (weight * a[:, :WI]).astype(bf16))
        decay = spread(jnp.broadcast_to(jnp.exp(tot), (8, 128)))[0:1, :]
        state[...] = decay * state[...] + add

    states = swap(state, carried, 3)
    states.start()
    moves.put("cin", "pre", "steps_out", "cum_out")
    gather3.forward(0, 2)

    gather5.finish()
    moves.put("wf2")

    def gate_input(i):
        rows = rows_of(i)
        zf[rows, :] = nn(normed[rows, :], wf2[:, 0:WI])
        z_out[rows, :] = zf[rows, :].astype(bf16)

    loop(blocks, gate_input)
    moves.put("z_out")

    states.wait_recv()
    gather3.forward(2)
    carried[...] = jnp.where(c > 0, carried[...], 0.0)
    mask = iota((L, L), 0) >= iota((L, L), 1)
    for i in range(blocks):
        rows = pl.ds(i * L, L)
        if i > 0:
            decay = spread(jnp.exp(tot_out[i - 1]))[0:1, :]
            carried[...] = carried[...] * decay
        start[i] = start[i] + carried[...]
        s0 = start[i].astype(bf16)
        steps, cum = steps_out[rows, :], cum_out[rows, :]
        x = act[rows, 0:WI]
        xl = x.astype(bf16)
        in_map = act[rows, WI : WI + N].astype(bf16)
        out_map = act[rows, WI + N : CH].astype(bf16)
        gram = nt(out_map, in_map)
        cum_t, steps_t = cum.T, steps.T
        inner = []
        for pair in range(HL // 2):
            halves = []
            for half in range(2):
                h = 2 * pair + half
                decay = jnp.exp(jnp.where(mask, cum[:, h : h + 1] - cum_t[h : h + 1, :], FILL))
                mixing = gram * decay * steps_t[h : h + 1, :]
                halves.append(nn(mixing.astype(bf16), pair_columns(xl, pair)))
            inner.append(jnp.where(low128, halves[0], halves[1]))
        y = jnp.concatenate(inner, axis=1)
        y = y + spread(jnp.exp(cum)) * nn(out_map, s0) + chan[1:2, :] * x
        ssd[rows, :] = y.astype(bf16)
        zz = zf[rows, :]
        gated = y * zz * sigmoid(zz)
        gated_low[rows, :] = (gated * chan[0:1, :]).astype(bf16)
        square[:, rows] = row_sums_of(gated * gated)
        if i == 1:
            gather4.forward(0, 2)

    squares = RowTotal(slots, qs, qr)
    squares.start(square[...])
    gather4.forward(2)
    gather3.finish()
    gather4.finish()
    square[...] = squares.finish()
    for copy in (tail, keys, vals, states):
        copy.wait_send()


def forward(shards, *args):
    t, r = args[0].shape[0], args[1].shape[0]
    out = [
        ((D, 384), bf16),
        ((D, 1024), bf16),
        ((D, CG), bf16),
        ((D, FFL), bf16),
        ((t, D), bf16),
        ((8, D), f32),
        ((t, WI), bf16),
        ((t, CH), bf16),
        ((t, 128), f32),
        ((8, CH), f32),
        ((8, 128), f32),
        ((8, WI), f32),
        ((t, CH), f32),
        ((8, CH), f32),
        ((t, 128), bf16),
        ((2, t, 128), bf16),
        ((2, t, 128), bf16),
        ((t, 128), f32),
        ((t, 128), bf16),
        ((8, t), f32),
        ((t, WI), bf16),
        ((t // L, N, WI), f32),
        ((t, 128), f32),
        ((t, 128), f32),
        ((t // L, 8, 128), f32),
        ((t, WI), bf16),
        ((8, t), f32),
    ]
    dma = pltpu.SemaphoreType.DMA
    scratch = (
        [
            pltpu.VMEM((TP, 8, t), f32),
            pltpu.VMEM((16, DI + 2 * N), f32),
            pltpu.VMEM((r, 384), bf16),
            pltpu.VMEM((r, 1024), bf16),
            pltpu.VMEM((r, CG), bf16),
            pltpu.VMEM((t, 128), f32),
            pltpu.VMEM((t, WI), f32),
            pltpu.VMEM((t + 8, CH), f32),
            pltpu.VMEM((t, CH), f32),
            pltpu.VMEM((N, WI), f32),
            pltpu.VMEM((N, WI), f32),
            pltpu.VMEM((2 * L, 128), f32),
            pltpu.VMEM((2, 2 * L, 128), f32),
            pltpu.VMEM((16, CH), bf16),
        ]
        + Gather.sems(shards) * 5
        + [dma((4,)), dma((4,)), dma((TP,)), dma((TP,))]
    )
    return call_staged(
        functools.partial(forward_kernel, shards),
        args,
        out,
        {"table": 17},
        dict(zip(FORWARD_EARLY, FORWARD_AT)),
        scratch,
        compiler_params=pltpu.CompilerParams(
            collective_id=1, has_side_effects=True, vmem_limit_bytes=VLIMIT
        ),
        name="mix_forward",
    )


def ffn_kernel(
    shards, moves,
    hid, cot, gl, att, total_square, wb, wg, w_up, w_down, gains, length,
    osend, grad_own, chip, hid_own, gain_grad, ggl, grad_att, dots,
    grads, grad_res, partial, seed, low_two, proj, act, gg, gu, gown, back,
    unit, scale_keep, sqall, wm, wm_own, a1, a2, a3, a4, b1, b2, b3, b4,
    zs, fs, cs, zr, own_sem, ms, mr, ws, wr, sqs, sqr, s1, r1, ns, nr, gs, gr, hs, hr,
):
    t = hid.shape[0]
    tp, c = lax.axis_index("tp"), lax.axis_index("ctx")
    blocks = t // L
    sub = L // TP
    width = D // TP
    wm_own[:, 0:FFL] = w_up[...]
    wm_own[:, FFL:] = nt(eye(w_down.shape[1]), w_down[...]).astype(bf16)
    greet(shards, True)
    gather = Gather(shards, wm_own, wm, zs, fs, cs, zr, own_sem)
    gather.start()
    mlp_sum = ChipSum(shards, grads, chip, pl.ds(CG, CB - CG), ms, mr)
    out_sum = ChipSum(shards, grads, chip, pl.ds(CO, CG - CO), ws, wr)

    def peer(d):
        return lax.rem(tp + d, TP)

    def part(b, owner):
        return pl.ds(pl.multiple_of(b * L + owner * sub, sub), sub)

    def kept(b):
        return rows_of(b, sub)

    first = SquareScatter((a1, a2, a3, a4), (s1, r1))
    norms = SquareGather(low_two, part, (ns, nr))
    gradients = SquareScatter((b1, b2, b3, b4), (gs, gr))
    residuals = SquareGather(grad_res, part, (hs, hr))

    limit = length[0] - c * t

    def mask_seed(i):
        rows = rows_of(i)
        live = iota((L, D), 0) + i * L < limit
        seed[rows, :] = jnp.where(live, cot[rows, :].astype(f32), 0.0).astype(bf16)

    gain = gains[1:2, :]
    gain_grad[...] = jnp.zeros_like(gain_grad)

    def mix(b):
        rows = rows_of(b)
        scale = lax.rsqrt(total_square[:, rows] / DI + EPS)
        column = wide(as_column(scale), D)
        partial[rows, :] = nt(gl[rows, :], wb[:, CO:CW]) * column + nt(att[rows, :], wb[:, CW:CG])
        first.start(b, partial, lambda owner: part(b, owner))

    def norm(b):
        own = part(b, tp)
        hid_own[kept(b), :] = hid[own, :]
        acc = hid[own, :].astype(f32) + partial[own, :] + first.finish(b)
        scale = lax.rsqrt(jnp.mean(acc * acc, -1, keepdims=True) + EPS)
        scale_keep[kept(b), :] = jnp.broadcast_to(scale, (sub, 128))
        u = acc * scale
        unit[kept(b), :] = u
        low_two[own, :] = (u * gain).astype(bf16)
        norms.start(b)

    def hidden_units(b):
        rows = rows_of(b)
        norms.finish(b)
        low = low_two[rows, :]
        gate, up = nn(low, wg[...]), nn(low, wm[:, 0:FFL])
        sig = sigmoid(gate)
        silu = gate * sig
        hidden_act = (silu * up).astype(bf16)
        act[rows, :] = hidden_act
        ga = nn(seed[rows, :], wm[:, FFL:])
        g1 = (ga * up * (sig * (1.0 + gate * (1.0 - sig)))).astype(bf16)
        g2 = (ga * silu).astype(bf16)
        gg[rows, :] = g1
        gu[rows, :] = g2
        back[...] = nt(g1, wg[...]) + nt(g2, wm[:, 0:FFL])
        gown[kept(b), :] = back[kept(tp), :]
        gradients.start(b, back, kept)
        partial[rows, :] = partial[rows, :] + nt(hidden_act, wm[:, FFL:])
        mine = rows_of(tp, width)
        osend[0, rows, :] = (partial[rows, mine] + hid[rows, mine].astype(f32)).astype(bf16)
        for e in range(1, TP):
            osend[e, rows, :] = partial[rows, rows_of(peer(e), width)].astype(bf16)

    def norm_back(b):
        own = part(b, tp)
        g = gown[kept(b), :] + gradients.finish(b)
        u = unit[kept(b), :]
        gain_grad[...] += jnp.broadcast_to(jnp.sum(g * u, 0, keepdims=True), (8, D))
        weighted = g * gain
        mean = jnp.mean(weighted * u, -1, keepdims=True)
        res = seed[own, :].astype(f32) + scale_keep[kept(b), 0:1] * (weighted - u * mean)
        grad_own[kept(b), :] = res
        grad_res[own, :] = res.astype(bf16)
        residuals.start(b)

    def weight_grads(i):
        feats = rows_of(i)
        low = low_two[:, feats]
        grads[feats, CG:CU] = tn(low, gg[...]).astype(bf16)
        grads[feats, CU:CD] = tn(low, gu[...]).astype(bf16)

    def down_grads(i):
        feats = rows_of(i)
        grads[feats, CD:CB] = tn(seed[:, feats], act[...]).astype(bf16)

    def out_back(b):
        rows = rows_of(b)
        residuals.finish(b)
        square_scale = lax.rsqrt(total_square[:, rows] / DI + EPS)
        column = wide(as_column(square_scale), D)
        got = grad_res[rows, :]
        low = (column * got.astype(f32)).astype(bf16)
        proj[rows, :] = low
        product = nn(low, wb[:, CO:CW])
        ggl[rows, :] = product
        dots[:, rows] = row_sums_of(product * gl[rows, :].astype(f32))
        grad_att[rows, :] = nn(got, wb[:, CW:CG]).astype(bf16)

    def stage(s, delay, act_on):
        @pl.when((s >= delay) & (s < delay + blocks))
        def go():
            act_on(s - delay)

    def step(s):
        stage(s, 0, mix)

        @pl.when(s == 1)
        def masks():
            moves.get("hid", "cot", "wg")
            loop(blocks, mask_seed)

        @pl.when(s == 2)
        def pieces():
            gather.forward(0, 2)

        stage(s, 1, first.relay)
        stage(s, 2, norm)
        stage(s, 3, norms.relay)

        @pl.when(s == 3)
        def weights():
            gather.forward(2)
            gather.finish()

        stage(s, 4, hidden_units)

        @pl.when(s == blocks + 5)
        def more():
            loop(D // L, down_grads)
            mlp_sum.start()

        stage(s, 6, norm_back)

        @pl.when(s == blocks + 6)
        def norms_done():
            moves.put("grad_own")

        stage(s, 7, residuals.relay)

        @pl.when(s == blocks + 4)
        def fill():
            moves.put("osend")
            loop(D // L, weight_grads)

        stage(s, 5, gradients.relay)
        stage(s, 8, out_back)

    loop(blocks + 8, step)

    def out_grads(i):
        feats = rows_of(i)
        grads[feats, CO:CW] = tn(proj[:, feats], gl[...]).astype(bf16)
        grads[feats, CW:CG] = tn(grad_res[:, feats], att[...]).astype(bf16)

    totals = RowTotal(sqall, sqs, sqr)
    totals.start(dots[...])
    loop(D // L, out_grads)
    out_sum.start()
    mlp_sum.finish()
    dots[...] = totals.finish()
    out_sum.finish()

    def sent(b):
        for exchange in (first, norms, gradients, residuals):
            exchange.sent(b)

    loop(blocks, sent)


def ffn(shards, *args):
    t = args[0].shape[0]
    blocks, sub = t // L, L // TP
    kept = blocks * sub
    out = [
        ((TP, t, D // TP), bf16),
        ((kept, D), f32),
        ((shards, D // (2 * shards), CB), bf16),
        ((kept, D), bf16),
        ((8, D), f32),
        ((t, WI), f32),
        ((t, 128), bf16),
        ((8, t), f32),
    ]
    dma = pltpu.SemaphoreType.DMA
    scratch = (
        [
            pltpu.VMEM((D, CB), bf16),
            pltpu.VMEM((t, D), bf16),
            pltpu.VMEM((t, D), f32),
            pltpu.VMEM((t, D), bf16),
            pltpu.VMEM((t, D), bf16),
            pltpu.VMEM((t, D), bf16),
            pltpu.VMEM((t, FFL), bf16),
            pltpu.VMEM((t, FFL), bf16),
            pltpu.VMEM((t, FFL), bf16),
            pltpu.VMEM((kept, D), f32),
            pltpu.VMEM((L, D), f32),
            pltpu.VMEM((kept, D), f32),
            pltpu.VMEM((kept, 128), f32),
            pltpu.VMEM((TP, 8, t), f32),
            pltpu.VMEM((D, 2 * FFL), bf16),
            pltpu.VMEM((D // (2 * shards), 2 * FFL), bf16),
        ]
        + SquareScatter.scratch(blocks, sub) * 2
        + Gather.sems(shards)
        + [dma((shards,))] * 4
        + [dma((TP,))] * 2
        + [dma((TP, blocks))] * 8
    )
    return call_staged(
        functools.partial(ffn_kernel, shards),
        args,
        out,
        {"hid": 0, "cot": 1, "wg": 6},
        {"osend": 0, "grad_own": 1},
        scratch,
        compiler_params=pltpu.CompilerParams(
            collective_id=2, has_side_effects=True, vmem_limit_bytes=VLIMIT
        ),
        name="feed_forward",
    )


def backward_kernel(
    shards, moves,
    ggl, grad_att, dots_in, total_square, chip, osend,
    pre, cin, hist, q_low, kk, vv, att, lse_row, ssd, start, steps_in, cum_in, tot_in, dt_raw, z_in,
    taps, prm, chan, normed, wf1, wf2, hid_own, grad_own, gains, gain_two, table_all, length,
    output, low, grad_e, grad_l, grad_b, shared, vecs,
    table, own_out, lin, small, orecv, dk, dv, dy, dpre, ends, dstate, carry, kv_out, kv_in, pad,
    edge_out, edge_in, gown, back, gain_one, grads_e, grads_l, misc, misc_low, misc_sum, shsend,
    vec_sib, vec_z,
    ln0, ln1, ln2, ln3, ln4, ln5,
    e0, e1, e2, e3, e4, e5, e6, e7, e8,
    l0, l1, l2, l3, l4, l5, l6, l7, l8,
    m0, m1, m2, m3, m4, m5, m6, m7, m8,
    g0, g1, g2, g3,
    table_sem, own_sem, vcs, vcr, vzs, vzr, xs, xr, os, orr, ss, sr, vts, vtr, gs, gr, hs, hr,
):
    z, c, tp = lax.axis_index("shard"), lax.axis_index("ctx"), lax.axis_index("tp")
    t = cin.shape[0]
    blocks, sub = t // L, L // TP
    get_table = pltpu.make_async_copy(table_all.at[rows_of(c, t)], table, table_sem)
    get_table.start()
    greet(shards, True)
    scatter = LineSum(shards, chip, ln0, ln1, ln2, ln3, ln4, ln5)
    scatter0 = Scatter(shards, grads_e, e0, e1, e2, e3, e4, e5, e6, e7, e8)
    scatter1 = Scatter(shards, grads_l, l0, l1, l2, l3, l4, l5, l6, l7, l8)
    scatter2 = Scatter(shards, misc_low, m0, m1, m2, m3, m4, m5, m6, m7, m8)
    moves.get("chip")
    scatter.start()

    def swap(src, dst, i):
        return remote(src, dst, xs.at[i], xr.at[i], ctx=1 - c)

    def peer(d):
        return lax.rem(tp + d, TP)

    def to_all(ref, send, recv, d):
        return remote(ref.at[tp], ref.at[tp], send.at[d], recv.at[tp], tp=peer(d))

    def from_all(ref, send, recv, d):
        return remote(ref.at[tp], ref.at[peer(d)], send.at[d], recv.at[peer(d)], tp=peer(d))


    def out_to(d):
        return remote(osend.at[d], orecv.at[TP - 1 - d], os.at[d], orr.at[TP - 1 - d], tp=peer(d))

    def out_from(d):
        return remote(osend.at[d], orecv.at[d - 1], os.at[d], orr.at[d - 1], tp=peer(d))

    get_own = pltpu.make_async_copy(osend.at[0], own_out, own_sem)
    get_own.start()
    for d in range(1, TP):
        out_to(d).start()
    conv_grads = small.at[:, 0:CH]
    chan_grads = small.at[:, CH : CH + WI]
    head_grads = small.at[:, CH + WI : CH + WI + 128]
    low128 = low_lanes((L, 128))
    small[...] = jnp.zeros_like(small)

    def gated_back(i):
        rows = rows_of(i)
        share = dots_in[:, rows] / ((total_square[:, rows] / DI + EPS) * DI)
        column = wide(as_column(share), WI)
        zz, y = z_in[rows, :].astype(f32), ssd[rows, :].astype(f32)
        sig = sigmoid(zz)
        silu = zz * sig
        gated = y * silu
        product = ggl[rows, :]
        chan_grads[0:1, :] += jnp.sum(product * gated, 0, keepdims=True)
        grad_gated = product * chan[0:1, :] - column * gated
        grad_y = grad_gated * silu
        dy[rows, :] = grad_y
        lin[rows, CZ:CX] = (grad_gated * y * (sig * (1.0 + zz * (1.0 - sig)))).astype(bf16)
        v = pre[rows, WI + N : CH]
        out_map = (v * sigmoid(v)).astype(bf16)
        ends[i] = tn(out_map, (spread(jnp.exp(cum_in[rows, :])) * grad_y).astype(bf16))

    loop(blocks, gated_back)
    dstate[...] = jnp.zeros_like(dstate)

    def chain(k):
        i = blocks - 1 - k
        add = ends[i]
        ends[i] = dstate[...]
        dstate[...] = spread(jnp.exp(tot_in[i]))[0:1, :] * dstate[...] + add

    loop(blocks, chain)
    states = swap(dstate, carry, 0)
    states.start()

    scale = HD ** (-0.5)
    limit = length[0] - c * t
    dk[...] = jnp.zeros_like(dk)
    dv[...] = jnp.zeros_like(dv)
    get_table.wait()
    moves.get("grad_att", "q_low", "kk", "vv", "att", "lse_row")
    head_of = ((iota((8, 128), 1) // HD) == iota((8, 128), 0)).astype(bf16)

    def stacked(v):
        return jnp.concatenate([own_half(v, 0), own_half(v, 1)], axis=0).astype(bf16)

    def side_by_side(v):
        return jnp.concatenate([v[0:1, :], v[1:2, :]], axis=1)

    for i in range(blocks):
        rows = pl.ds(i * L, L)
        width = (i + 1) * L
        q2 = stacked(q_low[rows, :].astype(f32))
        go = grad_att[rows, :].astype(f32)
        go2 = stacked(go)
        row_dot = side_by_side(row_sums_of(go * att[rows, :], head_of))
        logs = side_by_side(lse_row[:, rows])
        turn = rotary_of(table, rows)

        def keys_of(part, size, masked):
            k, v = kk[part, 0:size, :], vv[part, 0:size, :]
            s = nt(k, q2) * scale - logs
            if masked:
                at = iota(s.shape, 1) % L + i * L
                row = iota(s.shape, 0)
                s = jnp.where((row <= at) & (row < limit), s, FILL)
            p = jnp.exp(s)
            ds = (p * (nt(v, go2) - row_dot)).astype(bf16)
            dv[part, 0:size, :] += nn(p.astype(bf16), go2)
            dk[part, 0:size, :] += nn(ds, q2)
            out = tn(ds, k) * scale
            out = jnp.where(low128, out[:L], out[L:])
            return out * turn[0] - swap_half(out) * turn[1]

        back[:, 0:128] = keys_of(0, width, True)

        @pl.when(c > 0)
        def earlier():
            back[:, 0:128] += keys_of(1, t, False)

        lin[rows, CQ:CK] = back[:, 0:128].astype(bf16)
        if i == 1:
            scatter.relay()

    def key_values(part, rows):
        gk, gv = dk[part, rows, :] * scale, dv[part, rows, :]
        return jnp.where(low128, gk + pltpu.roll(gk, 64, 1), gv + pltpu.roll(gv, 64, 1))

    def pack(i):
        rows = rows_of(i)
        kv_out[rows, :] = key_values(1, rows).astype(bf16)

    loop(blocks, pack)
    pairs = swap(kv_out, kv_in, 1)
    pairs.start()

    moves.get("start", "steps_in", "dt_raw", "cin", "normed", "wf1", "wf2", "hid_own", "grad_own")
    pad[0:16, :] = jnp.concatenate([jnp.zeros((8, CH), f32), hist[...]], axis=0).astype(bf16)

    def fill(i):
        pad[pl.ds(pl.multiple_of(i * L + 16, 16), L), :] = cin[rows_of(i), :]

    loop(blocks, fill)
    states.wait_recv()
    carry[...] = jnp.where(c == 0, carry[...], 0.0)

    def add_carry(k):
        i = blocks - 1 - k
        ends[i] = ends[i] + carry[...]
        carry[...] = spread(jnp.exp(tot_in[i]))[0:1, :] * carry[...]

    loop(blocks, add_carry)
    mask = iota((L, L), 0) >= iota((L, L), 1)
    ones = lower_ones()
    lane = iota((L, 128), 1)

    def scan_back(i):
        rows = rows_of(i)
        v = pre[rows, :]
        sig = sigmoid(v)
        a = v * sig
        x = a[:, :WI]
        xl, bl, cl = x.astype(bf16), a[:, WI : WI + N].astype(bf16), a[:, WI + N :].astype(bf16)
        steps, cum = steps_in[rows, :], cum_in[rows, :]
        tot = cum[L - 1 : L, :]
        ecum, wend = jnp.exp(cum), jnp.exp(tot - cum)
        weight = wend * steps
        ecum_x, weight_x = spread(ecum), spread(weight)
        grad_y = dy[rows, :]
        dyl = grad_y.astype(bf16)
        s0, d1 = start[i], ends[i]
        s0l, d1l = s0.astype(bf16), d1.astype(bf16)
        bd, cs = nn(bl, d1l), nn(cl, s0l)
        dw = fold(x * bd)
        crossing = jnp.broadcast_to(jnp.sum(s0 * d1, 0, keepdims=True), (8, WI))
        dtot = jnp.sum(weight * dw, 0, keepdims=True) + jnp.exp(tot) * fold(crossing)[0:1, :]
        gram = nt(cl, bl)
        cum_t, steps_t = cum.T, steps.T
        dgram = jnp.zeros((L, L), f32)
        row_sums = jnp.zeros((L, 128), f32)
        col_sums, inner = [], []
        for pair in range(HL // 2):
            xp, dp = pair_columns(xl, pair), pair_columns(dyl, pair)
            dpf = pair_columns(grad_y, pair)
            halves = []
            for half in range(2):
                h = 2 * pair + half
                decay = jnp.exp(jnp.where(mask, cum[:, h : h + 1] - cum_t[h : h + 1, :], FILL))
                q = nt(own_half(dpf, half).astype(bf16), xp)
                mixed = gram * decay
                srow = steps_t[h : h + 1, :]
                f = mixed * q
                col_sums.append(jnp.sum(f, 0, keepdims=True))
                row_sums = jnp.where(lane == h, jnp.sum(f * srow, -1, keepdims=True), row_sums)
                dgram = dgram + decay * srow * q
                halves.append(tn((mixed * srow).astype(bf16), dp))
            inner.append(jnp.where(low128, halves[0], halves[1]))
        cols = jnp.concatenate(col_sums + [jnp.zeros((128 - HL, L), f32)], axis=0).T
        dcum = fold(grad_y * cs) * ecum - weight * dw + row_sums - steps * cols
        dcum = dcum + jnp.where(iota((L, 128), 0) == L - 1, dtot, 0.0)
        drate = unpacked(tn(ones, packed(dcum)))
        rate_of = prm[1:2, :]
        raw = dt_raw[rows, :] + prm[0:1, :]
        dstep = (wend * dw + cols + drate * rate_of) * sigmoid(raw)
        dstep = jnp.where(lane < HL, dstep, 0.0)
        lin[rows, CS:CA] = dstep.astype(bf16)
        head_grads[0:1, :] += jnp.sum(dstep, 0, keepdims=True)
        head_grads[1:2, :] += jnp.sum(drate * steps * rate_of, 0, keepdims=True)
        head_grads[2:3, :] += jnp.sum(fold(grad_y * x), 0, keepdims=True)
        slope = sig * (1.0 + v * (1.0 - sig))
        dx = chan[1:2, :] * grad_y + weight_x * bd + jnp.concatenate(inner, axis=1)
        dg = dgram.astype(bf16)
        db = tn(dg, cl) + nt((weight_x * x).astype(bf16), d1l)
        dc = nn(dg, bl) + nt((ecum_x * grad_y).astype(bf16), s0l)
        dpre[rows, 0:WI] = dx * slope[:, :WI]
        dpre[rows, WI : WI + N] = db * slope[:, WI : WI + N]
        dpre[rows, WI + N : CH] = dc * slope[:, WI + N :]

    edge = swap(edge_out, edge_in, 2)

    def keys_back(i):
        rows = rows_of(i)
        v = key_values(0, rows) + kv_in[rows, :].astype(f32)
        cosine, sine = rotary_of(table, rows)
        cosine = jnp.where(low128, cosine, 1.0)
        sine = jnp.where(low128, sine, 0.0)
        lin[rows, CK:CS] = (v * cosine - swap_half(v) * sine).astype(bf16)

    def conv_back(b):
        rows = rows_of(b)
        later = dpre[pl.ds(pl.multiple_of(b * L, L), L + 8), :]
        earlier = pad[pl.ds(pl.multiple_of(b * L, L), L + 16), :].astype(f32)
        g = later[0:L]
        conv_grads[4:5, :] += jnp.sum(g, 0, keepdims=True)
        total = jnp.zeros_like(g)
        for j in range(CONVW):
            total = total + taps[j : j + 1, :] * later[CONVW - 1 - j : CONVW - 1 - j + L]
            conv_grads[j : j + 1, :] += jnp.sum(g * earlier[13 + j : 13 + j + L], 0, keepdims=True)
        lin[rows, CX:CQ] = total.astype(bf16)

    def part(b, owner):
        return pl.ds(pl.multiple_of(b * L + owner * sub, sub), sub)

    def kept(b):
        return rows_of(b, sub)

    grads_in = SquareScatter((g0, g1, g2, g3), (gs, gr))
    lows = SquareGather(low, part, (hs, hr))

    def product(b):
        rows = rows_of(b)
        back[...] = nt(lin[rows, CZ:CQ], wf2[...]) + nt(lin[rows, CQ:CA], wf1[...])
        gown[kept(b), :] = back[kept(tp), :]
        grads_in.start(b, back, kept)

    gain_one[...] = jnp.zeros_like(gain_one)

    def norm_back(b):
        own = part(b, tp)
        g = gown[kept(b), :] + grads_in.finish(b)
        x = hid_own[kept(b), :].astype(f32)
        scale = lax.rsqrt(jnp.mean(x * x, -1, keepdims=True) + EPS)
        unit = x * scale
        gain_one[...] += jnp.broadcast_to(jnp.sum(g * unit, 0, keepdims=True), (8, D))
        weighted = g * gains[0:1, :]
        mean = jnp.mean(weighted * unit, -1, keepdims=True)
        low[own, :] = (grad_own[kept(b), :] + scale * (weighted - unit * mean)).astype(bf16)
        lows.start(b)

    def early_grads(i):
        feats = rows_of(i)
        grads_e[feats, 0:WI] = tn(normed[:, feats], lin[:, CZ:CX]).astype(bf16)
        grads_e[feats, WI:] = tn(normed[:, feats], lin[:, CQ:CS]).astype(bf16)

    def step(k):
        @pl.when(k < blocks)
        def scan():
            scan_back(lax.rem(2 * blocks - 1 - k + c, blocks))

        @pl.when(k == 0)
        def first():
            @pl.when(c > 0)
            def give():
                edge_out[...] = dpre[0:8, :]
                edge.start()

            pairs.wait_recv()
            loop(blocks, keys_back)
            loop(D // L, early_grads)
            scatter0.start()
            dpre[pl.ds(t, 8), :] = jnp.zeros((8, CH), f32)

            @pl.when(c == 0)
            def take():
                edge.wait_recv()
                dpre[pl.ds(t, 8), :] = edge_in[...]

        @pl.when(k >= 1)
        def there():
            conv_back(blocks - k)
            product(blocks - k)

        @pl.when(k == 1)
        def on():
            scatter0.middle()

        @pl.when(k == 3)
        def further():
            scatter0.relay()

        @pl.when(k >= 2)
        def over():
            grads_in.relay(blocks + 1 - k)

        @pl.when(k >= 3)
        def again():
            norm_back(blocks + 2 - k)

        @pl.when(k >= 4)
        def last():
            lows.relay(blocks + 3 - k)

    loop(blocks + 1, step)
    vec_core = remote(small, vec_sib, vcs.at[0], vcr.at[0], ctx=1 - c)
    vec_core.start()

    def weight_grads(i):
        feats = rows_of(i)
        grads_l[feats, :] = tn(normed[:, feats], lin[:, CX:CQ]).astype(bf16)
        misc[feats, :] = tn(normed[:, feats], lin[:, CS:CA])

    loop(D // L, weight_grads)
    scatter1.start()
    grads_in.relay(0)
    norm_back(1)
    lows.relay(2)

    def vec_to_shard(k):
        zz = lax.rem(z + k, shards)
        return remote(vec_z.at[z], vec_z.at[z], vzs.at[zz], vzr.at[z], shard=zz)

    def vec_from_shard(k):
        zz = lax.rem(z + k, shards)
        return remote(vec_z.at[z], vec_z.at[zz], vzs.at[zz], vzr.at[zz], shard=zz)

    vec_core.wait_recv()
    vec_z[z] = small[...] + vec_sib[...]
    loop(shards - 1, lambda k: vec_to_shard(k + 1).start())
    scatter1.middle()
    norm_back(0)
    lows.relay(1)
    gain_rows = jnp.where(iota((8, D), 0) == 0, gain_one[...], gain_two[...])
    row, lane8 = iota((8, 128), 0), iota((8, 128), 1)
    pick = ((row < 2) & (lane8 == GAIN_COL + row)).astype(f32)
    misc_low[...] = (misc[...] + tn(gain_rows, pick, HI)).astype(bf16)
    scatter2.start()
    get_own.wait()
    total = own_out[...].astype(f32)
    for d in range(1, TP):
        out_from(d).wait_recv()
        total = total + orecv[d - 1].astype(f32)
    output[...] = total.astype(bf16)
    scatter1.relay()
    scatter2.middle()
    lows.relay(0)
    loop(shards - 1, lambda k: vec_from_shard(k + 1).wait_recv())
    vecs[tp] = lax.fori_loop(1, shards, lambda k, total: total + vec_z[k], vec_z[0])
    for d in range(1, TP):
        to_all(vecs, vts, vtr, d).start()
    scatter.finish(grad_b)
    moves.put("grad_b")
    scatter2.relay()
    scatter0.finish(grad_e)
    scatter1.finish(grad_l)
    scatter2.finish(misc_sum)
    few = grad_e.shape[0] // TP
    for i in range(TP):
        shsend[i, :, 0:256] = grad_l[i * few : (i + 1) * few, WI:CH]
        shsend[i, :, 256:384] = grad_e[i * few : (i + 1) * few, WI + 128 : CH]
        shsend[i, :, 384:512] = misc_sum[i * few : (i + 1) * few, :]

    def share_to(d):
        return remote(shsend.at[peer(d)], shared.at[tp], ss.at[d], sr.at[tp], tp=peer(d))

    def share_from(d):
        return remote(shsend.at[peer(d)], shared.at[peer(d)], ss.at[d], sr.at[peer(d)], tp=peer(d))

    for d in range(1, TP):
        share_to(d).start()
    shared[tp] = shsend[tp]

    def arrived(b):
        lows.finish(b)
        lows.sent(b)
        grads_in.sent(b)

    loop(blocks, arrived)
    for d in range(1, TP):
        share_from(d).wait_recv()
        from_all(vecs, vts, vtr, d).wait_recv()

    @pl.when(c > 0)
    def given():
        edge.wait_send()

    for copy in (states, pairs, vec_core):
        copy.wait_send()
    loop(shards - 1, lambda k: vec_to_shard(k + 1).wait_send())
    for d in range(1, TP):
        out_to(d).wait_send()
        share_to(d).wait_send()
        to_all(vecs, vts, vtr, d).wait_send()


def backward(shards, *args):
    t = args[0].shape[0]
    rows = D // (2 * shards)
    blocks, sub = t // L, L // TP
    vec = (8, CH + WI + 128)
    out = [
        ((t, D // TP), bf16),
        ((t, D), bf16),
        ((rows, CH), f32),
        ((rows, CH), f32),
        ((rows, CB), f32),
        ((TP, rows // TP, 512), f32),
        ((TP, *vec), f32),
    ]
    dma = pltpu.SemaphoreType.DMA
    scratch = (
        [
            pltpu.VMEM((t, 128), f32),
            pltpu.VMEM((t, D // TP), bf16),
            pltpu.VMEM((t, CA), bf16),
            pltpu.VMEM(vec, f32),
            pltpu.VMEM((TP - 1, t, D // TP), bf16),
            pltpu.VMEM((2, t, 128), f32),
            pltpu.VMEM((2, t, 128), f32),
            pltpu.VMEM((t, WI), f32),
            pltpu.VMEM((t + 8, CH), f32),
            pltpu.VMEM((t // L, N, WI), f32),
            pltpu.VMEM((N, WI), f32),
            pltpu.VMEM((N, WI), f32),
            pltpu.VMEM((t, 128), bf16),
            pltpu.VMEM((t, 128), bf16),
            pltpu.VMEM((t + 16, CH), bf16),
            pltpu.VMEM((8, CH), f32),
            pltpu.VMEM((8, CH), f32),
            pltpu.VMEM((blocks * sub, D), f32),
            pltpu.VMEM((L, D), f32),
            pltpu.VMEM((8, D), f32),
            pltpu.VMEM((D, CH), bf16),
            pltpu.VMEM((D, CH), bf16),
            pltpu.VMEM((D, 128), f32),
            pltpu.VMEM((D, 128), bf16),
            pltpu.VMEM((rows, 128), f32),
            pltpu.VMEM((TP, rows // TP, 512), f32),
            pltpu.VMEM(vec, f32),
            pltpu.VMEM((shards, *vec), f32),
        ]
        + LineSum.scratch(shards, D, CB)
        + Scatter.scratch(shards, D, CH)
        + Scatter.scratch(shards, D, CH)
        + Scatter.scratch(shards, D, 128)
        + SquareScatter.scratch(blocks, sub)
        + [dma(()), dma(()), dma((1,)), dma((1,)), dma((shards,)), dma((shards,)), dma((3,)), dma((3,))]
        + [dma((TP,))] * 6
        + [dma((TP, blocks))] * 4
    )
    return call_staged(
        functools.partial(backward_kernel, shards),
        args,
        out,
        dict(zip(BACKWARD_LATE, BACKWARD_AT)),
        {"grad_b": 4},
        scratch,
        left=(5, len(args) - 2),
        compiler_params=pltpu.CompilerParams(
            collective_id=3, has_side_effects=True, vmem_limit_bytes=VMOST
        ),
        name="mix_backward",
    )


def pack_kernel(
    low, output, grad_e, grad_l, grad_b, shared, vecs,
    grad_hidden, out, g_z, g_x, g_q, g_gate, g_up, g_out, g_o, g_down, g_shared, g_dt, g_one,
    g_two, g_conv, g_conv_b, g_gate_gain, g_bias, g_decay, g_skip, g_chan,
):
    grad_hidden[...] = low[...].astype(f32)
    out[...] = output[...]

    @pl.when(pl.program_id(0) == 0)
    def rest():
        g_z[...] = grad_e[:, 0:WI]
        g_x[...] = grad_l[:, 0:WI]
        g_q[...] = grad_e[:, WI : WI + 128]
        g_gate[...] = grad_b[:, CG:CU]
        g_up[...] = grad_b[:, CU:CD]
        g_out[...] = turned_over(grad_b[:, CO:CW])
        g_o[...] = turned_over(grad_b[:, CW:CG])
        g_down[...] = turned_over(grad_b[:, CD:CB])
        first, second = shared[0] + shared[1], shared[2] + shared[3]
        both = first + second
        g_shared[:, 0 : 2 * N] = both[:, 0 : 2 * N]
        kv1, kv2 = first[:, 256:384], second[:, 256:384]
        low_half = low_lanes(kv1.shape)
        g_shared[:, 2 * N : 2 * N + 128] = jnp.where(low_half, kv1, pltpu.roll(kv2, 64, 1))
        g_shared[:, 2 * N + 128 :] = jnp.where(low_half, pltpu.roll(kv1, 64, 1), kv2)
        gains = turned_over(both[:, 384:512])[GAIN_COL : GAIN_COL + 8]
        g_one[...] = gains[0]
        g_two[...] = gains[1]
        steps = jnp.zeros((both.shape[0], 128), f32)
        heads = jnp.zeros((8, 128), f32)
        g_chan[...] = jnp.zeros_like(g_chan)
        for i in range(TP):
            lane = iota(steps.shape, 1) // HL == i
            steps = jnp.where(lane, pltpu.roll(shared[i, :, 384:512], i * HL, 1), steps)
            lane = iota(heads.shape, 1) // HL == i
            heads = jnp.where(lane, pltpu.roll(vecs[i, :, CH + WI : CH + WI + 128], i * HL, 1), heads)
            mine = slice(i * WI, (i + 1) * WI)
            g_conv[:, mine] = vecs[i, 0:CONVW, 0:WI]
            g_chan[0:1, mine] = vecs[i, CONVW : CONVW + 1, 0:WI]
            g_chan[1:2, mine] = vecs[i, 0:1, CH : CH + WI]
        maps = vecs[0, :, WI:CH] + vecs[1, :, WI:CH] + vecs[2, :, WI:CH] + vecs[3, :, WI:CH]
        g_conv[:, DI:] = maps[0:CONVW]
        g_chan[0:1, DI:] = maps[CONVW : CONVW + 1]
        g_dt[...] = turned_over(steps)[0:H]
        g_bias[...] = heads[0, 0:H]
        g_decay[...] = heads[1, 0:H]
        g_skip[...] = heads[2, 0:H]
        g_conv_b[...] = g_chan[0, :]
        g_gate_gain[...] = g_chan[1, 0:DI]


def pack(low, output, grad_e, grad_l, grad_b, shared, vecs):
    t, r, few = low.shape[0], grad_e.shape[0], shared.shape[1]
    out = [
        (t, D), output.shape, (r, WI), (r, WI), (r, 128), (r, FFL), (r, FFL), (WI, r), (128, r), (FFL, r),
        (few, 512), (H, few), (few,), (few,), (CONVW, DI + 2 * N), (DI + 2 * N,), (DI,), (H,), (H,),
        (H,),
    ]
    rows = pl.BlockSpec((L, D), lambda i: (i, 0))
    few_rows = pl.BlockSpec((L, output.shape[1]), lambda i: (i, 0))
    kinds = [f32, bf16] + [f32] * (len(out) - 2)

    def whole(shape):
        return pl.BlockSpec(shape, lambda i: (0,) * len(shape))

    return pl.pallas_call(
        pack_kernel,
        grid=(t // L,),
        out_shape=[jax.ShapeDtypeStruct(o, k) for o, k in zip(out, kinds)],
        in_specs=[rows, few_rows] + [whole(v.shape) for v in (grad_e, grad_l, grad_b, shared, vecs)],
        out_specs=[rows, few_rows] + [whole(o) for o in out[2:]],
        scratch_shapes=[pltpu.VMEM((8, DI + 2 * N), f32)],
        compiler_params=pltpu.CompilerParams(vmem_limit_bytes=VLIMIT),
        name="lay_out",
    )(low, output, grad_e, grad_l, grad_b, shared, vecs)


def rotary_table(count):
    inverse = rope_base ** (-2.0 * np.arange(HD // 2, dtype=np.float32) / HD)
    angles = np.arange(count, dtype=np.float32)[:, None] * inverse.astype(np.float32)[None, :]
    both = np.concatenate([np.cos(angles), np.sin(angles)], axis=1)
    return np.tile(both, (1, 2)).astype(np.float32)


def local(
    hidden, cotangent, lengths, norm1_gain, w_z, w_x, w_shared, w_dt, dt_bias, a_log, d_skip,
    conv_w, conv_b, gated_gain, w_out, w_q, w_o, norm2_gain, w_gate, w_up, w_down,
):
    t = hidden.shape[1]
    shards = lax.axis_size("shard")
    hid, cot = hidden[0], cotangent[0]
    table = jnp.asarray(rotary_table(lax.axis_size("ctx") * t))
    (
        wf1, wf2, wo, wg, normed, gains, z, cin, dt, taps, prm, chan,
        pre, hist, q_low, kk, vv, att, att_low, lse_row, ssd, start, steps, cum, tot, gl, square,
    ) = forward(
        shards, hid, w_z, w_x, w_shared, w_dt.T, w_q, w_out, w_o, w_gate,
        norm1_gain[None], norm2_gain[None], conv_w, conv_b, gated_gain, dt_bias, a_log, d_skip,
        table, lengths,
    )
    osend, grad_own, chip, hid_own, gain_two, ggl, grad_att, dots = ffn(
        shards, hid, cot, gl, att_low, square, wo, wg, w_up, w_down, gains, lengths
    )
    output, grad_hidden, grad_e, grad_l, grad_b, shared, vecs = backward(
        shards, ggl, grad_att, dots, square, chip, osend, pre, cin, hist, q_low, kk, vv, att,
        lse_row, ssd, start, steps, cum, tot, dt, z, taps, prm, chan, normed, wf1, wf2,
        hid_own, grad_own, gains, gain_two, table, lengths,
    )
    (
        grad_full, output_full, g_z, g_x, g_q, g_gate, g_up, g_out, g_o, g_down, g_shared, g_dt, g_one,
        g_two, g_conv, g_conv_b, g_gate_gain, g_bias, g_decay, g_skip,
    ) = pack(grad_hidden, output, grad_e, grad_l, grad_b, shared, vecs)
    return (
        output_full[None],
        grad_full[None],
        g_one,
        g_z,
        g_x,
        g_shared,
        g_dt.T,
        g_bias,
        g_decay,
        g_skip,
        g_conv,
        g_conv_b,
        g_gate_gain,
        g_out,
        g_q,
        g_o,
        g_two,
        g_gate,
        g_up,
        g_down,
    )


def solution(mesh):
    placed = (
        P("shard", "ctx", None),
        P("shard", "ctx", None),
        P("shard"),
        P(("shard", "ctx")),
        P(("shard", "ctx"), "tp"),
        P(("shard", "ctx"), "tp"),
        P(("shard", "ctx"), None),
        P(("shard", "ctx"), None),
        P(),
        P(),
        P(),
        P(),
        P(),
        P(),
        P("tp", ("shard", "ctx")),
        P(("shard", "ctx"), "tp"),
        P("tp", ("shard", "ctx")),
        P(("shard", "ctx")),
        P(("shard", "ctx"), "tp"),
        P(("shard", "ctx"), "tp"),
        P("tp", ("shard", "ctx")),
    )
    return jax.shard_map(
        local,
        mesh=mesh,
        in_specs=placed,
        out_specs=(
            P("shard", "ctx", "tp"),
            P("shard", "ctx", None),
            P(("shard", "ctx", "tp")),
            P(("shard", "ctx"), "tp"),
            P(("shard", "ctx"), "tp"),
            P(("shard", "ctx", "tp"), None),
            P(("shard", "ctx", "tp"), None),
            P(),
            P(),
            P(),
            P(),
            P(),
            P(),
            P("tp", ("shard", "ctx")),
            P(("shard", "ctx"), "tp"),
            P("tp", ("shard", "ctx")),
            P(("shard", "ctx", "tp")),
            P(("shard", "ctx"), "tp"),
            P(("shard", "ctx"), "tp"),
            P("tp", ("shard", "ctx")),
        ),
        check_vma=False,
    )
```
